32 devices in a mesh: img: 8 (over y, x, core), rows: 4 (over z).
Axes of the slice: x: 2, y: 2, z: 4, core: 2. Of those that a mesh axis runs over, the one named last changes fastest.
Arguments:
- image_in: bfloat16 [640, 16, 16, 1024], P('img', 'rows'), may hold values from -8 to 8, as said below
- extent: int32 [640], P('img'), may hold values from 6 to 14, as said below
- weight_in1: bfloat16 [1024, 512], replicated, may hold values from -0.1875 to 0.1875
- weight_mid1: bfloat16 [512, 3, 3, 512], replicated, may hold values from -0.09375 to 0.09375
- weight_out1: bfloat16 [512, 2048], replicated, may hold values from -0.25 to 0.25
- weight_skip: bfloat16 [1024, 2048], replicated, may hold values from -0.1875 to 0.1875
- weight_in2: bfloat16 [2048, 512], replicated, may hold values from -0.125 to 0.125
- weight_mid2: bfloat16 [512, 3, 3, 512], replicated, may hold values from -0.09375 to 0.09375
- weight_out2: bfloat16 [512, 2048], replicated, may hold values from -0.25 to 0.25
- gain_in1: float32 [512], replicated, may hold values from 0.5 to 1.5
- shift_in1: float32 [512], replicated, may hold values from 0.2 to 1.2
- gain_mid1: float32 [512], replicated, may hold values from 0.5 to 1.5
- shift_mid1: float32 [512], replicated, may hold values from 0.2 to 1.2
- gain_out1: float32 [2048], replicated, may hold values from 0.5 to 1.5
- shift_out1: float32 [2048], replicated, may hold values from 0.2 to 1.2
- gain_skip: float32 [2048], replicated, may hold values from 0.5 to 1.5
- shift_skip: float32 [2048], replicated, may hold values from 0.2 to 1.2
- gain_in2: float32 [512], replicated, may hold values from 0.5 to 1.5
- shift_in2: float32 [512], replicated, may hold values from 0.2 to 1.2
- gain_mid2: float32 [512], replicated, may hold values from 0.5 to 1.5
- shift_mid2: float32 [512], replicated, may hold values from 0.2 to 1.2
- gain_out2: float32 [2048], replicated, may hold values from 0.5 to 1.5
- shift_out2: float32 [2048], replicated, may hold values from 0.2 to 1.2
- cotangent: bfloat16 [640, 8, 8, 2048], P('img', 'rows'), may hold values from -6 to 6
Outputs:
- block_out: bfloat16 [640, 8, 8, 2048], P('img', 'rows')
- grad_image: bfloat16 [640, 16, 16, 1024], P('img', 'rows')
- grad_weight_in1: float32 [1024, 512], P('img')
- grad_weight_mid1: float32 [512, 3, 3, 512], P('img')
- grad_weight_out1: float32 [512, 2048], P('img')
- grad_weight_skip: float32 [1024, 2048], P('img')
- grad_weight_in2: float32 [2048, 512], P('img')
- grad_weight_mid2: float32 [512, 3, 3, 512], P('img')
- grad_weight_out2: float32 [512, 2048], P('img')
- grad_gain_in1: float32 [512], replicated
- grad_shift_in1: float32 [512], replicated
- grad_gain_mid1: float32 [512], replicated
- grad_shift_mid1: float32 [512], replicated
- grad_gain_out1: float32 [2048], replicated
- grad_shift_out1: float32 [2048], replicated
- grad_gain_skip: float32 [2048], replicated
- grad_shift_skip: float32 [2048], replicated
- grad_gain_in2: float32 [512], replicated
- grad_shift_in2: float32 [512], replicated
- grad_gain_mid2: float32 [512], replicated
- grad_shift_mid2: float32 [512], replicated
- grad_gain_out2: float32 [2048], replicated
- grad_shift_out2: float32 [2048], replicated
The draws below stay inside these ranges and needn't reach their ends.
Inputs may be any that keep to these rules, and one draw needn't show every extreme that they name: `extent`: each image's valid height and width within its padded map: 14 for a global view or 6 for a small crop, and both kinds occur in every draw; pixels at or past it are padding. `image_in`: activations of the previous section; padding pixels hold values that the mask removes.
All inputs are finite; a program needn't handle non-finite values.
Results may differ from the reference program's by a relative error of at most 0.02.
Values may be sent and summed in bfloat16 or wider, within the bound.
A program may use at most 384 MiB of HBM per device.

```python
import jax
import jax.numpy as jnp
from jax import lax

IN = 1024
MID = 512
OUT = 2048
GRID = 16
NB = 640


def draw_image_in(key, part):
    key_noise, key_direction = jax.random.split(key)
    position = jnp.arange(NB, dtype=jnp.float32) / max(NB - 1, 1)
    spread_img = 0.6 + 1.2 * position
    offset = 0.5 * position
    normal_part = jax.random.normal(key_noise, (NB, GRID, GRID, IN), jnp.float32)
    direction = jax.random.normal(key_direction, (IN,), jnp.float32)
    values = normal_part * spread_img[:, None, None, None] + offset[:, None, None, None] * direction
    return jnp.clip(values, -8.0, 8.0).astype(jnp.bfloat16)


def draw_extent(key, part):
    chooser = jax.random.randint(key, (NB,), 0, 3)
    valid_side = jnp.where(chooser == 0, 14, 6).astype(jnp.int32)
    return valid_side.at[0].set(14).at[NB - 1].set(6)


def block_scale(key, dims, cuts, low, largest):
    def one(dim, parts):
        heights = jax.random.uniform(jax.random.fold_in(jax.random.fold_in(key, 6), dim), (parts,), jnp.float32, low / len(cuts), largest / len(cuts))
        return jnp.repeat(jnp.exp(heights), dims[dim] // parts).reshape((-1,) + (1,) * (len(dims) - dim - 1))

    factor_of = one(*cuts[0])
    for cut in cuts[1:]:
        factor_of = factor_of * one(*cut)
    return factor_of


def bell_draw(stream_key, dims, deviation, reach, pieces=(), kind=jnp.bfloat16):
    drawn = deviation * jax.random.normal(stream_key, dims, jnp.float32)
    if pieces:
        drawn = drawn * block_scale(stream_key, dims, pieces, -0.22, 0.18)
    return jnp.clip(drawn, -reach, reach).astype(kind)


def setup_inputs(seed: int = 0) -> dict:
    splits = jax.random.split(jax.random.key(seed), 25)
    return {
        "image_in": draw_image_in(jax.random.fold_in(splits[24], 71), 0),
        "extent": draw_extent(jax.random.fold_in(splits[24], 71), 0),
        "weight_in1": bell_draw(splits[2], (IN, MID), IN ** -0.5, 0.1875),
        "weight_mid1": bell_draw(splits[3], (MID, 3, 3, MID), (9 * MID) ** -0.5, 0.09375),
        "weight_out1": bell_draw(splits[4], (MID, OUT), MID ** -0.5, 0.25),
        "weight_skip": bell_draw(splits[5], (IN, OUT), IN ** -0.5, 0.1875),
        "weight_in2": bell_draw(splits[6], (OUT, MID), OUT ** -0.5, 0.125),
        "weight_mid2": bell_draw(splits[7], (MID, 3, 3, MID), (9 * MID) ** -0.5, 0.09375),
        "weight_out2": bell_draw(splits[8], (MID, OUT), MID ** -0.5, 0.25),
        "gain_in1": jnp.clip(jax.random.uniform(splits[9], (MID,), jnp.float32, 0.5, 1.5), 0.5, 1.5),
        "shift_in1": jnp.clip(jax.random.uniform(splits[10], (MID,), jnp.float32, 0.2, 1.2), 0.2, 1.2),
        "gain_mid1": jnp.clip(jax.random.uniform(splits[11], (MID,), jnp.float32, 0.5, 1.5), 0.5, 1.5),
        "shift_mid1": jnp.clip(jax.random.uniform(splits[12], (MID,), jnp.float32, 0.2, 1.2), 0.2, 1.2),
        "gain_out1": jnp.clip(jax.random.uniform(splits[13], (OUT,), jnp.float32, 0.5, 1.5), 0.5, 1.5),
        "shift_out1": jnp.clip(jax.random.uniform(splits[14], (OUT,), jnp.float32, 0.2, 1.2), 0.2, 1.2),
        "gain_skip": jnp.clip(jax.random.uniform(splits[15], (OUT,), jnp.float32, 0.5, 1.5), 0.5, 1.5),
        "shift_skip": jnp.clip(jax.random.uniform(splits[16], (OUT,), jnp.float32, 0.2, 1.2), 0.2, 1.2),
        "gain_in2": jnp.clip(jax.random.uniform(splits[17], (MID,), jnp.float32, 0.5, 1.5), 0.5, 1.5),
        "shift_in2": jnp.clip(jax.random.uniform(splits[18], (MID,), jnp.float32, 0.2, 1.2), 0.2, 1.2),
        "gain_mid2": jnp.clip(jax.random.uniform(splits[19], (MID,), jnp.float32, 0.5, 1.5), 0.5, 1.5),
        "shift_mid2": jnp.clip(jax.random.uniform(splits[20], (MID,), jnp.float32, 0.2, 1.2), 0.2, 1.2),
        "gain_out2": jnp.clip(jax.random.uniform(splits[21], (OUT,), jnp.float32, 0.5, 1.5), 0.5, 1.5),
        "shift_out2": jnp.clip(jax.random.uniform(splits[22], (OUT,), jnp.float32, 0.2, 1.2), 0.2, 1.2),
        "cotangent": bell_draw(splits[23], (NB, GRID // 2, GRID // 2, OUT), 1.0, 6.0, ((0, 8), (1, 4))),
    }


@jax.custom_vjp
def low(v):
    return lax.optimization_barrier(v.astype(jnp.bfloat16)).astype(jnp.float32)

@jax.custom_vjp
def low_back(v):
    return v

def low_keep(v):
    return (low(v), None)

def low_pass(kept, grad):
    return (grad,)

def back_keep(v):
    return (v, None)

def back_low(kept, grad):
    return (low(grad),)
low.defvjp(low_keep, low_pass)
low_back.defvjp(back_keep, back_low)
EPSILON = 1e-05
HIGHEST_PRECISION = lax.Precision.HIGHEST

def pixel_masks(extent):
    full_rows = jnp.arange(GRID, dtype=jnp.int32)
    half_rows = jnp.arange(GRID // 2, dtype=jnp.int32)
    inside = (full_rows[None, :] < extent[:, None]).astype(jnp.float32)
    inside_low = (half_rows[None, :] < (extent // 2)[:, None]).astype(jnp.float32)
    mask_in = (inside[:, :, None] * inside[:, None, :])[..., None]
    mask_out = (inside_low[:, :, None] * inside_low[:, None, :])[..., None]
    return (mask_in, mask_out)

def pointwise(values, weight):
    return jnp.einsum('bhwc,cd->bhwd', values, weight, precision=HIGHEST_PRECISION)

def batch_norm(values, validity, pixels, gain_vector, shift_vector):
    centre = lax.optimization_barrier(jnp.sum(values * validity, axis=(0, 1, 2))) / pixels
    centred = values - centre
    spread = lax.optimization_barrier(jnp.sum(centred * centred * validity, axis=(0, 1, 2))) / pixels
    return centred * lax.rsqrt(spread + EPSILON) * gain_vector + shift_vector

def strided(values, weight):
    padded = jnp.pad(values, ((0, 0), (1, 0), (1, 0), (0, 0)))
    length = values.shape[1]
    running = jnp.zeros((values.shape[0], length // 2, length // 2, weight.shape[3]), jnp.float32)
    for row_tap in range(3):
        for col_tap in range(3):
            window = padded[:, row_tap:row_tap + length:2, col_tap:col_tap + length:2, :]
            running = running + jnp.einsum('bhwc,cd->bhwd', window, weight[:, row_tap, col_tap, :], precision=HIGHEST_PRECISION)
    return running

def padded_conv(values, weight):
    padded = jnp.pad(values, ((0, 0), (1, 1), (1, 1), (0, 0)))
    length = values.shape[1]
    running = jnp.zeros((values.shape[0], length, length, weight.shape[3]), jnp.float32)
    for row_tap in range(3):
        for col_tap in range(3):
            window = padded[:, row_tap:row_tap + length, col_tap:col_tap + length, :]
            running = running + jnp.einsum('bhwc,cd->bhwd', window, weight[:, row_tap, col_tap, :], precision=HIGHEST_PRECISION)
    return running

def reference(image_in, extent, weight_in1, weight_mid1, weight_out1, weight_skip, weight_in2, weight_mid2, weight_out2, gain_in1, shift_in1, gain_mid1, shift_mid1, gain_out1, shift_out1, gain_skip, shift_skip, gain_in2, shift_in2, gain_mid2, shift_mid2, gain_out2, shift_out2, cotangent):
    mask_in, mask_out = pixel_masks(extent)
    pixel_in = jnp.sum(mask_in)
    pixel_out = jnp.sum(mask_out)
    params = (weight_in1.astype(jnp.float32), weight_mid1.astype(jnp.float32), weight_out1.astype(jnp.float32), weight_skip.astype(jnp.float32), weight_in2.astype(jnp.float32), weight_mid2.astype(jnp.float32), weight_out2.astype(jnp.float32), gain_in1, shift_in1, gain_mid1, shift_mid1, gain_out1, shift_out1, gain_skip, shift_skip, gain_in2, shift_in2, gain_mid2, shift_mid2, gain_out2, shift_out2)

    def forward(image, weights):
        kernel_in1, kernel_mid1, kernel_out1, kernel_skip, kernel_in2, kernel_mid2, kernel_out2, scale_in1, offset_in1, scale_mid1, offset_mid1, scale_out1, offset_out1, scale_skip, offset_skip, scale_in2, offset_in2, scale_mid2, offset_mid2, scale_out2, offset_out2 = weights
        masked = image * mask_in
        conv_out = low_back(pointwise(masked, kernel_in1))
        hidden = low(mask_in * jax.nn.silu(batch_norm(conv_out, mask_in, pixel_in, scale_in1, offset_in1)))
        conv_out = low_back(strided(hidden, kernel_mid1))
        hidden = low(mask_out * jax.nn.silu(batch_norm(conv_out, mask_out, pixel_out, scale_mid1, offset_mid1)))
        conv_out = low_back(pointwise(hidden, kernel_out1))
        branch = batch_norm(conv_out, mask_out, pixel_out, scale_out1, offset_out1)
        conv_skip = low_back(pointwise(masked[:, ::2, ::2, :], kernel_skip))
        first_out = mask_out * jax.nn.silu(branch + batch_norm(conv_skip, mask_out, pixel_out, scale_skip, offset_skip))
        first_low = low(first_out)
        conv_out = low_back(pointwise(first_low, kernel_in2))
        hidden = low(mask_out * jax.nn.silu(batch_norm(conv_out, mask_out, pixel_out, scale_in2, offset_in2)))
        conv_out = low_back(padded_conv(hidden, kernel_mid2))
        hidden = low(mask_out * jax.nn.silu(batch_norm(conv_out, mask_out, pixel_out, scale_mid2, offset_mid2)))
        conv_out = low_back(pointwise(hidden, kernel_out2))
        return mask_out * jax.nn.silu(batch_norm(conv_out, mask_out, pixel_out, scale_out2, offset_out2) + first_out)
    exact_out, pullback = jax.vjp(forward, image_in.astype(jnp.float32), params)
    grad_image, grads = pullback(cotangent.astype(jnp.float32))
    return (exact_out.astype(jnp.bfloat16), grad_image.astype(jnp.bfloat16), grads[0], grads[1], grads[2], grads[3], grads[4], grads[5], grads[6], grads[7], grads[8], grads[9], grads[10], grads[11], grads[12], grads[13], grads[14], grads[15], grads[16], grads[17], grads[18], grads[19], grads[20])
```

```python
import functools

import jax
import jax.numpy as jnp
import numpy as np
from jax import lax
from jax.experimental import pallas as pl
from jax.experimental.pallas import tpu as pltpu
from jax.sharding import PartitionSpec as P

EPSILON = 1e-05
F32 = jnp.float32
BF16 = jnp.bfloat16
LANES = 512
ROWS = 32
IMAGES = 16
VMEM_BYTES = 56 * 1024 * 1024
MESH = pl.DeviceIdType.MESH


def dot(a, b):
    return jnp.dot(a, b, preferred_element_type=F32)


def dot_t(a, b):
    return lax.dot_general(a, b, (((1,), (1,)), ((), ())), preferred_element_type=F32)


def load(ref, rows, lanes):
    value = ref[rows, lanes].astype(F32)
    return value.reshape(value.shape[0] // 8, 8, value.shape[1])


def store(ref, rows, lanes, value):
    ref[rows, lanes] = value.reshape(value.shape[0] * 8, value.shape[2]).astype(ref.dtype)


def load_mask(ref, rows):
    mask = load(ref, rows, slice(None))
    return jnp.concatenate([mask] * (LANES // 128), axis=-1)


def sweep(total, step, init, rows=ROWS):
    def body(i, carry):
        return step(pl.ds(pl.multiple_of(i * rows, rows), rows), i, carry)

    return lax.fori_loop(0, total // rows, body, init)


def lane_blocks(width):
    return [slice(k * LANES, (k + 1) * LANES) for k in range(width // LANES)]


def tall(row):
    return jnp.broadcast_to(row, (8, row.shape[-1]))


def column_sum(value):
    return jnp.sum(value, axis=0)


def total_of(part):
    return jnp.sum(part, axis=0, keepdims=True)


def zeros8():
    return jnp.zeros((8, LANES), F32)


def tally(first, parts, centre_ref, stats_ref):
    width = parts[0][0].shape[-1]

    @pl.when(first)
    def _():
        stats_ref[...] = jnp.zeros_like(stats_ref)

    for lanes in lane_blocks(width):
        sums = (zeros8(), zeros8())
        for acc, mask_ref, dev in parts:

            def add(rows, i, carry, acc=acc, mask_ref=mask_ref):
                mask = load_mask(mask_ref, rows)
                return (
                    carry[0] + column_sum(load(acc, rows, lanes) * mask),
                    carry[1] + column_sum(mask),
                )

            sums = sweep(acc.shape[0], add, sums)
        total, count = total_of(sums[0]), total_of(sums[1])
        centre = total / jnp.maximum(count, 1.0)
        centre_ref[:, lanes] = centre
        centre8 = tall(centre)
        squares = zeros8()
        for acc, mask_ref, dev in parts:

            def square(rows, i, carry, acc=acc, mask_ref=mask_ref, dev=dev):
                away = load(acc, rows, lanes) - centre8
                store(dev, rows, lanes, away)
                return carry + column_sum(load_mask(mask_ref, rows) * away * away)

            squares = sweep(acc.shape[0], square, squares)
        squares = total_of(squares)
        count_old, mean_old, squares_old = (
            stats_ref[0:1, lanes],
            stats_ref[1:2, lanes],
            stats_ref[2:3, lanes],
        )
        both = count_old + count
        share = count / jnp.maximum(both, 1.0)
        delta = centre - mean_old
        stats_ref[0:1, lanes] = both
        stats_ref[1:2, lanes] = mean_old + delta * share
        stats_ref[2:3, lanes] = squares_old + squares + delta * delta * count_old * share


def affine(stats_ref, gain_ref, shift_ref, centre_ref, lanes):
    scale = lax.rsqrt(stats_ref[2:3, lanes] + EPSILON)
    slope = gain_ref[:, lanes] * scale
    base = shift_ref[:, lanes] + (centre_ref[:, lanes] - stats_ref[1:2, lanes]) * slope
    return tall(0.5 * slope), tall(0.5 * base)


def silu_half(half):
    return half + half * jnp.tanh(half)


def gate_half(half):
    tanh = jnp.tanh(half)
    return (0.5 + 0.5 * tanh) * (1.0 + half * (1.0 - tanh))


def silu_and_gate(half):
    tanh = jnp.tanh(half)
    return half + half * tanh, (0.5 + 0.5 * tanh) * (1.0 + half * (1.0 - tanh))


def back_coefs(stats_ref, gain_ref, centre_ref, sums, lanes):
    shift_sum, gain_sum = sums
    pixels = stats_ref[0:1, lanes]
    scale = lax.rsqrt(stats_ref[2:3, lanes] + EPSILON)
    slope = gain_ref[:, lanes] * scale
    per_pixel = slope / pixels
    away = (centre_ref[:, lanes] - stats_ref[1:2, lanes]) * scale
    return (
        tall(slope),
        tall(-per_pixel * scale * gain_sum),
        tall(-per_pixel * (shift_sum + away * gain_sum)),
    )


def unit_sum(stats_ref, centre_ref, lanes, gn_sum, gd_sum):
    scale = lax.rsqrt(stats_ref[2:3, lanes] + EPSILON)
    return scale * (gd_sum + (centre_ref[:, lanes] - stats_ref[1:2, lanes]) * gn_sum)


def accumulate(first, ref, row, lanes, value):
    old = jnp.where(first, jnp.zeros_like(value), ref[row : row + 1, lanes])
    ref[row : row + 1, lanes] = old + value


def shifted(value, by):
    if by == 0:
        return value
    rolled = pltpu.roll(value, (-by) % 8, axis=1)
    column = lax.broadcasted_iota(jnp.int32, value.shape, 1)
    return jnp.where(column == (0 if by < 0 else 7), 0.0, rolled)


def from_above(value, edge, rows_low):
    if rows_low == 1:
        return edge
    images = value.shape[0] // rows_low
    image = value.reshape((images, rows_low) + value.shape[1:])
    return jnp.concatenate([edge[:, None], image[:, :-1]], axis=1).reshape(value.shape)


def from_below(value, edge, rows_low):
    if rows_low == 1:
        return edge
    images = value.shape[0] // rows_low
    image = value.reshape((images, rows_low) + value.shape[1:])
    return jnp.concatenate([image[:, 1:], edge[:, None]], axis=1).reshape(value.shape)


def edge_rows(i, rows_low):
    return pl.ds(pl.multiple_of(i * (ROWS // rows_low), ROWS // rows_low), ROWS // rows_low)


def first_step():
    return pl.program_id(0) == 0


def split_kernel(image_ref, perm_ref, mask_ref, weight_ref, planes_ref, dev_ref, centre_ref, stats_ref, acc):
    planes, low, _ = planes_ref.shape
    group = perm_ref.shape[0]
    part = group // planes
    for g in range(image_ref.shape[0] // group):
        mask = jnp.concatenate(
            [mask_ref[p, g * part : (g + 1) * part, :] for p in range(planes)], axis=0
        )
        mask = jnp.concatenate([mask] * (group // 128), axis=1)
        perm = (perm_ref[...].astype(F32) * mask).astype(BF16)
        moved = dot(perm, image_ref[g * group : (g + 1) * group, :]).astype(BF16)
        for p in range(planes):
            planes_ref[p, g * part : (g + 1) * part, :] = moved[p * part : (p + 1) * part]
    for p in range(planes):
        acc[p] = dot(planes_ref[p], weight_ref[...])
    tally(
        first_step(),
        [(acc.at[p], mask_ref.at[p], dev_ref.at[p]) for p in range(planes)],
        centre_ref,
        stats_ref,
    )


def skip_kernel(plane_ref, mask_ref, weight_ref, before_ref, dev_ref, centre_ref, stats_ref, acc, mine):
    acc[...] = dot(plane_ref[...], weight_ref[...])
    tally(first_step(), [(acc, mask_ref, dev_ref)], centre_ref, mine)
    start = before_ref.shape[1]
    stats_ref[:, :start] = before_ref[...]
    stats_ref[:, start:] = mine[...]


def mid1_kernel(
    rows_low,
    dev_in,
    centre_in,
    mask_ref,
    halo,
    halo_centre,
    halo_mask,
    stats_in,
    gain,
    shift,
    mask_out,
    weight,
    hidden,
    dev_out,
    centre_out,
    stats_out,
    taps,
    acc,
):
    low, width = acc.shape
    for lanes in lane_blocks(width):
        slope, base = affine(stats_in, gain, shift, centre_in, lanes)
        slope_edge, base_edge = affine(stats_in, gain, shift, halo_centre, lanes)

        def act(p, rows):
            mask = load_mask(mask_ref.at[p], rows)
            value = silu_half(load(dev_in.at[p], rows, lanes) * slope + base) * mask
            store(hidden.at[p], rows, lanes, value)
            return value

        def act_edge(q, i):
            rows = edge_rows(i, rows_low)
            half = load(halo.at[q], rows, lanes) * slope_edge + base_edge
            return silu_half(half) * load_mask(halo_mask.at[q], rows)

        def step(rows, i, carry):
            act(0, rows)
            store(taps.at[0], rows, lanes, shifted(act(1, rows), -1))
            store(taps.at[1], rows, lanes, from_above(act(2, rows), act_edge(0, i), rows_low))
            odd = act(3, rows)
            store(taps.at[2], rows, lanes, shifted(odd, -1))
            above = from_above(odd, act_edge(1, i), rows_low)
            store(taps.at[3], rows, lanes, above)
            store(taps.at[4], rows, lanes, shifted(above, -1))
            return carry

        sweep(low, step, 0)

    def tap(t, u):
        k = (3 * t + u) * width
        return weight[:, k : k + width]

    total = dot(hidden[0], tap(1, 1))
    total += dot(hidden[1], tap(1, 2))
    total += dot(taps[0], tap(1, 0))
    total += dot(hidden[2], tap(2, 1))
    total += dot(taps[1], tap(0, 1))
    total += dot(hidden[3], tap(2, 2))
    total += dot(taps[2], tap(2, 0))
    total += dot(taps[3], tap(0, 2))
    total += dot(taps[4], tap(0, 0))
    acc[...] = total
    tally(first_step(), [(acc, mask_out, dev_out)], centre_out, stats_out)


def expand_kernel(
    dev_in, centre_in, stats_in, gain, shift, mask, weight, hidden, dev_out, centre_out, stats_out, acc
):
    for lanes in lane_blocks(dev_in.shape[1]):
        slope, base = affine(stats_in, gain, shift, centre_in, lanes)

        def step(rows, i, carry):
            half = load(dev_in, rows, lanes) * slope + base
            store(hidden, rows, lanes, silu_half(half) * load_mask(mask, rows))
            return carry

        sweep(dev_in.shape[0], step, 0)
    acc[...] = dot(hidden[...], weight[...])
    tally(first_step(), [(acc, mask, dev_out)], centre_out, stats_out)


def join_kernel(
    dev_a,
    centre_a,
    stats_a,
    gain_a,
    shift_a,
    dev_b,
    centre_b,
    stats_b,
    gain_b,
    shift_b,
    mask,
    weight,
    first_low,
    dev_out,
    centre_out,
    stats_out,
    acc,
):
    for lanes in lane_blocks(dev_a.shape[1]):
        slope_a, base_a = affine(stats_a, gain_a, shift_a, centre_a, lanes)
        slope_b, base_b = affine(stats_b, gain_b, shift_b, centre_b, lanes)
        base = base_a + base_b

        def step(rows, i, carry):
            half = load(dev_a, rows, lanes) * slope_a + load(dev_b, rows, lanes) * slope_b + base
            store(first_low, rows, lanes, silu_half(half) * load_mask(mask, rows))
            return carry

        sweep(dev_a.shape[0], step, 0)
    acc[...] = dot(first_low[...], weight[...])
    tally(first_step(), [(acc, mask, dev_out)], centre_out, stats_out)


def mid2_kernel(
    rows_low,
    dev_in,
    centre_in,
    halo,
    halo_centre,
    halo_mask,
    stats_in,
    gain,
    shift,
    mask,
    weight,
    hidden,
    dev_out,
    centre_out,
    stats_out,
    taps,
    acc,
):
    low, width = acc.shape
    for lanes in lane_blocks(width):
        slope, base = affine(stats_in, gain, shift, centre_in, lanes)
        edges = [affine(stats_in, gain, shift, halo_centre.at[e], lanes) for e in range(2)]

        def act_edge(e, i):
            rows = edge_rows(i, rows_low)
            half = load(halo.at[e], rows, lanes) * edges[e][0] + edges[e][1]
            return silu_half(half) * load_mask(halo_mask.at[e], rows)

        def step(rows, i, carry):
            value = silu_half(load(dev_in, rows, lanes) * slope + base) * load_mask(mask, rows)
            store(hidden, rows, lanes, value)
            lines = (
                from_above(value, act_edge(0, i), rows_low),
                value,
                from_below(value, act_edge(1, i), rows_low),
            )
            for t in range(3):
                for u in range(3):
                    store(taps.at[3 * t + u], rows, lanes, shifted(lines[t], u - 1))
            return carry

        sweep(low, step, 0)
    total = dot(taps[0], weight[:, :width])
    for k in range(1, 9):
        total += dot(taps[k], weight[:, k * width : (k + 1) * width])
    acc[...] = total
    tally(first_step(), [(acc, mask, dev_out)], centre_out, stats_out)


def final_kernel(dev, centre, stats, gain, shift, first_low, cot, mask, block_out, gn_ref, sums):
    first = first_step()
    for lanes in lane_blocks(dev.shape[1]):
        slope, base = affine(stats, gain, shift, centre, lanes)

        def step(rows, i, carry):
            away = load(dev, rows, lanes)
            half = away * slope + base + 0.5 * load(first_low, rows, lanes)
            valid = load_mask(mask, rows)
            value, gate = silu_and_gate(half)
            store(block_out, rows, lanes, value * valid)
            gn = gate * valid * load(cot, rows, lanes)
            store(gn_ref, rows, lanes, gn)
            return carry[0] + column_sum(gn), carry[1] + column_sum(gn * away)

        gn_sum, gd_sum = sweep(dev.shape[0], step, (zeros8(), zeros8()))
        gn_sum, gd_sum = total_of(gn_sum), total_of(gd_sum)
        accumulate(first, sums, 0, lanes, gn_sum)
        accumulate(first, sums, 1, lanes, unit_sum(stats, centre, lanes, gn_sum, gd_sum))


def scaled(gn, away, mask, coefs):
    return (gn * coefs[0] + away * coefs[1] + coefs[2]) * mask


def gate_sums(first, grads, dev, centre, stats, gain, shift, mask, gn_ref, sums, parts):
    width = gn_ref.shape[-1]
    planes = range(parts) if parts else [None]
    for lanes in lane_blocks(width):
        slope, base = affine(stats, gain, shift, centre, lanes)
        carry = (zeros8(), zeros8())
        for p in planes:
            grad_p, dev_p, mask_p, gn_p = (
                r if p is None else r.at[p] for r in (grads, dev, mask, gn_ref)
            )

            def step(rows, i, carry, grad_p=grad_p, dev_p=dev_p, mask_p=mask_p, gn_p=gn_p):
                away = load(dev_p, rows, lanes)
                gate = gate_half(away * slope + base) * load_mask(mask_p, rows)
                gn = gate * load(grad_p, rows, lanes)
                store(gn_p, rows, lanes, gn)
                return carry[0] + column_sum(gn), carry[1] + column_sum(gn * away)

            carry = sweep(grad_p.shape[0], step, carry)
        gn_sum, gd_sum = total_of(carry[0]), total_of(carry[1])
        accumulate(first, sums, 0, lanes, gn_sum)
        accumulate(first, sums, 1, lanes, unit_sum(stats, centre, lanes, gn_sum, gd_sum))


def back_expand_kernel(
    gn,
    dev,
    centre,
    stats,
    gain,
    sums_in,
    mask,
    weight,
    dev_m,
    centre_m,
    stats_m,
    gain_m,
    shift_m,
    ga,
    gn_m,
    sums_m,
    acc,
):
    for lanes in lane_blocks(dev.shape[1]):
        coefs = back_coefs(
            stats, gain, centre, (sums_in[0:1, lanes], sums_in[1:2, lanes]), lanes
        )

        def step(rows, i, carry):
            away = load(dev, rows, lanes)
            store(ga, rows, lanes, scaled(load(gn, rows, lanes), away, load_mask(mask, rows), coefs))
            return carry

        sweep(dev.shape[0], step, 0)
    acc[...] = dot_t(ga[...], weight[...])
    gate_sums(first_step(), acc, dev_m, centre_m, stats_m, gain_m, shift_m, mask, gn_m, sums_m, 0)


def back_mid2_kernel(
    rows_low,
    gn,
    dev,
    centre,
    halo_gn,
    halo_dev,
    halo_centre,
    halo_mask,
    stats,
    gain,
    sums_in,
    mask,
    weight,
    dev_m,
    centre_m,
    stats_m,
    gain_m,
    shift_m,
    views,
    gn_m,
    sums_m,
    acc,
):
    low, width = acc.shape
    for lanes in lane_blocks(width):
        sums = (sums_in[0:1, lanes], sums_in[1:2, lanes])
        coefs = back_coefs(stats, gain, centre, sums, lanes)
        edges = [back_coefs(stats, gain, halo_centre.at[e], sums, lanes) for e in range(2)]

        def edge(e, i):
            rows = edge_rows(i, rows_low)
            return scaled(
                load(halo_gn.at[e], rows, lanes),
                load(halo_dev.at[e], rows, lanes),
                load_mask(halo_mask.at[e], rows),
                edges[e],
            )

        def step(rows, i, carry):
            value = scaled(
                load(gn, rows, lanes), load(dev, rows, lanes), load_mask(mask, rows), coefs
            )
            lines = (
                from_below(value, edge(1, i), rows_low),
                value,
                from_above(value, edge(0, i), rows_low),
            )
            for t in range(3):
                for u in range(3):
                    start = (3 * t + u) * width + lanes.start
                    store(views, rows, slice(start, start + LANES), shifted(lines[t], 1 - u))
            return carry

        sweep(low, step, 0)
    acc[...] = dot_t(views[...], weight[...])
    gate_sums(first_step(), acc, dev_m, centre_m, stats_m, gain_m, shift_m, mask, gn_m, sums_m, 0)


def back_join_kernel(
    gn_in,
    dev_in,
    centre_in,
    stats_in,
    gain_in,
    sums_in,
    mask,
    weight,
    residual,
    dev_a,
    centre_a,
    stats_a,
    gain_a,
    shift_a,
    dev_b,
    centre_b,
    stats_b,
    gain_b,
    shift_b,
    ga,
    gs_ref,
    sums,
    acc,
):
    first = first_step()
    for lanes in lane_blocks(dev_in.shape[1]):
        coefs = back_coefs(
            stats_in, gain_in, centre_in, (sums_in[0:1, lanes], sums_in[1:2, lanes]), lanes
        )

        def step(rows, i, carry):
            away = load(dev_in, rows, lanes)
            value = scaled(load(gn_in, rows, lanes), away, load_mask(mask, rows), coefs)
            store(ga, rows, lanes, value)
            return carry

        sweep(dev_in.shape[0], step, 0)
    acc[...] = dot_t(ga[...], weight[...])
    for lanes in lane_blocks(dev_a.shape[1]):
        slope_a, base_a = affine(stats_a, gain_a, shift_a, centre_a, lanes)
        slope_b, base_b = affine(stats_b, gain_b, shift_b, centre_b, lanes)
        base = base_a + base_b

        def gate(rows, i, carry):
            away_a, away_b = load(dev_a, rows, lanes), load(dev_b, rows, lanes)
            half = away_a * slope_a + away_b * slope_b + base
            grad = load(residual, rows, lanes) + load(acc, rows, lanes)
            gs = gate_half(half) * load_mask(mask, rows) * grad
            store(gs_ref, rows, lanes, gs)
            return (
                carry[0] + column_sum(gs),
                carry[1] + column_sum(gs * away_a),
                carry[2] + column_sum(gs * away_b),
            )

        carry = sweep(dev_a.shape[0], gate, (zeros8(), zeros8(), zeros8()))
        gs_sum, a_sum, b_sum = (total_of(part) for part in carry)
        accumulate(first, sums, 0, lanes, gs_sum)
        accumulate(first, sums, 1, lanes, unit_sum(stats_a, centre_a, lanes, gs_sum, a_sum))
        accumulate(first, sums, 2, lanes, unit_sum(stats_b, centre_b, lanes, gs_sum, b_sum))


def back_split_kernel(
    gs,
    dev_a,
    centre_a,
    stats_a,
    gain_a,
    dev_b,
    centre_b,
    stats_b,
    gain_b,
    sums_in,
    mask,
    weight_a,
    weight_b,
    dev_m,
    centre_m,
    stats_m,
    gain_m,
    shift_m,
    ga_a,
    ga_b,
    gn_m,
    sums_m,
    grad_skip,
    acc,
):
    for lanes in lane_blocks(dev_a.shape[1]):
        shift_sum = sums_in[0:1, lanes]
        coefs_a = back_coefs(stats_a, gain_a, centre_a, (shift_sum, sums_in[1:2, lanes]), lanes)
        coefs_b = back_coefs(stats_b, gain_b, centre_b, (shift_sum, sums_in[2:3, lanes]), lanes)

        def step(rows, i, carry):
            value, valid = load(gs, rows, lanes), load_mask(mask, rows)
            store(ga_a, rows, lanes, scaled(value, load(dev_a, rows, lanes), valid, coefs_a))
            store(ga_b, rows, lanes, scaled(value, load(dev_b, rows, lanes), valid, coefs_b))
            return carry

        sweep(dev_a.shape[0], step, 0)
    grad_skip[...] = dot_t(ga_b[...], weight_b[...]).astype(BF16)
    acc[...] = dot_t(ga_a[...], weight_a[...])
    gate_sums(first_step(), acc, dev_m, centre_m, stats_m, gain_m, shift_m, mask, gn_m, sums_m, 0)


def back_mid1_kernel(
    rows_low,
    gn,
    dev,
    centre,
    halo_gn,
    halo_dev,
    halo_centre,
    halo_mask,
    stats,
    gain,
    sums_in,
    mask,
    weight,
    dev_m,
    centre_m,
    mask_m,
    stats_m,
    gain_m,
    shift_m,
    views,
    gn_m,
    sums_m,
    acc,
):
    _, low, width = acc.shape
    for lanes in lane_blocks(width):
        sums = (sums_in[0:1, lanes], sums_in[1:2, lanes])
        coefs = back_coefs(stats, gain, centre, sums, lanes)
        coefs_edge = back_coefs(stats, gain, halo_centre, sums, lanes)

        def step(rows, i, carry):
            value = scaled(
                load(gn, rows, lanes), load(dev, rows, lanes), load_mask(mask, rows), coefs
            )
            some = edge_rows(i, rows_low)
            edge = scaled(
                load(halo_gn, some, lanes),
                load(halo_dev, some, lanes),
                load_mask(halo_mask, some),
                coefs_edge,
            )
            below = from_below(value, edge, rows_low)
            for k, view in enumerate((below, value, shifted(value, 1), shifted(below, 1))):
                start = k * width + lanes.start
                store(views, rows, slice(start, start + LANES), view)
            return carry

        sweep(low, step, 0)

    def view(k):
        return views[:, k * width : (k + 1) * width]

    def tap(t, u):
        k = (3 * t + u) * width
        return weight[:, k : k + width]

    acc[0] = dot_t(view(1), tap(1, 1))
    acc[1] = dot_t(view(1), tap(1, 2)) + dot_t(view(2), tap(1, 0))
    acc[2] = dot_t(view(1), tap(2, 1)) + dot_t(view(0), tap(0, 1))
    acc[3] = (
        dot_t(view(1), tap(2, 2))
        + dot_t(view(2), tap(2, 0))
        + dot_t(view(0), tap(0, 2))
        + dot_t(view(3), tap(0, 0))
    )
    gate_sums(
        first_step(), acc, dev_m, centre_m, stats_m, gain_m, shift_m, mask_m, gn_m, sums_m, 4
    )


def back_image_kernel(
    gn, dev, centre, stats, gain, sums_in, mask_ref, weight, grad_skip, perm_ref, ga, image, planes_ref
):
    planes, low, width = ga.shape
    for lanes in lane_blocks(width):
        coefs = back_coefs(
            stats, gain, centre, (sums_in[0:1, lanes], sums_in[1:2, lanes]), lanes
        )
        for p in range(planes):

            def step(rows, i, carry):
                away = load(dev.at[p], rows, lanes)
                valid = load_mask(mask_ref.at[p], rows)
                value = scaled(load(gn.at[p], rows, lanes), away, valid, coefs)
                store(ga.at[p], rows, lanes, value)
                return carry

            sweep(low, step, 0)
    planes_ref[0] = (dot_t(ga[0], weight[...]) + grad_skip[...].astype(F32)).astype(BF16)
    for p in range(1, planes):
        planes_ref[p] = dot_t(ga[p], weight[...]).astype(BF16)
    group = perm_ref.shape[0]
    part = group // planes
    for g in range(image.shape[0] // group):
        rows = slice(g * part, (g + 1) * part)
        mask = jnp.concatenate([mask_ref[p, rows, :] for p in range(planes)], axis=0)
        mask = jnp.concatenate([mask] * (group // 128), axis=1)
        perm = (perm_ref[...].astype(F32) * mask).astype(BF16)
        here = jnp.concatenate([planes_ref[p, rows, :] for p in range(planes)], axis=0)
        back = lax.dot_general(
            perm, here, (((0,), (0,)), ((), ())), preferred_element_type=F32
        )
        image[g * group : (g + 1) * group, :] = back.astype(BF16)


def spec_of(shape, kind, blocks):
    if kind == "rows":
        return pl.BlockSpec((shape[0] // blocks, shape[1]), lambda b: (b, 0))
    if kind == "planes":
        return pl.BlockSpec((shape[0], shape[1] // blocks, shape[2]), lambda b: (0, b, 0))
    if kind == "plane0":
        return pl.BlockSpec((None, shape[1] // blocks, shape[2]), lambda b: (0, b, 0))
    if kind == "each":
        return pl.BlockSpec((None,) + tuple(shape[1:]), lambda b: (b, 0, 0))
    if kind == "each2":
        return pl.BlockSpec((2, None) + tuple(shape[2:]), lambda b: (0, b, 0, 0))
    zero = (0,) * len(shape)
    return pl.BlockSpec(tuple(shape), lambda b: zero, pipeline_mode=pl.Buffered(1))


def out_spec(shape, kind, blocks):
    if kind == "all":
        zero = (0,) * len(shape)
        return pl.BlockSpec(tuple(shape), lambda b: zero)
    return spec_of(shape, kind, blocks)


def stage(kernel, blocks, ins, outs, scratch=(), flops=0):
    moved = sum(x.size * x.dtype.itemsize for x, _ in ins)
    moved += sum(int(np.prod(s)) * jnp.dtype(d).itemsize for s, d, _ in outs)
    return pl.pallas_call(
        kernel,
        grid=(blocks,),
        in_specs=[spec_of(x.shape, kind, blocks) for x, kind in ins],
        out_specs=[out_spec(s, kind, blocks) for s, _, kind in outs],
        out_shape=[jax.ShapeDtypeStruct(s, d) for s, d, _ in outs],
        scratch_shapes=[pltpu.VMEM(s, d) for s, d in scratch],
        compiler_params=pltpu.CompilerParams(
            dimension_semantics=("arbitrary",), vmem_limit_bytes=VMEM_BYTES
        ),
        cost_estimate=pl.CostEstimate(flops=flops, bytes_accessed=moved, transcendentals=0),
    )(*[x for x, _ in ins])


def merge_rows(buf, peers, merge, mean_only):
    if not merge:
        total = buf[0]
        for k in range(1, peers):
            total = total + buf[k]
        return total
    counts = [buf[k, 0:1, :] for k in range(peers)]
    means = [buf[k, 1:2, :] for k in range(peers)]
    count, weighted = counts[0], counts[0] * means[0]
    for k in range(1, peers):
        count = count + counts[k]
        weighted = weighted + counts[k] * means[k]
    safe = jnp.maximum(count, 1.0)
    mean = weighted / safe
    squares = jnp.zeros_like(mean)
    for k in range(peers):
        squares = squares + buf[k, 2:3, :] + counts[k] * jnp.square(means[k] - mean)
    if mean_only:
        squares = squares / safe
    return jnp.concatenate([count, mean, squares], axis=0)


def sync_kernel(rows_n, img_n, merge, widths, mine, *refs):
    outs = refs[: len(widths)]
    buf_r, buf_i, part, send_r, recv_r, send_i, recv_i = refs[len(widths) :]
    row, img = lax.axis_index("rows"), lax.axis_index("img")
    barrier = pltpu.get_barrier_semaphore()
    for k in range(1, rows_n):
        peer = lax.rem(row + k, rows_n)
        pl.semaphore_signal(barrier, inc=1, device_id={"rows": peer}, device_id_type=MESH)
    for k in range(1, img_n):
        peer = lax.rem(img + k, img_n)
        pl.semaphore_signal(barrier, inc=1, device_id={"img": peer}, device_id_type=MESH)
    pl.semaphore_wait(barrier, rows_n + img_n - 2)
    copies = []

    def exchange(axis, me, peers, source, buf, send, recv):
        for k in range(1, peers):
            copy = pltpu.make_async_remote_copy(
                src_ref=source,
                dst_ref=buf.at[me],
                send_sem=send.at[k],
                recv_sem=recv.at[me],
                device_id={axis: lax.rem(me + k, peers)},
                device_id_type=MESH,
            )
            copy.start()
            copies.append(copy)
        buf[pl.ds(me, 1)] = source[...][None]
        for k in range(1, peers):
            peer = lax.rem(me + k, peers)
            pltpu.make_async_remote_copy(
                src_ref=source,
                dst_ref=buf.at[peer],
                send_sem=send.at[k],
                recv_sem=recv.at[peer],
                device_id={axis: peer},
                device_id_type=MESH,
            ).wait_recv()

    exchange("rows", row, rows_n, mine, buf_r, send_r, recv_r)
    part[...] = merge_rows(buf_r, rows_n, merge, False)
    exchange("img", img, img_n, part, buf_i, send_i, recv_i)
    total = merge_rows(buf_i, img_n, merge, True)
    start = 0
    for out, width in zip(outs, widths):
        out[...] = total[:, start : start + width]
        start += width
    for copy in copies:
        copy.wait_send()


class Sync:
    def __init__(self, rows_n, img_n):
        self.rows_n, self.img_n = rows_n, img_n
        self.ids = {}

    def __call__(self, mine, merge, widths=None):
        lines, width = mine.shape
        widths = widths or (width,)
        key = (merge, lines, tuple(widths))
        ident = self.ids.setdefault(key, len(self.ids))
        shape = (lines, width)
        dma = pltpu.SemaphoreType.DMA
        out = pl.pallas_call(
            functools.partial(sync_kernel, self.rows_n, self.img_n, merge, widths),
            in_specs=[pl.BlockSpec(memory_space=pltpu.VMEM)],
            out_specs=[pl.BlockSpec(memory_space=pltpu.VMEM)] * len(widths),
            out_shape=[jax.ShapeDtypeStruct((lines, w), F32) for w in widths],
            scratch_shapes=[
                pltpu.VMEM((self.rows_n,) + shape, F32),
                pltpu.VMEM((self.img_n,) + shape, F32),
                pltpu.VMEM(shape, F32),
                dma((self.rows_n,)),
                dma((self.rows_n,)),
                dma((self.img_n,)),
                dma((self.img_n,)),
            ],
            compiler_params=pltpu.CompilerParams(collective_id=ident, has_side_effects=True),
            cost_estimate=pl.CostEstimate(
                flops=12_000_000_000, bytes_accessed=1_000_000, transcendentals=0
            ),
        )(mine)
        return out[0] if len(widths) == 1 else out


def to_next(x, peers):
    return lax.ppermute(x, "rows", [(i, i + 1) for i in range(peers - 1)])


def to_previous(x, peers):
    return lax.ppermute(x, "rows", [(i + 1, i) for i in range(peers - 1)])


def lanes128(mask):
    return jnp.broadcast_to(mask.astype(F32)[..., None], mask.shape + (128,))


def body(
    image_in,
    extent,
    weight_in1,
    weight_mid1,
    weight_out1,
    weight_skip,
    weight_in2,
    weight_mid2,
    weight_out2,
    gain_in1,
    shift_in1,
    gain_mid1,
    shift_mid1,
    gain_out1,
    shift_out1,
    gain_skip,
    shift_skip,
    gain_in2,
    shift_in2,
    gain_mid2,
    shift_mid2,
    gain_out2,
    shift_out2,
    cotangent,
):
    images, rows_here, columns, inputs = image_in.shape
    middle, outputs = weight_out1.shape
    rows_low, cols_low = rows_here // 2, columns // 2
    low = images * rows_low * cols_low
    rows_n, img_n = lax.axis_size("rows"), lax.axis_size("img")
    blocks = images // IMAGES
    per_block = low // blocks
    edge = images * cols_low
    sync = Sync(rows_n, img_n)
    run = functools.partial(stage, blocks=blocks)

    row0 = lax.axis_index("rows") * rows_here
    half = extent // 2

    def inside(rows, cols, side):
        kept = (rows[None, :, None] >= 0) & (rows[None, :, None] < side[:, None, None])
        return kept & (cols[None, None, :] < side[:, None, None])

    low_rows = jnp.arange(rows_low, dtype=jnp.int32)
    low_cols = jnp.arange(cols_low, dtype=jnp.int32)
    mask_in = jnp.stack(
        [
            inside(row0 + 2 * low_rows + p, 2 * low_cols + q, extent).reshape(-1)
            for p in range(2)
            for q in range(2)
        ]
    )
    mask_in = lanes128(mask_in)
    mask_out = lanes128(inside(row0 // 2 + low_rows, low_cols, half).reshape(-1))
    above = jnp.stack([row0 - 1])
    mask_above = lanes128(
        jnp.stack([inside(above, 2 * low_cols + q, extent).reshape(-1) for q in range(2)])
    )
    mask_edges = lanes128(
        jnp.stack(
            [
                inside(jnp.stack([line]), low_cols, half).reshape(-1)
                for line in (row0 // 2 - 1, row0 // 2 + rows_low)
            ]
        )
    )

    group_images = 256 // (rows_here * columns)
    order = np.arange(256).reshape(group_images, rows_low, 2, cols_low, 2)
    order = order.transpose(2, 4, 0, 1, 3).reshape(-1)
    perm = jnp.asarray(np.eye(256, dtype=np.float32)[order], BF16)

    def row(vector):
        return vector.reshape(1, -1)

    g_in1, s_in1, g_mid1, s_mid1 = row(gain_in1), row(shift_in1), row(gain_mid1), row(shift_mid1)
    g_out1, s_out1, g_skip, s_skip = row(gain_out1), row(shift_out1), row(gain_skip), row(shift_skip)
    g_in2, s_in2, g_mid2, s_mid2 = row(gain_in2), row(shift_in2), row(gain_mid2), row(shift_mid2)
    g_out2, s_out2 = row(gain_out2), row(shift_out2)
    kernel_mid1 = weight_mid1.reshape(middle, 9 * middle)
    kernel_mid2 = weight_mid2.reshape(middle, 9 * middle)
    cot = cotangent.reshape(low, outputs)

    dev_mid_out = [
        ((low, middle), BF16, "rows"),
        ((blocks, 1, middle), F32, "each"),
        ((3, middle), F32, "all"),
    ]
    dev_out_out = [
        ((low, outputs), BF16, "rows"),
        ((blocks, 1, outputs), F32, "each"),
        ((3, outputs), F32, "all"),
    ]
    unit_flops = 2 * low * middle * middle

    planes, d_in1, c_in1, t_in1 = run(
        split_kernel,
        ins=[
            (image_in.reshape(4 * low, inputs), "rows"),
            (perm, "all"),
            (mask_in, "planes"),
            (weight_in1, "all"),
        ],
        outs=[
            ((4, low, inputs), BF16, "planes"),
            ((4, low, middle), BF16, "planes"),
            ((blocks, 1, middle), F32, "each"),
            ((3, middle), F32, "all"),
        ],
        scratch=[((4, per_block, middle), F32)],
        flops=12 * unit_flops,
    )
    last = d_in1.reshape(2, 2, images, rows_low, cols_low, middle)[1, :, :, rows_low - 1]
    halo_in1 = to_next(last.reshape(2, edge, middle), rows_n)
    halo_c_in1 = to_next(c_in1, rows_n)
    d_skip, c_skip, t_in1 = run(
        skip_kernel,
        ins=[(planes, "plane0"), (mask_out, "rows"), (weight_skip, "all"), (t_in1, "all")],
        outs=dev_out_out[:2] + [((3, middle + outputs), F32, "all")],
        scratch=[((per_block, outputs), F32), ((3, outputs), F32)],
        flops=8 * unit_flops,
    )
    n_in1, n_skip = sync(t_in1, True, (middle, outputs))
    hid_in1, d_mid1, c_mid1, t_mid1 = run(
        functools.partial(mid1_kernel, rows_low),
        ins=[
            (d_in1, "planes"),
            (c_in1, "each"),
            (mask_in, "planes"),
            (halo_in1, "planes"),
            (halo_c_in1, "each"),
            (mask_above, "planes"),
            (n_in1, "all"),
            (g_in1, "all"),
            (s_in1, "all"),
            (mask_out, "rows"),
            (kernel_mid1, "all"),
        ],
        outs=[((4, low, middle), BF16, "planes")] + dev_mid_out,
        scratch=[((5, per_block, middle), BF16), ((per_block, middle), F32)],
        flops=9 * unit_flops,
    )
    n_mid1 = sync(t_mid1, True)
    image_mid1 = d_mid1.reshape(images, rows_low, cols_low, middle)
    halo_mid1 = to_previous(image_mid1[:, 0].reshape(edge, middle), rows_n)
    halo_c_mid1 = to_previous(c_mid1, rows_n)
    hid_mid1, d_out1, c_out1, t_out1 = run(
        expand_kernel,
        ins=[
            (d_mid1, "rows"),
            (c_mid1, "each"),
            (n_mid1, "all"),
            (g_mid1, "all"),
            (s_mid1, "all"),
            (mask_out, "rows"),
            (weight_out1, "all"),
        ],
        outs=[((low, middle), BF16, "rows")] + dev_out_out,
        scratch=[((per_block, outputs), F32)],
        flops=4 * unit_flops,
    )
    n_out1 = sync(t_out1, True)
    join = [
        (d_out1, "rows"),
        (c_out1, "each"),
        (n_out1, "all"),
        (g_out1, "all"),
        (s_out1, "all"),
        (d_skip, "rows"),
        (c_skip, "each"),
        (n_skip, "all"),
        (g_skip, "all"),
        (s_skip, "all"),
    ]
    first_low, d_in2, c_in2, t_in2 = run(
        join_kernel,
        ins=join + [(mask_out, "rows"), (weight_in2, "all")],
        outs=[((low, outputs), BF16, "rows")] + dev_mid_out,
        scratch=[((per_block, middle), F32)],
        flops=4 * unit_flops,
    )

    def edges_of(x):
        image = x.reshape(images, rows_low, cols_low, middle)
        return jnp.stack(
            [
                to_next(image[:, rows_low - 1].reshape(edge, middle), rows_n),
                to_previous(image[:, 0].reshape(edge, middle), rows_n),
            ]
        )

    def centres_of(c):
        return jnp.stack([to_next(c, rows_n), to_previous(c, rows_n)])

    halo_in2, halo_c_in2 = edges_of(d_in2), centres_of(c_in2)
    n_in2 = sync(t_in2, True)
    hid_in2, d_mid2, c_mid2, t_mid2 = run(
        functools.partial(mid2_kernel, rows_low),
        ins=[
            (d_in2, "rows"),
            (c_in2, "each"),
            (halo_in2, "planes"),
            (halo_c_in2, "each2"),
            (mask_edges, "planes"),
            (n_in2, "all"),
            (g_in2, "all"),
            (s_in2, "all"),
            (mask_out, "rows"),
            (kernel_mid2, "all"),
        ],
        outs=[((low, middle), BF16, "rows")] + dev_mid_out,
        scratch=[((9, per_block, middle), BF16), ((per_block, middle), F32)],
        flops=9 * unit_flops,
    )
    n_mid2 = sync(t_mid2, True)
    halo_mid2, halo_c_mid2 = edges_of(d_mid2), centres_of(c_mid2)
    hid_mid2, d_out2, c_out2, t_out2 = run(
        expand_kernel,
        ins=[
            (d_mid2, "rows"),
            (c_mid2, "each"),
            (n_mid2, "all"),
            (g_mid2, "all"),
            (s_mid2, "all"),
            (mask_out, "rows"),
            (weight_out2, "all"),
        ],
        outs=[((low, middle), BF16, "rows")] + dev_out_out,
        scratch=[((per_block, outputs), F32)],
        flops=4 * unit_flops,
    )
    n_out2 = sync(t_out2, True)
    block_out, gn_out2, z_out2 = run(
        final_kernel,
        ins=[
            (d_out2, "rows"),
            (c_out2, "each"),
            (n_out2, "all"),
            (g_out2, "all"),
            (s_out2, "all"),
            (first_low, "rows"),
            (cot, "rows"),
            (mask_out, "rows"),
        ],
        outs=[
            ((low, outputs), BF16, "rows"),
            ((low, outputs), BF16, "rows"),
            ((2, outputs), F32, "all"),
        ],
    )

    z_out2 = sync(z_out2, False)
    gn_mid_out = [((low, middle), BF16, "rows"), ((2, middle), F32, "all")]
    ga_out2, gn_mid2, z_mid2 = run(
        back_expand_kernel,
        ins=[
            (gn_out2, "rows"),
            (d_out2, "rows"),
            (c_out2, "each"),
            (n_out2, "all"),
            (g_out2, "all"),
            (z_out2, "all"),
            (mask_out, "rows"),
            (weight_out2, "all"),
            (d_mid2, "rows"),
            (c_mid2, "each"),
            (n_mid2, "all"),
            (g_mid2, "all"),
            (s_mid2, "all"),
        ],
        outs=[((low, outputs), BF16, "rows")] + gn_mid_out,
        scratch=[((per_block, middle), F32)],
        flops=4 * unit_flops,
    )
    halo_gn_mid2 = edges_of(gn_mid2)
    z_mid2 = sync(z_mid2, False)
    views2, gn_in2, z_in2 = run(
        functools.partial(back_mid2_kernel, rows_low),
        ins=[
            (gn_mid2, "rows"),
            (d_mid2, "rows"),
            (c_mid2, "each"),
            (halo_gn_mid2, "planes"),
            (halo_mid2, "planes"),
            (halo_c_mid2, "each2"),
            (mask_edges, "planes"),
            (n_mid2, "all"),
            (g_mid2, "all"),
            (z_mid2, "all"),
            (mask_out, "rows"),
            (kernel_mid2, "all"),
            (d_in2, "rows"),
            (c_in2, "each"),
            (n_in2, "all"),
            (g_in2, "all"),
            (s_in2, "all"),
        ],
        outs=[((low, 9 * middle), BF16, "rows")] + gn_mid_out,
        scratch=[((per_block, middle), F32)],
        flops=9 * unit_flops,
    )
    z_in2 = sync(z_in2, False)
    ga_in2, gs1, z_sum1 = run(
        back_join_kernel,
        ins=[
            (gn_in2, "rows"),
            (d_in2, "rows"),
            (c_in2, "each"),
            (n_in2, "all"),
            (g_in2, "all"),
            (z_in2, "all"),
            (mask_out, "rows"),
            (weight_in2, "all"),
            (gn_out2, "rows"),
        ]
        + join,
        outs=[
            ((low, middle), BF16, "rows"),
            ((low, outputs), BF16, "rows"),
            ((3, outputs), F32, "all"),
        ],
        scratch=[((per_block, outputs), F32)],
        flops=4 * unit_flops,
    )

    z_sum1 = sync(z_sum1, False)
    ga_out1, ga_skip, gn_mid1, z_mid1, grad_skip_in = run(
        back_split_kernel,
        ins=[
            (gs1, "rows"),
            (d_out1, "rows"),
            (c_out1, "each"),
            (n_out1, "all"),
            (g_out1, "all"),
            (d_skip, "rows"),
            (c_skip, "each"),
            (n_skip, "all"),
            (g_skip, "all"),
            (z_sum1, "all"),
            (mask_out, "rows"),
            (weight_out1, "all"),
            (weight_skip, "all"),
            (d_mid1, "rows"),
            (c_mid1, "each"),
            (n_mid1, "all"),
            (g_mid1, "all"),
            (s_mid1, "all"),
        ],
        outs=[((low, outputs), BF16, "rows"), ((low, outputs), BF16, "rows")]
        + gn_mid_out
        + [((low, inputs), BF16, "rows")],
        scratch=[((per_block, middle), F32)],
        flops=12 * unit_flops,
    )
    first_rows = gn_mid1.reshape(images, rows_low, cols_low, middle)[:, 0]
    halo_gn_mid1 = to_previous(first_rows.reshape(edge, middle), rows_n)
    z_mid1 = sync(z_mid1, False)
    views1, gn_in1, z_in1 = run(
        functools.partial(back_mid1_kernel, rows_low),
        ins=[
            (gn_mid1, "rows"),
            (d_mid1, "rows"),
            (c_mid1, "each"),
            (halo_gn_mid1, "rows"),
            (halo_mid1, "rows"),
            (halo_c_mid1, "each"),
            (mask_edges[1], "rows"),
            (n_mid1, "all"),
            (g_mid1, "all"),
            (z_mid1, "all"),
            (mask_out, "rows"),
            (kernel_mid1, "all"),
            (d_in1, "planes"),
            (c_in1, "each"),
            (mask_in, "planes"),
            (n_in1, "all"),
            (g_in1, "all"),
            (s_in1, "all"),
        ],
        outs=[
            ((low, 4 * middle), BF16, "rows"),
            ((4, low, middle), BF16, "planes"),
            ((2, middle), F32, "all"),
        ],
        scratch=[((4, per_block, middle), F32)],
        flops=9 * unit_flops,
    )
    z_in1 = sync(z_in1, False)
    ga_in1, grad_image = run(
        back_image_kernel,
        ins=[
            (gn_in1, "planes"),
            (d_in1, "planes"),
            (c_in1, "each"),
            (n_in1, "all"),
            (g_in1, "all"),
            (z_in1, "all"),
            (mask_in, "planes"),
            (weight_in1, "all"),
            (grad_skip_in, "rows"),
            (perm, "all"),
        ],
        outs=[((4, low, middle), BF16, "planes"), ((4 * low, inputs), BF16, "rows")],
        scratch=[((4, per_block, inputs), BF16)],
        flops=12 * unit_flops,
    )

    def weight_term(values, upstream):
        return lax.dot_general(
            values, upstream, (((0,), (0,)), ((), ())), preferred_element_type=F32
        ).astype(BF16)

    def reduced(grad):
        shard = lax.psum_scatter(grad, "img", scatter_dimension=0, tiled=True)
        return lax.psum(shard, "rows").astype(F32)

    dw_out2 = reduced(weight_term(hid_mid2, ga_out2))
    dw_mid2 = reduced(weight_term(hid_in2, views2))
    dw_in2 = reduced(weight_term(first_low, ga_in2))
    dw_out1 = reduced(weight_term(hid_mid1, ga_out1))
    dw_skip = reduced(weight_term(planes[0], ga_skip))
    m = middle
    dw_00 = weight_term(hid_in1[0], views1[:, m : 2 * m])
    dw_01 = weight_term(hid_in1[1], views1[:, m : 3 * m])
    dw_10 = weight_term(hid_in1[2], views1[:, : 2 * m])
    dw_11 = weight_term(hid_in1[3], views1)
    dw_mid1 = jnp.concatenate(
        [
            dw_11[:, 3 * m :],
            dw_10[:, :m],
            dw_11[:, :m],
            dw_01[:, m:],
            dw_00,
            dw_01[:, :m],
            dw_11[:, 2 * m : 3 * m],
            dw_10[:, m:],
            dw_11[:, m : 2 * m],
        ],
        axis=1,
    )
    dw_mid1 = reduced(dw_mid1)
    dw_in1 = reduced(
        weight_term(planes.reshape(4 * low, inputs), ga_in1.reshape(4 * low, middle))
    )
    kernel_shape = (middle // img_n, 3, 3, middle)
    return (
        block_out.reshape(images, rows_low, cols_low, outputs),
        grad_image.reshape(images, rows_here, columns, inputs),
        dw_in1,
        dw_mid1.reshape(kernel_shape),
        dw_out1,
        dw_skip,
        dw_in2,
        dw_mid2.reshape(kernel_shape),
        dw_out2,
        z_in1[1],
        z_in1[0],
        z_mid1[1],
        z_mid1[0],
        z_sum1[1],
        z_sum1[0],
        z_sum1[2],
        z_sum1[0],
        z_in2[1],
        z_in2[0],
        z_mid2[1],
        z_mid2[0],
        z_out2[1],
        z_out2[0],
    )


def solution(mesh):
    image = P("img", "rows", None, None)
    in_specs = (image, P("img")) + (P(),) * 21 + (image,)
    out_specs = (
        image,
        image,
        P("img", None),
        P("img", None, None, None),
        P("img", None),
        P("img", None),
        P("img", None),
        P("img", None, None, None),
        P("img", None),
    ) + (P(),) * 14
    return jax.shard_map(body, mesh=mesh, in_specs=in_specs, out_specs=out_specs, check_vma=False)
```

```python
import functools

import jax
import jax.numpy as jnp
import numpy as np
from jax import lax
from jax.experimental import pallas as pl
from jax.experimental.pallas import tpu as pltpu
from jax.sharding import PartitionSpec as P

EPSILON = 1e-05
F32 = jnp.float32
BF16 = jnp.bfloat16
LANES = 512
ROWS = 32
IMAGES = 16
VMEM_BYTES = 56 * 1024 * 1024
MESH = pl.DeviceIdType.MESH
BY_ROWS, BY_PLANES, FIRST_PLANE, BY_BLOCK, PAIR_BLOCK, WHOLE = range(6)


def dot(a, b):
    return jnp.dot(a, b, preferred_element_type=F32)


def dot_t(a, b):
    return lax.dot_general(a, b, (((1,), (1,)), ((), ())), preferred_element_type=F32)


def load(ref, rows, lanes):
    value = ref[rows, lanes].astype(F32)
    return value.reshape(value.shape[0] // 8, 8, value.shape[1])


def store(ref, rows, lanes, value):
    ref[rows, lanes] = value.reshape(value.shape[0] * 8, value.shape[2]).astype(ref.dtype)


def load_mask(ref, rows):
    mask = load(ref, rows, slice(None))
    return jnp.concatenate([mask] * (LANES // 128), axis=-1)


def sweep(total, step, init, rows=ROWS):
    def body(i, carry):
        return step(pl.ds(pl.multiple_of(i * rows, rows), rows), i, carry)

    return lax.fori_loop(0, total // rows, body, init)


def lane_blocks(width):
    return [slice(k * LANES, (k + 1) * LANES) for k in range(width // LANES)]


def tall(row):
    return jnp.broadcast_to(row, (8, row.shape[-1]))


def column_sum(value):
    return jnp.sum(value, axis=0)


def total_of(part):
    return jnp.sum(part, axis=0, keepdims=True)


def zeros8():
    return jnp.zeros((8, LANES), F32)


def tally(first, parts, centre_ref, stats_ref):
    width = parts[0][0].shape[-1]

    @pl.when(first)
    def _():
        stats_ref[...] = jnp.zeros_like(stats_ref)

    for lanes in lane_blocks(width):
        sums = (zeros8(), zeros8())
        for acc, mask_ref, dev in parts:

            def add(rows, i, carry, acc=acc, mask_ref=mask_ref):
                mask = load_mask(mask_ref, rows)
                return (
                    carry[0] + column_sum(load(acc, rows, lanes) * mask),
                    carry[1] + column_sum(mask),
                )

            sums = sweep(acc.shape[0], add, sums)
        total, count = total_of(sums[0]), total_of(sums[1])
        centre = total / jnp.maximum(count, 1.0)
        centre_ref[:, lanes] = centre
        centre8 = tall(centre)
        squares = zeros8()
        for acc, mask_ref, dev in parts:

            def square(rows, i, carry, acc=acc, mask_ref=mask_ref, dev=dev):
                away = load(acc, rows, lanes) - centre8
                store(dev, rows, lanes, away)
                return carry + column_sum(load_mask(mask_ref, rows) * away * away)

            squares = sweep(acc.shape[0], square, squares)
        squares = total_of(squares)
        count_old, mean_old, squares_old = (
            stats_ref[0:1, lanes],
            stats_ref[1:2, lanes],
            stats_ref[2:3, lanes],
        )
        both = count_old + count
        share = count / jnp.maximum(both, 1.0)
        delta = centre - mean_old
        stats_ref[0:1, lanes] = both
        stats_ref[1:2, lanes] = mean_old + delta * share
        stats_ref[2:3, lanes] = squares_old + squares + delta * delta * count_old * share


def affine(stats_ref, gain_ref, shift_ref, centre_ref, lanes):
    scale = lax.rsqrt(stats_ref[2:3, lanes] + EPSILON)
    slope = gain_ref[:, lanes] * scale
    base = shift_ref[:, lanes] + (centre_ref[:, lanes] - stats_ref[1:2, lanes]) * slope
    return tall(0.5 * slope), tall(0.5 * base)


def silu_half(half):
    return half + half * jnp.tanh(half)


def gate_half(half):
    tanh = jnp.tanh(half)
    return (0.5 + 0.5 * tanh) * (1.0 + half * (1.0 - tanh))


def silu_and_gate(half):
    tanh = jnp.tanh(half)
    return half + half * tanh, (0.5 + 0.5 * tanh) * (1.0 + half * (1.0 - tanh))


def back_coefs(stats_ref, gain_ref, centre_ref, sums, lanes):
    shift_sum, gain_sum = sums
    pixels = stats_ref[0:1, lanes]
    scale = lax.rsqrt(stats_ref[2:3, lanes] + EPSILON)
    slope = gain_ref[:, lanes] * scale
    per_pixel = slope / pixels
    away = (centre_ref[:, lanes] - stats_ref[1:2, lanes]) * scale
    return (
        tall(slope),
        tall(-per_pixel * scale * gain_sum),
        tall(-per_pixel * (shift_sum + away * gain_sum)),
    )


def unit_sum(stats_ref, centre_ref, lanes, gn_sum, gd_sum):
    scale = lax.rsqrt(stats_ref[2:3, lanes] + EPSILON)
    return scale * (gd_sum + (centre_ref[:, lanes] - stats_ref[1:2, lanes]) * gn_sum)


def accumulate(first, ref, row, lanes, value):
    old = jnp.where(first, jnp.zeros_like(value), ref[row : row + 1, lanes])
    ref[row : row + 1, lanes] = old + value


def shifted(value, by):
    if by == 0:
        return value
    rolled = pltpu.roll(value, (-by) % 8, axis=1)
    column = lax.broadcasted_iota(jnp.int32, value.shape, 1)
    return jnp.where(column == (0 if by < 0 else 7), 0.0, rolled)


def from_above(value, edge, rows_low):
    if rows_low == 1:
        return edge
    images = value.shape[0] // rows_low
    image = value.reshape((images, rows_low) + value.shape[1:])
    return jnp.concatenate([edge[:, None], image[:, :-1]], axis=1).reshape(value.shape)


def from_below(value, edge, rows_low):
    if rows_low == 1:
        return edge
    images = value.shape[0] // rows_low
    image = value.reshape((images, rows_low) + value.shape[1:])
    return jnp.concatenate([image[:, 1:], edge[:, None]], axis=1).reshape(value.shape)


def edge_rows(i, rows_low):
    return pl.ds(pl.multiple_of(i * (ROWS // rows_low), ROWS // rows_low), ROWS // rows_low)


def first_step():
    return pl.program_id(0) == 0


def open_kernel(
    image_ref,
    perm_ref,
    mask_ref,
    mask_out,
    weight_ref,
    weight_skip,
    planes_ref,
    dev_ref,
    centre_ref,
    dev_skip,
    centre_skip,
    stats_ref,
    acc,
    acc_skip,
):
    planes, low, _ = planes_ref.shape
    group = perm_ref.shape[0]
    part = group // planes
    for g in range(image_ref.shape[0] // group):
        mask = jnp.concatenate(
            [mask_ref[p, g * part : (g + 1) * part, :] for p in range(planes)], axis=0
        )
        mask = jnp.concatenate([mask] * (group // 128), axis=1)
        perm = (perm_ref[...].astype(F32) * mask).astype(BF16)
        moved = dot(perm, image_ref[g * group : (g + 1) * group, :]).astype(BF16)
        for p in range(planes):
            planes_ref[p, g * part : (g + 1) * part, :] = moved[p * part : (p + 1) * part]
    for p in range(planes):
        acc[p] = dot(planes_ref[p], weight_ref[...])
    width = acc.shape[-1]
    tally(
        first_step(),
        [(acc.at[p], mask_ref.at[p], dev_ref.at[p]) for p in range(planes)],
        centre_ref,
        stats_ref.at[:, :width],
    )
    acc_skip[...] = dot(planes_ref[0], weight_skip[...])
    tally(first_step(), [(acc_skip, mask_out, dev_skip)], centre_skip, stats_ref.at[:, width:])


def mid1_kernel(
    rows_low,
    dev_in,
    centre_in,
    mask_ref,
    halo,
    halo_centre,
    halo_mask,
    stats_in,
    gain,
    shift,
    mask_out,
    weight,
    hidden,
    dev_out,
    centre_out,
    stats_out,
    taps,
    acc,
):
    low, width = acc.shape
    for lanes in lane_blocks(width):
        slope, base = affine(stats_in, gain, shift, centre_in, lanes)
        slope_edge, base_edge = affine(stats_in, gain, shift, halo_centre, lanes)

        def act(p, rows):
            mask = load_mask(mask_ref.at[p], rows)
            value = silu_half(load(dev_in.at[p], rows, lanes) * slope + base) * mask
            store(hidden.at[p], rows, lanes, value)
            return value

        def act_edge(q, i):
            rows = edge_rows(i, rows_low)
            half = load(halo.at[q], rows, lanes) * slope_edge + base_edge
            return silu_half(half) * load_mask(halo_mask.at[q], rows)

        def step(rows, i, carry):
            act(0, rows)
            store(taps.at[0], rows, lanes, shifted(act(1, rows), -1))
            store(taps.at[1], rows, lanes, from_above(act(2, rows), act_edge(0, i), rows_low))
            odd = act(3, rows)
            store(taps.at[2], rows, lanes, shifted(odd, -1))
            above = from_above(odd, act_edge(1, i), rows_low)
            store(taps.at[3], rows, lanes, above)
            store(taps.at[4], rows, lanes, shifted(above, -1))
            return carry

        sweep(low, step, 0)

    def tap(t, u):
        k = (3 * t + u) * width
        return weight[k : k + width]

    total = dot(hidden[0], tap(1, 1))
    total += dot(hidden[1], tap(1, 2))
    total += dot(taps[0], tap(1, 0))
    total += dot(hidden[2], tap(2, 1))
    total += dot(taps[1], tap(0, 1))
    total += dot(hidden[3], tap(2, 2))
    total += dot(taps[2], tap(2, 0))
    total += dot(taps[3], tap(0, 2))
    total += dot(taps[4], tap(0, 0))
    acc[...] = total
    tally(first_step(), [(acc, mask_out, dev_out)], centre_out, stats_out)


def expand_kernel(
    dev_in, centre_in, stats_in, gain, shift, mask, weight, hidden, dev_out, centre_out, stats_out, acc
):
    for lanes in lane_blocks(dev_in.shape[1]):
        slope, base = affine(stats_in, gain, shift, centre_in, lanes)

        def step(rows, i, carry):
            half = load(dev_in, rows, lanes) * slope + base
            store(hidden, rows, lanes, silu_half(half) * load_mask(mask, rows))
            return carry

        sweep(dev_in.shape[0], step, 0)
    acc[...] = dot(hidden[...], weight[...])
    tally(first_step(), [(acc, mask, dev_out)], centre_out, stats_out)


def join_kernel(
    dev_a,
    centre_a,
    stats_a,
    gain_a,
    shift_a,
    dev_b,
    centre_b,
    stats_b,
    gain_b,
    shift_b,
    mask,
    weight,
    first_low,
    dev_out,
    centre_out,
    stats_out,
    acc,
):
    for lanes in lane_blocks(dev_a.shape[1]):
        slope_a, base_a = affine(stats_a, gain_a, shift_a, centre_a, lanes)
        slope_b, base_b = affine(stats_b, gain_b, shift_b, centre_b, lanes)
        base = base_a + base_b

        def step(rows, i, carry):
            half = load(dev_a, rows, lanes) * slope_a + load(dev_b, rows, lanes) * slope_b + base
            store(first_low, rows, lanes, silu_half(half) * load_mask(mask, rows))
            return carry

        sweep(dev_a.shape[0], step, 0)
    acc[...] = dot(first_low[...], weight[...])
    tally(first_step(), [(acc, mask, dev_out)], centre_out, stats_out)


def mid2_kernel(
    rows_low,
    dev_in,
    centre_in,
    halo,
    halo_centre,
    halo_mask,
    stats_in,
    gain,
    shift,
    mask,
    weight,
    hidden,
    dev_out,
    centre_out,
    stats_out,
    taps,
    acc,
):
    low, width = acc.shape
    for lanes in lane_blocks(width):
        slope, base = affine(stats_in, gain, shift, centre_in, lanes)
        edges = [affine(stats_in, gain, shift, halo_centre.at[e], lanes) for e in range(2)]

        def act_edge(e, i):
            rows = edge_rows(i, rows_low)
            half = load(halo.at[e], rows, lanes) * edges[e][0] + edges[e][1]
            return silu_half(half) * load_mask(halo_mask.at[e], rows)

        def step(rows, i, carry):
            value = silu_half(load(dev_in, rows, lanes) * slope + base) * load_mask(mask, rows)
            store(hidden, rows, lanes, value)
            lines = (
                from_above(value, act_edge(0, i), rows_low),
                value,
                from_below(value, act_edge(1, i), rows_low),
            )
            for t in range(3):
                for u in range(3):
                    start = (3 * t + u) * width + lanes.start
                    store(taps, rows, slice(start, start + LANES), shifted(lines[t], u - 1))
            return carry

        sweep(low, step, 0)
    acc[...] = dot(taps[...], weight[...])
    tally(first_step(), [(acc, mask, dev_out)], centre_out, stats_out)


def final_kernel(dev, centre, stats, gain, shift, first_low, cot, mask, block_out, gn_ref, sums):
    first = first_step()
    for lanes in lane_blocks(dev.shape[1]):
        slope, base = affine(stats, gain, shift, centre, lanes)

        def step(rows, i, carry):
            away = load(dev, rows, lanes)
            half = away * slope + base + 0.5 * load(first_low, rows, lanes)
            valid = load_mask(mask, rows)
            value, gate = silu_and_gate(half)
            store(block_out, rows, lanes, value * valid)
            gn = gate * valid * load(cot, rows, lanes)
            store(gn_ref, rows, lanes, gn)
            return carry[0] + column_sum(gn), carry[1] + column_sum(gn * away)

        gn_sum, gd_sum = sweep(dev.shape[0], step, (zeros8(), zeros8()))
        gn_sum, gd_sum = total_of(gn_sum), total_of(gd_sum)
        accumulate(first, sums, 0, lanes, gn_sum)
        accumulate(first, sums, 1, lanes, unit_sum(stats, centre, lanes, gn_sum, gd_sum))


def scaled(gn, away, mask, coefs):
    return (gn * coefs[0] + away * coefs[1] + coefs[2]) * mask


def gate_sums(first, grads, dev, centre, stats, gain, shift, mask, gn_ref, sums, parts):
    width = gn_ref.shape[-1]
    planes = range(parts) if parts else [None]
    for lanes in lane_blocks(width):
        slope, base = affine(stats, gain, shift, centre, lanes)
        carry = (zeros8(), zeros8())
        for p in planes:
            grad_p, dev_p, mask_p, gn_p = (
                r if p is None else r.at[p] for r in (grads, dev, mask, gn_ref)
            )

            def step(rows, i, carry, grad_p=grad_p, dev_p=dev_p, mask_p=mask_p, gn_p=gn_p):
                away = load(dev_p, rows, lanes)
                gate = gate_half(away * slope + base) * load_mask(mask_p, rows)
                gn = gate * load(grad_p, rows, lanes)
                store(gn_p, rows, lanes, gn)
                return carry[0] + column_sum(gn), carry[1] + column_sum(gn * away)

            carry = sweep(grad_p.shape[0], step, carry)
        gn_sum, gd_sum = total_of(carry[0]), total_of(carry[1])
        accumulate(first, sums, 0, lanes, gn_sum)
        accumulate(first, sums, 1, lanes, unit_sum(stats, centre, lanes, gn_sum, gd_sum))


def back_expand_kernel(
    gn,
    dev,
    centre,
    stats,
    gain,
    sums_in,
    mask,
    weight,
    dev_m,
    centre_m,
    stats_m,
    gain_m,
    shift_m,
    ga,
    gn_m,
    sums_m,
    acc,
):
    for lanes in lane_blocks(dev.shape[1]):
        coefs = back_coefs(
            stats, gain, centre, (sums_in[0:1, lanes], sums_in[1:2, lanes]), lanes
        )

        def step(rows, i, carry):
            away = load(dev, rows, lanes)
            store(ga, rows, lanes, scaled(load(gn, rows, lanes), away, load_mask(mask, rows), coefs))
            return carry

        sweep(dev.shape[0], step, 0)
    acc[...] = dot_t(ga[...], weight[...])
    gate_sums(first_step(), acc, dev_m, centre_m, stats_m, gain_m, shift_m, mask, gn_m, sums_m, 0)


def back_mid2_kernel(
    rows_low,
    gn,
    dev,
    centre,
    halo_gn,
    halo_dev,
    halo_centre,
    halo_mask,
    stats,
    gain,
    sums_in,
    mask,
    weight,
    dev_m,
    centre_m,
    stats_m,
    gain_m,
    shift_m,
    views,
    gn_m,
    sums_m,
    acc,
):
    low, width = acc.shape
    for lanes in lane_blocks(width):
        sums = (sums_in[0:1, lanes], sums_in[1:2, lanes])
        coefs = back_coefs(stats, gain, centre, sums, lanes)
        edges = [back_coefs(stats, gain, halo_centre.at[e], sums, lanes) for e in range(2)]

        def edge(e, i):
            rows = edge_rows(i, rows_low)
            return scaled(
                load(halo_gn.at[e], rows, lanes),
                load(halo_dev.at[e], rows, lanes),
                load_mask(halo_mask.at[e], rows),
                edges[e],
            )

        def step(rows, i, carry):
            value = scaled(
                load(gn, rows, lanes), load(dev, rows, lanes), load_mask(mask, rows), coefs
            )
            lines = (
                from_below(value, edge(1, i), rows_low),
                value,
                from_above(value, edge(0, i), rows_low),
            )
            for t in range(3):
                for u in range(3):
                    start = (3 * t + u) * width + lanes.start
                    store(views, rows, slice(start, start + LANES), shifted(lines[t], 1 - u))
            return carry

        sweep(low, step, 0)
    total = dot_t(views[:, :width], weight[:width])
    for k in range(width, 9 * width, width):
        total += dot_t(views[:, k : k + width], weight[k : k + width])
    acc[...] = total
    gate_sums(first_step(), acc, dev_m, centre_m, stats_m, gain_m, shift_m, mask, gn_m, sums_m, 0)


def back_join_kernel(
    gn_in,
    dev_in,
    centre_in,
    stats_in,
    gain_in,
    sums_in,
    mask,
    weight,
    residual,
    dev_a,
    centre_a,
    stats_a,
    gain_a,
    shift_a,
    dev_b,
    centre_b,
    stats_b,
    gain_b,
    shift_b,
    ga,
    gs_ref,
    sums,
    acc,
):
    first = first_step()
    for lanes in lane_blocks(dev_in.shape[1]):
        coefs = back_coefs(
            stats_in, gain_in, centre_in, (sums_in[0:1, lanes], sums_in[1:2, lanes]), lanes
        )

        def step(rows, i, carry):
            away = load(dev_in, rows, lanes)
            value = scaled(load(gn_in, rows, lanes), away, load_mask(mask, rows), coefs)
            store(ga, rows, lanes, value)
            return carry

        sweep(dev_in.shape[0], step, 0)
    acc[...] = dot_t(ga[...], weight[...])
    for lanes in lane_blocks(dev_a.shape[1]):
        slope_a, base_a = affine(stats_a, gain_a, shift_a, centre_a, lanes)
        slope_b, base_b = affine(stats_b, gain_b, shift_b, centre_b, lanes)
        base = base_a + base_b

        def gate(rows, i, carry):
            away_a, away_b = load(dev_a, rows, lanes), load(dev_b, rows, lanes)
            half = away_a * slope_a + away_b * slope_b + base
            grad = load(residual, rows, lanes) + load(acc, rows, lanes)
            gs = gate_half(half) * load_mask(mask, rows) * grad
            store(gs_ref, rows, lanes, gs)
            return (
                carry[0] + column_sum(gs),
                carry[1] + column_sum(gs * away_a),
                carry[2] + column_sum(gs * away_b),
            )

        carry = sweep(dev_a.shape[0], gate, (zeros8(), zeros8(), zeros8()))
        gs_sum, a_sum, b_sum = (total_of(part) for part in carry)
        accumulate(first, sums, 0, lanes, gs_sum)
        accumulate(first, sums, 1, lanes, unit_sum(stats_a, centre_a, lanes, gs_sum, a_sum))
        accumulate(first, sums, 2, lanes, unit_sum(stats_b, centre_b, lanes, gs_sum, b_sum))


def back_split_kernel(
    gs,
    dev_a,
    centre_a,
    stats_a,
    gain_a,
    dev_b,
    centre_b,
    stats_b,
    gain_b,
    sums_in,
    mask,
    weight_a,
    weight_b,
    dev_m,
    centre_m,
    stats_m,
    gain_m,
    shift_m,
    ga_a,
    ga_b,
    gn_m,
    grad_skip,
    sums_m,
    acc,
):
    for lanes in lane_blocks(dev_a.shape[1]):
        shift_sum = sums_in[0:1, lanes]
        coefs_a = back_coefs(stats_a, gain_a, centre_a, (shift_sum, sums_in[1:2, lanes]), lanes)
        coefs_b = back_coefs(stats_b, gain_b, centre_b, (shift_sum, sums_in[2:3, lanes]), lanes)

        def step(rows, i, carry):
            value, valid = load(gs, rows, lanes), load_mask(mask, rows)
            store(ga_a, rows, lanes, scaled(value, load(dev_a, rows, lanes), valid, coefs_a))
            store(ga_b, rows, lanes, scaled(value, load(dev_b, rows, lanes), valid, coefs_b))
            return carry

        sweep(dev_a.shape[0], step, 0)
    grad_skip[...] = dot_t(ga_b[...], weight_b[...]).astype(BF16)
    acc[...] = dot_t(ga_a[...], weight_a[...])
    gate_sums(first_step(), acc, dev_m, centre_m, stats_m, gain_m, shift_m, mask, gn_m, sums_m, 0)


def back_mid1_kernel(
    rows_low,
    gn,
    dev,
    centre,
    halo_gn,
    halo_dev,
    halo_centre,
    halo_mask,
    stats,
    gain,
    sums_in,
    mask,
    weight,
    dev_m,
    centre_m,
    mask_m,
    stats_m,
    gain_m,
    shift_m,
    views,
    gn_m,
    sums_m,
    acc,
):
    _, low, width = acc.shape
    for lanes in lane_blocks(width):
        sums = (sums_in[0:1, lanes], sums_in[1:2, lanes])
        coefs = back_coefs(stats, gain, centre, sums, lanes)
        coefs_edge = back_coefs(stats, gain, halo_centre, sums, lanes)

        def step(rows, i, carry):
            value = scaled(
                load(gn, rows, lanes), load(dev, rows, lanes), load_mask(mask, rows), coefs
            )
            some = edge_rows(i, rows_low)
            edge = scaled(
                load(halo_gn, some, lanes),
                load(halo_dev, some, lanes),
                load_mask(halo_mask, some),
                coefs_edge,
            )
            below = from_below(value, edge, rows_low)
            for k, view in enumerate((below, value, shifted(value, 1), shifted(below, 1))):
                start = k * width + lanes.start
                store(views, rows, slice(start, start + LANES), view)
            return carry

        sweep(low, step, 0)

    def view(k):
        return views[:, k * width : (k + 1) * width]

    def tap(t, u):
        k = (3 * t + u) * width
        return weight[k : k + width]

    acc[0] = dot_t(view(1), tap(1, 1))
    acc[1] = dot_t(view(1), tap(1, 2)) + dot_t(view(2), tap(1, 0))
    acc[2] = dot_t(view(1), tap(2, 1)) + dot_t(view(0), tap(0, 1))
    acc[3] = (
        dot_t(view(1), tap(2, 2))
        + dot_t(view(2), tap(2, 0))
        + dot_t(view(0), tap(0, 2))
        + dot_t(view(3), tap(0, 0))
    )
    gate_sums(
        first_step(), acc, dev_m, centre_m, stats_m, gain_m, shift_m, mask_m, gn_m, sums_m, 4
    )


def back_image_kernel(
    gn, dev, centre, stats, gain, sums_in, mask_ref, weight, grad_skip, perm_ref, ga, image, planes_ref
):
    planes, low, width = ga.shape
    for lanes in lane_blocks(width):
        coefs = back_coefs(
            stats, gain, centre, (sums_in[0:1, lanes], sums_in[1:2, lanes]), lanes
        )
        for p in range(planes):

            def step(rows, i, carry):
                away = load(dev.at[p], rows, lanes)
                valid = load_mask(mask_ref.at[p], rows)
                value = scaled(load(gn.at[p], rows, lanes), away, valid, coefs)
                store(ga.at[p], rows, lanes, value)
                return carry

            sweep(low, step, 0)
    planes_ref[0] = (dot_t(ga[0], weight[...]) + grad_skip[...].astype(F32)).astype(BF16)
    for p in range(1, planes):
        planes_ref[p] = dot_t(ga[p], weight[...]).astype(BF16)
    group = perm_ref.shape[0]
    part = group // planes
    for g in range(image.shape[0] // group):
        rows = slice(g * part, (g + 1) * part)
        mask = jnp.concatenate([mask_ref[p, rows, :] for p in range(planes)], axis=0)
        mask = jnp.concatenate([mask] * (group // 128), axis=1)
        perm = (perm_ref[...].astype(F32) * mask).astype(BF16)
        here = jnp.concatenate([planes_ref[p, rows, :] for p in range(planes)], axis=0)
        back = lax.dot_general(
            perm, here, (((0,), (0,)), ((), ())), preferred_element_type=F32
        )
        image[g * group : (g + 1) * group, :] = back.astype(BF16)


def spec_of(shape, kind, blocks):
    if kind == BY_ROWS:
        return pl.BlockSpec((shape[0] // blocks, shape[1]), lambda b: (b, 0))
    if kind == BY_PLANES:
        return pl.BlockSpec((shape[0], shape[1] // blocks, shape[2]), lambda b: (0, b, 0))
    if kind == FIRST_PLANE:
        return pl.BlockSpec((None, shape[1] // blocks, shape[2]), lambda b: (0, b, 0))
    if kind == BY_BLOCK:
        return pl.BlockSpec((None,) + tuple(shape[1:]), lambda b: (b, 0, 0))
    if kind == PAIR_BLOCK:
        return pl.BlockSpec((2, None) + tuple(shape[2:]), lambda b: (0, b, 0, 0))
    zero = (0,) * len(shape)
    return pl.BlockSpec(tuple(shape), lambda b: zero, pipeline_mode=pl.Buffered(1))


def out_spec(shape, kind, blocks):
    if kind == WHOLE:
        zero = (0,) * len(shape)
        return pl.BlockSpec(tuple(shape), lambda b: zero)
    return spec_of(shape, kind, blocks)


def stage(kernel, blocks, ins, outs, scratch=(), flops=0):
    return call(kernel, blocks, ins, outs, scratch, flops, [], [], {})


def call(kernel, blocks, ins, outs, scratch, flops, more_specs, more_shapes, params):
    moved = sum(x.size * x.dtype.itemsize for x, _ in ins)
    moved += sum(int(np.prod(s)) * jnp.dtype(d).itemsize for s, d, _ in outs)
    made = [pltpu.VMEM(*item) if isinstance(item, tuple) else item for item in scratch]
    return pl.pallas_call(
        kernel,
        grid=(blocks,),
        in_specs=[spec_of(x.shape, kind, blocks) for x, kind in ins],
        out_specs=[out_spec(s, kind, blocks) for s, _, kind in outs] + more_specs,
        out_shape=[jax.ShapeDtypeStruct(s, d) for s, d, _ in outs] + more_shapes,
        scratch_shapes=made,
        compiler_params=pltpu.CompilerParams(
            dimension_semantics=("arbitrary",), vmem_limit_bytes=VMEM_BYTES, **params
        ),
        cost_estimate=pl.CostEstimate(flops=flops, bytes_accessed=moved, transcendentals=0),
    )(*[x for x, _ in ins])


def merge_rows(buf, peers, merge, mean_only):
    if not merge:
        total = buf[0]
        for k in range(1, peers):
            total = total + buf[k]
        return total
    counts = [buf[k, 0:1, :] for k in range(peers)]
    means = [buf[k, 1:2, :] for k in range(peers)]
    count, weighted = counts[0], counts[0] * means[0]
    for k in range(1, peers):
        count = count + counts[k]
        weighted = weighted + counts[k] * means[k]
    safe = jnp.maximum(count, 1.0)
    mean = weighted / safe
    squares = jnp.zeros_like(mean)
    for k in range(peers):
        squares = squares + buf[k, 2:3, :] + counts[k] * jnp.square(means[k] - mean)
    if mean_only:
        squares = squares / safe
    return jnp.concatenate([count, mean, squares], axis=0)


class Exchange:
    def __init__(self, rows_n, img_n, blocks):
        self.rows_n, self.img_n, self.blocks = rows_n, img_n, blocks
        self.calls = 0

    def __call__(
        self, kernel, ins, outs, merge, lines, widths, scratch=(), flops=0, edges=(), centres=None, edge=0
    ):
        ident, self.calls = self.calls, self.calls + 1
        total, dma = sum(widths), pltpu.SemaphoreType.DMA
        any_space = pl.BlockSpec(memory_space=pl.ANY)
        specs = [out_spec((lines, w), WHOLE, 1) for w in widths]
        shapes = [jax.ShapeDtypeStruct((lines, w), F32) for w in widths]
        extra = []
        if edges:
            middle = outs[edges[0][0]][0][-1]
            specs.append(any_space)
            shapes.append(jax.ShapeDtypeStruct((len(edges), edge, middle), BF16))
            extra += [
                ((len(edges), edge, middle), BF16),
                dma((len(edges), self.blocks)),
                dma((len(edges), self.blocks)),
                dma((len(edges),)),
            ]
        if centres:
            count, shape = len(centres[1]), outs[centres[0]][0]
            specs.append(any_space)
            shapes.append(jax.ShapeDtypeStruct((count,) + tuple(shape), F32))
            extra += [(tuple(shape), F32), dma((count,)), dma((count,)), dma((count,))]
        extra += [
            ((self.rows_n, lines, total), F32),
            ((self.img_n, lines, total), F32),
            ((lines, total), F32),
            dma((self.rows_n,)),
            dma((self.rows_n,)),
            dma((self.img_n,)),
            dma((self.img_n,)),
        ]
        return call(
            functools.partial(
                self.kernel, kernel, len(ins), len(outs), len(scratch), merge, widths, edges, centres
            ),
            self.blocks,
            ins,
            outs,
            [((lines, total), F32)] + list(scratch) + extra,
            flops,
            specs,
            shapes,
            dict(collective_id=ident, has_side_effects=True),
        )

    def kernel(self, kernel, ins_n, outs_n, scratch_n, merge, widths, edges, centres, *refs):
        rows_n, img_n, blocks = self.rows_n, self.img_n, self.blocks
        refs = list(refs)

        def take(count):
            taken = refs[:count]
            del refs[:count]
            return taken

        ins, outs, totals = take(ins_n), take(outs_n), take(len(widths))
        halo = take(1)[0] if edges else None
        halo_centres = take(1)[0] if centres else None
        mine = take(1)[0]
        scratch = take(scratch_n)
        if edges:
            edge_buf, edge_send, edge_recv, edge_local = take(4)
        if centres:
            centre_buf, centre_send, centre_recv, centre_local = take(4)
        buf_r, buf_i, part, send_r, recv_r, send_i, recv_i = refs
        block = pl.program_id(0)
        row, img = lax.axis_index("rows"), lax.axis_index("img")
        barrier = pltpu.get_barrier_semaphore()

        @pl.when(block == 0)
        def _():
            for k in range(1, rows_n):
                peer = {"rows": lax.rem(row + k, rows_n)}
                pl.semaphore_signal(barrier, inc=1, device_id=peer, device_id_type=MESH)
            for k in range(1, img_n):
                peer = {"img": lax.rem(img + k, img_n)}
                pl.semaphore_signal(barrier, inc=1, device_id=peer, device_id_type=MESH)

        kernel(*ins, *outs, mine, *scratch)

        @pl.when(block == 0)
        def _():
            pl.semaphore_wait(barrier, rows_n + img_n - 2)

        def remote(source, target, send, recv, peer):
            return pltpu.make_async_remote_copy(
                src_ref=source,
                dst_ref=target,
                send_sem=send,
                recv_sem=recv,
                device_id=peer,
                device_id_type=MESH,
            )

        def sends(direction):
            return row < rows_n - 1 if direction > 0 else row > 0

        def receives(direction):
            return row > 0 if direction > 0 else row < rows_n - 1

        if edges:
            some = edge_buf.shape[1] // blocks

            def edge_copy(e, b):
                here = pl.ds(pl.multiple_of(b * some, some), some)
                return remote(
                    edge_buf.at[e, here],
                    halo.at[e, here],
                    edge_send.at[e, b],
                    edge_recv.at[e, b],
                    {"rows": row + edges[e][3]},
                )

            for e, (out, plane, last_row, direction) in enumerate(edges):
                source = outs[out] if plane is None else outs[out].at[plane]
                here = pl.ds(pl.multiple_of(block * some, some), some)
                for lanes in lane_blocks(source.shape[1]):
                    value = load(source, slice(None), lanes)
                    lines = value.reshape((some // 8, -1) + value.shape[1:])
                    store(edge_buf.at[e], here, lanes, lines[:, -1 if last_row else 0])

                @pl.when(sends(direction))
                def _(e=e):
                    edge_copy(e, block).start()

        if centres:
            centre_buf[pl.ds(block, 1)] = outs[centres[0]][...][None]

        def exchange(axis, me, peers, source, buf, send, recv):
            copies = []
            for k in range(1, peers):
                peer = {axis: lax.rem(me + k, peers)}
                copies.append(remote(source, buf.at[me], send.at[k], recv.at[me], peer))
                copies[-1].start()
            buf[pl.ds(me, 1)] = source[...][None]
            for k in range(1, peers):
                peer = lax.rem(me + k, peers)
                remote(source, buf.at[peer], send.at[k], recv.at[peer], {axis: peer}).wait_recv()
            return copies

        @pl.when(block == blocks - 1)
        def _():
            def centre_copy(k):
                peer = {"rows": row + centres[1][k]}
                return remote(
                    centre_buf, halo_centres.at[k], centre_send.at[k], centre_recv.at[k], peer
                )

            directions = centres[1] if centres else ()
            for k, direction in enumerate(directions):

                @pl.when(sends(direction))
                def _(k=k):
                    centre_copy(k).start()

            copies = exchange("rows", row, rows_n, mine, buf_r, send_r, recv_r)
            part[...] = merge_rows(buf_r, rows_n, merge, False)
            copies += exchange("img", img, img_n, part, buf_i, send_i, recv_i)
            total = merge_rows(buf_i, img_n, merge, True)
            start = 0
            for out, width in zip(totals, widths):
                out[...] = total[:, start : start + width]
                start += width
            for k, direction in enumerate(directions):
                own = pltpu.make_async_copy(centre_buf, halo_centres.at[k], centre_local.at[k])

                @pl.when(receives(direction))
                def _(k=k):
                    centre_copy(k).wait_recv()

                @pl.when(jnp.logical_not(receives(direction)))
                def _(own=own):
                    own.start()
                    own.wait()

                @pl.when(sends(direction))
                def _(k=k):
                    centre_copy(k).wait_send()

            for e, spec in enumerate(edges):
                own = pltpu.make_async_copy(edge_buf.at[e], halo.at[e], edge_local.at[e])

                @pl.when(receives(spec[3]))
                def _(e=e):
                    for b in range(blocks):
                        edge_copy(e, b).wait_recv()

                @pl.when(jnp.logical_not(receives(spec[3])))
                def _(own=own):
                    own.start()
                    own.wait()

                @pl.when(sends(spec[3]))
                def _(e=e):
                    for b in range(blocks):
                        edge_copy(e, b).wait_send()

            for copy in copies:
                copy.wait_send()


CHUNK_ROWS = 64
CHUNK_LANES = 1024


HID_MID2, GA_OUT2, HID_IN2, VIEWS2, FIRST, GA_IN2, HID_MID1, GA_OUT1, GA_SKIP, VIEWS1 = range(10)
HID, PLANE, GA_IN1 = 10, 14, 18
ONE, TWO, HALF, QUAD, DEEP = range(5)
WIDTHS = {ONE: (512, 1024), TWO: (1024, 512), HALF: (512, 512), QUAD: (1024, 256), DEEP: (1024, 512)}


def plan_jobs():
    chunks = [[(ONE, 0, HID_MID2, 0, GA_OUT2, 1024 * k)] for k in range(2)]
    chunks += [[(ONE, 0, HID_IN2, 0, VIEWS2, 1024 * k)] for k in range(4)]
    chunks += [[(HALF, 0, HID_IN2, 0, VIEWS2, 4096), (HALF, 1, HID, 0, VIEWS1, 512)]]
    chunks += [[(QUAD, h, FIRST, 1024 * h, GA_IN2, 256 * k) for h in range(2)] for k in range(2)]
    chunks += [[(DEEP, p, PLANE + p, 0, GA_IN1 + p, 0) for p in range(4)]]
    chunks += [[(ONE, 0, HID_MID1, 0, GA_OUT1, 1024 * k)] for k in range(2)]
    chunks += [[(TWO, 0, PLANE, 0, GA_SKIP, 512 * k)] for k in range(4)]
    chunks += [[(ONE, 0, HID + 1, 0, VIEWS1, 512)], [(ONE, 0, HID + 2, 0, VIEWS1, 0)]]
    chunks += [[(ONE, 0, HID + 3, 0, VIEWS1, 1024 * k)] for k in range(2)]
    return chunks


def weights_kernel(
    rows_n,
    hid_mid2,
    ga_out2,
    hid_in2,
    views2,
    first_low,
    ga_in2,
    hid_mid1,
    ga_out1,
    planes,
    ga_skip,
    hid_in1,
    views1,
    ga_in1,
    done,
    lhs_buf,
    rhs_buf,
    deep,
    chunk_buf,
    own,
    got1,
    got2a,
    got2b,
    got3a,
    got3b,
    got_low,
    got_high,
    lhs_sem,
    rhs_sem,
    *sems,
):
    (s1, r1, s2a, r2a, s2b, r2b, s3a, r3a, s3b, r3b, s_up, r_low, s_down, r_high, b_up, b_down, r_back) = sems
    sources = [hid_mid2, ga_out2, hid_in2, views2, first_low, ga_in2, hid_mid1, ga_out1, ga_skip, views1]
    for stack in (hid_in1, planes, ga_in1):
        sources += [stack.at[p] for p in range(4)]
    chunks = plan_jobs()
    jobs = [job for chunk in chunks for job in chunk]
    count = len(chunks)
    depth = chunk_buf.shape[0]
    img, z = lax.axis_index("img"), lax.axis_index("rows")
    y, x, c = img // 4, lax.rem(img // 2, 2), lax.rem(img, 2)
    root = rows_n // 2
    sibling = {"img": img + 1 - 2 * c}
    beside_x = {"img": img + 2 - 4 * x}
    beside_y = {"img": img + 4 - 8 * y}
    higher, lower = {"rows": z + 1}, {"rows": z - 1}
    half = CHUNK_LANES // 2
    left, right = slice(0, half), slice(half, 2 * half)

    def fetch(index):
        kind, _, lhs, lhs_start, rhs, rhs_start = jobs[index]
        lhs_width, rhs_width = WIDTHS[kind]
        slot = index % 2
        return (
            pltpu.make_async_copy(
                sources[lhs].at[:, lhs_start : lhs_start + lhs_width],
                lhs_buf.at[slot, :, :lhs_width],
                lhs_sem.at[slot],
            ),
            pltpu.make_async_copy(
                sources[rhs].at[:, rhs_start : rhs_start + rhs_width],
                rhs_buf.at[slot, :, :rhs_width],
                rhs_sem.at[slot],
            ),
        )

    for copy in fetch(0):
        copy.start()

    barrier = pltpu.get_barrier_semaphore()
    for peer in (sibling, beside_x, beside_y):
        pl.semaphore_signal(barrier, inc=1, device_id=peer, device_id_type=MESH)

    @pl.when(z > 0)
    def _():
        pl.semaphore_signal(barrier, inc=1, device_id=lower, device_id_type=MESH)

    @pl.when(z < rows_n - 1)
    def _():
        pl.semaphore_signal(barrier, inc=1, device_id=higher, device_id_type=MESH)

    pl.semaphore_wait(barrier, 3 + jnp.minimum(z, 1) + jnp.minimum(rows_n - 1 - z, 1))

    def put(slot, result, first, parts):
        width = CHUNK_LANES // parts
        rows = CHUNK_ROWS
        for m in range(result.shape[0] // (rows * parts)):
            shard = first + m
            for h in range(parts):
                piece = result[(m * parts + h) * rows : (m * parts + h + 1) * rows]
                chunk_buf[slot, shard // 4, shard // 2 % 2, shard % 2, :, h * width : (h + 1) * width] = piece

    def multiply(index, slot):
        kind, part = jobs[index][:2]
        lhs_width, rhs_width = WIDTHS[kind]
        here = index % 2

        def product():
            return lax.dot_general(
                lhs_buf[here, :, :lhs_width],
                rhs_buf[here, :, :rhs_width],
                (((0,), (0,)), ((), ())),
                preferred_element_type=F32,
            )

        if kind == ONE:
            put(slot, product().astype(BF16), 0, 1)
        elif kind == TWO:
            put(slot, product().astype(BF16), 0, 2)
        elif kind == QUAD:
            put(slot, product().astype(BF16), 4 * part, 4)
        elif kind == HALF:
            result = product().astype(BF16)
            for m in range(8):
                piece = result[m * CHUNK_ROWS : (m + 1) * CHUNK_ROWS]
                chunk_buf[slot, m // 4, m // 2 % 2, m % 2, :, (left, right)[part]] = piece
        elif part == 0:
            deep[...] = product()
        elif part == 3:
            put(slot, (deep[...] + product()).astype(BF16), 0, 2)
        else:
            deep[...] += product()

    def remote(source, target, send, recv, peer):
        return pltpu.make_async_remote_copy(
            src_ref=source,
            dst_ref=target,
            send_sem=send,
            recv_sem=recv,
            device_id=peer,
            device_id_type=MESH,
        )

    def to_core(t):
        source = chunk_buf.at[lax.rem(t, depth), :, :, 1 - c]
        return remote(source, got1.at[t], s1.at[t], r1.at[t], sibling)

    def to_2a(t):
        return remote(own.at[t, :, 1 - x, :, left], got2a.at[t], s2a.at[t], r2a.at[t], beside_x)

    def to_2b(t):
        return remote(own.at[t, 1 - y, :, :, right], got2b.at[t], s2b.at[t], r2b.at[t], beside_y)

    def to_3a(t):
        return remote(own.at[t, 1 - y, x, :, left], got3a.at[t], s3a.at[t], r3a.at[t], beside_y)

    def to_3b(t):
        return remote(own.at[t, y, 1 - x, :, right], got3b.at[t], s3b.at[t], r3b.at[t], beside_x)

    def up(t):
        return remote(own.at[t, y, x], got_low.at[t], s_up.at[t], r_low.at[t], higher)

    def down(t):
        return remote(own.at[t, y, x], got_high.at[t], s_down.at[t], r_high.at[t], lower)

    def back_up(t):
        return remote(done.at[t], done.at[t], b_up.at[t], r_back.at[t], higher)

    def back_down(t):
        return remote(done.at[t], done.at[t], b_down.at[t], r_back.at[t], lower)

    def compute(t):
        @pl.when(t >= depth)
        def _():
            to_core(t - depth).wait_send()

        slot = lax.rem(t, depth)
        index = 0
        for k, chunk in enumerate(chunks):
            first = index
            index += len(chunk)

            @pl.when(t == k)
            def _(first=first, chunk=chunk):
                for n in range(first, first + len(chunk)):
                    for copy in fetch(n):
                        copy.wait()
                    if n + 1 < len(jobs):
                        for copy in fetch(n + 1):
                            copy.start()
                    multiply(n, slot)

        to_core(t).start()

    def stage1(t):
        to_core(t).wait_recv()
        slot = lax.rem(t, depth)
        for a in range(2):
            for b in range(2):
                own[t, a, b] = chunk_buf[slot, a, b, c] + got1[t, a, b]
        to_2a(t).start()
        to_2b(t).start()

    def stage2(t):
        to_2a(t).wait_recv()
        for a in range(2):
            own[t, a, x, :, left] = own[t, a, x, :, left] + got2a[t, a]
        to_3a(t).start()
        to_2b(t).wait_recv()
        for a in range(2):
            own[t, y, a, :, right] = own[t, y, a, :, right] + got2b[t, a]
        to_3b(t).start()

    def stage3(t):
        to_3a(t).wait_recv()
        own[t, y, x, :, left] = own[t, y, x, :, left] + got3a[t]
        to_3b(t).wait_recv()
        own[t, y, x, :, right] = own[t, y, x, :, right] + got3b[t]

        @pl.when(z == 0)
        def _():
            up(t).start()

        @pl.when(z == rows_n - 1)
        def _():
            down(t).start()

    def stage4(t):
        @pl.when((z > 0) & (z < root))
        def _():
            up(t).wait_recv()
            own[t, y, x] = own[t, y, x] + got_low[t]
            up(t).start()

        @pl.when((z < rows_n - 1) & (z > root))
        def _():
            down(t).wait_recv()
            own[t, y, x] = own[t, y, x] + got_high[t]
            down(t).start()

    def stage5(t):
        @pl.when(z == root)
        def _():
            up(t).wait_recv()
            down(t).wait_recv()
            total = own[t, y, x].astype(F32) + got_low[t].astype(F32) + got_high[t].astype(F32)
            done[t] = total.astype(BF16)
            back_up(t).start()
            back_down(t).start()

    def stage6(t):
        @pl.when(z > root)
        def _():
            back_up(t).wait_recv()

            @pl.when(z < rows_n - 1)
            def _():
                back_up(t).start()

        @pl.when((z < root) & (z > 0))
        def _():
            back_down(t).wait_recv()
            back_down(t).start()

    def stage7(t):
        @pl.when(z == 0)
        def _():
            back_down(t).wait_recv()

    stages = (compute, stage1, stage2, stage3, stage4, stage5, stage6, stage7)

    def step(s, carry):
        for lag, work in enumerate(stages):
            t = s - lag

            @pl.when((t >= 0) & (t < count))
            def _(t=t, work=work):
                work(t)

        return carry

    lax.fori_loop(0, count + len(stages) - 1, step, 0)

    def finish(t, carry):
        @pl.when(t >= count - depth)
        def _():
            to_core(t).wait_send()

        for copy in (to_2a(t), to_2b(t), to_3a(t), to_3b(t)):
            copy.wait_send()

        @pl.when(z < root)
        def _():
            up(t).wait_send()

        @pl.when(z > root)
        def _():
            down(t).wait_send()

        @pl.when((z >= root) & (z < rows_n - 1))
        def _():
            back_up(t).wait_send()

        @pl.when((z <= root) & (z > 0))
        def _():
            back_down(t).wait_send()

        return carry

    lax.fori_loop(0, count, finish, 0)


def summed_weights(rows_n, ident, operands):
    count = len(plan_jobs())
    low = operands[0].shape[0]
    rows, lanes = CHUNK_ROWS, CHUNK_LANES
    dma = pltpu.SemaphoreType.DMA
    depth = 3
    buffers = [
        (2, low, 1024),
        (2, low, 1024),
        None,
        (depth, 2, 2, 2, rows, lanes),
        (count, 2, 2, rows, lanes),
        (count, 2, 2, rows, lanes),
        (count, 2, rows, lanes // 2),
        (count, 2, rows, lanes // 2),
        (count, rows, lanes // 2),
        (count, rows, lanes // 2),
        (count, rows, lanes),
        (count, rows, lanes),
    ]
    scratch = [pltpu.VMEM(b, BF16) if b else pltpu.VMEM((1024, 512), F32) for b in buffers]
    return pl.pallas_call(
        functools.partial(weights_kernel, rows_n),
        in_specs=[pl.BlockSpec(memory_space=pl.ANY)] * len(operands),
        out_specs=pl.BlockSpec(memory_space=pltpu.VMEM),
        out_shape=jax.ShapeDtypeStruct((count, rows, lanes), BF16),
        scratch_shapes=scratch + [dma((2,)), dma((2,))] + [dma((count,))] * 17,
        compiler_params=pltpu.CompilerParams(
            collective_id=ident, has_side_effects=True, vmem_limit_bytes=63 * 1024 * 1024
        ),
        cost_estimate=pl.CostEstimate(
            flops=40_000_000_000, bytes_accessed=100_000_000, transcendentals=0
        ),
    )(*operands)


def unpack_kernel(sums_n, done, *refs):
    sums, outs = refs[:sums_n], refs[sums_n:]
    in1, mid1, out1, skip, in2, mid2, out2 = outs[:7]
    rows, lanes = CHUNK_ROWS, CHUNK_LANES
    half = lanes // 2

    def wide(k):
        return done[k].astype(F32)

    def stacked(first, count, parts, out):
        width = lanes // parts
        for k in range(count):
            for h in range(parts):
                piece = done[first + k, :, h * width : (h + 1) * width]
                out[h * rows : (h + 1) * rows, k * width : (k + 1) * width] = piece.astype(F32)

    for k in range(2):
        out2[:, k * lanes : (k + 1) * lanes] = wide(k)
        out1[:, k * lanes : (k + 1) * lanes] = wide(10 + k)
    taps2 = [(2 + k // 2, k % 2) for k in range(8)] + [(6, 0)]
    taps1 = [(19, 1), (17, 0), (18, 0), (16, 1), (6, 1), (16, 0), (19, 0), (17, 1), (18, 1)]
    for out, taps in ((mid1, taps1), (mid2, taps2)):
        for k, (chunk, side) in enumerate(taps):
            out[k] = done[chunk, :, side * half : (side + 1) * half].astype(F32)
    stacked(7, 2, 4, in2)
    stacked(9, 1, 2, in1)
    stacked(12, 4, 2, skip)
    rest = list(outs[7:])
    for ref in sums:
        for k in range(ref.shape[0]):
            rest.pop(0)[...] = ref[k : k + 1, :]


def unpack(done, sums):
    rows = CHUNK_ROWS
    shapes = [(128, 512), (9, rows, 512), (rows, 2048), (128, 2048), (256, 512), (9, rows, 512), (rows, 2048)]
    shapes += [(1, x.shape[1]) for x in sums for _ in range(x.shape[0])]
    vmem = pl.BlockSpec(memory_space=pltpu.VMEM)
    outs = pl.pallas_call(
        functools.partial(unpack_kernel, len(sums)),
        in_specs=[vmem] * (1 + len(sums)),
        out_specs=[vmem] * len(shapes),
        out_shape=[jax.ShapeDtypeStruct(shape, F32) for shape in shapes],
        compiler_params=pltpu.CompilerParams(vmem_limit_bytes=32 * 1024 * 1024),
    )(done, *sums)
    return outs[:7], [x.reshape(-1) for x in outs[7:]]


def lanes128(mask):
    return jnp.broadcast_to(mask.astype(F32)[..., None], mask.shape + (128,))


def body(
    image_in,
    extent,
    weight_in1,
    weight_mid1,
    weight_out1,
    weight_skip,
    weight_in2,
    weight_mid2,
    weight_out2,
    gain_in1,
    shift_in1,
    gain_mid1,
    shift_mid1,
    gain_out1,
    shift_out1,
    gain_skip,
    shift_skip,
    gain_in2,
    shift_in2,
    gain_mid2,
    shift_mid2,
    gain_out2,
    shift_out2,
    cotangent,
):
    images, rows_here, columns, inputs = image_in.shape
    middle, outputs = weight_out1.shape
    rows_low, cols_low = rows_here // 2, columns // 2
    low = images * rows_low * cols_low
    rows_n, img_n = lax.axis_size("rows"), lax.axis_size("img")
    blocks = images // IMAGES
    per_block = low // blocks
    edge = images * cols_low
    run = Exchange(rows_n, img_n, blocks)

    row0 = lax.axis_index("rows") * rows_here
    half = extent // 2

    def inside(rows, cols, side):
        kept = (rows[None, :, None] >= 0) & (rows[None, :, None] < side[:, None, None])
        return kept & (cols[None, None, :] < side[:, None, None])

    low_rows = jnp.arange(rows_low, dtype=jnp.int32)
    low_cols = jnp.arange(cols_low, dtype=jnp.int32)
    mask_in = jnp.stack(
        [
            inside(row0 + 2 * low_rows + p, 2 * low_cols + q, extent).reshape(-1)
            for p in range(2)
            for q in range(2)
        ]
    )
    mask_in = lanes128(mask_in)
    mask_out = lanes128(inside(row0 // 2 + low_rows, low_cols, half).reshape(-1))
    above = jnp.stack([row0 - 1])
    mask_above = lanes128(
        jnp.stack([inside(above, 2 * low_cols + q, extent).reshape(-1) for q in range(2)])
    )
    mask_edges = lanes128(
        jnp.stack(
            [
                inside(jnp.stack([line]), low_cols, half).reshape(-1)
                for line in (row0 // 2 - 1, row0 // 2 + rows_low)
            ]
        )
    )

    group_images = 256 // (rows_here * columns)
    order = np.arange(256).reshape(group_images, rows_low, 2, cols_low, 2)
    order = order.transpose(2, 4, 0, 1, 3).reshape(-1)
    perm = jnp.asarray(np.eye(256, dtype=np.float32)[order], BF16)

    def row(vector):
        return vector.reshape(1, -1)

    g_in1, s_in1, g_mid1, s_mid1 = row(gain_in1), row(shift_in1), row(gain_mid1), row(shift_mid1)
    g_out1, s_out1, g_skip, s_skip = row(gain_out1), row(shift_out1), row(gain_skip), row(shift_skip)
    g_in2, s_in2, g_mid2, s_mid2 = row(gain_in2), row(shift_in2), row(gain_mid2), row(shift_mid2)
    g_out2, s_out2 = row(gain_out2), row(shift_out2)
    kernel_mid1 = weight_mid1.transpose(1, 2, 0, 3).reshape(9 * middle, middle)
    kernel_mid2 = weight_mid2.transpose(1, 2, 0, 3).reshape(9 * middle, middle)
    cot = cotangent.reshape(low, outputs)

    dev_mid_out = [((low, middle), BF16, BY_ROWS), ((blocks, 1, middle), F32, BY_BLOCK)]
    dev_out_out = [((low, outputs), BF16, BY_ROWS), ((blocks, 1, outputs), F32, BY_BLOCK)]
    hidden_out = [((low, middle), BF16, BY_ROWS)]
    wide_out = [((low, outputs), BF16, BY_ROWS)]
    acc_mid, acc_out = ((per_block, middle), F32), ((per_block, outputs), F32)
    unit_flops = 2 * low * middle * middle

    def normal(dev, centre, stats, gain, shift, kind=BY_ROWS):
        return [(dev, kind), (centre, BY_BLOCK), (stats, WHOLE), (gain, WHOLE), (shift, WHOLE)]

    planes, d_in1, c_in1, d_skip, c_skip, n_in1, n_skip, halo_in1, halo_c_in1 = run(
        open_kernel,
        [
            (image_in.reshape(4 * low, inputs), BY_ROWS),
            (perm, WHOLE),
            (mask_in, BY_PLANES),
            (mask_out, BY_ROWS),
            (weight_in1, WHOLE),
            (weight_skip, WHOLE),
        ],
        [
            ((4, low, inputs), BF16, BY_PLANES),
            ((4, low, middle), BF16, BY_PLANES),
            ((blocks, 1, middle), F32, BY_BLOCK),
        ]
        + dev_out_out,
        True,
        3,
        (middle, outputs),
        scratch=[((4, per_block, middle), F32), acc_out],
        flops=20 * unit_flops,
        edges=[(1, 2, True, 1), (1, 3, True, 1)],
        centres=(2, (1,)),
        edge=edge,
    )
    hid_in1, d_mid1, c_mid1, n_mid1, halo_mid1, halo_c_mid1 = run(
        functools.partial(mid1_kernel, rows_low),
        [
            (d_in1, BY_PLANES),
            (c_in1, BY_BLOCK),
            (mask_in, BY_PLANES),
            (halo_in1, BY_PLANES),
            (halo_c_in1[0], BY_BLOCK),
            (mask_above, BY_PLANES),
            (n_in1, WHOLE),
            (g_in1, WHOLE),
            (s_in1, WHOLE),
            (mask_out, BY_ROWS),
            (kernel_mid1, WHOLE),
        ],
        [((4, low, middle), BF16, BY_PLANES)] + dev_mid_out,
        True,
        3,
        (middle,),
        scratch=[((5, per_block, middle), BF16), acc_mid],
        flops=9 * unit_flops,
        edges=[(1, None, False, -1)],
        centres=(2, (-1,)),
        edge=edge,
    )
    hid_mid1, d_out1, c_out1, n_out1 = run(
        expand_kernel,
        normal(d_mid1, c_mid1, n_mid1, g_mid1, s_mid1) + [(mask_out, BY_ROWS), (weight_out1, WHOLE)],
        hidden_out + dev_out_out,
        True,
        3,
        (outputs,),
        scratch=[acc_out],
        flops=4 * unit_flops,
    )
    join = normal(d_out1, c_out1, n_out1, g_out1, s_out1) + normal(d_skip, c_skip, n_skip, g_skip, s_skip)
    both = [(1, None, True, 1), (1, None, False, -1)]
    first_low, d_in2, c_in2, n_in2, halo_in2, halo_c_in2 = run(
        join_kernel,
        join + [(mask_out, BY_ROWS), (weight_in2, WHOLE)],
        wide_out + dev_mid_out,
        True,
        3,
        (middle,),
        scratch=[acc_mid],
        flops=4 * unit_flops,
        edges=both,
        centres=(2, (1, -1)),
        edge=edge,
    )

    hid_in2, d_mid2, c_mid2, n_mid2, halo_mid2, halo_c_mid2 = run(
        functools.partial(mid2_kernel, rows_low),
        [
            (d_in2, BY_ROWS),
            (c_in2, BY_BLOCK),
            (halo_in2, BY_PLANES),
            (halo_c_in2, PAIR_BLOCK),
            (mask_edges, BY_PLANES),
            (n_in2, WHOLE),
            (g_in2, WHOLE),
            (s_in2, WHOLE),
            (mask_out, BY_ROWS),
            (kernel_mid2, WHOLE),
        ],
        hidden_out + dev_mid_out,
        True,
        3,
        (middle,),
        scratch=[((per_block, 9 * middle), BF16), acc_mid],
        flops=9 * unit_flops,
        edges=both,
        centres=(2, (1, -1)),
        edge=edge,
    )
    hid_mid2, d_out2, c_out2, n_out2 = run(
        expand_kernel,
        normal(d_mid2, c_mid2, n_mid2, g_mid2, s_mid2) + [(mask_out, BY_ROWS), (weight_out2, WHOLE)],
        hidden_out + dev_out_out,
        True,
        3,
        (outputs,),
        scratch=[acc_out],
        flops=4 * unit_flops,
    )
    block_out, gn_out2, z_out2 = run(
        final_kernel,
        normal(d_out2, c_out2, n_out2, g_out2, s_out2)
        + [(first_low, BY_ROWS), (cot, BY_ROWS), (mask_out, BY_ROWS)],
        wide_out + wide_out,
        False,
        2,
        (outputs,),
    )

    ga_out2, gn_mid2, z_mid2, halo_gn_mid2 = run(
        back_expand_kernel,
        [
            (gn_out2, BY_ROWS),
            (d_out2, BY_ROWS),
            (c_out2, BY_BLOCK),
            (n_out2, WHOLE),
            (g_out2, WHOLE),
            (z_out2, WHOLE),
            (mask_out, BY_ROWS),
            (weight_out2, WHOLE),
        ]
        + normal(d_mid2, c_mid2, n_mid2, g_mid2, s_mid2),
        wide_out + hidden_out,
        False,
        2,
        (middle,),
        scratch=[acc_mid],
        flops=4 * unit_flops,
        edges=both,
        edge=edge,
    )
    views2, gn_in2, z_in2 = run(
        functools.partial(back_mid2_kernel, rows_low),
        [
            (gn_mid2, BY_ROWS),
            (d_mid2, BY_ROWS),
            (c_mid2, BY_BLOCK),
            (halo_gn_mid2, BY_PLANES),
            (halo_mid2, BY_PLANES),
            (halo_c_mid2, PAIR_BLOCK),
            (mask_edges, BY_PLANES),
            (n_mid2, WHOLE),
            (g_mid2, WHOLE),
            (z_mid2, WHOLE),
            (mask_out, BY_ROWS),
            (kernel_mid2, WHOLE),
        ]
        + normal(d_in2, c_in2, n_in2, g_in2, s_in2),
        [((low, 9 * middle), BF16, BY_ROWS)] + hidden_out,
        False,
        2,
        (middle,),
        scratch=[acc_mid],
        flops=9 * unit_flops,
    )
    ga_in2, gs1, z_sum1 = run(
        back_join_kernel,
        [
            (gn_in2, BY_ROWS),
            (d_in2, BY_ROWS),
            (c_in2, BY_BLOCK),
            (n_in2, WHOLE),
            (g_in2, WHOLE),
            (z_in2, WHOLE),
            (mask_out, BY_ROWS),
            (weight_in2, WHOLE),
            (gn_out2, BY_ROWS),
        ]
        + join,
        hidden_out + wide_out,
        False,
        3,
        (outputs,),
        scratch=[acc_out],
        flops=4 * unit_flops,
    )

    ga_out1, ga_skip, gn_mid1, grad_skip_in, z_mid1, halo_gn_mid1 = run(
        back_split_kernel,
        [
            (gs1, BY_ROWS),
            (d_out1, BY_ROWS),
            (c_out1, BY_BLOCK),
            (n_out1, WHOLE),
            (g_out1, WHOLE),
            (d_skip, BY_ROWS),
            (c_skip, BY_BLOCK),
            (n_skip, WHOLE),
            (g_skip, WHOLE),
            (z_sum1, WHOLE),
            (mask_out, BY_ROWS),
            (weight_out1, WHOLE),
            (weight_skip, WHOLE),
        ]
        + normal(d_mid1, c_mid1, n_mid1, g_mid1, s_mid1),
        wide_out + wide_out + hidden_out + [((low, inputs), BF16, BY_ROWS)],
        False,
        2,
        (middle,),
        scratch=[acc_mid],
        flops=12 * unit_flops,
        edges=[(2, None, False, -1)],
        edge=edge,
    )
    views1, gn_in1, z_in1 = run(
        functools.partial(back_mid1_kernel, rows_low),
        [
            (gn_mid1, BY_ROWS),
            (d_mid1, BY_ROWS),
            (c_mid1, BY_BLOCK),
            (halo_gn_mid1[0], BY_ROWS),
            (halo_mid1[0], BY_ROWS),
            (halo_c_mid1[0], BY_BLOCK),
            (mask_edges[1], BY_ROWS),
            (n_mid1, WHOLE),
            (g_mid1, WHOLE),
            (z_mid1, WHOLE),
            (mask_out, BY_ROWS),
            (kernel_mid1, WHOLE),
            (d_in1, BY_PLANES),
            (c_in1, BY_BLOCK),
            (mask_in, BY_PLANES),
            (n_in1, WHOLE),
            (g_in1, WHOLE),
            (s_in1, WHOLE),
        ],
        [((low, 4 * middle), BF16, BY_ROWS), ((4, low, middle), BF16, BY_PLANES)],
        False,
        2,
        (middle,),
        scratch=[((4, per_block, middle), F32)],
        flops=9 * unit_flops,
    )
    ga_in1, grad_image = stage(
        back_image_kernel,
        blocks,
        [
            (gn_in1, BY_PLANES),
            (d_in1, BY_PLANES),
            (c_in1, BY_BLOCK),
            (n_in1, WHOLE),
            (g_in1, WHOLE),
            (z_in1, WHOLE),
            (mask_in, BY_PLANES),
            (weight_in1, WHOLE),
            (grad_skip_in, BY_ROWS),
            (perm, WHOLE),
        ],
        [((4, low, middle), BF16, BY_PLANES), ((4 * low, inputs), BF16, BY_ROWS)],
        scratch=[((4, per_block, inputs), BF16)],
        flops=12 * unit_flops,
    )
    sums = [z_in1, z_mid1, z_sum1, z_in2, z_mid2, z_out2]

    if (rows_n, img_n) == (4, 8):
        done = summed_weights(
            rows_n,
            run.calls,
            [
                hid_mid2,
                ga_out2,
                hid_in2,
                views2,
                first_low,
                ga_in2,
                hid_mid1,
                ga_out1,
                planes,
                ga_skip,
                hid_in1,
                views1,
                ga_in1,
            ],
        )
        grads, rows_of = unpack(done, sums)
        dw_in1, dw_mid1, dw_out1, dw_skip, dw_in2, dw_mid2, dw_out2 = grads
        dw_mid1, dw_mid2 = (
            g.reshape(3, 3, -1, middle).transpose(2, 0, 1, 3) for g in (dw_mid1, dw_mid2)
        )
    else:
        def weight_term(values, upstream):
            return lax.dot_general(
                values, upstream, (((0,), (0,)), ((), ())), preferred_element_type=F32
            ).astype(BF16)

        def reduced(grad):
            shard = lax.psum_scatter(grad, "img", scatter_dimension=0, tiled=True)
            return lax.psum(shard, "rows").astype(F32)

        dw_out2 = reduced(weight_term(hid_mid2, ga_out2))
        dw_mid2 = reduced(weight_term(hid_in2, views2))
        dw_in2 = reduced(weight_term(first_low, ga_in2))
        dw_out1 = reduced(weight_term(hid_mid1, ga_out1))
        dw_skip = reduced(weight_term(planes[0], ga_skip))
        m = middle
        dw_00 = weight_term(hid_in1[0], views1[:, m : 2 * m])
        dw_01 = weight_term(hid_in1[1], views1[:, m : 3 * m])
        dw_10 = weight_term(hid_in1[2], views1[:, : 2 * m])
        dw_11 = weight_term(hid_in1[3], views1)
        dw_mid1 = jnp.concatenate(
            [
                dw_11[:, 3 * m :],
                dw_10[:, :m],
                dw_11[:, :m],
                dw_01[:, m:],
                dw_00,
                dw_01[:, :m],
                dw_11[:, 2 * m : 3 * m],
                dw_10[:, m:],
                dw_11[:, m : 2 * m],
            ],
            axis=1,
        )
        dw_mid1 = reduced(dw_mid1)
        dw_in1 = reduced(
            weight_term(planes.reshape(4 * low, inputs), ga_in1.reshape(4 * low, middle))
        )
        rows_of = [x[k] for x in sums for k in range(x.shape[0])]
    kernel_shape = (middle // img_n, 3, 3, middle)
    (
        shift_in1_g,
        gain_in1_g,
        shift_mid1_g,
        gain_mid1_g,
        shift_sum1_g,
        gain_out1_g,
        gain_skip_g,
        shift_in2_g,
        gain_in2_g,
        shift_mid2_g,
        gain_mid2_g,
        shift_out2_g,
        gain_out2_g,
    ) = rows_of
    return (
        block_out.reshape(images, rows_low, cols_low, outputs),
        grad_image.reshape(images, rows_here, columns, inputs),
        dw_in1,
        dw_mid1.reshape(kernel_shape),
        dw_out1,
        dw_skip,
        dw_in2,
        dw_mid2.reshape(kernel_shape),
        dw_out2,
        gain_in1_g,
        shift_in1_g,
        gain_mid1_g,
        shift_mid1_g,
        gain_out1_g,
        shift_sum1_g,
        gain_skip_g,
        shift_sum1_g,
        gain_in2_g,
        shift_in2_g,
        gain_mid2_g,
        shift_mid2_g,
        gain_out2_g,
        shift_out2_g,
    )


def solution(mesh):
    image = P("img", "rows", None, None)
    in_specs = (image, P("img")) + (P(),) * 21 + (image,)
    out_specs = (
        image,
        image,
        P("img", None),
        P("img", None, None, None),
        P("img", None),
        P("img", None),
        P("img", None),
        P("img", None, None, None),
        P("img", None),
    ) + (P(),) * 14
    return jax.shard_map(body, mesh=mesh, in_specs=in_specs, out_specs=out_specs, check_vma=False)
```

```python
import functools

import jax
import jax.numpy as jnp
import numpy as np
from jax import lax
from jax.experimental import pallas as pl
from jax.experimental.pallas import tpu as pltpu
from jax.sharding import PartitionSpec as P

EPSILON = 1e-05
F32 = jnp.float32
BF16 = jnp.bfloat16
LANES = 512
ROWS = 32
IMAGES = 16
VMEM_BYTES = 40 * 1024 * 1024
MESH = pl.DeviceIdType.MESH
BY_ROWS, BY_PLANES, FIRST_PLANE, BY_BLOCK, PAIR_BLOCK, WHOLE = range(6)


def dot(a, b):
    return jnp.dot(a, b, preferred_element_type=F32)


def dot_t(a, b):
    return lax.dot_general(a, b, (((1,), (1,)), ((), ())), preferred_element_type=F32)


def load(ref, rows, lanes):
    value = ref[rows, lanes].astype(F32)
    return value.reshape(value.shape[0] // 8, 8, value.shape[1])


def store(ref, rows, lanes, value):
    ref[rows, lanes] = value.reshape(value.shape[0] * 8, value.shape[2]).astype(ref.dtype)


def load_mask(ref, rows):
    mask = load(ref, rows, slice(None))
    return jnp.concatenate([mask] * (LANES // 128), axis=-1)


def sweep(total, step, init, rows=ROWS):
    def body(i, carry):
        return step(pl.ds(pl.multiple_of(i * rows, rows), rows), i, carry)

    return lax.fori_loop(0, total // rows, body, init, unroll=True)


def lane_blocks(width):
    return [slice(k * LANES, (k + 1) * LANES) for k in range(width // LANES)]


def tall(row):
    return jnp.broadcast_to(row, (8, row.shape[-1]))


def column_sum(value):
    return jnp.sum(value, axis=0)


def total_of(part):
    return jnp.sum(part, axis=0, keepdims=True)


def zeros8():
    return jnp.zeros((8, LANES), F32)


def tally(first, parts, centre_ref, stats_ref, fill=None):
    width = parts[0][0].shape[-1]
    for lanes in lane_blocks(width):
        if fill is not None:
            fill(lanes)
        sums = (zeros8(), zeros8())
        for acc, mask_ref, dev in parts:

            def add(rows, i, carry, acc=acc, mask_ref=mask_ref):
                mask = load_mask(mask_ref, rows)
                return (
                    carry[0] + column_sum(load(acc, rows, lanes) * mask),
                    carry[1] + column_sum(mask),
                )

            sums = sweep(acc.shape[0], add, sums)
        total, count = total_of(sums[0]), total_of(sums[1])
        centre = total / jnp.maximum(count, 1.0)
        centre_ref[:, lanes] = centre
        centre8 = tall(centre)
        squares = zeros8()
        for acc, mask_ref, dev in parts:

            def square(rows, i, carry, acc=acc, mask_ref=mask_ref, dev=dev):
                away = load(acc, rows, lanes) - centre8
                store(dev, rows, lanes, away)
                return carry + column_sum(load_mask(mask_ref, rows) * away * away)

            squares = sweep(acc.shape[0], square, squares)
        squares = total_of(squares)
        count_old, mean_old, squares_old = (
            jnp.where(first, jnp.zeros_like(count), stats_ref[k : k + 1, lanes]) for k in range(3)
        )
        both = count_old + count
        share = count / jnp.maximum(both, 1.0)
        delta = centre - mean_old
        stats_ref[0:1, lanes] = both
        stats_ref[1:2, lanes] = mean_old + delta * share
        stats_ref[2:3, lanes] = squares_old + squares + delta * delta * count_old * share


def affine(stats_ref, gain_ref, shift_ref, centre_ref, lanes):
    scale = lax.rsqrt(stats_ref[2:3, lanes] + EPSILON)
    slope = gain_ref[:, lanes] * scale
    base = shift_ref[:, lanes] + (centre_ref[:, lanes] - stats_ref[1:2, lanes]) * slope
    return tall(0.5 * slope), tall(0.5 * base)


def silu_half(half):
    return half + half * jnp.tanh(half)


def gate_half(half):
    tanh = jnp.tanh(half)
    return (0.5 + 0.5 * tanh) * (1.0 + half * (1.0 - tanh))


def silu_and_gate(half):
    tanh = jnp.tanh(half)
    return half + half * tanh, (0.5 + 0.5 * tanh) * (1.0 + half * (1.0 - tanh))


def back_coefs(stats_ref, gain_ref, centre_ref, sums, lanes):
    shift_sum, gain_sum = sums
    pixels = stats_ref[0:1, lanes]
    scale = lax.rsqrt(stats_ref[2:3, lanes] + EPSILON)
    slope = gain_ref[:, lanes] * scale
    per_pixel = slope / pixels
    away = (centre_ref[:, lanes] - stats_ref[1:2, lanes]) * scale
    return (
        tall(slope),
        tall(-per_pixel * scale * gain_sum),
        tall(-per_pixel * (shift_sum + away * gain_sum)),
    )


def unit_sum(stats_ref, centre_ref, lanes, gn_sum, gd_sum):
    scale = lax.rsqrt(stats_ref[2:3, lanes] + EPSILON)
    return scale * (gd_sum + (centre_ref[:, lanes] - stats_ref[1:2, lanes]) * gn_sum)


def accumulate(first, ref, row, lanes, value):
    old = jnp.where(first, jnp.zeros_like(value), ref[row : row + 1, lanes])
    ref[row : row + 1, lanes] = old + value


def shifted(value, by):
    if by == 0:
        return value
    rolled = pltpu.roll(value, (-by) % 8, axis=1)
    column = lax.broadcasted_iota(jnp.int32, value.shape, 1)
    return jnp.where(column == (0 if by < 0 else 7), 0.0, rolled)


def from_above(value, edge, rows_low):
    if rows_low == 1:
        return edge
    images = value.shape[0] // rows_low
    image = value.reshape((images, rows_low) + value.shape[1:])
    return jnp.concatenate([edge[:, None], image[:, :-1]], axis=1).reshape(value.shape)


def from_below(value, edge, rows_low):
    if rows_low == 1:
        return edge
    images = value.shape[0] // rows_low
    image = value.reshape((images, rows_low) + value.shape[1:])
    return jnp.concatenate([image[:, 1:], edge[:, None]], axis=1).reshape(value.shape)


def edge_rows(i, rows_low):
    return pl.ds(pl.multiple_of(i * (ROWS // rows_low), ROWS // rows_low), ROWS // rows_low)


def first_step():
    return pl.program_id(0) == 0


def open_kernel(
    image_ref,
    perm_ref,
    mask_ref,
    mask_out,
    weight_ref,
    weight_skip,
    planes_ref,
    dev_ref,
    centre_ref,
    dev_skip,
    centre_skip,
    stats_ref,
    acc,
    acc_skip,
    flush,
):
    planes, low, _ = planes_ref.shape
    group = perm_ref.shape[0]
    part = group // planes
    for g in range(image_ref.shape[0] // group):
        mask = jnp.concatenate(
            [mask_ref[p, g * part : (g + 1) * part, :] for p in range(planes)], axis=0
        )
        mask = jnp.concatenate([mask] * (group // 128), axis=1)
        perm = (perm_ref[...].astype(F32) * mask).astype(BF16)
        moved = dot(perm, image_ref[g * group : (g + 1) * group, :]).astype(BF16)
        for p in range(planes):
            planes_ref[p, g * part : (g + 1) * part, :] = moved[p * part : (p + 1) * part]
    for p in range(planes):
        acc[p] = dot(planes_ref[p], weight_ref[...])
    width = acc.shape[-1]
    tally(
        first_step(),
        [(acc.at[p], mask_ref.at[p], dev_ref.at[p]) for p in range(planes)],
        centre_ref,
        stats_ref.at[:, :width],
    )
    flush()

    def fill(lanes):
        acc_skip[:, lanes] = dot(planes_ref[0], weight_skip[:, lanes])

    tally(first_step(), [(acc_skip, mask_out, dev_skip)], centre_skip, stats_ref.at[:, width:], fill)


def mid1_kernel(
    rows_low,
    dev_in,
    centre_in,
    mask_ref,
    halo,
    halo_centre,
    halo_mask,
    stats_in,
    gain,
    shift,
    mask_out,
    weight,
    hidden,
    dev_out,
    centre_out,
    stats_out,
    taps,
    acc,
):
    low, width = acc.shape
    steps = []
    for lanes in lane_blocks(width):
        slope, base = affine(stats_in, gain, shift, centre_in, lanes)
        slope_edge, base_edge = affine(stats_in, gain, shift, halo_centre, lanes)

        def act(p, rows, lanes=lanes, slope=slope, base=base):
            mask = load_mask(mask_ref.at[p], rows)
            value = silu_half(load(dev_in.at[p], rows, lanes) * slope + base) * mask
            store(hidden.at[p], rows, lanes, value)
            return value

        def act_edge(q, i, lanes=lanes, slope_edge=slope_edge, base_edge=base_edge):
            rows = edge_rows(i, rows_low)
            half = load(halo.at[q], rows, lanes) * slope_edge + base_edge
            return silu_half(half) * load_mask(halo_mask.at[q], rows)

        def step0(rows, i, carry):
            act(0, rows)
            return carry

        def step1(rows, i, carry):
            store(taps.at[0], rows, lanes, shifted(act(1, rows), -1))
            return carry

        def step2(rows, i, carry):
            store(taps.at[1], rows, lanes, from_above(act(2, rows), act_edge(0, i), rows_low))
            return carry

        def step3(rows, i, carry):
            odd = act(3, rows)
            store(taps.at[2], rows, lanes, shifted(odd, -1))
            above = from_above(odd, act_edge(1, i), rows_low)
            store(taps.at[3], rows, lanes, above)
            store(taps.at[4], rows, lanes, shifted(above, -1))
            return carry

        steps.append((step0, step1, step2, step3))

    def tap(t, u):
        k = (3 * t + u) * width
        return weight[k : k + width]

    def plane(p):
        for some in steps:
            sweep(low, some[p], 0)

    plane(0)
    plane(1)
    acc[...] = dot(hidden[0], tap(1, 1))
    plane(2)
    acc[...] += dot(hidden[1], tap(1, 2)) + dot(taps[0], tap(1, 0))
    plane(3)
    acc[...] += dot(hidden[2], tap(2, 1)) + dot(taps[1], tap(0, 1))
    acc[...] += (
        dot(hidden[3], tap(2, 2))
        + dot(taps[2], tap(2, 0))
        + dot(taps[3], tap(0, 2))
        + dot(taps[4], tap(0, 0))
    )
    tally(first_step(), [(acc, mask_out, dev_out)], centre_out, stats_out)


def expand_kernel(
    dev_in, centre_in, stats_in, gain, shift, mask, weight, hidden, dev_out, centre_out, stats_out, acc
):
    for lanes in lane_blocks(dev_in.shape[1]):
        slope, base = affine(stats_in, gain, shift, centre_in, lanes)

        def step(rows, i, carry):
            half = load(dev_in, rows, lanes) * slope + base
            store(hidden, rows, lanes, silu_half(half) * load_mask(mask, rows))
            return carry

        sweep(dev_in.shape[0], step, 0)

    def fill(lanes):
        acc[:, lanes] = dot(hidden[...], weight[:, lanes])

    tally(first_step(), [(acc, mask, dev_out)], centre_out, stats_out, fill)


def join_kernel(
    dev_a,
    centre_a,
    stats_a,
    gain_a,
    shift_a,
    dev_b,
    centre_b,
    stats_b,
    gain_b,
    shift_b,
    mask,
    weight,
    first_low,
    dev_out,
    centre_out,
    stats_out,
    acc,
):
    for lanes in lane_blocks(dev_a.shape[1]):
        slope_a, base_a = affine(stats_a, gain_a, shift_a, centre_a, lanes)
        slope_b, base_b = affine(stats_b, gain_b, shift_b, centre_b, lanes)
        base = base_a + base_b

        def step(rows, i, carry):
            half = load(dev_a, rows, lanes) * slope_a + load(dev_b, rows, lanes) * slope_b + base
            store(first_low, rows, lanes, silu_half(half) * load_mask(mask, rows))
            return carry

        sweep(dev_a.shape[0], step, 0)
        part = dot(first_low[:, lanes], weight[lanes, :])
        acc[...] = part if lanes.start == 0 else acc[...] + part
    tally(first_step(), [(acc, mask, dev_out)], centre_out, stats_out)


def mid2_kernel(
    rows_low,
    dev_in,
    centre_in,
    halo,
    halo_centre,
    halo_mask,
    stats_in,
    gain,
    shift,
    mask,
    weight,
    hidden,
    dev_out,
    centre_out,
    stats_out,
    taps,
    acc,
):
    low, width = acc.shape
    for lanes in lane_blocks(width):
        slope, base = affine(stats_in, gain, shift, centre_in, lanes)
        edges = [affine(stats_in, gain, shift, halo_centre.at[e], lanes) for e in range(2)]

        def act_edge(e, i):
            rows = edge_rows(i, rows_low)
            half = load(halo.at[e], rows, lanes) * edges[e][0] + edges[e][1]
            return silu_half(half) * load_mask(halo_mask.at[e], rows)

        def step(rows, i, carry):
            value = silu_half(load(dev_in, rows, lanes) * slope + base) * load_mask(mask, rows)
            store(hidden, rows, lanes, value)
            lines = (
                from_above(value, act_edge(0, i), rows_low),
                value,
                from_below(value, act_edge(1, i), rows_low),
            )
            for t in range(3):
                for u in range(3):
                    start = (3 * t + u) * width + lanes.start
                    store(taps, rows, slice(start, start + LANES), shifted(lines[t], u - 1))
            return carry

        sweep(low, step, 0)
    acc[...] = dot(taps[...], weight[...])
    tally(first_step(), [(acc, mask, dev_out)], centre_out, stats_out)


def final_kernel(dev, centre, stats, gain, shift, first_low, cot, mask, block_out, gn_ref, sums):
    first = first_step()
    for lanes in lane_blocks(dev.shape[1]):
        slope, base = affine(stats, gain, shift, centre, lanes)

        def step(rows, i, carry):
            away = load(dev, rows, lanes)
            half = away * slope + base + 0.5 * load(first_low, rows, lanes)
            valid = load_mask(mask, rows)
            value, gate = silu_and_gate(half)
            store(block_out, rows, lanes, value * valid)
            gn = gate * valid * load(cot, rows, lanes)
            store(gn_ref, rows, lanes, gn)
            return carry[0] + column_sum(gn), carry[1] + column_sum(gn * away)

        gn_sum, gd_sum = sweep(dev.shape[0], step, (zeros8(), zeros8()))
        gn_sum, gd_sum = total_of(gn_sum), total_of(gd_sum)
        accumulate(first, sums, 0, lanes, gn_sum)
        accumulate(first, sums, 1, lanes, unit_sum(stats, centre, lanes, gn_sum, gd_sum))


def scaled(gn, away, mask, coefs):
    return (gn * coefs[0] + away * coefs[1] + coefs[2]) * mask


def gate_sums(first, grads, dev, centre, stats, gain, shift, mask, gn_ref, sums, parts, fill=None):
    width = gn_ref.shape[-1]
    planes = range(parts) if parts else [None]
    for lanes in lane_blocks(width):
        slope, base = affine(stats, gain, shift, centre, lanes)
        carry = (zeros8(), zeros8())
        for p in planes:
            if fill is not None and lanes.start == 0:
                fill[p]()
            grad_p, dev_p, mask_p, gn_p = (
                r if p is None else r.at[p] for r in (grads, dev, mask, gn_ref)
            )

            def step(rows, i, carry, grad_p=grad_p, dev_p=dev_p, mask_p=mask_p, gn_p=gn_p):
                away = load(dev_p, rows, lanes)
                gate = gate_half(away * slope + base) * load_mask(mask_p, rows)
                gn = gate * load(grad_p, rows, lanes)
                store(gn_p, rows, lanes, gn)
                return carry[0] + column_sum(gn), carry[1] + column_sum(gn * away)

            carry = sweep(grad_p.shape[0], step, carry)
        gn_sum, gd_sum = total_of(carry[0]), total_of(carry[1])
        accumulate(first, sums, 0, lanes, gn_sum)
        accumulate(first, sums, 1, lanes, unit_sum(stats, centre, lanes, gn_sum, gd_sum))


def back_expand_kernel(
    gn,
    dev,
    centre,
    stats,
    gain,
    sums_in,
    mask,
    weight,
    dev_m,
    centre_m,
    stats_m,
    gain_m,
    shift_m,
    ga,
    gn_m,
    sums_m,
    acc,
):
    for lanes in lane_blocks(dev.shape[1]):
        coefs = back_coefs(
            stats, gain, centre, (sums_in[0:1, lanes], sums_in[1:2, lanes]), lanes
        )

        def step(rows, i, carry):
            away = load(dev, rows, lanes)
            store(ga, rows, lanes, scaled(load(gn, rows, lanes), away, load_mask(mask, rows), coefs))
            return carry

        sweep(dev.shape[0], step, 0)
        part = dot_t(ga[:, lanes], weight[:, lanes])
        acc[...] = part if lanes.start == 0 else acc[...] + part
    gate_sums(first_step(), acc, dev_m, centre_m, stats_m, gain_m, shift_m, mask, gn_m, sums_m, 0)


def back_mid2_kernel(
    rows_low,
    gn,
    dev,
    centre,
    halo_gn,
    halo_dev,
    halo_centre,
    halo_mask,
    stats,
    gain,
    sums_in,
    mask,
    weight,
    dev_m,
    centre_m,
    stats_m,
    gain_m,
    shift_m,
    views,
    gn_m,
    sums_m,
    acc,
):
    low, width = acc.shape
    for lanes in lane_blocks(width):
        sums = (sums_in[0:1, lanes], sums_in[1:2, lanes])
        coefs = back_coefs(stats, gain, centre, sums, lanes)
        edges = [back_coefs(stats, gain, halo_centre.at[e], sums, lanes) for e in range(2)]

        def edge(e, i):
            rows = edge_rows(i, rows_low)
            return scaled(
                load(halo_gn.at[e], rows, lanes),
                load(halo_dev.at[e], rows, lanes),
                load_mask(halo_mask.at[e], rows),
                edges[e],
            )

        def step(rows, i, carry):
            value = scaled(
                load(gn, rows, lanes), load(dev, rows, lanes), load_mask(mask, rows), coefs
            )
            lines = (
                from_below(value, edge(1, i), rows_low),
                value,
                from_above(value, edge(0, i), rows_low),
            )
            for t in range(3):
                for u in range(3):
                    start = (3 * t + u) * width + lanes.start
                    store(views, rows, slice(start, start + LANES), shifted(lines[t], 1 - u))
            return carry

        sweep(low, step, 0)
    total = dot_t(views[:, :width], weight[:width])
    for k in range(width, 9 * width, width):
        total += dot_t(views[:, k : k + width], weight[k : k + width])
    acc[...] = total
    gate_sums(first_step(), acc, dev_m, centre_m, stats_m, gain_m, shift_m, mask, gn_m, sums_m, 0)


def back_join_kernel(
    gn_in,
    dev_in,
    centre_in,
    stats_in,
    gain_in,
    sums_in,
    mask,
    weight,
    residual,
    dev_a,
    centre_a,
    stats_a,
    gain_a,
    shift_a,
    dev_b,
    centre_b,
    stats_b,
    gain_b,
    shift_b,
    ga,
    gs_ref,
    sums,
    acc,
):
    first = first_step()
    for lanes in lane_blocks(dev_in.shape[1]):
        coefs = back_coefs(
            stats_in, gain_in, centre_in, (sums_in[0:1, lanes], sums_in[1:2, lanes]), lanes
        )

        def step(rows, i, carry):
            away = load(dev_in, rows, lanes)
            value = scaled(load(gn_in, rows, lanes), away, load_mask(mask, rows), coefs)
            store(ga, rows, lanes, value)
            return carry

        sweep(dev_in.shape[0], step, 0)
    for lanes in lane_blocks(dev_a.shape[1]):
        acc[:, lanes] = dot_t(ga[...], weight[lanes, :])
        slope_a, base_a = affine(stats_a, gain_a, shift_a, centre_a, lanes)
        slope_b, base_b = affine(stats_b, gain_b, shift_b, centre_b, lanes)
        base = base_a + base_b

        def gate(rows, i, carry):
            away_a, away_b = load(dev_a, rows, lanes), load(dev_b, rows, lanes)
            half = away_a * slope_a + away_b * slope_b + base
            grad = load(residual, rows, lanes) + load(acc, rows, lanes)
            gs = gate_half(half) * load_mask(mask, rows) * grad
            store(gs_ref, rows, lanes, gs)
            return (
                carry[0] + column_sum(gs),
                carry[1] + column_sum(gs * away_a),
                carry[2] + column_sum(gs * away_b),
            )

        carry = sweep(dev_a.shape[0], gate, (zeros8(), zeros8(), zeros8()))
        gs_sum, a_sum, b_sum = (total_of(part) for part in carry)
        accumulate(first, sums, 0, lanes, gs_sum)
        accumulate(first, sums, 1, lanes, unit_sum(stats_a, centre_a, lanes, gs_sum, a_sum))
        accumulate(first, sums, 2, lanes, unit_sum(stats_b, centre_b, lanes, gs_sum, b_sum))


def back_split_kernel(
    gs,
    dev_a,
    centre_a,
    stats_a,
    gain_a,
    dev_b,
    centre_b,
    stats_b,
    gain_b,
    sums_in,
    mask,
    weight_a,
    weight_b,
    dev_m,
    centre_m,
    stats_m,
    gain_m,
    shift_m,
    ga_a,
    ga_b,
    gn_m,
    grad_skip,
    sums_m,
    acc,
    acc_skip,
):
    for lanes in lane_blocks(dev_a.shape[1]):
        shift_sum = sums_in[0:1, lanes]
        coefs_a = back_coefs(stats_a, gain_a, centre_a, (shift_sum, sums_in[1:2, lanes]), lanes)
        coefs_b = back_coefs(stats_b, gain_b, centre_b, (shift_sum, sums_in[2:3, lanes]), lanes)

        def step(rows, i, carry):
            value, valid = load(gs, rows, lanes), load_mask(mask, rows)
            store(ga_a, rows, lanes, scaled(value, load(dev_a, rows, lanes), valid, coefs_a))
            store(ga_b, rows, lanes, scaled(value, load(dev_b, rows, lanes), valid, coefs_b))
            return carry

        sweep(dev_a.shape[0], step, 0)
        part = dot_t(ga_a[:, lanes], weight_a[:, lanes])
        acc[...] = part if lanes.start == 0 else acc[...] + part
        part = dot_t(ga_b[:, lanes], weight_b[:, lanes])
        acc_skip[...] = part if lanes.start == 0 else acc_skip[...] + part
    grad_skip[...] = acc_skip[...].astype(BF16)
    gate_sums(first_step(), acc, dev_m, centre_m, stats_m, gain_m, shift_m, mask, gn_m, sums_m, 0)


def back_mid1_kernel(
    rows_low,
    gn,
    dev,
    centre,
    halo_gn,
    halo_dev,
    halo_centre,
    halo_mask,
    stats,
    gain,
    sums_in,
    mask,
    weight,
    dev_m,
    centre_m,
    mask_m,
    stats_m,
    gain_m,
    shift_m,
    views,
    gn_m,
    sums_m,
    acc,
):
    _, low, width = acc.shape
    for lanes in lane_blocks(width):
        sums = (sums_in[0:1, lanes], sums_in[1:2, lanes])
        coefs = back_coefs(stats, gain, centre, sums, lanes)
        coefs_edge = back_coefs(stats, gain, halo_centre, sums, lanes)

        def step(rows, i, carry):
            value = scaled(
                load(gn, rows, lanes), load(dev, rows, lanes), load_mask(mask, rows), coefs
            )
            some = edge_rows(i, rows_low)
            edge = scaled(
                load(halo_gn, some, lanes),
                load(halo_dev, some, lanes),
                load_mask(halo_mask, some),
                coefs_edge,
            )
            below = from_below(value, edge, rows_low)
            for k, view in enumerate((below, value, shifted(value, 1), shifted(below, 1))):
                start = k * width + lanes.start
                store(views, rows, slice(start, start + LANES), view)
            return carry

        sweep(low, step, 0)

    def view(k):
        return views[:, k * width : (k + 1) * width]

    def tap(t, u):
        k = (3 * t + u) * width
        return weight[k : k + width]

    def plane0():
        acc[0] = dot_t(view(1), tap(1, 1))

    def plane1():
        acc[1] = dot_t(view(1), tap(1, 2)) + dot_t(view(2), tap(1, 0))

    def plane2():
        acc[2] = dot_t(view(1), tap(2, 1)) + dot_t(view(0), tap(0, 1))

    def plane3():
        acc[3] = (
            dot_t(view(1), tap(2, 2))
            + dot_t(view(2), tap(2, 0))
            + dot_t(view(0), tap(0, 2))
            + dot_t(view(3), tap(0, 0))
        )

    gate_sums(
        first_step(),
        acc,
        dev_m,
        centre_m,
        stats_m,
        gain_m,
        shift_m,
        mask_m,
        gn_m,
        sums_m,
        4,
        (plane0, plane1, plane2, plane3),
    )


def back_image_kernel(
    gn,
    dev,
    centre,
    stats,
    gain,
    sums_in,
    mask_ref,
    weight,
    grad_skip,
    perm_ref,
    handed,
    ga,
    image,
    hand,
    planes_ref,
):
    planes, low, width = ga.shape
    for p in range(planes):
        for lanes in lane_blocks(width):
            coefs = back_coefs(
                stats, gain, centre, (sums_in[0:1, lanes], sums_in[1:2, lanes]), lanes
            )

            def step(rows, i, carry):
                away = load(dev.at[p], rows, lanes)
                valid = load_mask(mask_ref.at[p], rows)
                value = scaled(load(gn.at[p], rows, lanes), away, valid, coefs)
                store(ga.at[p], rows, lanes, value)
                return carry

            sweep(low, step, 0)
        grad = dot_t(ga[p], weight[...])
        if p == 0:
            grad += grad_skip[...].astype(F32)
        planes_ref[p] = grad.astype(BF16)
    hand[...] = handed[...]
    group = perm_ref.shape[0]
    part = group // planes
    for g in range(image.shape[0] // group):
        rows = slice(g * part, (g + 1) * part)
        mask = jnp.concatenate([mask_ref[p, rows, :] for p in range(planes)], axis=0)
        mask = jnp.concatenate([mask] * (group // 128), axis=1)
        perm = (perm_ref[...].astype(F32) * mask).astype(BF16)
        here = jnp.concatenate([planes_ref[p, rows, :] for p in range(planes)], axis=0)
        back = lax.dot_general(
            perm, here, (((0,), (0,)), ((), ())), preferred_element_type=F32
        )
        image[g * group : (g + 1) * group, :] = back.astype(BF16)


def spec_of(shape, kind, blocks):
    if kind == BY_ROWS:
        return pl.BlockSpec((shape[0] // blocks, shape[1]), lambda b: (b, 0))
    if kind == BY_PLANES:
        return pl.BlockSpec((shape[0], shape[1] // blocks, shape[2]), lambda b: (0, b, 0))
    if kind == FIRST_PLANE:
        return pl.BlockSpec((None, shape[1] // blocks, shape[2]), lambda b: (0, b, 0))
    if kind == BY_BLOCK:
        return pl.BlockSpec((None,) + tuple(shape[1:]), lambda b: (b, 0, 0))
    if kind == PAIR_BLOCK:
        return pl.BlockSpec((2, None) + tuple(shape[2:]), lambda b: (0, b, 0, 0))
    zero = (0,) * len(shape)
    return pl.BlockSpec(tuple(shape), lambda b: zero, pipeline_mode=pl.Buffered(1))


def out_spec(shape, kind, blocks):
    if kind == WHOLE:
        zero = (0,) * len(shape)
        return pl.BlockSpec(tuple(shape), lambda b: zero)
    return spec_of(shape, kind, blocks)


def stage(kernel, blocks, ins, outs, scratch=(), flops=0):
    return call(kernel, blocks, ins, outs, scratch, flops, [], [], {})


def call(kernel, blocks, ins, outs, scratch, flops, more_specs, more_shapes, params):
    moved = sum(x.size * x.dtype.itemsize for x, _ in ins)
    moved += sum(int(np.prod(s)) * jnp.dtype(d).itemsize for s, d, _ in outs)
    made = [pltpu.VMEM(*item) if isinstance(item, tuple) else item for item in scratch]
    return pl.pallas_call(
        kernel,
        grid=(blocks,),
        in_specs=[spec_of(x.shape, kind, blocks) for x, kind in ins],
        out_specs=[out_spec(s, kind, blocks) for s, _, kind in outs] + more_specs,
        out_shape=[jax.ShapeDtypeStruct(s, d) for s, d, _ in outs] + more_shapes,
        scratch_shapes=made,
        compiler_params=pltpu.CompilerParams(
            dimension_semantics=("arbitrary",), vmem_limit_bytes=VMEM_BYTES, **params
        ),
        cost_estimate=pl.CostEstimate(flops=flops, bytes_accessed=moved, transcendentals=0),
    )(*[x for x, _ in ins])


def merge_rows(buf, peers, merge, mean_only):
    if not merge:
        total = buf[0]
        for k in range(1, peers):
            total = total + buf[k]
        return total
    counts = [buf[k, 0:1, :] for k in range(peers)]
    means = [buf[k, 1:2, :] for k in range(peers)]
    count, weighted = counts[0], counts[0] * means[0]
    for k in range(1, peers):
        count = count + counts[k]
        weighted = weighted + counts[k] * means[k]
    safe = jnp.maximum(count, 1.0)
    mean = weighted / safe
    squares = jnp.zeros_like(mean)
    for k in range(peers):
        squares = squares + buf[k, 2:3, :] + counts[k] * jnp.square(means[k] - mean)
    if mean_only:
        squares = squares / safe
    return jnp.concatenate([count, mean, squares], axis=0)


class Exchange:
    def __init__(self, rows_n, img_n, blocks):
        self.rows_n, self.img_n, self.blocks = rows_n, img_n, blocks
        self.calls = 0

    def __call__(
        self,
        kernel,
        ins,
        outs,
        merge,
        lines,
        widths,
        scratch=(),
        flops=0,
        edges=(),
        centres=None,
        edge=0,
        early=False,
    ):
        ident, self.calls = self.calls, self.calls + 1
        total, dma = sum(widths), pltpu.SemaphoreType.DMA
        any_space = pl.BlockSpec(memory_space=pl.ANY)
        specs = [out_spec((lines, w), WHOLE, 1) for w in widths]
        shapes = [jax.ShapeDtypeStruct((lines, w), F32) for w in widths]
        extra = []
        if edges:
            middle = outs[edges[0][0]][0][-1]
            specs.append(any_space)
            shapes.append(jax.ShapeDtypeStruct((len(edges), edge, middle), BF16))
            extra += [
                ((len(edges), edge, middle), BF16),
                dma((len(edges), self.blocks)),
                dma((len(edges), self.blocks)),
                dma((len(edges),)),
            ]
        if centres:
            count, shape = len(centres[1]), outs[centres[0]][0]
            specs.append(any_space)
            shapes.append(jax.ShapeDtypeStruct((count,) + tuple(shape), F32))
            extra += [(tuple(shape), F32), dma((count,)), dma((count,)), dma((count,))]
        extra += [
            ((self.rows_n, lines, total), F32),
            ((self.img_n, lines, total), F32),
            ((lines, total), F32),
            dma((self.rows_n,)),
            dma((self.rows_n,)),
            dma((self.img_n,)),
            dma((self.img_n,)),
        ]
        return call(
            functools.partial(
                self.kernel, kernel, len(ins), len(outs), len(scratch), merge, widths, edges, centres, early
            ),
            self.blocks,
            ins,
            outs,
            [((lines, total), F32)] + list(scratch) + extra,
            flops,
            specs,
            shapes,
            dict(collective_id=ident, has_side_effects=True),
        )

    def kernel(self, kernel, ins_n, outs_n, scratch_n, merge, widths, edges, centres, early, *refs):
        rows_n, img_n, blocks = self.rows_n, self.img_n, self.blocks
        refs = list(refs)

        def take(count):
            taken = refs[:count]
            del refs[:count]
            return taken

        ins, outs, totals = take(ins_n), take(outs_n), take(len(widths))
        halo = take(1)[0] if edges else None
        halo_centres = take(1)[0] if centres else None
        mine = take(1)[0]
        scratch = take(scratch_n)
        if edges:
            edge_buf, edge_send, edge_recv, edge_local = take(4)
        if centres:
            centre_buf, centre_send, centre_recv, centre_local = take(4)
        buf_r, buf_i, part, send_r, recv_r, send_i, recv_i = refs
        block = pl.program_id(0)
        row, img = lax.axis_index("rows"), lax.axis_index("img")
        barrier = pltpu.get_barrier_semaphore()

        @pl.when(block == 0)
        def _():
            for k in range(1, rows_n):
                peer = {"rows": lax.rem(row + k, rows_n)}
                pl.semaphore_signal(barrier, inc=1, device_id=peer, device_id_type=MESH)
            for k in range(1, img_n):
                peer = {"img": lax.rem(img + k, img_n)}
                pl.semaphore_signal(barrier, inc=1, device_id=peer, device_id_type=MESH)

        def remote(source, target, send, recv, peer):
            return pltpu.make_async_remote_copy(
                src_ref=source,
                dst_ref=target,
                send_sem=send,
                recv_sem=recv,
                device_id=peer,
                device_id_type=MESH,
            )

        def sends(direction):
            return row < rows_n - 1 if direction > 0 else row > 0

        def receives(direction):
            return row > 0 if direction > 0 else row < rows_n - 1

        def edge_copy(e, b):
            some = edge_buf.shape[1] // blocks
            here = pl.ds(pl.multiple_of(b * some, some), some)
            return remote(
                edge_buf.at[e, here],
                halo.at[e, here],
                edge_send.at[e, b],
                edge_recv.at[e, b],
                {"rows": row + edges[e][3]},
            )

        def keep_edges():
            some = edge_buf.shape[1] // blocks
            here = pl.ds(pl.multiple_of(block * some, some), some)
            for e, (out, plane, last_row, _) in enumerate(edges):
                source = outs[out] if plane is None else outs[out].at[plane]
                for lanes in lane_blocks(source.shape[1]):
                    value = load(source, slice(None), lanes)
                    lines = value.reshape((some // 8, -1) + value.shape[1:])
                    store(edge_buf.at[e], here, lanes, lines[:, -1 if last_row else 0])

        def send_edges():
            for e, spec in enumerate(edges):

                @pl.when(sends(spec[3]))
                def _(e=e):
                    edge_copy(e, block).start()

        def greet():
            @pl.when(block == 0)
            def _():
                pl.semaphore_wait(barrier, rows_n + img_n - 2)

        def flush():
            greet()
            keep_edges()
            send_edges()

        if early:
            kernel(*ins, *outs, mine, *scratch, flush)
        else:
            kernel(*ins, *outs, mine, *scratch)
            greet()
            if edges:
                keep_edges()

                @pl.when(block < blocks - 1)
                def _():
                    send_edges()

        if centres:
            centre_buf[pl.ds(block, 1)] = outs[centres[0]][...][None]

        def exchange(axis, me, peers, source, buf, send, recv, then=None):
            copies = []
            for k in range(1, peers):
                peer = {axis: lax.rem(me + k, peers)}
                copies.append(remote(source, buf.at[me], send.at[k], recv.at[me], peer))
                copies[-1].start()
            if then is not None:
                then()
            buf[pl.ds(me, 1)] = source[...][None]
            for k in range(1, peers):
                peer = lax.rem(me + k, peers)
                remote(source, buf.at[peer], send.at[k], recv.at[peer], {axis: peer}).wait_recv()
            return copies

        @pl.when(block == blocks - 1)
        def _():
            def centre_copy(k):
                peer = {"rows": row + centres[1][k]}
                return remote(
                    centre_buf, halo_centres.at[k], centre_send.at[k], centre_recv.at[k], peer
                )

            directions = centres[1] if centres else ()

            def rest():
                for k, direction in enumerate(directions):

                    @pl.when(sends(direction))
                    def _(k=k):
                        centre_copy(k).start()

                if edges and not early:
                    send_edges()

            copies = exchange("rows", row, rows_n, mine, buf_r, send_r, recv_r, rest)
            part[...] = merge_rows(buf_r, rows_n, merge, False)
            copies += exchange("img", img, img_n, part, buf_i, send_i, recv_i)
            total = merge_rows(buf_i, img_n, merge, True)
            start = 0
            for out, width in zip(totals, widths):
                out[...] = total[:, start : start + width]
                start += width
            for k, direction in enumerate(directions):
                own = pltpu.make_async_copy(centre_buf, halo_centres.at[k], centre_local.at[k])

                @pl.when(receives(direction))
                def _(k=k):
                    centre_copy(k).wait_recv()

                @pl.when(jnp.logical_not(receives(direction)))
                def _(own=own):
                    own.start()
                    own.wait()

                @pl.when(sends(direction))
                def _(k=k):
                    centre_copy(k).wait_send()

            for e, spec in enumerate(edges):
                own = pltpu.make_async_copy(edge_buf.at[e], halo.at[e], edge_local.at[e])

                @pl.when(receives(spec[3]))
                def _(e=e):
                    for b in range(blocks):
                        edge_copy(e, b).wait_recv()

                @pl.when(jnp.logical_not(receives(spec[3])))
                def _(own=own):
                    own.start()
                    own.wait()

                @pl.when(sends(spec[3]))
                def _(e=e):
                    for b in range(blocks):
                        edge_copy(e, b).wait_send()

            for copy in copies:
                copy.wait_send()


CHUNK_ROWS = 64
CHUNK_LANES = 1024


HID_MID2, GA_OUT2, HID_IN2, VIEWS2, FIRST, GA_IN2, HID_MID1, GA_OUT1, GA_SKIP, VIEWS1 = range(10)
HID, PLANE, GA_IN1 = 10, 14, 18
ONE, TWO, HALF, QUAD, DEEP = range(5)
WIDTHS = {ONE: (512, 1024), TWO: (1024, 512), HALF: (512, 512), QUAD: (1024, 256), DEEP: (1024, 512)}


def plan_jobs():
    chunks = [[(ONE, 0, HID_MID2, 0, GA_OUT2, 1024 * k)] for k in range(2)]
    chunks += [[(ONE, 0, HID_IN2, 0, VIEWS2, 1024 * k)] for k in range(4)]
    chunks += [[(HALF, 0, HID_IN2, 0, VIEWS2, 4096), (HALF, 1, HID, 0, VIEWS1, 512)]]
    chunks += [[(QUAD, h, FIRST, 1024 * h, GA_IN2, 256 * k) for h in range(2)] for k in range(2)]
    chunks += [[(DEEP, p, PLANE + p, 0, GA_IN1 + p, 0) for p in range(4)]]
    chunks += [[(ONE, 0, HID_MID1, 0, GA_OUT1, 1024 * k)] for k in range(2)]
    chunks += [[(TWO, 0, PLANE, 0, GA_SKIP, 512 * k)] for k in range(4)]
    chunks += [[(ONE, 0, HID + 1, 0, VIEWS1, 512)], [(ONE, 0, HID + 2, 0, VIEWS1, 0)]]
    chunks += [[(ONE, 0, HID + 3, 0, VIEWS1, 1024 * k)] for k in range(2)]
    return chunks


def weights_kernel(
    rows_n,
    hid_mid2,
    ga_out2,
    hid_in2,
    views2,
    first_low,
    ga_in2,
    hid_mid1,
    ga_out1,
    planes,
    ga_skip,
    hid_in1,
    views1,
    ga_in1,
    done,
    lhs_buf,
    rhs_buf,
    deep,
    chunk_buf,
    own,
    got1,
    got2a,
    got2b,
    got3a,
    got3b,
    got_low,
    got_high,
    lhs_sem,
    rhs_sem,
    *sems,
):
    (s1, r1, s2a, r2a, s2b, r2b, s3a, r3a, s3b, r3b, s_up, r_low, s_down, r_high, b_up, b_down, r_back) = sems
    sources = [hid_mid2, ga_out2, hid_in2, views2, first_low, ga_in2, hid_mid1, ga_out1, ga_skip, views1]
    for stack in (hid_in1, planes, ga_in1):
        sources += [stack.at[p] for p in range(4)]
    chunks = plan_jobs()
    jobs = [job for chunk in chunks for job in chunk]
    count = len(chunks)
    depth = chunk_buf.shape[0]
    img, z = lax.axis_index("img"), lax.axis_index("rows")
    y, x, c = img // 4, lax.rem(img // 2, 2), lax.rem(img, 2)
    root = rows_n // 2
    sibling = {"img": img + 1 - 2 * c}
    beside_x = {"img": img + 2 - 4 * x}
    beside_y = {"img": img + 4 - 8 * y}
    higher, lower = {"rows": z + 1}, {"rows": z - 1}
    half = CHUNK_LANES // 2
    left, right = slice(0, half), slice(half, 2 * half)

    def fetch(index):
        kind, _, lhs, lhs_start, rhs, rhs_start = jobs[index]
        lhs_width, rhs_width = WIDTHS[kind]
        slot = index % 2
        return (
            pltpu.make_async_copy(
                sources[lhs].at[:, lhs_start : lhs_start + lhs_width],
                lhs_buf.at[slot, :, :lhs_width],
                lhs_sem.at[slot],
            ),
            pltpu.make_async_copy(
                sources[rhs].at[:, rhs_start : rhs_start + rhs_width],
                rhs_buf.at[slot, :, :rhs_width],
                rhs_sem.at[slot],
            ),
        )

    for copy in fetch(0):
        copy.start()

    barrier = pltpu.get_barrier_semaphore()
    for peer in (sibling, beside_x, beside_y):
        pl.semaphore_signal(barrier, inc=1, device_id=peer, device_id_type=MESH)

    @pl.when(z > 0)
    def _():
        pl.semaphore_signal(barrier, inc=1, device_id=lower, device_id_type=MESH)

    @pl.when(z < rows_n - 1)
    def _():
        pl.semaphore_signal(barrier, inc=1, device_id=higher, device_id_type=MESH)

    pl.semaphore_wait(barrier, 3 + jnp.minimum(z, 1) + jnp.minimum(rows_n - 1 - z, 1))

    def put(slot, result, first, parts):
        width = CHUNK_LANES // parts
        rows = CHUNK_ROWS
        for m in range(result.shape[0] // (rows * parts)):
            shard = first + m
            for h in range(parts):
                piece = result[(m * parts + h) * rows : (m * parts + h + 1) * rows]
                chunk_buf[slot, shard // 4, shard // 2 % 2, shard % 2, :, h * width : (h + 1) * width] = piece

    def multiply(index, slot):
        kind, part = jobs[index][:2]
        lhs_width, rhs_width = WIDTHS[kind]
        here = index % 2

        def product():
            return lax.dot_general(
                lhs_buf[here, :, :lhs_width],
                rhs_buf[here, :, :rhs_width],
                (((0,), (0,)), ((), ())),
                preferred_element_type=F32,
            )

        if kind == ONE:
            put(slot, product().astype(BF16), 0, 1)
        elif kind == TWO:
            put(slot, product().astype(BF16), 0, 2)
        elif kind == QUAD:
            put(slot, product().astype(BF16), 4 * part, 4)
        elif kind == HALF:
            result = product().astype(BF16)
            for m in range(8):
                piece = result[m * CHUNK_ROWS : (m + 1) * CHUNK_ROWS]
                chunk_buf[slot, m // 4, m // 2 % 2, m % 2, :, (left, right)[part]] = piece
        elif part == 0:
            deep[...] = product()
        elif part == 3:
            put(slot, (deep[...] + product()).astype(BF16), 0, 2)
        else:
            deep[...] += product()

    def remote(source, target, send, recv, peer):
        return pltpu.make_async_remote_copy(
            src_ref=source,
            dst_ref=target,
            send_sem=send,
            recv_sem=recv,
            device_id=peer,
            device_id_type=MESH,
        )

    def to_core(t):
        source = chunk_buf.at[lax.rem(t, depth), :, :, 1 - c]
        return remote(source, got1.at[t], s1.at[t], r1.at[t], sibling)

    def to_2a(t):
        return remote(own.at[t, :, 1 - x, :, left], got2a.at[t], s2a.at[t], r2a.at[t], beside_x)

    def to_2b(t):
        return remote(own.at[t, 1 - y, :, :, right], got2b.at[t], s2b.at[t], r2b.at[t], beside_y)

    def to_3a(t):
        return remote(own.at[t, 1 - y, x, :, left], got3a.at[t], s3a.at[t], r3a.at[t], beside_y)

    def to_3b(t):
        return remote(own.at[t, y, 1 - x, :, right], got3b.at[t], s3b.at[t], r3b.at[t], beside_x)

    def up(t):
        return remote(own.at[t, y, x], got_low.at[t], s_up.at[t], r_low.at[t], higher)

    def down(t):
        return remote(own.at[t, y, x], got_high.at[t], s_down.at[t], r_high.at[t], lower)

    def back_up(t):
        return remote(done.at[t], done.at[t], b_up.at[t], r_back.at[t], higher)

    def back_down(t):
        return remote(done.at[t], done.at[t], b_down.at[t], r_back.at[t], lower)

    def compute(t):
        @pl.when(t >= depth)
        def _():
            to_core(t - depth).wait_send()

        slot = lax.rem(t, depth)
        index = 0
        for k, chunk in enumerate(chunks):
            first = index
            index += len(chunk)

            @pl.when(t == k)
            def _(first=first, chunk=chunk):
                for n in range(first, first + len(chunk)):
                    for copy in fetch(n):
                        copy.wait()
                    if n + 1 < len(jobs):
                        for copy in fetch(n + 1):
                            copy.start()
                    multiply(n, slot)

        to_core(t).start()

    def stage1(t):
        to_core(t).wait_recv()
        slot = lax.rem(t, depth)
        for a in range(2):
            for b in range(2):
                own[t, a, b] = chunk_buf[slot, a, b, c] + got1[t, a, b]
        to_2a(t).start()
        to_2b(t).start()

    def stage2(t):
        to_2a(t).wait_recv()
        for a in range(2):
            own[t, a, x, :, left] = own[t, a, x, :, left] + got2a[t, a]
        to_3a(t).start()
        to_2b(t).wait_recv()
        for a in range(2):
            own[t, y, a, :, right] = own[t, y, a, :, right] + got2b[t, a]
        to_3b(t).start()

    def stage3(t):
        to_3a(t).wait_recv()
        own[t, y, x, :, left] = own[t, y, x, :, left] + got3a[t]
        to_3b(t).wait_recv()
        own[t, y, x, :, right] = own[t, y, x, :, right] + got3b[t]

        @pl.when(z == 0)
        def _():
            up(t).start()

        @pl.when(z == rows_n - 1)
        def _():
            down(t).start()

    def stage4(t):
        @pl.when((z > 0) & (z < root))
        def _():
            up(t).wait_recv()
            own[t, y, x] = own[t, y, x] + got_low[t]
            up(t).start()

        @pl.when((z < rows_n - 1) & (z > root))
        def _():
            down(t).wait_recv()
            own[t, y, x] = own[t, y, x] + got_high[t]
            down(t).start()

    def stage5(t):
        @pl.when(z == root)
        def _():
            up(t).wait_recv()
            down(t).wait_recv()
            total = own[t, y, x].astype(F32) + got_low[t].astype(F32) + got_high[t].astype(F32)
            done[t] = total.astype(BF16)
            back_up(t).start()
            back_down(t).start()

    def stage6(t):
        @pl.when(z > root)
        def _():
            back_up(t).wait_recv()

            @pl.when(z < rows_n - 1)
            def _():
                back_up(t).start()

        @pl.when((z < root) & (z > 0))
        def _():
            back_down(t).wait_recv()
            back_down(t).start()

    def stage7(t):
        @pl.when(z == 0)
        def _():
            back_down(t).wait_recv()

    stages = (compute, stage1, stage2, stage3, stage4, stage5, stage6, stage7)

    def step(s, carry):
        for lag, work in enumerate(stages):
            t = s - lag

            @pl.when((t >= 0) & (t < count))
            def _(t=t, work=work):
                work(t)

        return carry

    lax.fori_loop(0, count + len(stages) - 1, step, 0)

    def finish(t, carry):
        @pl.when(t >= count - depth)
        def _():
            to_core(t).wait_send()

        for copy in (to_2a(t), to_2b(t), to_3a(t), to_3b(t)):
            copy.wait_send()

        @pl.when(z < root)
        def _():
            up(t).wait_send()

        @pl.when(z > root)
        def _():
            down(t).wait_send()

        @pl.when((z >= root) & (z < rows_n - 1))
        def _():
            back_up(t).wait_send()

        @pl.when((z <= root) & (z > 0))
        def _():
            back_down(t).wait_send()

        return carry

    lax.fori_loop(0, count, finish, 0)


def summed_weights(rows_n, ident, operands):
    count = len(plan_jobs())
    low = operands[0].shape[0]
    rows, lanes = CHUNK_ROWS, CHUNK_LANES
    dma = pltpu.SemaphoreType.DMA
    depth = 3
    buffers = [
        (2, low, 1024),
        (2, low, 1024),
        None,
        (depth, 2, 2, 2, rows, lanes),
        (count, 2, 2, rows, lanes),
        (count, 2, 2, rows, lanes),
        (count, 2, rows, lanes // 2),
        (count, 2, rows, lanes // 2),
        (count, rows, lanes // 2),
        (count, rows, lanes // 2),
        (count, rows, lanes),
        (count, rows, lanes),
    ]
    scratch = [pltpu.VMEM(b, BF16) if b else pltpu.VMEM((1024, 512), F32) for b in buffers]
    return pl.pallas_call(
        functools.partial(weights_kernel, rows_n),
        in_specs=[pl.BlockSpec(memory_space=pl.ANY)] * len(operands),
        out_specs=pl.BlockSpec(memory_space=pltpu.VMEM),
        out_shape=jax.ShapeDtypeStruct((count, rows, lanes), BF16),
        scratch_shapes=scratch + [dma((2,)), dma((2,))] + [dma((count,))] * 17,
        compiler_params=pltpu.CompilerParams(
            collective_id=ident, has_side_effects=True, vmem_limit_bytes=63 * 1024 * 1024
        ),
        cost_estimate=pl.CostEstimate(
            flops=40_000_000_000, bytes_accessed=100_000_000, transcendentals=0
        ),
    )(*operands)


def unpack_kernel(sums_n, done, *refs):
    sums, outs = refs[:sums_n], refs[sums_n:]
    in1, mid1, out1, skip, in2, mid2, out2 = outs[:7]
    rows, lanes = CHUNK_ROWS, CHUNK_LANES
    half = lanes // 2

    def wide(k):
        return done[k].astype(F32)

    def stacked(first, count, parts, out):
        width = lanes // parts
        for k in range(count):
            for h in range(parts):
                piece = done[first + k, :, h * width : (h + 1) * width]
                out[h * rows : (h + 1) * rows, k * width : (k + 1) * width] = piece.astype(F32)

    for k in range(2):
        out2[:, k * lanes : (k + 1) * lanes] = wide(k)
        out1[:, k * lanes : (k + 1) * lanes] = wide(10 + k)
    taps2 = [(2 + k // 2, k % 2) for k in range(8)] + [(6, 0)]
    taps1 = [(19, 1), (17, 0), (18, 0), (16, 1), (6, 1), (16, 0), (19, 0), (17, 1), (18, 1)]
    for out, taps in ((mid1, taps1), (mid2, taps2)):
        for k, (chunk, side) in enumerate(taps):
            out[k] = done[chunk, :, side * half : (side + 1) * half].astype(F32)
    stacked(7, 2, 4, in2)
    stacked(9, 1, 2, in1)
    stacked(12, 4, 2, skip)
    rest = list(outs[7:])
    for ref in sums:
        for k in range(ref.shape[0]):
            rest.pop(0)[...] = ref[k : k + 1, :]


def unpack(done, sums):
    rows = CHUNK_ROWS
    shapes = [(128, 512), (9, rows, 512), (rows, 2048), (128, 2048), (256, 512), (9, rows, 512), (rows, 2048)]
    shapes += [(1, x.shape[1]) for x in sums for _ in range(x.shape[0])]
    vmem = pl.BlockSpec(memory_space=pltpu.VMEM)
    outs = pl.pallas_call(
        functools.partial(unpack_kernel, len(sums)),
        in_specs=[vmem] * (1 + len(sums)),
        out_specs=[vmem] * len(shapes),
        out_shape=[jax.ShapeDtypeStruct(shape, F32) for shape in shapes],
        compiler_params=pltpu.CompilerParams(vmem_limit_bytes=32 * 1024 * 1024),
    )(done, *sums)
    return outs[:7], [x.reshape(-1) for x in outs[7:]]


def masks_kernel(rows_low, extent, mask_in, mask_out, mask_above, mask_edges):
    side = extent[...]
    side_low = side // 2
    low0 = lax.axis_index("rows") * rows_low
    column = lax.broadcasted_iota(jnp.int32, side.shape, 1)

    def inside(row, col, limit):
        kept = (row >= 0) & (row < limit) & (col < limit)
        return jnp.where(kept, 1.0, 0.0)

    for i in range(rows_low):
        for p in range(2):
            for q in range(2):
                mask_in[2 * p + q, :, i] = inside(2 * (low0 + i) + p, 2 * column + q, side)
        mask_out[:, i] = inside(low0 + i, column, side_low)
    for q in range(2):
        mask_above[q, :, 0] = inside(2 * low0 - 1, 2 * column + q, side)
    mask_edges[0, :, 0] = inside(low0 - 1, column, side_low)
    mask_edges[1, :, 0] = inside(low0 + rows_low, column, side_low)


def masks_of(extent, rows_low):
    images, columns, lanes = extent.shape
    vmem = pl.BlockSpec(memory_space=pltpu.VMEM)
    shapes = [
        (4, images, rows_low, columns, lanes),
        (images, rows_low, columns, lanes),
        (2, images, 1, columns, lanes),
        (2, images, 1, columns, lanes),
    ]
    return pl.pallas_call(
        functools.partial(masks_kernel, rows_low),
        in_specs=[vmem],
        out_specs=[vmem] * 4,
        out_shape=[jax.ShapeDtypeStruct(shape, F32) for shape in shapes],
        compiler_params=pltpu.CompilerParams(vmem_limit_bytes=24 * 1024 * 1024),
    )(extent)


def body(
    image_in,
    extent,
    weight_in1,
    weight_mid1,
    weight_out1,
    weight_skip,
    weight_in2,
    weight_mid2,
    weight_out2,
    gain_in1,
    shift_in1,
    gain_mid1,
    shift_mid1,
    gain_out1,
    shift_out1,
    gain_skip,
    shift_skip,
    gain_in2,
    shift_in2,
    gain_mid2,
    shift_mid2,
    gain_out2,
    shift_out2,
    cotangent,
):
    images, rows_here, columns, inputs = image_in.shape
    middle, outputs = weight_out1.shape
    rows_low, cols_low = rows_here // 2, columns // 2
    low = images * rows_low * cols_low
    rows_n, img_n = lax.axis_size("rows"), lax.axis_size("img")
    blocks = images // IMAGES
    per_block = low // blocks
    edge = images * cols_low
    run = Exchange(rows_n, img_n, blocks)


    columns8 = jnp.broadcast_to(extent[:, None, None], (images, cols_low, 128))
    mask_in, mask_out, mask_above, mask_edges = (
        m.reshape(m.shape[:-4] + (-1, 128)) for m in masks_of(columns8, rows_low)
    )

    group_images = 256 // (rows_here * columns)
    order = np.arange(256).reshape(group_images, rows_low, 2, cols_low, 2)
    order = order.transpose(2, 4, 0, 1, 3).reshape(-1)
    perm = jnp.asarray(np.eye(256, dtype=np.float32)[order], BF16)

    def row(vector):
        return vector.reshape(1, -1)

    g_in1, s_in1, g_mid1, s_mid1 = row(gain_in1), row(shift_in1), row(gain_mid1), row(shift_mid1)
    g_out1, s_out1, g_skip, s_skip = row(gain_out1), row(shift_out1), row(gain_skip), row(shift_skip)
    g_in2, s_in2, g_mid2, s_mid2 = row(gain_in2), row(shift_in2), row(gain_mid2), row(shift_mid2)
    g_out2, s_out2 = row(gain_out2), row(shift_out2)
    kernel_mid1 = weight_mid1.transpose(1, 2, 0, 3).reshape(9 * middle, middle)
    kernel_mid2 = weight_mid2.transpose(1, 2, 0, 3).reshape(9 * middle, middle)
    cot = cotangent.reshape(low, outputs)

    dev_mid_out = [((low, middle), BF16, BY_ROWS), ((blocks, 1, middle), F32, BY_BLOCK)]
    dev_out_out = [((low, outputs), BF16, BY_ROWS), ((blocks, 1, outputs), F32, BY_BLOCK)]
    hidden_out = [((low, middle), BF16, BY_ROWS)]
    wide_out = [((low, outputs), BF16, BY_ROWS)]
    acc_mid, acc_out = ((per_block, middle), F32), ((per_block, outputs), F32)
    unit_flops = 2 * low * middle * middle

    def normal(dev, centre, stats, gain, shift, kind=BY_ROWS):
        return [(dev, kind), (centre, BY_BLOCK), (stats, WHOLE), (gain, WHOLE), (shift, WHOLE)]

    planes, d_in1, c_in1, d_skip, c_skip, n_in1, n_skip, halo_in1, halo_c_in1 = run(
        open_kernel,
        [
            (image_in.reshape(4 * low, inputs), BY_ROWS),
            (perm, WHOLE),
            (mask_in, BY_PLANES),
            (mask_out, BY_ROWS),
            (weight_in1, WHOLE),
            (weight_skip, WHOLE),
        ],
        [
            ((4, low, inputs), BF16, BY_PLANES),
            ((4, low, middle), BF16, BY_PLANES),
            ((blocks, 1, middle), F32, BY_BLOCK),
        ]
        + dev_out_out,
        True,
        3,
        (middle, outputs),
        scratch=[((4, per_block, middle), F32), acc_out],
        flops=20 * unit_flops,
        edges=[(1, 2, True, 1), (1, 3, True, 1)],
        centres=(2, (1,)),
        edge=edge,
        early=True,
    )
    hid_in1, d_mid1, c_mid1, n_mid1, halo_mid1, halo_c_mid1 = run(
        functools.partial(mid1_kernel, rows_low),
        [
            (d_in1, BY_PLANES),
            (c_in1, BY_BLOCK),
            (mask_in, BY_PLANES),
            (halo_in1, BY_PLANES),
            (halo_c_in1[0], BY_BLOCK),
            (mask_above, BY_PLANES),
            (n_in1, WHOLE),
            (g_in1, WHOLE),
            (s_in1, WHOLE),
            (mask_out, BY_ROWS),
            (kernel_mid1, WHOLE),
        ],
        [((4, low, middle), BF16, BY_PLANES)] + dev_mid_out,
        True,
        3,
        (middle,),
        scratch=[((5, per_block, middle), BF16), acc_mid],
        flops=9 * unit_flops,
        edges=[(1, None, False, -1)],
        centres=(2, (-1,)),
        edge=edge,
    )
    hid_mid1, d_out1, c_out1, n_out1 = run(
        expand_kernel,
        normal(d_mid1, c_mid1, n_mid1, g_mid1, s_mid1) + [(mask_out, BY_ROWS), (weight_out1, WHOLE)],
        hidden_out + dev_out_out,
        True,
        3,
        (outputs,),
        scratch=[acc_out],
        flops=4 * unit_flops,
    )
    join = normal(d_out1, c_out1, n_out1, g_out1, s_out1) + normal(d_skip, c_skip, n_skip, g_skip, s_skip)
    both = [(1, None, True, 1), (1, None, False, -1)]
    first_low, d_in2, c_in2, n_in2, halo_in2, halo_c_in2 = run(
        join_kernel,
        join + [(mask_out, BY_ROWS), (weight_in2, WHOLE)],
        wide_out + dev_mid_out,
        True,
        3,
        (middle,),
        scratch=[acc_mid],
        flops=4 * unit_flops,
        edges=both,
        centres=(2, (1, -1)),
        edge=edge,
    )

    hid_in2, d_mid2, c_mid2, n_mid2, halo_mid2, halo_c_mid2 = run(
        functools.partial(mid2_kernel, rows_low),
        [
            (d_in2, BY_ROWS),
            (c_in2, BY_BLOCK),
            (halo_in2, BY_PLANES),
            (halo_c_in2, PAIR_BLOCK),
            (mask_edges, BY_PLANES),
            (n_in2, WHOLE),
            (g_in2, WHOLE),
            (s_in2, WHOLE),
            (mask_out, BY_ROWS),
            (kernel_mid2, WHOLE),
        ],
        hidden_out + dev_mid_out,
        True,
        3,
        (middle,),
        scratch=[((per_block, 9 * middle), BF16), acc_mid],
        flops=9 * unit_flops,
        edges=both,
        centres=(2, (1, -1)),
        edge=edge,
    )
    hid_mid2, d_out2, c_out2, n_out2 = run(
        expand_kernel,
        normal(d_mid2, c_mid2, n_mid2, g_mid2, s_mid2) + [(mask_out, BY_ROWS), (weight_out2, WHOLE)],
        hidden_out + dev_out_out,
        True,
        3,
        (outputs,),
        scratch=[acc_out],
        flops=4 * unit_flops,
    )
    block_out, gn_out2, z_out2 = run(
        final_kernel,
        normal(d_out2, c_out2, n_out2, g_out2, s_out2)
        + [(first_low, BY_ROWS), (cot, BY_ROWS), (mask_out, BY_ROWS)],
        wide_out + wide_out,
        False,
        2,
        (outputs,),
    )

    ga_out2, gn_mid2, z_mid2, halo_gn_mid2 = run(
        back_expand_kernel,
        [
            (gn_out2, BY_ROWS),
            (d_out2, BY_ROWS),
            (c_out2, BY_BLOCK),
            (n_out2, WHOLE),
            (g_out2, WHOLE),
            (z_out2, WHOLE),
            (mask_out, BY_ROWS),
            (weight_out2, WHOLE),
        ]
        + normal(d_mid2, c_mid2, n_mid2, g_mid2, s_mid2),
        wide_out + hidden_out,
        False,
        2,
        (middle,),
        scratch=[acc_mid],
        flops=4 * unit_flops,
        edges=both,
        edge=edge,
    )
    views2, gn_in2, z_in2 = run(
        functools.partial(back_mid2_kernel, rows_low),
        [
            (gn_mid2, BY_ROWS),
            (d_mid2, BY_ROWS),
            (c_mid2, BY_BLOCK),
            (halo_gn_mid2, BY_PLANES),
            (halo_mid2, BY_PLANES),
            (halo_c_mid2, PAIR_BLOCK),
            (mask_edges, BY_PLANES),
            (n_mid2, WHOLE),
            (g_mid2, WHOLE),
            (z_mid2, WHOLE),
            (mask_out, BY_ROWS),
            (kernel_mid2, WHOLE),
        ]
        + normal(d_in2, c_in2, n_in2, g_in2, s_in2),
        [((low, 9 * middle), BF16, BY_ROWS)] + hidden_out,
        False,
        2,
        (middle,),
        scratch=[acc_mid],
        flops=9 * unit_flops,
    )
    ga_in2, gs1, z_sum1 = run(
        back_join_kernel,
        [
            (gn_in2, BY_ROWS),
            (d_in2, BY_ROWS),
            (c_in2, BY_BLOCK),
            (n_in2, WHOLE),
            (g_in2, WHOLE),
            (z_in2, WHOLE),
            (mask_out, BY_ROWS),
            (weight_in2, WHOLE),
            (gn_out2, BY_ROWS),
        ]
        + join,
        hidden_out + wide_out,
        False,
        3,
        (outputs,),
        scratch=[acc_out],
        flops=4 * unit_flops,
    )

    ga_out1, ga_skip, gn_mid1, grad_skip_in, z_mid1, halo_gn_mid1 = run(
        back_split_kernel,
        [
            (gs1, BY_ROWS),
            (d_out1, BY_ROWS),
            (c_out1, BY_BLOCK),
            (n_out1, WHOLE),
            (g_out1, WHOLE),
            (d_skip, BY_ROWS),
            (c_skip, BY_BLOCK),
            (n_skip, WHOLE),
            (g_skip, WHOLE),
            (z_sum1, WHOLE),
            (mask_out, BY_ROWS),
            (weight_out1, WHOLE),
            (weight_skip, WHOLE),
        ]
        + normal(d_mid1, c_mid1, n_mid1, g_mid1, s_mid1),
        wide_out + wide_out + hidden_out + [((low, inputs), BF16, BY_ROWS)],
        False,
        2,
        (middle,),
        scratch=[acc_mid, ((per_block, inputs), F32)],
        flops=12 * unit_flops,
        edges=[(2, None, False, -1)],
        edge=edge,
    )
    views1, gn_in1, z_in1 = run(
        functools.partial(back_mid1_kernel, rows_low),
        [
            (gn_mid1, BY_ROWS),
            (d_mid1, BY_ROWS),
            (c_mid1, BY_BLOCK),
            (halo_gn_mid1[0], BY_ROWS),
            (halo_mid1[0], BY_ROWS),
            (halo_c_mid1[0], BY_BLOCK),
            (mask_edges[1], BY_ROWS),
            (n_mid1, WHOLE),
            (g_mid1, WHOLE),
            (z_mid1, WHOLE),
            (mask_out, BY_ROWS),
            (kernel_mid1, WHOLE),
            (d_in1, BY_PLANES),
            (c_in1, BY_BLOCK),
            (mask_in, BY_PLANES),
            (n_in1, WHOLE),
            (g_in1, WHOLE),
            (s_in1, WHOLE),
        ],
        [((low, 4 * middle), BF16, BY_ROWS), ((4, low, middle), BF16, BY_PLANES)],
        False,
        2,
        (middle,),
        scratch=[((4, per_block, middle), F32)],
        flops=9 * unit_flops,
    )
    ga_in1, grad_image, block_out = stage(
        back_image_kernel,
        blocks,
        [
            (gn_in1, BY_PLANES),
            (d_in1, BY_PLANES),
            (c_in1, BY_BLOCK),
            (n_in1, WHOLE),
            (g_in1, WHOLE),
            (z_in1, WHOLE),
            (mask_in, BY_PLANES),
            (weight_in1, WHOLE),
            (grad_skip_in, BY_ROWS),
            (perm, WHOLE),
            (block_out, BY_ROWS),
        ],
        [((4, low, middle), BF16, BY_PLANES), ((4 * low, inputs), BF16, BY_ROWS)] + wide_out,
        scratch=[((4, per_block, inputs), BF16)],
        flops=12 * unit_flops,
    )
    sums = [z_in1, z_mid1, z_sum1, z_in2, z_mid2, z_out2]

    if (rows_n, img_n) == (4, 8):
        done = summed_weights(
            rows_n,
            run.calls,
            [
                hid_mid2,
                ga_out2,
                hid_in2,
                views2,
                first_low,
                ga_in2,
                hid_mid1,
                ga_out1,
                planes,
                ga_skip,
                hid_in1,
                views1,
                ga_in1,
            ],
        )
        grads, rows_of = unpack(done, sums)
        dw_in1, dw_mid1, dw_out1, dw_skip, dw_in2, dw_mid2, dw_out2 = grads
        dw_mid1, dw_mid2 = (
            g.reshape(3, 3, -1, middle).transpose(2, 0, 1, 3) for g in (dw_mid1, dw_mid2)
        )
    else:
        def weight_term(values, upstream):
            return lax.dot_general(
                values, upstream, (((0,), (0,)), ((), ())), preferred_element_type=F32
            ).astype(BF16)

        def reduced(grad):
            shard = lax.psum_scatter(grad, "img", scatter_dimension=0, tiled=True)
            return lax.psum(shard, "rows").astype(F32)

        dw_out2 = reduced(weight_term(hid_mid2, ga_out2))
        dw_mid2 = reduced(weight_term(hid_in2, views2))
        dw_in2 = reduced(weight_term(first_low, ga_in2))
        dw_out1 = reduced(weight_term(hid_mid1, ga_out1))
        dw_skip = reduced(weight_term(planes[0], ga_skip))
        m = middle
        dw_00 = weight_term(hid_in1[0], views1[:, m : 2 * m])
        dw_01 = weight_term(hid_in1[1], views1[:, m : 3 * m])
        dw_10 = weight_term(hid_in1[2], views1[:, : 2 * m])
        dw_11 = weight_term(hid_in1[3], views1)
        dw_mid1 = jnp.concatenate(
            [
                dw_11[:, 3 * m :],
                dw_10[:, :m],
                dw_11[:, :m],
                dw_01[:, m:],
                dw_00,
                dw_01[:, :m],
                dw_11[:, 2 * m : 3 * m],
                dw_10[:, m:],
                dw_11[:, m : 2 * m],
            ],
            axis=1,
        )
        dw_mid1 = reduced(dw_mid1)
        dw_in1 = reduced(
            weight_term(planes.reshape(4 * low, inputs), ga_in1.reshape(4 * low, middle))
        )
        rows_of = [x[k] for x in sums for k in range(x.shape[0])]
    kernel_shape = (middle // img_n, 3, 3, middle)
    (
        shift_in1_g,
        gain_in1_g,
        shift_mid1_g,
        gain_mid1_g,
        shift_sum1_g,
        gain_out1_g,
        gain_skip_g,
        shift_in2_g,
        gain_in2_g,
        shift_mid2_g,
        gain_mid2_g,
        shift_out2_g,
        gain_out2_g,
    ) = rows_of
    return (
        block_out.reshape(images, rows_low, cols_low, outputs),
        grad_image.reshape(images, rows_here, columns, inputs),
        dw_in1,
        dw_mid1.reshape(kernel_shape),
        dw_out1,
        dw_skip,
        dw_in2,
        dw_mid2.reshape(kernel_shape),
        dw_out2,
        gain_in1_g,
        shift_in1_g,
        gain_mid1_g,
        shift_mid1_g,
        gain_out1_g,
        shift_sum1_g,
        gain_skip_g,
        shift_sum1_g,
        gain_in2_g,
        shift_in2_g,
        gain_mid2_g,
        shift_mid2_g,
        gain_out2_g,
        shift_out2_g,
    )


def solution(mesh):
    image = P("img", "rows", None, None)
    in_specs = (image, P("img")) + (P(),) * 21 + (image,)
    out_specs = (
        image,
        image,
        P("img", None),
        P("img", None, None, None),
        P("img", None),
        P("img", None),
        P("img", None),
        P("img", None, None, None),
        P("img", None),
    ) + (P(),) * 14
    return jax.shard_map(body, mesh=mesh, in_specs=in_specs, out_specs=out_specs, check_vma=False)
```

```python
import functools

import jax
import jax.numpy as jnp
import numpy as np
from jax import lax
from jax.experimental import pallas as pl
from jax.experimental.pallas import tpu as pltpu
from jax.sharding import PartitionSpec as P

EPSILON = 1e-05
F32 = jnp.float32
BF16 = jnp.bfloat16
LANES = 512
ROWS = 32
IMAGES = 16
VMEM_BYTES = 48 * 1024 * 1024
MESH = pl.DeviceIdType.MESH
BY_ROWS, BY_PLANES, FIRST_PLANE, BY_BLOCK, PAIR_BLOCK, WHOLE, APART = range(7)


def dot(a, b):
    return jnp.dot(a, b, preferred_element_type=F32)


def dot_t(a, b):
    return lax.dot_general(a, b, (((1,), (1,)), ((), ())), preferred_element_type=F32)


def load(ref, rows, lanes):
    value = ref[rows, lanes].astype(F32)
    return value.reshape(value.shape[0] // 8, 8, value.shape[1])


def store(ref, rows, lanes, value):
    ref[rows, lanes] = value.reshape(value.shape[0] * 8, value.shape[2]).astype(ref.dtype)


def load_mask(ref, rows):
    mask = load(ref, rows, slice(None))
    return jnp.concatenate([mask] * (LANES // 128), axis=-1)


def sweep(total, step, init, rows=ROWS):
    def body(i, carry):
        return step(pl.ds(pl.multiple_of(i * rows, rows), rows), i, carry)

    return lax.fori_loop(0, total // rows, body, init, unroll=True)


def lane_blocks(width):
    return [slice(k * LANES, (k + 1) * LANES) for k in range(width // LANES)]


def tall(row):
    return jnp.broadcast_to(row, (8, row.shape[-1]))


def column_sum(value):
    return jnp.sum(value, axis=0)


def total_of(part):
    return jnp.sum(part, axis=0, keepdims=True)


def zeros8():
    return jnp.zeros((8, LANES), F32)


def tally(first, parts, centre_ref, stats_ref, fill=None):
    width = parts[0][0].shape[-1]
    for lanes in lane_blocks(width):
        if fill is not None:
            fill(lanes)
        sums = (zeros8(), zeros8())
        for acc, mask_ref, dev in parts:

            def add(rows, i, carry, acc=acc, mask_ref=mask_ref):
                mask = load_mask(mask_ref, rows)
                return (
                    carry[0] + column_sum(load(acc, rows, lanes) * mask),
                    carry[1] + column_sum(mask),
                )

            sums = sweep(acc.shape[0], add, sums)
        total, count = total_of(sums[0]), total_of(sums[1])
        centre = total / jnp.maximum(count, 1.0)
        centre_ref[:, lanes] = centre
        centre8 = tall(centre)
        squares = zeros8()
        for acc, mask_ref, dev in parts:

            def square(rows, i, carry, acc=acc, mask_ref=mask_ref, dev=dev):
                away = load(acc, rows, lanes) - centre8
                store(dev, rows, lanes, away)
                return carry + column_sum(load_mask(mask_ref, rows) * away * away)

            squares = sweep(acc.shape[0], square, squares)
        squares = total_of(squares)
        count_old, mean_old, squares_old = (
            jnp.where(first, jnp.zeros_like(count), stats_ref[k : k + 1, lanes]) for k in range(3)
        )
        both = count_old + count
        share = count / jnp.maximum(both, 1.0)
        delta = centre - mean_old
        stats_ref[0:1, lanes] = both
        stats_ref[1:2, lanes] = mean_old + delta * share
        stats_ref[2:3, lanes] = squares_old + squares + delta * delta * count_old * share


def affine(stats_ref, gain_ref, shift_ref, centre_ref, lanes):
    scale = lax.rsqrt(stats_ref[2:3, lanes] + EPSILON)
    slope = gain_ref[:, lanes] * scale
    base = shift_ref[:, lanes] + (centre_ref[:, lanes] - stats_ref[1:2, lanes]) * slope
    return tall(0.5 * slope), tall(0.5 * base)


def silu_half(half):
    return half + half * jnp.tanh(half)


def gate_half(half):
    tanh = jnp.tanh(half)
    return (0.5 + 0.5 * tanh) * (1.0 + half * (1.0 - tanh))


def silu_and_gate(half):
    tanh = jnp.tanh(half)
    return half + half * tanh, (0.5 + 0.5 * tanh) * (1.0 + half * (1.0 - tanh))


def back_coefs(stats_ref, gain_ref, centre_ref, sums, lanes):
    shift_sum, gain_sum = sums
    pixels = stats_ref[0:1, lanes]
    scale = lax.rsqrt(stats_ref[2:3, lanes] + EPSILON)
    slope = gain_ref[:, lanes] * scale
    per_pixel = slope / pixels
    away = (centre_ref[:, lanes] - stats_ref[1:2, lanes]) * scale
    return (
        tall(slope),
        tall(-per_pixel * scale * gain_sum),
        tall(-per_pixel * (shift_sum + away * gain_sum)),
    )


def unit_sum(stats_ref, centre_ref, lanes, gn_sum, gd_sum):
    scale = lax.rsqrt(stats_ref[2:3, lanes] + EPSILON)
    return scale * (gd_sum + (centre_ref[:, lanes] - stats_ref[1:2, lanes]) * gn_sum)


def accumulate(first, ref, row, lanes, value):
    old = jnp.where(first, jnp.zeros_like(value), ref[row : row + 1, lanes])
    ref[row : row + 1, lanes] = old + value


def shifted(value, by):
    if by == 0:
        return value
    rolled = pltpu.roll(value, (-by) % 8, axis=1)
    column = lax.broadcasted_iota(jnp.int32, value.shape, 1)
    return jnp.where(column == (0 if by < 0 else 7), 0.0, rolled)


def from_above(value, edge, rows_low):
    if rows_low == 1:
        return edge
    images = value.shape[0] // rows_low
    image = value.reshape((images, rows_low) + value.shape[1:])
    return jnp.concatenate([edge[:, None], image[:, :-1]], axis=1).reshape(value.shape)


def from_below(value, edge, rows_low):
    if rows_low == 1:
        return edge
    images = value.shape[0] // rows_low
    image = value.reshape((images, rows_low) + value.shape[1:])
    return jnp.concatenate([image[:, 1:], edge[:, None]], axis=1).reshape(value.shape)


def edge_rows(i, rows_low):
    return pl.ds(pl.multiple_of(i * (ROWS // rows_low), ROWS // rows_low), ROWS // rows_low)


def either(upto, early, late, rows, lanes):
    here = pl.program_id(0) < upto
    return jnp.where(here, load(early, rows, lanes), load(late, rows, lanes))


def first_step():
    return pl.program_id(0) == 0


def open_kernel(
    image_ref,
    perm_ref,
    mask_ref,
    mask_out,
    weight_ref,
    weight_skip,
    planes_ref,
    dev_ref,
    centre_ref,
    dev_skip,
    centre_skip,
    stats_ref,
    acc,
    acc_skip,
    flush,
):
    planes, low, _ = planes_ref.shape
    group = perm_ref.shape[0]
    part = group // planes
    for g in range(image_ref.shape[0] // group):
        mask = jnp.concatenate(
            [mask_ref[p, g * part : (g + 1) * part, :] for p in range(planes)], axis=0
        )
        mask = jnp.concatenate([mask] * (group // 128), axis=1)
        perm = (perm_ref[...].astype(F32) * mask).astype(BF16)
        moved = dot(perm, image_ref[g * group : (g + 1) * group, :]).astype(BF16)
        for p in range(planes):
            planes_ref[p, g * part : (g + 1) * part, :] = moved[p * part : (p + 1) * part]
    for p in range(planes):
        acc[p] = dot(planes_ref[p], weight_ref[...])
    width = acc.shape[-1]
    tally(
        first_step(),
        [(acc.at[p], mask_ref.at[p], dev_ref.at[p]) for p in range(planes)],
        centre_ref,
        stats_ref.at[:, :width],
    )
    flush()

    def fill(lanes):
        acc_skip[:, lanes] = dot(planes_ref[0], weight_skip[:, lanes])

    tally(first_step(), [(acc_skip, mask_out, dev_skip)], centre_skip, stats_ref.at[:, width:], fill)


def mid1_kernel(
    rows_low,
    dev_in,
    centre_in,
    mask_ref,
    halo,
    halo_centre,
    halo_mask,
    stats_in,
    gain,
    shift,
    mask_out,
    weight,
    hidden,
    dev_out,
    centre_out,
    stats_out,
    taps,
    acc,
):
    low, width = acc.shape
    steps = []
    for lanes in lane_blocks(width):
        slope, base = affine(stats_in, gain, shift, centre_in, lanes)
        slope_edge, base_edge = affine(stats_in, gain, shift, halo_centre, lanes)

        def act(p, rows, lanes=lanes, slope=slope, base=base):
            mask = load_mask(mask_ref.at[p], rows)
            value = silu_half(load(dev_in.at[p], rows, lanes) * slope + base) * mask
            store(hidden.at[p], rows, lanes, value)
            return value

        def act_edge(q, i, lanes=lanes, slope_edge=slope_edge, base_edge=base_edge):
            rows = edge_rows(i, rows_low)
            half = load(halo.at[q], rows, lanes) * slope_edge + base_edge
            return silu_half(half) * load_mask(halo_mask.at[q], rows)

        def step0(rows, i, carry):
            act(0, rows)
            return carry

        def step1(rows, i, carry):
            store(taps.at[0], rows, lanes, shifted(act(1, rows), -1))
            return carry

        def step2(rows, i, carry):
            store(taps.at[1], rows, lanes, from_above(act(2, rows), act_edge(0, i), rows_low))
            return carry

        def step3(rows, i, carry):
            odd = act(3, rows)
            store(taps.at[2], rows, lanes, shifted(odd, -1))
            above = from_above(odd, act_edge(1, i), rows_low)
            store(taps.at[3], rows, lanes, above)
            store(taps.at[4], rows, lanes, shifted(above, -1))
            return carry

        steps.append((step0, step1, step2, step3))

    def tap(t, u):
        k = (3 * t + u) * width
        return weight[k : k + width]

    def plane(p):
        for some in steps:
            sweep(low, some[p], 0)

    plane(0)
    plane(1)
    acc[...] = dot(hidden[0], tap(1, 1))
    plane(2)
    acc[...] += dot(hidden[1], tap(1, 2)) + dot(taps[0], tap(1, 0))
    plane(3)
    acc[...] += dot(hidden[2], tap(2, 1)) + dot(taps[1], tap(0, 1))
    acc[...] += (
        dot(hidden[3], tap(2, 2))
        + dot(taps[2], tap(2, 0))
        + dot(taps[3], tap(0, 2))
        + dot(taps[4], tap(0, 0))
    )
    tally(first_step(), [(acc, mask_out, dev_out)], centre_out, stats_out)


def expand_kernel(
    dev_in, centre_in, stats_in, gain, shift, mask, weight, hidden, dev_out, centre_out, stats_out, acc
):
    for lanes in lane_blocks(dev_in.shape[1]):
        slope, base = affine(stats_in, gain, shift, centre_in, lanes)

        def step(rows, i, carry):
            half = load(dev_in, rows, lanes) * slope + base
            store(hidden, rows, lanes, silu_half(half) * load_mask(mask, rows))
            return carry

        sweep(dev_in.shape[0], step, 0)

    def fill(lanes):
        acc[:, lanes] = dot(hidden[...], weight[:, lanes])

    tally(first_step(), [(acc, mask, dev_out)], centre_out, stats_out, fill)


def join_kernel(
    dev_a,
    centre_a,
    stats_a,
    gain_a,
    shift_a,
    dev_b,
    centre_b,
    stats_b,
    gain_b,
    shift_b,
    mask,
    weight,
    first_low,
    dev_out,
    centre_out,
    stats_out,
    acc,
):
    for lanes in lane_blocks(dev_a.shape[1]):
        slope_a, base_a = affine(stats_a, gain_a, shift_a, centre_a, lanes)
        slope_b, base_b = affine(stats_b, gain_b, shift_b, centre_b, lanes)
        base = base_a + base_b

        def step(rows, i, carry):
            half = load(dev_a, rows, lanes) * slope_a + load(dev_b, rows, lanes) * slope_b + base
            store(first_low, rows, lanes, silu_half(half) * load_mask(mask, rows))
            return carry

        sweep(dev_a.shape[0], step, 0)
        part = dot(first_low[:, lanes], weight[lanes, :])
        acc[...] = part if lanes.start == 0 else acc[...] + part
    tally(first_step(), [(acc, mask, dev_out)], centre_out, stats_out)


def mid2_kernel(
    rows_low,
    dev_in,
    centre_in,
    halo,
    halo_centre,
    halo_mask,
    stats_in,
    gain,
    shift,
    mask,
    weight,
    hidden,
    dev_out,
    centre_out,
    stats_out,
    taps,
    acc,
):
    low, width = acc.shape
    for lanes in lane_blocks(width):
        slope, base = affine(stats_in, gain, shift, centre_in, lanes)
        edges = [affine(stats_in, gain, shift, halo_centre.at[e], lanes) for e in range(2)]

        def act_edge(e, i):
            rows = edge_rows(i, rows_low)
            half = load(halo.at[e], rows, lanes) * edges[e][0] + edges[e][1]
            return silu_half(half) * load_mask(halo_mask.at[e], rows)

        def step(rows, i, carry):
            value = silu_half(load(dev_in, rows, lanes) * slope + base) * load_mask(mask, rows)
            store(hidden, rows, lanes, value)
            lines = (
                from_above(value, act_edge(0, i), rows_low),
                value,
                from_below(value, act_edge(1, i), rows_low),
            )
            for t in range(3):
                for u in range(3):
                    start = (3 * t + u) * width + lanes.start
                    store(taps, rows, slice(start, start + LANES), shifted(lines[t], u - 1))
            return carry

        sweep(low, step, 0)
    acc[...] = dot(taps[...], weight[...])
    tally(first_step(), [(acc, mask, dev_out)], centre_out, stats_out)


def final_kernel(dev, centre, stats, gain, shift, first_low, cot, mask, block_out, gn_ref, sums):
    first = first_step()
    for lanes in lane_blocks(dev.shape[1]):
        slope, base = affine(stats, gain, shift, centre, lanes)

        def step(rows, i, carry):
            away = load(dev, rows, lanes)
            half = away * slope + base + 0.5 * load(first_low, rows, lanes)
            valid = load_mask(mask, rows)
            value, gate = silu_and_gate(half)
            store(block_out, rows, lanes, value * valid)
            gn = gate * valid * load(cot, rows, lanes)
            store(gn_ref, rows, lanes, gn)
            return carry[0] + column_sum(gn), carry[1] + column_sum(gn * away)

        gn_sum, gd_sum = sweep(dev.shape[0], step, (zeros8(), zeros8()))
        gn_sum, gd_sum = total_of(gn_sum), total_of(gd_sum)
        accumulate(first, sums, 0, lanes, gn_sum)
        accumulate(first, sums, 1, lanes, unit_sum(stats, centre, lanes, gn_sum, gd_sum))


def scaled(gn, away, mask, coefs):
    return (gn * coefs[0] + away * coefs[1] + coefs[2]) * mask


def gate_sums(first, grads, dev, centre, stats, gain, shift, mask, gn_ref, sums, parts, fill=None):
    width = gn_ref.shape[-1]
    planes = range(parts) if parts else [None]
    for lanes in lane_blocks(width):
        slope, base = affine(stats, gain, shift, centre, lanes)
        carry = (zeros8(), zeros8())
        for p in planes:
            if fill is not None and lanes.start == 0:
                fill[p]()
            grad_p, dev_p, mask_p, gn_p = (
                r if p is None else r.at[p] for r in (grads, dev, mask, gn_ref)
            )

            def step(rows, i, carry, grad_p=grad_p, dev_p=dev_p, mask_p=mask_p, gn_p=gn_p):
                away = load(dev_p, rows, lanes)
                gate = gate_half(away * slope + base) * load_mask(mask_p, rows)
                gn = gate * load(grad_p, rows, lanes)
                store(gn_p, rows, lanes, gn)
                return carry[0] + column_sum(gn), carry[1] + column_sum(gn * away)

            carry = sweep(grad_p.shape[0], step, carry)
        gn_sum, gd_sum = total_of(carry[0]), total_of(carry[1])
        accumulate(first, sums, 0, lanes, gn_sum)
        accumulate(first, sums, 1, lanes, unit_sum(stats, centre, lanes, gn_sum, gd_sum))


def back_expand_kernel(
    gn,
    dev,
    centre,
    stats,
    gain,
    sums_in,
    mask,
    weight,
    dev_m,
    centre_m,
    stats_m,
    gain_m,
    shift_m,
    ga,
    gn_m,
    sums_m,
    acc,
):
    for lanes in lane_blocks(dev.shape[1]):
        coefs = back_coefs(
            stats, gain, centre, (sums_in[0:1, lanes], sums_in[1:2, lanes]), lanes
        )

        def step(rows, i, carry):
            away = load(dev, rows, lanes)
            store(ga, rows, lanes, scaled(load(gn, rows, lanes), away, load_mask(mask, rows), coefs))
            return carry

        sweep(dev.shape[0], step, 0)
        part = dot_t(ga[:, lanes], weight[:, lanes])
        acc[...] = part if lanes.start == 0 else acc[...] + part
    gate_sums(first_step(), acc, dev_m, centre_m, stats_m, gain_m, shift_m, mask, gn_m, sums_m, 0)


def back_mid2_kernel(
    rows_low,
    upto,
    gn,
    dev,
    centre,
    halo_gn,
    halo_dev,
    rest_dev,
    halo_centre,
    halo_mask,
    stats,
    gain,
    sums_in,
    mask,
    weight,
    dev_m,
    centre_m,
    stats_m,
    gain_m,
    shift_m,
    views,
    gn_m,
    sums_m,
    acc,
):
    low, width = acc.shape
    for lanes in lane_blocks(width):
        sums = (sums_in[0:1, lanes], sums_in[1:2, lanes])
        coefs = back_coefs(stats, gain, centre, sums, lanes)
        edges = [back_coefs(stats, gain, halo_centre.at[e], sums, lanes) for e in range(2)]

        def edge(e, i):
            rows = edge_rows(i, rows_low)
            return scaled(
                load(halo_gn.at[e], rows, lanes),
                either(upto, halo_dev.at[e], rest_dev.at[e], rows, lanes),
                load_mask(halo_mask.at[e], rows),
                edges[e],
            )

        def step(rows, i, carry):
            value = scaled(
                load(gn, rows, lanes), load(dev, rows, lanes), load_mask(mask, rows), coefs
            )
            lines = (
                from_below(value, edge(1, i), rows_low),
                value,
                from_above(value, edge(0, i), rows_low),
            )
            for t in range(3):
                for u in range(3):
                    start = (3 * t + u) * width + lanes.start
                    store(views, rows, slice(start, start + LANES), shifted(lines[t], 1 - u))
            return carry

        sweep(low, step, 0)
    total = dot_t(views[:, :width], weight[:width])
    for k in range(width, 9 * width, width):
        total += dot_t(views[:, k : k + width], weight[k : k + width])
    acc[...] = total
    gate_sums(first_step(), acc, dev_m, centre_m, stats_m, gain_m, shift_m, mask, gn_m, sums_m, 0)


def back_join_kernel(
    gn_in,
    dev_in,
    centre_in,
    stats_in,
    gain_in,
    sums_in,
    mask,
    weight,
    residual,
    dev_a,
    centre_a,
    stats_a,
    gain_a,
    shift_a,
    dev_b,
    centre_b,
    stats_b,
    gain_b,
    shift_b,
    ga,
    gs_ref,
    sums,
    acc,
):
    first = first_step()
    for lanes in lane_blocks(dev_in.shape[1]):
        coefs = back_coefs(
            stats_in, gain_in, centre_in, (sums_in[0:1, lanes], sums_in[1:2, lanes]), lanes
        )

        def step(rows, i, carry):
            away = load(dev_in, rows, lanes)
            value = scaled(load(gn_in, rows, lanes), away, load_mask(mask, rows), coefs)
            store(ga, rows, lanes, value)
            return carry

        sweep(dev_in.shape[0], step, 0)
    for lanes in lane_blocks(dev_a.shape[1]):
        acc[:, lanes] = dot_t(ga[...], weight[lanes, :])
        slope_a, base_a = affine(stats_a, gain_a, shift_a, centre_a, lanes)
        slope_b, base_b = affine(stats_b, gain_b, shift_b, centre_b, lanes)
        base = base_a + base_b

        def gate(rows, i, carry):
            away_a, away_b = load(dev_a, rows, lanes), load(dev_b, rows, lanes)
            half = away_a * slope_a + away_b * slope_b + base
            grad = load(residual, rows, lanes) + load(acc, rows, lanes)
            gs = gate_half(half) * load_mask(mask, rows) * grad
            store(gs_ref, rows, lanes, gs)
            return (
                carry[0] + column_sum(gs),
                carry[1] + column_sum(gs * away_a),
                carry[2] + column_sum(gs * away_b),
            )

        carry = sweep(dev_a.shape[0], gate, (zeros8(), zeros8(), zeros8()))
        gs_sum, a_sum, b_sum = (total_of(part) for part in carry)
        accumulate(first, sums, 0, lanes, gs_sum)
        accumulate(first, sums, 1, lanes, unit_sum(stats_a, centre_a, lanes, gs_sum, a_sum))
        accumulate(first, sums, 2, lanes, unit_sum(stats_b, centre_b, lanes, gs_sum, b_sum))


def back_split_kernel(
    gs,
    dev_a,
    centre_a,
    stats_a,
    gain_a,
    dev_b,
    centre_b,
    stats_b,
    gain_b,
    sums_in,
    mask,
    weight_a,
    weight_b,
    dev_m,
    centre_m,
    stats_m,
    gain_m,
    shift_m,
    ga_a,
    ga_b,
    gn_m,
    grad_skip,
    sums_m,
    acc,
    acc_skip,
):
    for lanes in lane_blocks(dev_a.shape[1]):
        shift_sum = sums_in[0:1, lanes]
        coefs_a = back_coefs(stats_a, gain_a, centre_a, (shift_sum, sums_in[1:2, lanes]), lanes)
        coefs_b = back_coefs(stats_b, gain_b, centre_b, (shift_sum, sums_in[2:3, lanes]), lanes)

        def step(rows, i, carry):
            value, valid = load(gs, rows, lanes), load_mask(mask, rows)
            store(ga_a, rows, lanes, scaled(value, load(dev_a, rows, lanes), valid, coefs_a))
            store(ga_b, rows, lanes, scaled(value, load(dev_b, rows, lanes), valid, coefs_b))
            return carry

        sweep(dev_a.shape[0], step, 0)
        part = dot_t(ga_a[:, lanes], weight_a[:, lanes])
        acc[...] = part if lanes.start == 0 else acc[...] + part
        part = dot_t(ga_b[:, lanes], weight_b[:, lanes])
        acc_skip[...] = part if lanes.start == 0 else acc_skip[...] + part
    grad_skip[...] = acc_skip[...].astype(BF16)
    gate_sums(first_step(), acc, dev_m, centre_m, stats_m, gain_m, shift_m, mask, gn_m, sums_m, 0)


def back_mid1_kernel(
    rows_low,
    upto,
    gn,
    dev,
    centre,
    halo_gn,
    halo_dev,
    rest_dev,
    halo_centre,
    halo_mask,
    stats,
    gain,
    sums_in,
    mask,
    weight,
    dev_m,
    centre_m,
    mask_m,
    stats_m,
    gain_m,
    shift_m,
    views,
    gn_m,
    sums_m,
    acc,
):
    _, low, width = acc.shape
    for lanes in lane_blocks(width):
        sums = (sums_in[0:1, lanes], sums_in[1:2, lanes])
        coefs = back_coefs(stats, gain, centre, sums, lanes)
        coefs_edge = back_coefs(stats, gain, halo_centre, sums, lanes)

        def step(rows, i, carry):
            value = scaled(
                load(gn, rows, lanes), load(dev, rows, lanes), load_mask(mask, rows), coefs
            )
            some = edge_rows(i, rows_low)
            edge = scaled(
                load(halo_gn, some, lanes),
                either(upto, halo_dev.at[0], rest_dev.at[0], some, lanes),
                load_mask(halo_mask, some),
                coefs_edge,
            )
            below = from_below(value, edge, rows_low)
            for k, view in enumerate((below, value, shifted(value, 1), shifted(below, 1))):
                start = k * width + lanes.start
                store(views, rows, slice(start, start + LANES), view)
            return carry

        sweep(low, step, 0)

    def view(k):
        return views[:, k * width : (k + 1) * width]

    def tap(t, u):
        k = (3 * t + u) * width
        return weight[k : k + width]

    def plane0():
        acc[0] = dot_t(view(1), tap(1, 1))

    def plane1():
        acc[1] = dot_t(view(1), tap(1, 2)) + dot_t(view(2), tap(1, 0))

    def plane2():
        acc[2] = dot_t(view(1), tap(2, 1)) + dot_t(view(0), tap(0, 1))

    def plane3():
        acc[3] = (
            dot_t(view(1), tap(2, 2))
            + dot_t(view(2), tap(2, 0))
            + dot_t(view(0), tap(0, 2))
            + dot_t(view(3), tap(0, 0))
        )

    gate_sums(
        first_step(),
        acc,
        dev_m,
        centre_m,
        stats_m,
        gain_m,
        shift_m,
        mask_m,
        gn_m,
        sums_m,
        4,
        (plane0, plane1, plane2, plane3),
    )


def back_image_kernel(
    gn,
    dev,
    centre,
    stats,
    gain,
    sums_in,
    mask_ref,
    weight,
    grad_skip,
    perm_ref,
    handed,
    ga,
    image,
    hand,
    planes_ref,
):
    planes, low, width = ga.shape
    for p in range(planes):
        for lanes in lane_blocks(width):
            coefs = back_coefs(
                stats, gain, centre, (sums_in[0:1, lanes], sums_in[1:2, lanes]), lanes
            )

            def step(rows, i, carry):
                away = load(dev.at[p], rows, lanes)
                valid = load_mask(mask_ref.at[p], rows)
                value = scaled(load(gn.at[p], rows, lanes), away, valid, coefs)
                store(ga.at[p], rows, lanes, value)
                return carry

            sweep(low, step, 0)
        grad = dot_t(ga[p], weight[...])
        if p == 0:
            grad += grad_skip[...].astype(F32)
        planes_ref[p] = grad.astype(BF16)
    hand[...] = handed[...]
    group = perm_ref.shape[0]
    part = group // planes
    for g in range(image.shape[0] // group):
        rows = slice(g * part, (g + 1) * part)
        mask = jnp.concatenate([mask_ref[p, rows, :] for p in range(planes)], axis=0)
        mask = jnp.concatenate([mask] * (group // 128), axis=1)
        perm = (perm_ref[...].astype(F32) * mask).astype(BF16)
        here = jnp.concatenate([planes_ref[p, rows, :] for p in range(planes)], axis=0)
        back = lax.dot_general(
            perm, here, (((0,), (0,)), ((), ())), preferred_element_type=F32
        )
        image[g * group : (g + 1) * group, :] = back.astype(BF16)


def spec_of(shape, kind, blocks):
    if isinstance(kind, pl.BlockSpec):
        return kind
    if kind == BY_ROWS:
        return pl.BlockSpec((shape[0] // blocks, shape[1]), lambda b: (b, 0))
    if kind == BY_PLANES:
        return pl.BlockSpec((shape[0], shape[1] // blocks, shape[2]), lambda b: (0, b, 0))
    if kind == FIRST_PLANE:
        return pl.BlockSpec((None, shape[1] // blocks, shape[2]), lambda b: (0, b, 0))
    if kind == BY_BLOCK:
        return pl.BlockSpec((None,) + tuple(shape[1:]), lambda b: (b, 0, 0))
    if kind == PAIR_BLOCK:
        return pl.BlockSpec((2, None) + tuple(shape[2:]), lambda b: (0, b, 0, 0))
    if kind == APART:
        return pl.BlockSpec(memory_space=pl.ANY)
    zero = (0,) * len(shape)
    return pl.BlockSpec(tuple(shape), lambda b: zero, pipeline_mode=pl.Buffered(1))


def out_spec(shape, kind, blocks):
    if not isinstance(kind, pl.BlockSpec) and kind == WHOLE:
        zero = (0,) * len(shape)
        return pl.BlockSpec(tuple(shape), lambda b: zero)
    return spec_of(shape, kind, blocks)


def placed(shape, dtype, kind, late=False):
    return pltpu.HBM(shape, dtype) if late else jax.ShapeDtypeStruct(shape, dtype)


def stage(kernel, blocks, ins, outs, scratch=(), flops=0):
    return call(kernel, blocks, ins, outs, scratch, flops, [], [], {})


def call(kernel, blocks, ins, outs, scratch, flops, more_specs, more_shapes, params):
    moved = sum(x.size * x.dtype.itemsize for x, _ in ins)
    moved += sum(int(np.prod(item[0])) * jnp.dtype(item[1]).itemsize for item in outs)
    made = [pltpu.VMEM(*item) if isinstance(item, tuple) else item for item in scratch]
    return pl.pallas_call(
        kernel,
        grid=(blocks,),
        in_specs=[spec_of(x.shape, kind, blocks) for x, kind in ins],
        out_specs=[out_spec(item[0], item[2], blocks) for item in outs] + more_specs,
        out_shape=[placed(*item) for item in outs] + more_shapes,
        scratch_shapes=made,
        compiler_params=pltpu.CompilerParams(
            dimension_semantics=("arbitrary",), vmem_limit_bytes=VMEM_BYTES, **params
        ),
        cost_estimate=pl.CostEstimate(flops=flops, bytes_accessed=moved, transcendentals=0),
    )(*[x for x, _ in ins])


def merge_rows(buf, peers, merge, mean_only):
    if not merge:
        total = buf[0]
        for k in range(1, peers):
            total = total + buf[k]
        return total
    counts = [buf[k, 0:1, :] for k in range(peers)]
    means = [buf[k, 1:2, :] for k in range(peers)]
    count, weighted = counts[0], counts[0] * means[0]
    for k in range(1, peers):
        count = count + counts[k]
        weighted = weighted + counts[k] * means[k]
    safe = jnp.maximum(count, 1.0)
    mean = weighted / safe
    squares = jnp.zeros_like(mean)
    for k in range(peers):
        squares = squares + buf[k, 2:3, :] + counts[k] * jnp.square(means[k] - mean)
    if mean_only:
        squares = squares / safe
    return jnp.concatenate([count, mean, squares], axis=0)


class Exchange:
    def __init__(self, rows_n, img_n, blocks):
        self.rows_n, self.img_n, self.blocks = rows_n, img_n, blocks
        self.calls = 0

    def __call__(
        self,
        kernel,
        ins,
        outs,
        merge,
        lines,
        widths,
        scratch=(),
        flops=0,
        edges=(),
        centres=None,
        edge=0,
        early=False,
        upto=None,
        defer=1,
        relay=None,
    ):
        ident, self.calls = self.calls, self.calls + 1
        total, dma = sum(widths), pltpu.SemaphoreType.DMA
        any_space = pl.BlockSpec(memory_space=pl.ANY)
        specs = [out_spec((lines, w), WHOLE, 1) for w in widths]
        shapes = [jax.ShapeDtypeStruct((lines, w), F32) for w in widths]
        extra = []
        upto = upto or self.blocks
        kept = upto < self.blocks
        if edges:
            middle = outs[edges[0][0]][0][-1]
            some = edge // self.blocks
            specs.append(any_space)
            shapes.append(jax.ShapeDtypeStruct((len(edges), upto * some, middle), BF16))
            extra += [
                ((len(edges), edge, middle), BF16),
                dma((len(edges), self.blocks)),
                dma((len(edges), self.blocks)),
                dma((len(edges),)),
            ]
        if centres:
            count, shape = len(centres[1]), outs[centres[0]][0]
            specs.append(any_space)
            shapes.append(jax.ShapeDtypeStruct((count,) + tuple(shape), F32))
            extra += [(tuple(shape), F32), dma((count,)), dma((count,)), dma((count,))]
        if kept:
            spec = pl.BlockSpec((len(edges), some, middle), lambda b: (0, jnp.maximum(b - upto, 0), 0))
            outs = outs + [((len(edges), edge - upto * some, middle), BF16, spec, True)]
        if relay:
            ins = ins + [(relay[0], APART)]
            specs.append(any_space)
            shapes.append(jax.ShapeDtypeStruct(relay[0].shape, BF16))
            extra += [dma((len(relay[1]),))] * 3
        extra += [
            ((self.rows_n, lines, total), F32),
            ((self.img_n, lines, total), F32),
            ((lines, total), F32),
            dma((self.rows_n,)),
            dma((self.rows_n,)),
            dma((self.img_n,)),
            dma((self.img_n,)),
        ]
        return call(
            functools.partial(
                self.kernel,
                kernel,
                len(ins),
                len(outs),
                len(scratch),
                merge,
                widths,
                edges,
                centres,
                early,
                upto,
                defer,
                relay[1] if relay else (),
            ),
            self.blocks,
            ins,
            outs,
            [((lines, total), F32)] + list(scratch) + extra,
            flops,
            specs,
            shapes,
            dict(collective_id=ident, has_side_effects=True),
        )

    def kernel(
        self,
        kernel,
        ins_n,
        outs_n,
        scratch_n,
        merge,
        widths,
        edges,
        centres,
        early,
        upto,
        defer,
        relay,
        *refs,
    ):
        kept = upto < self.blocks
        rows_n, img_n, blocks = self.rows_n, self.img_n, self.blocks
        refs = list(refs)

        def take(count):
            taken = refs[:count]
            del refs[:count]
            return taken

        ins, outs, totals = take(ins_n), take(outs_n), take(len(widths))
        halo = take(1)[0] if edges else None
        halo_centres = take(1)[0] if centres else None
        relayed = take(1)[0] if relay else None
        carried = ins.pop() if relay else None
        kept_rows = outs.pop() if kept else None
        mine = take(1)[0]
        scratch = take(scratch_n)
        if edges:
            edge_buf, edge_send, edge_recv, edge_local = take(4)
        if centres:
            centre_buf, centre_send, centre_recv, centre_local = take(4)
        if relay:
            relay_send, relay_recv, relay_local = take(3)
        buf_r, buf_i, part, send_r, recv_r, send_i, recv_i = refs
        block = pl.program_id(0)
        row, img = lax.axis_index("rows"), lax.axis_index("img")
        barrier = pltpu.get_barrier_semaphore()

        @pl.when(block == 0)
        def _():
            for k in range(1, rows_n):
                peer = {"rows": lax.rem(row + k, rows_n)}
                pl.semaphore_signal(barrier, inc=1, device_id=peer, device_id_type=MESH)
            for k in range(1, img_n):
                peer = {"img": lax.rem(img + k, img_n)}
                pl.semaphore_signal(barrier, inc=1, device_id=peer, device_id_type=MESH)

        def remote(source, target, send, recv, peer):
            return pltpu.make_async_remote_copy(
                src_ref=source,
                dst_ref=target,
                send_sem=send,
                recv_sem=recv,
                device_id=peer,
                device_id_type=MESH,
            )

        def sends(direction):
            return row < rows_n - 1 if direction > 0 else row > 0

        def receives(direction):
            return row > 0 if direction > 0 else row < rows_n - 1

        def edge_copy(e, b):
            some = edge_buf.shape[1] // blocks
            here = pl.ds(pl.multiple_of(b * some, some), some)
            return remote(
                edge_buf.at[e, here],
                halo.at[e, here],
                edge_send.at[e, b],
                edge_recv.at[e, b],
                {"rows": row + edges[e][3]},
            )

        def keep_edges():
            some = edge_buf.shape[1] // blocks
            here = pl.ds(pl.multiple_of(block * some, some), some)
            for e, (out, plane, last_row, _) in enumerate(edges):
                source = outs[out] if plane is None else outs[out].at[plane]
                for lanes in lane_blocks(source.shape[1]):
                    value = load(source, slice(None), lanes)
                    lines = value.reshape((some // 8, -1) + value.shape[1:])
                    store(edge_buf.at[e], here, lanes, lines[:, -1 if last_row else 0])
                if kept:
                    kept_rows[e] = edge_buf[e, here]

        def send_edges(b):
            for e, spec in enumerate(edges):

                @pl.when(sends(spec[3]))
                def _(e=e):
                    edge_copy(e, b).start()

        def relay_copy(k):
            peer = {"rows": row + relay[k]}
            return remote(carried.at[k], relayed.at[k], relay_send.at[k], relay_recv.at[k], peer)

        def relay_own(k):
            return pltpu.make_async_copy(carried.at[k], relayed.at[k], relay_local.at[k])

        def greet():
            @pl.when(block == 0)
            def _():
                pl.semaphore_wait(barrier, rows_n + img_n - 2)
                for k, direction in enumerate(relay):

                    @pl.when(sends(direction))
                    def _(k=k):
                        relay_copy(k).start()

                    @pl.when(jnp.logical_not(receives(direction)))
                    def _(k=k):
                        relay_own(k).start()

        def flush():
            greet()
            keep_edges()
            send_edges(block)

        if early:
            kernel(*ins, *outs, mine, *scratch, flush)
        else:
            kernel(*ins, *outs, mine, *scratch)
            greet()
            if edges:
                keep_edges()

                @pl.when(block < jnp.minimum(blocks - defer, upto))
                def _():
                    send_edges(block)

        if centres:
            centre_buf[pl.ds(block, 1)] = outs[centres[0]][...][None]

        def exchange(axis, me, peers, source, buf, send, recv, then=None):
            copies = []
            for k in range(1, peers):
                peer = {axis: lax.rem(me + k, peers)}
                copies.append(remote(source, buf.at[me], send.at[k], recv.at[me], peer))
                copies[-1].start()
            if then is not None:
                then()
            buf[pl.ds(me, 1)] = source[...][None]
            for k in range(1, peers):
                peer = lax.rem(me + k, peers)
                remote(source, buf.at[peer], send.at[k], recv.at[peer], {axis: peer}).wait_recv()
            return copies

        @pl.when(block == blocks - 1)
        def _():
            def centre_copy(k):
                peer = {"rows": row + centres[1][k]}
                return remote(
                    centre_buf, halo_centres.at[k], centre_send.at[k], centre_recv.at[k], peer
                )

            directions = centres[1] if centres else ()

            def rest():
                for k, direction in enumerate(directions):

                    @pl.when(sends(direction))
                    def _(k=k):
                        centre_copy(k).start()

                if edges and not early:
                    for b in range(blocks - defer, upto):
                        send_edges(b)

            copies = exchange("rows", row, rows_n, mine, buf_r, send_r, recv_r, rest)
            part[...] = merge_rows(buf_r, rows_n, merge, False)
            copies += exchange("img", img, img_n, part, buf_i, send_i, recv_i)
            total = merge_rows(buf_i, img_n, merge, True)
            start = 0
            for out, width in zip(totals, widths):
                out[...] = total[:, start : start + width]
                start += width
            for k, direction in enumerate(directions):
                own = pltpu.make_async_copy(centre_buf, halo_centres.at[k], centre_local.at[k])

                @pl.when(receives(direction))
                def _(k=k):
                    centre_copy(k).wait_recv()

                @pl.when(jnp.logical_not(receives(direction)))
                def _(own=own):
                    own.start()
                    own.wait()

                @pl.when(sends(direction))
                def _(k=k):
                    centre_copy(k).wait_send()

            for k, direction in enumerate(relay):

                @pl.when(receives(direction))
                def _(k=k):
                    relay_copy(k).wait_recv()

                @pl.when(jnp.logical_not(receives(direction)))
                def _(k=k):
                    relay_own(k).wait()

                @pl.when(sends(direction))
                def _(k=k):
                    relay_copy(k).wait_send()

            for e, spec in enumerate(edges):
                mine_kept = edge_buf.at[e, : halo.shape[1]]
                own = pltpu.make_async_copy(mine_kept, halo.at[e], edge_local.at[e])

                @pl.when(receives(spec[3]))
                def _(e=e):
                    for b in range(upto):
                        edge_copy(e, b).wait_recv()

                @pl.when(jnp.logical_not(receives(spec[3])))
                def _(own=own):
                    own.start()
                    own.wait()

                @pl.when(sends(spec[3]))
                def _(e=e):
                    for b in range(upto):
                        edge_copy(e, b).wait_send()

            for copy in copies:
                copy.wait_send()


CHUNK_ROWS = 64
CHUNK_LANES = 1024


HID_MID2, GA_OUT2, HID_IN2, VIEWS2, FIRST, GA_IN2, HID_MID1, GA_OUT1, GA_SKIP, VIEWS1 = range(10)
HID, PLANE, GA_IN1 = 10, 14, 18
ONE, TWO, HALF, QUAD, DEEP = range(5)
WIDTHS = {ONE: (512, 1024), TWO: (1024, 512), HALF: (512, 512), QUAD: (1024, 256), DEEP: (1024, 512)}


def plan_jobs():
    chunks = [[(ONE, 0, HID_MID2, 0, GA_OUT2, 1024 * k)] for k in range(2)]
    chunks += [[(ONE, 0, HID_IN2, 0, VIEWS2, 1024 * k)] for k in range(4)]
    chunks += [[(HALF, 0, HID_IN2, 0, VIEWS2, 4096), (HALF, 1, HID, 0, VIEWS1, 512)]]
    chunks += [[(QUAD, h, FIRST, 1024 * h, GA_IN2, 256 * k) for h in range(2)] for k in range(2)]
    chunks += [[(DEEP, p, PLANE + p, 0, GA_IN1 + p, 0) for p in range(4)]]
    chunks += [[(ONE, 0, HID_MID1, 0, GA_OUT1, 1024 * k)] for k in range(2)]
    chunks += [[(TWO, 0, PLANE, 0, GA_SKIP, 512 * k)] for k in range(4)]
    chunks += [[(ONE, 0, HID + 1, 0, VIEWS1, 512)], [(ONE, 0, HID + 2, 0, VIEWS1, 0)]]
    chunks += [[(ONE, 0, HID + 3, 0, VIEWS1, 1024 * k)] for k in range(2)]
    return chunks


def weights_kernel(
    rows_n,
    hid_mid2,
    ga_out2,
    hid_in2,
    views2,
    first_low,
    ga_in2,
    hid_mid1,
    ga_out1,
    planes,
    ga_skip,
    hid_in1,
    views1,
    ga_in1,
    done,
    lhs_buf,
    rhs_buf,
    deep,
    chunk_buf,
    own,
    got1,
    got2a,
    got2b,
    got3a,
    got3b,
    got_low,
    got_high,
    lhs_sem,
    rhs_sem,
    *sems,
):
    (s1, r1, s2a, r2a, s2b, r2b, s3a, r3a, s3b, r3b, s_up, r_low, s_down, r_high, b_up, b_down, r_back) = sems
    sources = [hid_mid2, ga_out2, hid_in2, views2, first_low, ga_in2, hid_mid1, ga_out1, ga_skip, views1]
    for stack in (hid_in1, planes, ga_in1):
        sources += [stack.at[p] for p in range(4)]
    chunks = plan_jobs()
    jobs = [job for chunk in chunks for job in chunk]
    count = len(chunks)
    depth = chunk_buf.shape[0]
    img, z = lax.axis_index("img"), lax.axis_index("rows")
    y, x, c = img // 4, lax.rem(img // 2, 2), lax.rem(img, 2)
    root = rows_n // 2
    sibling = {"img": img + 1 - 2 * c}
    beside_x = {"img": img + 2 - 4 * x}
    beside_y = {"img": img + 4 - 8 * y}
    higher, lower = {"rows": z + 1}, {"rows": z - 1}
    half = CHUNK_LANES // 2
    left, right = slice(0, half), slice(half, 2 * half)

    def fetch(index):
        kind, _, lhs, lhs_start, rhs, rhs_start = jobs[index]
        lhs_width, rhs_width = WIDTHS[kind]
        slot = index % 2
        return (
            pltpu.make_async_copy(
                sources[lhs].at[:, lhs_start : lhs_start + lhs_width],
                lhs_buf.at[slot, :, :lhs_width],
                lhs_sem.at[slot],
            ),
            pltpu.make_async_copy(
                sources[rhs].at[:, rhs_start : rhs_start + rhs_width],
                rhs_buf.at[slot, :, :rhs_width],
                rhs_sem.at[slot],
            ),
        )

    for copy in fetch(0):
        copy.start()

    barrier = pltpu.get_barrier_semaphore()
    for peer in (sibling, beside_x, beside_y):
        pl.semaphore_signal(barrier, inc=1, device_id=peer, device_id_type=MESH)

    @pl.when(z > 0)
    def _():
        pl.semaphore_signal(barrier, inc=1, device_id=lower, device_id_type=MESH)

    @pl.when(z < rows_n - 1)
    def _():
        pl.semaphore_signal(barrier, inc=1, device_id=higher, device_id_type=MESH)

    pl.semaphore_wait(barrier, 3 + jnp.minimum(z, 1) + jnp.minimum(rows_n - 1 - z, 1))

    def put(slot, result, first, parts):
        width = CHUNK_LANES // parts
        rows = CHUNK_ROWS
        for m in range(result.shape[0] // (rows * parts)):
            shard = first + m
            for h in range(parts):
                piece = result[(m * parts + h) * rows : (m * parts + h + 1) * rows]
                chunk_buf[slot, shard // 4, shard // 2 % 2, shard % 2, :, h * width : (h + 1) * width] = piece

    def multiply(index, slot):
        kind, part = jobs[index][:2]
        lhs_width, rhs_width = WIDTHS[kind]
        here = index % 2

        def product():
            return lax.dot_general(
                lhs_buf[here, :, :lhs_width],
                rhs_buf[here, :, :rhs_width],
                (((0,), (0,)), ((), ())),
                preferred_element_type=F32,
            )

        if kind == ONE:
            put(slot, product().astype(BF16), 0, 1)
        elif kind == TWO:
            put(slot, product().astype(BF16), 0, 2)
        elif kind == QUAD:
            put(slot, product().astype(BF16), 4 * part, 4)
        elif kind == HALF:
            result = product().astype(BF16)
            for m in range(8):
                piece = result[m * CHUNK_ROWS : (m + 1) * CHUNK_ROWS]
                chunk_buf[slot, m // 4, m // 2 % 2, m % 2, :, (left, right)[part]] = piece
        elif part == 0:
            deep[...] = product()
        elif part == 3:
            put(slot, (deep[...] + product()).astype(BF16), 0, 2)
        else:
            deep[...] += product()

    def remote(source, target, send, recv, peer):
        return pltpu.make_async_remote_copy(
            src_ref=source,
            dst_ref=target,
            send_sem=send,
            recv_sem=recv,
            device_id=peer,
            device_id_type=MESH,
        )

    def to_core(t):
        source = chunk_buf.at[lax.rem(t, depth), :, :, 1 - c]
        return remote(source, got1.at[t], s1.at[t], r1.at[t], sibling)

    def to_2a(t):
        return remote(own.at[t, :, 1 - x, :, left], got2a.at[t], s2a.at[t], r2a.at[t], beside_x)

    def to_2b(t):
        return remote(own.at[t, 1 - y, :, :, right], got2b.at[t], s2b.at[t], r2b.at[t], beside_y)

    def to_3a(t):
        return remote(own.at[t, 1 - y, x, :, left], got3a.at[t], s3a.at[t], r3a.at[t], beside_y)

    def to_3b(t):
        return remote(own.at[t, y, 1 - x, :, right], got3b.at[t], s3b.at[t], r3b.at[t], beside_x)

    def up(t):
        return remote(own.at[t, y, x], got_low.at[t], s_up.at[t], r_low.at[t], higher)

    def down(t):
        return remote(own.at[t, y, x], got_high.at[t], s_down.at[t], r_high.at[t], lower)

    def back_up(t):
        return remote(done.at[t], done.at[t], b_up.at[t], r_back.at[t], higher)

    def back_down(t):
        return remote(done.at[t], done.at[t], b_down.at[t], r_back.at[t], lower)

    def compute(t):
        @pl.when(t >= depth)
        def _():
            to_core(t - depth).wait_send()

        slot = lax.rem(t, depth)
        index = 0
        for k, chunk in enumerate(chunks):
            first = index
            index += len(chunk)

            @pl.when(t == k)
            def _(first=first, chunk=chunk):
                for n in range(first, first + len(chunk)):
                    for copy in fetch(n):
                        copy.wait()
                    if n + 1 < len(jobs):
                        for copy in fetch(n + 1):
                            copy.start()
                    multiply(n, slot)

        to_core(t).start()

    def stage1(t):
        to_core(t).wait_recv()
        slot = lax.rem(t, depth)
        for a in range(2):
            for b in range(2):
                own[t, a, b] = chunk_buf[slot, a, b, c] + got1[t, a, b]
        to_2a(t).start()
        to_2b(t).start()

    def stage2(t):
        to_2a(t).wait_recv()
        for a in range(2):
            own[t, a, x, :, left] = own[t, a, x, :, left] + got2a[t, a]
        to_3a(t).start()
        to_2b(t).wait_recv()
        for a in range(2):
            own[t, y, a, :, right] = own[t, y, a, :, right] + got2b[t, a]
        to_3b(t).start()

    def stage3(t):
        to_3a(t).wait_recv()
        own[t, y, x, :, left] = own[t, y, x, :, left] + got3a[t]
        to_3b(t).wait_recv()
        own[t, y, x, :, right] = own[t, y, x, :, right] + got3b[t]

        @pl.when(z == 0)
        def _():
            up(t).start()

        @pl.when(z == rows_n - 1)
        def _():
            down(t).start()

    def stage4(t):
        @pl.when((z > 0) & (z < root))
        def _():
            up(t).wait_recv()
            own[t, y, x] = own[t, y, x] + got_low[t]
            up(t).start()

        @pl.when((z < rows_n - 1) & (z > root))
        def _():
            down(t).wait_recv()
            own[t, y, x] = own[t, y, x] + got_high[t]
            down(t).start()

    def stage5(t):
        @pl.when(z == root)
        def _():
            up(t).wait_recv()
            down(t).wait_recv()
            total = own[t, y, x].astype(F32) + got_low[t].astype(F32) + got_high[t].astype(F32)
            done[t] = total.astype(BF16)
            back_up(t).start()
            back_down(t).start()

    def stage6(t):
        @pl.when(z > root)
        def _():
            back_up(t).wait_recv()

            @pl.when(z < rows_n - 1)
            def _():
                back_up(t).start()

        @pl.when((z < root) & (z > 0))
        def _():
            back_down(t).wait_recv()
            back_down(t).start()

    def stage7(t):
        @pl.when(z == 0)
        def _():
            back_down(t).wait_recv()

    stages = (compute, stage1, stage2, stage3, stage4, stage5, stage6, stage7)

    def step(s, carry):
        for lag, work in enumerate(stages):
            t = s - lag

            @pl.when((t >= 0) & (t < count))
            def _(t=t, work=work):
                work(t)

        return carry

    lax.fori_loop(0, count + len(stages) - 1, step, 0)

    def finish(t, carry):
        @pl.when(t >= count - depth)
        def _():
            to_core(t).wait_send()

        for copy in (to_2a(t), to_2b(t), to_3a(t), to_3b(t)):
            copy.wait_send()

        @pl.when(z < root)
        def _():
            up(t).wait_send()

        @pl.when(z > root)
        def _():
            down(t).wait_send()

        @pl.when((z >= root) & (z < rows_n - 1))
        def _():
            back_up(t).wait_send()

        @pl.when((z <= root) & (z > 0))
        def _():
            back_down(t).wait_send()

        return carry

    lax.fori_loop(0, count, finish, 0)


def summed_weights(rows_n, ident, operands):
    count = len(plan_jobs())
    low = operands[0].shape[0]
    rows, lanes = CHUNK_ROWS, CHUNK_LANES
    dma = pltpu.SemaphoreType.DMA
    depth = 3
    buffers = [
        (2, low, 1024),
        (2, low, 1024),
        None,
        (depth, 2, 2, 2, rows, lanes),
        (count, 2, 2, rows, lanes),
        (count, 2, 2, rows, lanes),
        (count, 2, rows, lanes // 2),
        (count, 2, rows, lanes // 2),
        (count, rows, lanes // 2),
        (count, rows, lanes // 2),
        (count, rows, lanes),
        (count, rows, lanes),
    ]
    scratch = [pltpu.VMEM(b, BF16) if b else pltpu.VMEM((1024, 512), F32) for b in buffers]
    return pl.pallas_call(
        functools.partial(weights_kernel, rows_n),
        in_specs=[pl.BlockSpec(memory_space=pl.ANY)] * len(operands),
        out_specs=pl.BlockSpec(memory_space=pltpu.VMEM),
        out_shape=jax.ShapeDtypeStruct((count, rows, lanes), BF16),
        scratch_shapes=scratch + [dma((2,)), dma((2,))] + [dma((count,))] * 17,
        compiler_params=pltpu.CompilerParams(
            collective_id=ident, has_side_effects=True, vmem_limit_bytes=63 * 1024 * 1024
        ),
        cost_estimate=pl.CostEstimate(
            flops=40_000_000_000, bytes_accessed=100_000_000, transcendentals=0
        ),
    )(*operands)


def unpack_kernel(sums_n, done, *refs):
    sums, outs = refs[:sums_n], refs[sums_n:]
    in1, mid1, out1, skip, in2, mid2, out2 = outs[:7]
    rows, lanes = CHUNK_ROWS, CHUNK_LANES
    half = lanes // 2

    def wide(k):
        return done[k].astype(F32)

    def stacked(first, count, parts, out):
        width = lanes // parts
        for k in range(count):
            for h in range(parts):
                piece = done[first + k, :, h * width : (h + 1) * width]
                out[h * rows : (h + 1) * rows, k * width : (k + 1) * width] = piece.astype(F32)

    for k in range(2):
        out2[:, k * lanes : (k + 1) * lanes] = wide(k)
        out1[:, k * lanes : (k + 1) * lanes] = wide(10 + k)
    taps2 = [(2 + k // 2, k % 2) for k in range(8)] + [(6, 0)]
    taps1 = [(19, 1), (17, 0), (18, 0), (16, 1), (6, 1), (16, 0), (19, 0), (17, 1), (18, 1)]
    for out, taps in ((mid1, taps1), (mid2, taps2)):
        for k, (chunk, side) in enumerate(taps):
            out[k] = done[chunk, :, side * half : (side + 1) * half].astype(F32)
    stacked(7, 2, 4, in2)
    stacked(9, 1, 2, in1)
    stacked(12, 4, 2, skip)
    rest = list(outs[7:])
    for ref in sums:
        for k in range(ref.shape[0]):
            rest.pop(0)[...] = ref[k : k + 1, :]


def unpack(done, sums):
    rows = CHUNK_ROWS
    shapes = [(128, 512), (9, rows, 512), (rows, 2048), (128, 2048), (256, 512), (9, rows, 512), (rows, 2048)]
    shapes += [(1, x.shape[1]) for x in sums for _ in range(x.shape[0])]
    vmem = pl.BlockSpec(memory_space=pltpu.VMEM)
    outs = pl.pallas_call(
        functools.partial(unpack_kernel, len(sums)),
        in_specs=[vmem] * (1 + len(sums)),
        out_specs=[vmem] * len(shapes),
        out_shape=[jax.ShapeDtypeStruct(shape, F32) for shape in shapes],
        compiler_params=pltpu.CompilerParams(vmem_limit_bytes=32 * 1024 * 1024),
    )(done, *sums)
    return outs[:7], [x.reshape(-1) for x in outs[7:]]


def masks_kernel(rows_low, extent, mask_in, mask_out, mask_above, mask_edges):
    side = extent[...]
    side_low = side // 2
    low0 = lax.axis_index("rows") * rows_low
    column = lax.broadcasted_iota(jnp.int32, side.shape, 1)

    def inside(row, col, limit):
        kept = (row >= 0) & (row < limit) & (col < limit)
        return jnp.where(kept, 1.0, 0.0)

    for i in range(rows_low):
        for p in range(2):
            for q in range(2):
                mask_in[2 * p + q, :, i] = inside(2 * (low0 + i) + p, 2 * column + q, side)
        mask_out[:, i] = inside(low0 + i, column, side_low)
    for q in range(2):
        mask_above[q, :, 0] = inside(2 * low0 - 1, 2 * column + q, side)
    mask_edges[0, :, 0] = inside(low0 - 1, column, side_low)
    mask_edges[1, :, 0] = inside(low0 + rows_low, column, side_low)


def masks_of(extent, rows_low):
    images, columns, lanes = extent.shape
    vmem = pl.BlockSpec(memory_space=pltpu.VMEM)
    shapes = [
        (4, images, rows_low, columns, lanes),
        (images, rows_low, columns, lanes),
        (2, images, 1, columns, lanes),
        (2, images, 1, columns, lanes),
    ]
    return pl.pallas_call(
        functools.partial(masks_kernel, rows_low),
        in_specs=[vmem],
        out_specs=[vmem] * 4,
        out_shape=[jax.ShapeDtypeStruct(shape, F32) for shape in shapes],
        compiler_params=pltpu.CompilerParams(vmem_limit_bytes=24 * 1024 * 1024),
    )(extent)


def body(
    image_in,
    extent,
    weight_in1,
    weight_mid1,
    weight_out1,
    weight_skip,
    weight_in2,
    weight_mid2,
    weight_out2,
    gain_in1,
    shift_in1,
    gain_mid1,
    shift_mid1,
    gain_out1,
    shift_out1,
    gain_skip,
    shift_skip,
    gain_in2,
    shift_in2,
    gain_mid2,
    shift_mid2,
    gain_out2,
    shift_out2,
    cotangent,
):
    images, rows_here, columns, inputs = image_in.shape
    middle, outputs = weight_out1.shape
    rows_low, cols_low = rows_here // 2, columns // 2
    low = images * rows_low * cols_low
    rows_n, img_n = lax.axis_size("rows"), lax.axis_size("img")
    blocks = images // IMAGES
    per_block = low // blocks
    edge = images * cols_low
    run = Exchange(rows_n, img_n, blocks)
    upto = 3 * blocks // 5

    def early_blocks(x):
        shape = (x.shape[0], edge // blocks, x.shape[2])
        return x, pl.BlockSpec(shape, lambda b: (0, jnp.minimum(b, upto - 1), 0))

    def late_blocks(x):
        shape = (x.shape[0], edge // blocks, x.shape[2])
        return x, pl.BlockSpec(shape, lambda b: (0, jnp.maximum(b - upto, 0), 0))


    columns8 = jnp.broadcast_to(extent[:, None, None], (images, cols_low, 128))
    mask_in, mask_out, mask_above, mask_edges = (
        m.reshape(m.shape[:-4] + (-1, 128)) for m in masks_of(columns8, rows_low)
    )

    group_images = 256 // (rows_here * columns)
    order = np.arange(256).reshape(group_images, rows_low, 2, cols_low, 2)
    order = order.transpose(2, 4, 0, 1, 3).reshape(-1)
    perm = jnp.asarray(np.eye(256, dtype=np.float32)[order], BF16)

    def row(vector):
        return vector.reshape(1, -1)

    g_in1, s_in1, g_mid1, s_mid1 = row(gain_in1), row(shift_in1), row(gain_mid1), row(shift_mid1)
    g_out1, s_out1, g_skip, s_skip = row(gain_out1), row(shift_out1), row(gain_skip), row(shift_skip)
    g_in2, s_in2, g_mid2, s_mid2 = row(gain_in2), row(shift_in2), row(gain_mid2), row(shift_mid2)
    g_out2, s_out2 = row(gain_out2), row(shift_out2)
    kernel_mid1 = weight_mid1.transpose(1, 2, 0, 3).reshape(9 * middle, middle)
    kernel_mid2 = weight_mid2.transpose(1, 2, 0, 3).reshape(9 * middle, middle)
    cot = cotangent.reshape(low, outputs)

    dev_mid_out = [((low, middle), BF16, BY_ROWS), ((blocks, 1, middle), F32, BY_BLOCK)]
    dev_out_out = [((low, outputs), BF16, BY_ROWS), ((blocks, 1, outputs), F32, BY_BLOCK)]
    hidden_out = [((low, middle), BF16, BY_ROWS)]
    wide_out = [((low, outputs), BF16, BY_ROWS)]
    late_mid, late_wide = [hidden_out[0] + (True,)], [wide_out[0] + (True,)]
    acc_mid, acc_out = ((per_block, middle), F32), ((per_block, outputs), F32)
    unit_flops = 2 * low * middle * middle

    def normal(dev, centre, stats, gain, shift, kind=BY_ROWS):
        return [(dev, kind), (centre, BY_BLOCK), (stats, WHOLE), (gain, WHOLE), (shift, WHOLE)]

    planes, d_in1, c_in1, d_skip, c_skip, n_in1, n_skip, halo_in1, halo_c_in1 = run(
        open_kernel,
        [
            (image_in.reshape(4 * low, inputs), BY_ROWS),
            (perm, WHOLE),
            (mask_in, BY_PLANES),
            (mask_out, BY_ROWS),
            (weight_in1, WHOLE),
            (weight_skip, WHOLE),
        ],
        [
            ((4, low, inputs), BF16, BY_PLANES, True),
            ((4, low, middle), BF16, BY_PLANES),
            ((blocks, 1, middle), F32, BY_BLOCK),
        ]
        + dev_out_out,
        True,
        3,
        (middle, outputs),
        scratch=[((4, per_block, middle), F32), acc_out],
        flops=20 * unit_flops,
        edges=[(1, 2, True, 1), (1, 3, True, 1)],
        centres=(2, (1,)),
        edge=edge,
        early=True,
    )
    hid_in1, d_mid1, c_mid1, edges_mid1, n_mid1, halo_mid1, halo_c_mid1 = run(
        functools.partial(mid1_kernel, rows_low),
        [
            (d_in1, BY_PLANES),
            (c_in1, BY_BLOCK),
            (mask_in, BY_PLANES),
            (halo_in1, BY_PLANES),
            (halo_c_in1[0], BY_BLOCK),
            (mask_above, BY_PLANES),
            (n_in1, WHOLE),
            (g_in1, WHOLE),
            (s_in1, WHOLE),
            (mask_out, BY_ROWS),
            (kernel_mid1, WHOLE),
        ],
        [((4, low, middle), BF16, BY_PLANES, True)] + dev_mid_out,
        True,
        3,
        (middle,),
        scratch=[((5, per_block, middle), BF16), acc_mid],
        flops=9 * unit_flops,
        edges=[(1, None, False, -1)],
        upto=upto,
        centres=(2, (-1,)),
        edge=edge,
    )
    hid_mid1, d_out1, c_out1, n_out1, rest_mid1 = run(
        expand_kernel,
        normal(d_mid1, c_mid1, n_mid1, g_mid1, s_mid1) + [(mask_out, BY_ROWS), (weight_out1, WHOLE)],
        late_mid + dev_out_out,
        True,
        3,
        (outputs,),
        scratch=[acc_out],
        relay=(edges_mid1, (-1,)),
        flops=4 * unit_flops,
    )
    join = normal(d_out1, c_out1, n_out1, g_out1, s_out1) + normal(d_skip, c_skip, n_skip, g_skip, s_skip)
    both = [(1, None, True, 1), (1, None, False, -1)]
    first_low, d_in2, c_in2, n_in2, halo_in2, halo_c_in2 = run(
        join_kernel,
        join + [(mask_out, BY_ROWS), (weight_in2, WHOLE)],
        wide_out + dev_mid_out,
        True,
        3,
        (middle,),
        scratch=[acc_mid],
        flops=4 * unit_flops,
        defer=2,
        edges=both,
        centres=(2, (1, -1)),
        edge=edge,
    )

    hid_in2, d_mid2, c_mid2, edges_mid2, n_mid2, halo_mid2, halo_c_mid2 = run(
        functools.partial(mid2_kernel, rows_low),
        [
            (d_in2, BY_ROWS),
            (c_in2, BY_BLOCK),
            (halo_in2, BY_PLANES),
            (halo_c_in2, PAIR_BLOCK),
            (mask_edges, BY_PLANES),
            (n_in2, WHOLE),
            (g_in2, WHOLE),
            (s_in2, WHOLE),
            (mask_out, BY_ROWS),
            (kernel_mid2, WHOLE),
        ],
        late_mid + dev_mid_out,
        True,
        3,
        (middle,),
        scratch=[((per_block, 9 * middle), BF16), acc_mid],
        flops=9 * unit_flops,
        edges=both,
        upto=upto,
        centres=(2, (1, -1)),
        edge=edge,
    )
    hid_mid2, d_out2, c_out2, n_out2, rest_mid2 = run(
        expand_kernel,
        normal(d_mid2, c_mid2, n_mid2, g_mid2, s_mid2) + [(mask_out, BY_ROWS), (weight_out2, WHOLE)],
        late_mid + dev_out_out,
        True,
        3,
        (outputs,),
        scratch=[acc_out],
        relay=(edges_mid2, (1, -1)),
        flops=4 * unit_flops,
    )
    block_out, gn_out2, z_out2 = run(
        final_kernel,
        normal(d_out2, c_out2, n_out2, g_out2, s_out2)
        + [(first_low, BY_ROWS), (cot, BY_ROWS), (mask_out, BY_ROWS)],
        late_wide + wide_out,
        False,
        2,
        (outputs,),
    )

    ga_out2, gn_mid2, z_mid2, halo_gn_mid2 = run(
        back_expand_kernel,
        [
            (gn_out2, BY_ROWS),
            (d_out2, BY_ROWS),
            (c_out2, BY_BLOCK),
            (n_out2, WHOLE),
            (g_out2, WHOLE),
            (z_out2, WHOLE),
            (mask_out, BY_ROWS),
            (weight_out2, WHOLE),
        ]
        + normal(d_mid2, c_mid2, n_mid2, g_mid2, s_mid2),
        late_wide + hidden_out,
        False,
        2,
        (middle,),
        scratch=[acc_mid],
        flops=4 * unit_flops,
        defer=2,
        edges=both,
        edge=edge,
    )
    views2, gn_in2, z_in2 = run(
        functools.partial(back_mid2_kernel, rows_low, upto),
        [
            (gn_mid2, BY_ROWS),
            (d_mid2, BY_ROWS),
            (c_mid2, BY_BLOCK),
            (halo_gn_mid2, BY_PLANES),
            early_blocks(halo_mid2),
            late_blocks(rest_mid2),
            (halo_c_mid2, PAIR_BLOCK),
            (mask_edges, BY_PLANES),
            (n_mid2, WHOLE),
            (g_mid2, WHOLE),
            (z_mid2, WHOLE),
            (mask_out, BY_ROWS),
            (kernel_mid2, WHOLE),
        ]
        + normal(d_in2, c_in2, n_in2, g_in2, s_in2),
        [((low, 9 * middle), BF16, BY_ROWS, True)] + hidden_out,
        False,
        2,
        (middle,),
        scratch=[acc_mid],
        flops=9 * unit_flops,
    )
    ga_in2, gs1, z_sum1 = run(
        back_join_kernel,
        [
            (gn_in2, BY_ROWS),
            (d_in2, BY_ROWS),
            (c_in2, BY_BLOCK),
            (n_in2, WHOLE),
            (g_in2, WHOLE),
            (z_in2, WHOLE),
            (mask_out, BY_ROWS),
            (weight_in2, WHOLE),
            (gn_out2, BY_ROWS),
        ]
        + join,
        late_mid + wide_out,
        False,
        3,
        (outputs,),
        scratch=[acc_out],
        flops=4 * unit_flops,
    )

    ga_out1, ga_skip, gn_mid1, grad_skip_in, z_mid1, halo_gn_mid1 = run(
        back_split_kernel,
        [
            (gs1, BY_ROWS),
            (d_out1, BY_ROWS),
            (c_out1, BY_BLOCK),
            (n_out1, WHOLE),
            (g_out1, WHOLE),
            (d_skip, BY_ROWS),
            (c_skip, BY_BLOCK),
            (n_skip, WHOLE),
            (g_skip, WHOLE),
            (z_sum1, WHOLE),
            (mask_out, BY_ROWS),
            (weight_out1, WHOLE),
            (weight_skip, WHOLE),
        ]
        + normal(d_mid1, c_mid1, n_mid1, g_mid1, s_mid1),
        late_wide + late_wide + hidden_out + [((low, inputs), BF16, BY_ROWS, True)],
        False,
        2,
        (middle,),
        scratch=[acc_mid, ((per_block, inputs), F32)],
        flops=12 * unit_flops,
        edges=[(2, None, False, -1)],
        edge=edge,
    )
    views1, gn_in1, z_in1 = run(
        functools.partial(back_mid1_kernel, rows_low, upto),
        [
            (gn_mid1, BY_ROWS),
            (d_mid1, BY_ROWS),
            (c_mid1, BY_BLOCK),
            (halo_gn_mid1[0], BY_ROWS),
            early_blocks(halo_mid1),
            late_blocks(rest_mid1),
            (halo_c_mid1[0], BY_BLOCK),
            (mask_edges[1], BY_ROWS),
            (n_mid1, WHOLE),
            (g_mid1, WHOLE),
            (z_mid1, WHOLE),
            (mask_out, BY_ROWS),
            (kernel_mid1, WHOLE),
            (d_in1, BY_PLANES),
            (c_in1, BY_BLOCK),
            (mask_in, BY_PLANES),
            (n_in1, WHOLE),
            (g_in1, WHOLE),
            (s_in1, WHOLE),
        ],
        [((low, 4 * middle), BF16, BY_ROWS, True), ((4, low, middle), BF16, BY_PLANES)],
        False,
        2,
        (middle,),
        scratch=[((4, per_block, middle), F32)],
        flops=9 * unit_flops,
    )
    ga_in1, grad_image, block_out = stage(
        back_image_kernel,
        blocks,
        [
            (gn_in1, BY_PLANES),
            (d_in1, BY_PLANES),
            (c_in1, BY_BLOCK),
            (n_in1, WHOLE),
            (g_in1, WHOLE),
            (z_in1, WHOLE),
            (mask_in, BY_PLANES),
            (weight_in1, WHOLE),
            (grad_skip_in, BY_ROWS),
            (perm, WHOLE),
            (block_out, BY_ROWS),
        ],
        [((4, low, middle), BF16, BY_PLANES, True), ((4 * low, inputs), BF16, BY_ROWS)] + wide_out,
        scratch=[((4, per_block, inputs), BF16)],
        flops=12 * unit_flops,
    )
    sums = [z_in1, z_mid1, z_sum1, z_in2, z_mid2, z_out2]

    if (rows_n, img_n) == (4, 8):
        done = summed_weights(
            rows_n,
            run.calls,
            [
                hid_mid2,
                ga_out2,
                hid_in2,
                views2,
                first_low,
                ga_in2,
                hid_mid1,
                ga_out1,
                planes,
                ga_skip,
                hid_in1,
                views1,
                ga_in1,
            ],
        )
        grads, rows_of = unpack(done, sums)
        dw_in1, dw_mid1, dw_out1, dw_skip, dw_in2, dw_mid2, dw_out2 = grads
        dw_mid1, dw_mid2 = (
            g.reshape(3, 3, -1, middle).transpose(2, 0, 1, 3) for g in (dw_mid1, dw_mid2)
        )
    else:
        def weight_term(values, upstream):
            return lax.dot_general(
                values, upstream, (((0,), (0,)), ((), ())), preferred_element_type=F32
            ).astype(BF16)

        def reduced(grad):
            shard = lax.psum_scatter(grad, "img", scatter_dimension=0, tiled=True)
            return lax.psum(shard, "rows").astype(F32)

        dw_out2 = reduced(weight_term(hid_mid2, ga_out2))
        dw_mid2 = reduced(weight_term(hid_in2, views2))
        dw_in2 = reduced(weight_term(first_low, ga_in2))
        dw_out1 = reduced(weight_term(hid_mid1, ga_out1))
        dw_skip = reduced(weight_term(planes[0], ga_skip))
        m = middle
        dw_00 = weight_term(hid_in1[0], views1[:, m : 2 * m])
        dw_01 = weight_term(hid_in1[1], views1[:, m : 3 * m])
        dw_10 = weight_term(hid_in1[2], views1[:, : 2 * m])
        dw_11 = weight_term(hid_in1[3], views1)
        dw_mid1 = jnp.concatenate(
            [
                dw_11[:, 3 * m :],
                dw_10[:, :m],
                dw_11[:, :m],
                dw_01[:, m:],
                dw_00,
                dw_01[:, :m],
                dw_11[:, 2 * m : 3 * m],
                dw_10[:, m:],
                dw_11[:, m : 2 * m],
            ],
            axis=1,
        )
        dw_mid1 = reduced(dw_mid1)
        dw_in1 = reduced(
            weight_term(planes.reshape(4 * low, inputs), ga_in1.reshape(4 * low, middle))
        )
        rows_of = [x[k] for x in sums for k in range(x.shape[0])]
    kernel_shape = (middle // img_n, 3, 3, middle)
    (
        shift_in1_g,
        gain_in1_g,
        shift_mid1_g,
        gain_mid1_g,
        shift_sum1_g,
        gain_out1_g,
        gain_skip_g,
        shift_in2_g,
        gain_in2_g,
        shift_mid2_g,
        gain_mid2_g,
        shift_out2_g,
        gain_out2_g,
    ) = rows_of
    return (
        block_out.reshape(images, rows_low, cols_low, outputs),
        grad_image.reshape(images, rows_here, columns, inputs),
        dw_in1,
        dw_mid1.reshape(kernel_shape),
        dw_out1,
        dw_skip,
        dw_in2,
        dw_mid2.reshape(kernel_shape),
        dw_out2,
        gain_in1_g,
        shift_in1_g,
        gain_mid1_g,
        shift_mid1_g,
        gain_out1_g,
        shift_sum1_g,
        gain_skip_g,
        shift_sum1_g,
        gain_in2_g,
        shift_in2_g,
        gain_mid2_g,
        shift_mid2_g,
        gain_out2_g,
        shift_out2_g,
    )


def solution(mesh):
    image = P("img", "rows", None, None)
    in_specs = (image, P("img")) + (P(),) * 21 + (image,)
    out_specs = (
        image,
        image,
        P("img", None),
        P("img", None, None, None),
        P("img", None),
        P("img", None),
        P("img", None),
        P("img", None, None, None),
        P("img", None),
    ) + (P(),) * 14
    return jax.shard_map(body, mesh=mesh, in_specs=in_specs, out_specs=out_specs, check_vma=False)
```

```python
import functools

import jax
import jax.numpy as jnp
import numpy as np
from jax import lax
from jax.experimental import pallas as pl
from jax.experimental.pallas import tpu as pltpu
from jax.sharding import PartitionSpec as P

EPSILON = 1e-05
F32 = jnp.float32
BF16 = jnp.bfloat16
LANES = 512
ROWS = 32
IMAGES = 16
VMEM_BYTES = 48 * 1024 * 1024
MESH = pl.DeviceIdType.MESH
BY_ROWS, BY_PLANES, FIRST_PLANE, BY_BLOCK, PAIR_BLOCK, WHOLE, APART = range(7)


def dot(a, b):
    return jnp.dot(a, b, preferred_element_type=F32)


def dot_t(a, b):
    return lax.dot_general(a, b, (((1,), (1,)), ((), ())), preferred_element_type=F32)


def load(ref, rows, lanes):
    value = ref[rows, lanes].astype(F32)
    return value.reshape(value.shape[0] // 8, 8, value.shape[1])


def store(ref, rows, lanes, value):
    ref[rows, lanes] = value.reshape(value.shape[0] * 8, value.shape[2]).astype(ref.dtype)


def load_mask(ref, rows):
    mask = load(ref, rows, slice(None))
    return jnp.concatenate([mask] * (LANES // 128), axis=-1)


def sweep(total, step, init, rows=ROWS):
    def body(i, carry):
        return step(pl.ds(pl.multiple_of(i * rows, rows), rows), i, carry)

    return lax.fori_loop(0, total // rows, body, init, unroll=True)


def lane_blocks(width):
    return [slice(k * LANES, (k + 1) * LANES) for k in range(width // LANES)]


def tall(row):
    return jnp.broadcast_to(row, (8, row.shape[-1]))


def column_sum(value):
    return jnp.sum(value, axis=0)


def total_of(part):
    return jnp.sum(part, axis=0, keepdims=True)


def zeros8():
    return jnp.zeros((8, LANES), F32)


def tally(first, parts, centre_ref, stats_ref, fill=None):
    width = parts[0][0].shape[-1]
    for lanes in lane_blocks(width):
        if fill is not None:
            fill(lanes)
        sums = (zeros8(), zeros8())
        for acc, mask_ref, dev in parts:

            def add(rows, i, carry, acc=acc, mask_ref=mask_ref):
                mask = load_mask(mask_ref, rows)
                return (
                    carry[0] + column_sum(load(acc, rows, lanes) * mask),
                    carry[1] + column_sum(mask),
                )

            sums = sweep(acc.shape[0], add, sums)
        total, count = total_of(sums[0]), total_of(sums[1])
        centre = total / jnp.maximum(count, 1.0)
        centre_ref[:, lanes] = centre
        centre8 = tall(centre)
        squares = zeros8()
        for acc, mask_ref, dev in parts:

            def square(rows, i, carry, acc=acc, mask_ref=mask_ref, dev=dev):
                away = load(acc, rows, lanes) - centre8
                store(dev, rows, lanes, away)
                return carry + column_sum(load_mask(mask_ref, rows) * away * away)

            squares = sweep(acc.shape[0], square, squares)
        squares = total_of(squares)
        count_old, mean_old, squares_old = (
            jnp.where(first, jnp.zeros_like(count), stats_ref[k : k + 1, lanes]) for k in range(3)
        )
        both = count_old + count
        share = count / jnp.maximum(both, 1.0)
        delta = centre - mean_old
        stats_ref[0:1, lanes] = both
        stats_ref[1:2, lanes] = mean_old + delta * share
        stats_ref[2:3, lanes] = squares_old + squares + delta * delta * count_old * share


def affine(stats_ref, gain_ref, shift_ref, centre_ref, lanes):
    scale = lax.rsqrt(stats_ref[2:3, lanes] + EPSILON)
    slope = gain_ref[:, lanes] * scale
    base = shift_ref[:, lanes] + (centre_ref[:, lanes] - stats_ref[1:2, lanes]) * slope
    return tall(0.5 * slope), tall(0.5 * base)


def silu_half(half):
    return half + half * jnp.tanh(half)


def gate_half(half):
    tanh = jnp.tanh(half)
    return (0.5 + 0.5 * tanh) * (1.0 + half * (1.0 - tanh))


def silu_and_gate(half):
    tanh = jnp.tanh(half)
    return half + half * tanh, (0.5 + 0.5 * tanh) * (1.0 + half * (1.0 - tanh))


def back_coefs(stats_ref, gain_ref, centre_ref, sums, lanes):
    shift_sum, gain_sum = sums
    pixels = stats_ref[0:1, lanes]
    scale = lax.rsqrt(stats_ref[2:3, lanes] + EPSILON)
    slope = gain_ref[:, lanes] * scale
    per_pixel = slope / pixels
    away = (centre_ref[:, lanes] - stats_ref[1:2, lanes]) * scale
    return (
        tall(slope),
        tall(-per_pixel * scale * gain_sum),
        tall(-per_pixel * (shift_sum + away * gain_sum)),
    )


def unit_sum(stats_ref, centre_ref, lanes, gn_sum, gd_sum):
    scale = lax.rsqrt(stats_ref[2:3, lanes] + EPSILON)
    return scale * (gd_sum + (centre_ref[:, lanes] - stats_ref[1:2, lanes]) * gn_sum)


def accumulate(first, ref, row, lanes, value):
    old = jnp.where(first, jnp.zeros_like(value), ref[row : row + 1, lanes])
    ref[row : row + 1, lanes] = old + value


def shifted(value, by):
    if by == 0:
        return value
    rolled = pltpu.roll(value, (-by) % 8, axis=1)
    column = lax.broadcasted_iota(jnp.int32, value.shape, 1)
    return jnp.where(column == (0 if by < 0 else 7), 0.0, rolled)


def from_above(value, edge, rows_low):
    if rows_low == 1:
        return edge
    images = value.shape[0] // rows_low
    image = value.reshape((images, rows_low) + value.shape[1:])
    return jnp.concatenate([edge[:, None], image[:, :-1]], axis=1).reshape(value.shape)


def from_below(value, edge, rows_low):
    if rows_low == 1:
        return edge
    images = value.shape[0] // rows_low
    image = value.reshape((images, rows_low) + value.shape[1:])
    return jnp.concatenate([image[:, 1:], edge[:, None]], axis=1).reshape(value.shape)


def edge_rows(i, rows_low):
    return pl.ds(pl.multiple_of(i * (ROWS // rows_low), ROWS // rows_low), ROWS // rows_low)


def either(upto, early, late, rows, lanes):
    here = pl.program_id(0) < upto
    return jnp.where(here, load(early, rows, lanes), load(late, rows, lanes))


def first_step():
    return pl.program_id(0) == 0


def open_kernel(
    image_ref,
    perm_ref,
    mask_ref,
    mask_out,
    weight_ref,
    weight_skip,
    planes_ref,
    dev_ref,
    centre_ref,
    dev_skip,
    centre_skip,
    stats_ref,
    acc,
    acc_skip,
    flush,
):
    planes, low, _ = planes_ref.shape
    group = perm_ref.shape[0]
    part = group // planes
    for g in range(image_ref.shape[0] // group):
        mask = jnp.concatenate(
            [mask_ref[p, g * part : (g + 1) * part, :] for p in range(planes)], axis=0
        )
        mask = jnp.concatenate([mask] * (group // 128), axis=1)
        perm = perm_ref[...] * mask
        moved = dot(perm, image_ref[g * group : (g + 1) * group, :]).astype(BF16)
        for p in range(planes):
            planes_ref[p, g * part : (g + 1) * part, :] = moved[p * part : (p + 1) * part]
    for p in range(planes):
        acc[p] = dot(planes_ref[p], weight_ref[...])
    width = acc.shape[-1]
    tally(
        first_step(),
        [(acc.at[p], mask_ref.at[p], dev_ref.at[p]) for p in range(planes)],
        centre_ref,
        stats_ref.at[:, :width],
    )
    flush()

    def fill(lanes):
        acc_skip[:, lanes] = dot(planes_ref[0], weight_skip[:, lanes])

    tally(first_step(), [(acc_skip, mask_out, dev_skip)], centre_skip, stats_ref.at[:, width:], fill)


def mid1_kernel(
    rows_low,
    dev_in,
    centre_in,
    mask_ref,
    halo,
    halo_centre,
    halo_mask,
    stats_in,
    gain,
    shift,
    mask_out,
    weight,
    hidden,
    dev_out,
    centre_out,
    stats_out,
    taps,
    acc,
):
    low, width = acc.shape
    steps = []
    for lanes in lane_blocks(width):
        slope, base = affine(stats_in, gain, shift, centre_in, lanes)
        slope_edge, base_edge = affine(stats_in, gain, shift, halo_centre, lanes)

        def act(p, rows, lanes=lanes, slope=slope, base=base):
            mask = load_mask(mask_ref.at[p], rows)
            value = silu_half(load(dev_in.at[p], rows, lanes) * slope + base) * mask
            store(hidden.at[p], rows, lanes, value)
            return value

        def act_edge(q, i, lanes=lanes, slope_edge=slope_edge, base_edge=base_edge):
            rows = edge_rows(i, rows_low)
            half = load(halo.at[q], rows, lanes) * slope_edge + base_edge
            return silu_half(half) * load_mask(halo_mask.at[q], rows)

        def step0(rows, i, carry):
            act(0, rows)
            return carry

        def step1(rows, i, carry):
            store(taps.at[0], rows, lanes, shifted(act(1, rows), -1))
            return carry

        def step2(rows, i, carry):
            store(taps.at[1], rows, lanes, from_above(act(2, rows), act_edge(0, i), rows_low))
            return carry

        def step3(rows, i, carry):
            odd = act(3, rows)
            store(taps.at[2], rows, lanes, shifted(odd, -1))
            above = from_above(odd, act_edge(1, i), rows_low)
            store(taps.at[3], rows, lanes, above)
            store(taps.at[4], rows, lanes, shifted(above, -1))
            return carry

        steps.append((step0, step1, step2, step3))

    def tap(t, u):
        k = (3 * t + u) * width
        return weight[k : k + width]

    def plane(p):
        for some in steps:
            sweep(low, some[p], 0)

    plane(0)
    plane(1)
    acc[...] = dot(hidden[0], tap(1, 1))
    plane(2)
    acc[...] += dot(hidden[1], tap(1, 2)) + dot(taps[0], tap(1, 0))
    plane(3)
    acc[...] += dot(hidden[2], tap(2, 1)) + dot(taps[1], tap(0, 1))
    acc[...] += (
        dot(hidden[3], tap(2, 2))
        + dot(taps[2], tap(2, 0))
        + dot(taps[3], tap(0, 2))
        + dot(taps[4], tap(0, 0))
    )
    tally(first_step(), [(acc, mask_out, dev_out)], centre_out, stats_out)


def expand_kernel(
    dev_in, centre_in, stats_in, gain, shift, mask, weight, hidden, dev_out, centre_out, stats_out, acc
):
    for lanes in lane_blocks(dev_in.shape[1]):
        slope, base = affine(stats_in, gain, shift, centre_in, lanes)

        def step(rows, i, carry):
            half = load(dev_in, rows, lanes) * slope + base
            store(hidden, rows, lanes, silu_half(half) * load_mask(mask, rows))
            return carry

        sweep(dev_in.shape[0], step, 0)

    def fill(lanes):
        acc[:, lanes] = dot(hidden[...], weight[:, lanes])

    tally(first_step(), [(acc, mask, dev_out)], centre_out, stats_out, fill)


def join_kernel(
    dev_a,
    centre_a,
    stats_a,
    gain_a,
    shift_a,
    dev_b,
    centre_b,
    stats_b,
    gain_b,
    shift_b,
    mask,
    weight,
    first_low,
    dev_out,
    centre_out,
    stats_out,
    acc,
):
    for lanes in lane_blocks(dev_a.shape[1]):
        slope_a, base_a = affine(stats_a, gain_a, shift_a, centre_a, lanes)
        slope_b, base_b = affine(stats_b, gain_b, shift_b, centre_b, lanes)
        base = base_a + base_b

        def step(rows, i, carry):
            half = load(dev_a, rows, lanes) * slope_a + load(dev_b, rows, lanes) * slope_b + base
            store(first_low, rows, lanes, silu_half(half) * load_mask(mask, rows))
            return carry

        sweep(dev_a.shape[0], step, 0)
        part = dot(first_low[:, lanes], weight[lanes, :])
        acc[...] = part if lanes.start == 0 else acc[...] + part
    tally(first_step(), [(acc, mask, dev_out)], centre_out, stats_out)


def mid2_kernel(
    rows_low,
    dev_in,
    centre_in,
    halo,
    halo_centre,
    halo_mask,
    stats_in,
    gain,
    shift,
    mask,
    weight,
    hidden,
    dev_out,
    centre_out,
    stats_out,
    taps,
    acc,
):
    low, width = acc.shape
    for lanes in lane_blocks(width):
        slope, base = affine(stats_in, gain, shift, centre_in, lanes)
        edges = [affine(stats_in, gain, shift, halo_centre.at[e], lanes) for e in range(2)]

        def act_edge(e, i):
            rows = edge_rows(i, rows_low)
            half = load(halo.at[e], rows, lanes) * edges[e][0] + edges[e][1]
            return silu_half(half) * load_mask(halo_mask.at[e], rows)

        def step(rows, i, carry):
            value = silu_half(load(dev_in, rows, lanes) * slope + base) * load_mask(mask, rows)
            store(hidden, rows, lanes, value)
            lines = (
                from_above(value, act_edge(0, i), rows_low),
                value,
                from_below(value, act_edge(1, i), rows_low),
            )
            for t in range(3):
                for u in range(3):
                    start = (3 * t + u) * width + lanes.start
                    store(taps, rows, slice(start, start + LANES), shifted(lines[t], u - 1))
            return carry

        sweep(low, step, 0)
    acc[...] = dot(taps[...], weight[...])
    tally(first_step(), [(acc, mask, dev_out)], centre_out, stats_out)


def final_kernel(dev, centre, stats, gain, shift, first_low, cot, mask, block_out, gn_ref, sums):
    first = first_step()
    for lanes in lane_blocks(dev.shape[1]):
        slope, base = affine(stats, gain, shift, centre, lanes)

        def step(rows, i, carry):
            away = load(dev, rows, lanes)
            half = away * slope + base + 0.5 * load(first_low, rows, lanes)
            valid = load_mask(mask, rows)
            value, gate = silu_and_gate(half)
            store(block_out, rows, lanes, value * valid)
            gn = gate * valid * load(cot, rows, lanes)
            store(gn_ref, rows, lanes, gn)
            return carry[0] + column_sum(gn), carry[1] + column_sum(gn * away)

        gn_sum, gd_sum = sweep(dev.shape[0], step, (zeros8(), zeros8()))
        gn_sum, gd_sum = total_of(gn_sum), total_of(gd_sum)
        accumulate(first, sums, 0, lanes, gn_sum)
        accumulate(first, sums, 1, lanes, unit_sum(stats, centre, lanes, gn_sum, gd_sum))


def scaled(gn, away, mask, coefs):
    return (gn * coefs[0] + away * coefs[1] + coefs[2]) * mask


def gate_sums(first, grads, dev, centre, stats, gain, shift, mask, gn_ref, sums, parts, fill=None):
    width = gn_ref.shape[-1]
    planes = range(parts) if parts else [None]
    for lanes in lane_blocks(width):
        slope, base = affine(stats, gain, shift, centre, lanes)
        carry = (zeros8(), zeros8())
        for p in planes:
            if fill is not None and lanes.start == 0:
                fill[p]()
            grad_p, dev_p, mask_p, gn_p = (
                r if p is None else r.at[p] for r in (grads, dev, mask, gn_ref)
            )

            def step(rows, i, carry, grad_p=grad_p, dev_p=dev_p, mask_p=mask_p, gn_p=gn_p):
                away = load(dev_p, rows, lanes)
                gate = gate_half(away * slope + base) * load_mask(mask_p, rows)
                gn = gate * load(grad_p, rows, lanes)
                store(gn_p, rows, lanes, gn)
                return carry[0] + column_sum(gn), carry[1] + column_sum(gn * away)

            carry = sweep(grad_p.shape[0], step, carry)
        gn_sum, gd_sum = total_of(carry[0]), total_of(carry[1])
        accumulate(first, sums, 0, lanes, gn_sum)
        accumulate(first, sums, 1, lanes, unit_sum(stats, centre, lanes, gn_sum, gd_sum))


def back_expand_kernel(
    gn,
    dev,
    centre,
    stats,
    gain,
    sums_in,
    mask,
    weight,
    dev_m,
    centre_m,
    stats_m,
    gain_m,
    shift_m,
    ga,
    gn_m,
    sums_m,
    acc,
):
    for lanes in lane_blocks(dev.shape[1]):
        coefs = back_coefs(
            stats, gain, centre, (sums_in[0:1, lanes], sums_in[1:2, lanes]), lanes
        )

        def step(rows, i, carry):
            away = load(dev, rows, lanes)
            store(ga, rows, lanes, scaled(load(gn, rows, lanes), away, load_mask(mask, rows), coefs))
            return carry

        sweep(dev.shape[0], step, 0)
        part = dot_t(ga[:, lanes], weight[:, lanes])
        acc[...] = part if lanes.start == 0 else acc[...] + part
    gate_sums(first_step(), acc, dev_m, centre_m, stats_m, gain_m, shift_m, mask, gn_m, sums_m, 0)


def back_mid2_kernel(
    rows_low,
    upto,
    gn,
    dev,
    centre,
    halo_gn,
    halo_dev,
    rest_dev,
    halo_centre,
    halo_mask,
    stats,
    gain,
    sums_in,
    mask,
    weight,
    dev_m,
    centre_m,
    stats_m,
    gain_m,
    shift_m,
    views,
    gn_m,
    sums_m,
    acc,
):
    low, width = acc.shape
    for lanes in lane_blocks(width):
        sums = (sums_in[0:1, lanes], sums_in[1:2, lanes])
        coefs = back_coefs(stats, gain, centre, sums, lanes)
        edges = [back_coefs(stats, gain, halo_centre.at[e], sums, lanes) for e in range(2)]

        def edge(e, i):
            rows = edge_rows(i, rows_low)
            return scaled(
                load(halo_gn.at[e], rows, lanes),
                either(upto, halo_dev.at[e], rest_dev.at[e], rows, lanes),
                load_mask(halo_mask.at[e], rows),
                edges[e],
            )

        def step(rows, i, carry):
            value = scaled(
                load(gn, rows, lanes), load(dev, rows, lanes), load_mask(mask, rows), coefs
            )
            lines = (
                from_below(value, edge(1, i), rows_low),
                value,
                from_above(value, edge(0, i), rows_low),
            )
            for t in range(3):
                for u in range(3):
                    start = (3 * t + u) * width + lanes.start
                    store(views, rows, slice(start, start + LANES), shifted(lines[t], 1 - u))
            return carry

        sweep(low, step, 0)
    total = dot_t(views[:, :width], weight[:width])
    for k in range(width, 9 * width, width):
        total += dot_t(views[:, k : k + width], weight[k : k + width])
    acc[...] = total
    gate_sums(first_step(), acc, dev_m, centre_m, stats_m, gain_m, shift_m, mask, gn_m, sums_m, 0)


def back_join_kernel(
    gn_in,
    dev_in,
    centre_in,
    stats_in,
    gain_in,
    sums_in,
    mask,
    weight,
    residual,
    dev_a,
    centre_a,
    stats_a,
    gain_a,
    shift_a,
    dev_b,
    centre_b,
    stats_b,
    gain_b,
    shift_b,
    ga,
    gs_ref,
    sums,
    acc,
):
    first = first_step()
    for lanes in lane_blocks(dev_in.shape[1]):
        coefs = back_coefs(
            stats_in, gain_in, centre_in, (sums_in[0:1, lanes], sums_in[1:2, lanes]), lanes
        )

        def step(rows, i, carry):
            away = load(dev_in, rows, lanes)
            value = scaled(load(gn_in, rows, lanes), away, load_mask(mask, rows), coefs)
            store(ga, rows, lanes, value)
            return carry

        sweep(dev_in.shape[0], step, 0)
    for lanes in lane_blocks(dev_a.shape[1]):
        acc[:, lanes] = dot_t(ga[...], weight[lanes, :])
        slope_a, base_a = affine(stats_a, gain_a, shift_a, centre_a, lanes)
        slope_b, base_b = affine(stats_b, gain_b, shift_b, centre_b, lanes)
        base = base_a + base_b

        def gate(rows, i, carry):
            away_a, away_b = load(dev_a, rows, lanes), load(dev_b, rows, lanes)
            half = away_a * slope_a + away_b * slope_b + base
            grad = load(residual, rows, lanes) + load(acc, rows, lanes)
            gs = gate_half(half) * load_mask(mask, rows) * grad
            store(gs_ref, rows, lanes, gs)
            return (
                carry[0] + column_sum(gs),
                carry[1] + column_sum(gs * away_a),
                carry[2] + column_sum(gs * away_b),
            )

        carry = sweep(dev_a.shape[0], gate, (zeros8(), zeros8(), zeros8()))
        gs_sum, a_sum, b_sum = (total_of(part) for part in carry)
        accumulate(first, sums, 0, lanes, gs_sum)
        accumulate(first, sums, 1, lanes, unit_sum(stats_a, centre_a, lanes, gs_sum, a_sum))
        accumulate(first, sums, 2, lanes, unit_sum(stats_b, centre_b, lanes, gs_sum, b_sum))


def back_split_kernel(
    gs,
    dev_a,
    centre_a,
    stats_a,
    gain_a,
    dev_b,
    centre_b,
    stats_b,
    gain_b,
    sums_in,
    mask,
    weight_a,
    weight_b,
    dev_m,
    centre_m,
    stats_m,
    gain_m,
    shift_m,
    ga_a,
    ga_b,
    gn_m,
    grad_skip,
    sums_m,
    acc,
    acc_skip,
):
    for lanes in lane_blocks(dev_a.shape[1]):
        shift_sum = sums_in[0:1, lanes]
        coefs_a = back_coefs(stats_a, gain_a, centre_a, (shift_sum, sums_in[1:2, lanes]), lanes)
        coefs_b = back_coefs(stats_b, gain_b, centre_b, (shift_sum, sums_in[2:3, lanes]), lanes)

        def step(rows, i, carry):
            value, valid = load(gs, rows, lanes), load_mask(mask, rows)
            store(ga_a, rows, lanes, scaled(value, load(dev_a, rows, lanes), valid, coefs_a))
            store(ga_b, rows, lanes, scaled(value, load(dev_b, rows, lanes), valid, coefs_b))
            return carry

        sweep(dev_a.shape[0], step, 0)
        part = dot_t(ga_a[:, lanes], weight_a[:, lanes])
        acc[...] = part if lanes.start == 0 else acc[...] + part
        part = dot_t(ga_b[:, lanes], weight_b[:, lanes])
        acc_skip[...] = part if lanes.start == 0 else acc_skip[...] + part
    grad_skip[...] = acc_skip[...].astype(BF16)
    gate_sums(first_step(), acc, dev_m, centre_m, stats_m, gain_m, shift_m, mask, gn_m, sums_m, 0)


def back_mid1_kernel(
    rows_low,
    upto,
    gn,
    dev,
    centre,
    halo_gn,
    halo_dev,
    rest_dev,
    halo_centre,
    halo_mask,
    stats,
    gain,
    sums_in,
    mask,
    weight,
    dev_m,
    centre_m,
    mask_m,
    stats_m,
    gain_m,
    shift_m,
    views,
    gn_m,
    sums_m,
    acc,
):
    _, low, width = acc.shape
    for lanes in lane_blocks(width):
        sums = (sums_in[0:1, lanes], sums_in[1:2, lanes])
        coefs = back_coefs(stats, gain, centre, sums, lanes)
        coefs_edge = back_coefs(stats, gain, halo_centre, sums, lanes)

        def step(rows, i, carry):
            value = scaled(
                load(gn, rows, lanes), load(dev, rows, lanes), load_mask(mask, rows), coefs
            )
            some = edge_rows(i, rows_low)
            edge = scaled(
                load(halo_gn, some, lanes),
                either(upto, halo_dev.at[0], rest_dev.at[0], some, lanes),
                load_mask(halo_mask, some),
                coefs_edge,
            )
            below = from_below(value, edge, rows_low)
            for k, view in enumerate((below, value, shifted(value, 1), shifted(below, 1))):
                start = k * width + lanes.start
                store(views, rows, slice(start, start + LANES), view)
            return carry

        sweep(low, step, 0)

    def view(k):
        return views[:, k * width : (k + 1) * width]

    def tap(t, u):
        k = (3 * t + u) * width
        return weight[k : k + width]

    def plane0():
        acc[0] = dot_t(view(1), tap(1, 1))

    def plane1():
        acc[1] = dot_t(view(1), tap(1, 2)) + dot_t(view(2), tap(1, 0))

    def plane2():
        acc[2] = dot_t(view(1), tap(2, 1)) + dot_t(view(0), tap(0, 1))

    def plane3():
        acc[3] = (
            dot_t(view(1), tap(2, 2))
            + dot_t(view(2), tap(2, 0))
            + dot_t(view(0), tap(0, 2))
            + dot_t(view(3), tap(0, 0))
        )

    gate_sums(
        first_step(),
        acc,
        dev_m,
        centre_m,
        stats_m,
        gain_m,
        shift_m,
        mask_m,
        gn_m,
        sums_m,
        4,
        (plane0, plane1, plane2, plane3),
    )


def back_image_kernel(
    gn,
    dev,
    centre,
    stats,
    gain,
    sums_in,
    mask_ref,
    weight,
    grad_skip,
    perm_ref,
    handed,
    ga,
    image,
    hand,
    planes_ref,
):
    planes, low, width = ga.shape
    for p in range(planes):
        for lanes in lane_blocks(width):
            coefs = back_coefs(
                stats, gain, centre, (sums_in[0:1, lanes], sums_in[1:2, lanes]), lanes
            )

            def step(rows, i, carry):
                away = load(dev.at[p], rows, lanes)
                valid = load_mask(mask_ref.at[p], rows)
                value = scaled(load(gn.at[p], rows, lanes), away, valid, coefs)
                store(ga.at[p], rows, lanes, value)
                return carry

            sweep(low, step, 0)
        grad = dot_t(ga[p], weight[...])
        if p == 0:
            grad += grad_skip[...].astype(F32)
        planes_ref[p] = grad.astype(BF16)
    hand[...] = handed[...]
    group = perm_ref.shape[0]
    part = group // planes
    for g in range(image.shape[0] // group):
        rows = slice(g * part, (g + 1) * part)
        mask = jnp.concatenate([mask_ref[p, rows, :] for p in range(planes)], axis=0)
        mask = jnp.concatenate([mask] * (group // 128), axis=1)
        perm = perm_ref[...] * mask
        here = jnp.concatenate([planes_ref[p, rows, :] for p in range(planes)], axis=0)
        back = lax.dot_general(
            perm, here, (((0,), (0,)), ((), ())), preferred_element_type=F32
        )
        image[g * group : (g + 1) * group, :] = back.astype(BF16)


def spec_of(shape, kind, blocks):
    if isinstance(kind, pl.BlockSpec):
        return kind
    if kind == BY_ROWS:
        return pl.BlockSpec((shape[0] // blocks, shape[1]), lambda b: (b, 0))
    if kind == BY_PLANES:
        return pl.BlockSpec((shape[0], shape[1] // blocks, shape[2]), lambda b: (0, b, 0))
    if kind == FIRST_PLANE:
        return pl.BlockSpec((None, shape[1] // blocks, shape[2]), lambda b: (0, b, 0))
    if kind == BY_BLOCK:
        return pl.BlockSpec((None,) + tuple(shape[1:]), lambda b: (b, 0, 0))
    if kind == PAIR_BLOCK:
        return pl.BlockSpec((2, None) + tuple(shape[2:]), lambda b: (0, b, 0, 0))
    if kind == APART:
        return pl.BlockSpec(memory_space=pl.ANY)
    zero = (0,) * len(shape)
    return pl.BlockSpec(tuple(shape), lambda b: zero, pipeline_mode=pl.Buffered(1))


def out_spec(shape, kind, blocks):
    if not isinstance(kind, pl.BlockSpec) and kind == WHOLE:
        zero = (0,) * len(shape)
        return pl.BlockSpec(tuple(shape), lambda b: zero)
    return spec_of(shape, kind, blocks)


def placed(shape, dtype, kind, late=False):
    return pltpu.HBM(shape, dtype) if late else jax.ShapeDtypeStruct(shape, dtype)


def stage(kernel, blocks, ins, outs, scratch=(), flops=0):
    return call(kernel, blocks, ins, outs, scratch, flops, [], [], {})


def call(kernel, blocks, ins, outs, scratch, flops, more_specs, more_shapes, params):
    moved = sum(x.size * x.dtype.itemsize for x, _ in ins)
    moved += sum(int(np.prod(item[0])) * jnp.dtype(item[1]).itemsize for item in outs)
    made = [pltpu.VMEM(*item) if isinstance(item, tuple) else item for item in scratch]
    return pl.pallas_call(
        kernel,
        grid=(blocks,),
        in_specs=[spec_of(x.shape, kind, blocks) for x, kind in ins],
        out_specs=[out_spec(item[0], item[2], blocks) for item in outs] + more_specs,
        out_shape=[placed(*item) for item in outs] + more_shapes,
        scratch_shapes=made,
        compiler_params=pltpu.CompilerParams(
            dimension_semantics=("arbitrary",), vmem_limit_bytes=VMEM_BYTES, **params
        ),
        cost_estimate=pl.CostEstimate(flops=flops, bytes_accessed=moved, transcendentals=0),
    )(*[x for x, _ in ins])


def merge_rows(buf, peers, merge, mean_only):
    if not merge:
        total = buf[0]
        for k in range(1, peers):
            total = total + buf[k]
        return total
    counts = [buf[k, 0:1, :] for k in range(peers)]
    means = [buf[k, 1:2, :] for k in range(peers)]
    count, weighted = counts[0], counts[0] * means[0]
    for k in range(1, peers):
        count = count + counts[k]
        weighted = weighted + counts[k] * means[k]
    safe = jnp.maximum(count, 1.0)
    mean = weighted / safe
    squares = jnp.zeros_like(mean)
    for k in range(peers):
        squares = squares + buf[k, 2:3, :] + counts[k] * jnp.square(means[k] - mean)
    if mean_only:
        squares = squares / safe
    return jnp.concatenate([count, mean, squares], axis=0)


class Exchange:
    def __init__(self, rows_n, img_n, blocks):
        self.rows_n, self.img_n, self.blocks = rows_n, img_n, blocks
        self.calls = 0

    def __call__(
        self,
        kernel,
        ins,
        outs,
        merge,
        lines,
        widths,
        scratch=(),
        flops=0,
        edges=(),
        centres=None,
        edge=0,
        early=False,
        upto=None,
        defer=1,
        relay=None,
    ):
        ident, self.calls = self.calls, self.calls + 1
        total, dma = sum(widths), pltpu.SemaphoreType.DMA
        any_space = pl.BlockSpec(memory_space=pl.ANY)
        specs = [out_spec((lines, w), WHOLE, 1) for w in widths]
        shapes = [jax.ShapeDtypeStruct((lines, w), F32) for w in widths]
        extra = []
        upto = upto or self.blocks
        kept = upto < self.blocks
        if edges:
            middle = outs[edges[0][0]][0][-1]
            some = edge // self.blocks
            specs.append(any_space)
            shapes.append(jax.ShapeDtypeStruct((len(edges), upto * some, middle), BF16))
            extra += [
                ((len(edges), edge, middle), BF16),
                dma((len(edges), self.blocks)),
                dma((len(edges), self.blocks)),
                dma((len(edges),)),
            ]
        if centres:
            count, shape = len(centres[1]), outs[centres[0]][0]
            specs.append(any_space)
            shapes.append(jax.ShapeDtypeStruct((count,) + tuple(shape), F32))
            extra += [(tuple(shape), F32), dma((count,)), dma((count,)), dma((count,))]
        if kept:
            spec = pl.BlockSpec((len(edges), some, middle), lambda b: (0, jnp.maximum(b - upto, 0), 0))
            outs = outs + [((len(edges), edge - upto * some, middle), BF16, spec, True)]
        if relay:
            ins = ins + [(relay[0], APART)]
            specs.append(any_space)
            shapes.append(jax.ShapeDtypeStruct(relay[0].shape, BF16))
            extra += [dma((len(relay[1]),))] * 3
        extra += [
            ((self.rows_n, lines, total), F32),
            ((self.img_n, lines, total), F32),
            ((lines, total), F32),
            dma((self.rows_n,)),
            dma((self.rows_n,)),
            dma((self.img_n,)),
            dma((self.img_n,)),
        ]
        return call(
            functools.partial(
                self.kernel,
                kernel,
                len(ins),
                len(outs),
                len(scratch),
                merge,
                widths,
                edges,
                centres,
                early,
                upto,
                defer,
                relay[1] if relay else (),
            ),
            self.blocks,
            ins,
            outs,
            [((lines, total), F32)] + list(scratch) + extra,
            flops,
            specs,
            shapes,
            dict(collective_id=ident, has_side_effects=True),
        )

    def kernel(
        self,
        kernel,
        ins_n,
        outs_n,
        scratch_n,
        merge,
        widths,
        edges,
        centres,
        early,
        upto,
        defer,
        relay,
        *refs,
    ):
        kept = upto < self.blocks
        rows_n, img_n, blocks = self.rows_n, self.img_n, self.blocks
        refs = list(refs)

        def take(count):
            taken = refs[:count]
            del refs[:count]
            return taken

        ins, outs, totals = take(ins_n), take(outs_n), take(len(widths))
        halo = take(1)[0] if edges else None
        halo_centres = take(1)[0] if centres else None
        relayed = take(1)[0] if relay else None
        carried = ins.pop() if relay else None
        kept_rows = outs.pop() if kept else None
        mine = take(1)[0]
        scratch = take(scratch_n)
        if edges:
            edge_buf, edge_send, edge_recv, edge_local = take(4)
        if centres:
            centre_buf, centre_send, centre_recv, centre_local = take(4)
        if relay:
            relay_send, relay_recv, relay_local = take(3)
        buf_r, buf_i, part, send_r, recv_r, send_i, recv_i = refs
        block = pl.program_id(0)
        row, img = lax.axis_index("rows"), lax.axis_index("img")
        barrier = pltpu.get_barrier_semaphore()

        @pl.when(block == 0)
        def _():
            for k in range(1, rows_n):
                peer = {"rows": lax.rem(row + k, rows_n)}
                pl.semaphore_signal(barrier, inc=1, device_id=peer, device_id_type=MESH)
            for k in range(1, img_n):
                peer = {"img": lax.rem(img + k, img_n)}
                pl.semaphore_signal(barrier, inc=1, device_id=peer, device_id_type=MESH)

        def remote(source, target, send, recv, peer):
            return pltpu.make_async_remote_copy(
                src_ref=source,
                dst_ref=target,
                send_sem=send,
                recv_sem=recv,
                device_id=peer,
                device_id_type=MESH,
            )

        def sends(direction):
            return row < rows_n - 1 if direction > 0 else row > 0

        def receives(direction):
            return row > 0 if direction > 0 else row < rows_n - 1

        def edge_copy(e, b):
            some = edge_buf.shape[1] // blocks
            here = pl.ds(pl.multiple_of(b * some, some), some)
            return remote(
                edge_buf.at[e, here],
                halo.at[e, here],
                edge_send.at[e, b],
                edge_recv.at[e, b],
                {"rows": row + edges[e][3]},
            )

        def keep_edges():
            some = edge_buf.shape[1] // blocks
            here = pl.ds(pl.multiple_of(block * some, some), some)
            for e, (out, plane, last_row, _) in enumerate(edges):
                source = outs[out] if plane is None else outs[out].at[plane]
                for lanes in lane_blocks(source.shape[1]):
                    value = load(source, slice(None), lanes)
                    lines = value.reshape((some // 8, -1) + value.shape[1:])
                    store(edge_buf.at[e], here, lanes, lines[:, -1 if last_row else 0])
                if kept:
                    kept_rows[e] = edge_buf[e, here]

        def send_edges(b):
            for e, spec in enumerate(edges):

                @pl.when(sends(spec[3]))
                def _(e=e):
                    edge_copy(e, b).start()

        def relay_copy(k):
            peer = {"rows": row + relay[k]}
            return remote(carried.at[k], relayed.at[k], relay_send.at[k], relay_recv.at[k], peer)

        def relay_own(k):
            return pltpu.make_async_copy(carried.at[k], relayed.at[k], relay_local.at[k])

        def greet():
            @pl.when(block == 0)
            def _():
                pl.semaphore_wait(barrier, rows_n + img_n - 2)
                for k, direction in enumerate(relay):

                    @pl.when(sends(direction))
                    def _(k=k):
                        relay_copy(k).start()

                    @pl.when(jnp.logical_not(receives(direction)))
                    def _(k=k):
                        relay_own(k).start()

        def flush():
            greet()
            keep_edges()
            send_edges(block)

        if early:
            kernel(*ins, *outs, mine, *scratch, flush)
        else:
            kernel(*ins, *outs, mine, *scratch)
            greet()
            if edges:
                keep_edges()

                @pl.when(block < jnp.minimum(blocks - defer, upto))
                def _():
                    send_edges(block)

        if centres:
            centre_buf[pl.ds(block, 1)] = outs[centres[0]][...][None]

        def exchange(axis, me, peers, source, buf, send, recv, then=None):
            copies = []
            for k in range(1, peers):
                peer = {axis: lax.rem(me + k, peers)}
                copies.append(remote(source, buf.at[me], send.at[k], recv.at[me], peer))
                copies[-1].start()
            if then is not None:
                then()
            buf[pl.ds(me, 1)] = source[...][None]
            for k in range(1, peers):
                peer = lax.rem(me + k, peers)
                remote(source, buf.at[peer], send.at[k], recv.at[peer], {axis: peer}).wait_recv()
            return copies

        @pl.when(block == blocks - 1)
        def _():
            def centre_copy(k):
                peer = {"rows": row + centres[1][k]}
                return remote(
                    centre_buf, halo_centres.at[k], centre_send.at[k], centre_recv.at[k], peer
                )

            directions = centres[1] if centres else ()

            def rest():
                for k, direction in enumerate(directions):

                    @pl.when(sends(direction))
                    def _(k=k):
                        centre_copy(k).start()

                if edges and not early:
                    for b in range(blocks - defer, upto):
                        send_edges(b)

            copies = exchange("rows", row, rows_n, mine, buf_r, send_r, recv_r, rest)
            part[...] = merge_rows(buf_r, rows_n, merge, False)
            copies += exchange("img", img, img_n, part, buf_i, send_i, recv_i)
            total = merge_rows(buf_i, img_n, merge, True)
            start = 0
            for out, width in zip(totals, widths):
                out[...] = total[:, start : start + width]
                start += width
            for k, direction in enumerate(directions):
                own = pltpu.make_async_copy(centre_buf, halo_centres.at[k], centre_local.at[k])

                @pl.when(receives(direction))
                def _(k=k):
                    centre_copy(k).wait_recv()

                @pl.when(jnp.logical_not(receives(direction)))
                def _(own=own):
                    own.start()
                    own.wait()

                @pl.when(sends(direction))
                def _(k=k):
                    centre_copy(k).wait_send()

            for k, direction in enumerate(relay):

                @pl.when(receives(direction))
                def _(k=k):
                    relay_copy(k).wait_recv()

                @pl.when(jnp.logical_not(receives(direction)))
                def _(k=k):
                    relay_own(k).wait()

                @pl.when(sends(direction))
                def _(k=k):
                    relay_copy(k).wait_send()

            for e, spec in enumerate(edges):
                mine_kept = edge_buf.at[e, : halo.shape[1]]
                own = pltpu.make_async_copy(mine_kept, halo.at[e], edge_local.at[e])

                @pl.when(receives(spec[3]))
                def _(e=e):
                    for b in range(upto):
                        edge_copy(e, b).wait_recv()

                @pl.when(jnp.logical_not(receives(spec[3])))
                def _(own=own):
                    own.start()
                    own.wait()

                @pl.when(sends(spec[3]))
                def _(e=e):
                    for b in range(upto):
                        edge_copy(e, b).wait_send()

            for copy in copies:
                copy.wait_send()


CHUNK_ROWS = 64
CHUNK_LANES = 1024


HID_MID2, GA_OUT2, HID_IN2, VIEWS2, FIRST, GA_IN2, HID_MID1, GA_OUT1, GA_SKIP, VIEWS1 = range(10)
HID, PLANE, GA_IN1 = 10, 14, 18
ONE, TWO, HALF, QUAD, DEEP = range(5)
WIDTHS = {ONE: (512, 1024), TWO: (1024, 512), HALF: (512, 512), QUAD: (1024, 256), DEEP: (1024, 512)}


def plan_jobs():
    chunks = [[(ONE, 0, HID_MID2, 0, GA_OUT2, 1024 * k)] for k in range(2)]
    chunks += [[(ONE, 0, HID_IN2, 0, VIEWS2, 1024 * k)] for k in range(4)]
    chunks += [[(HALF, 0, HID_IN2, 0, VIEWS2, 4096), (HALF, 1, HID, 0, VIEWS1, 512)]]
    chunks += [[(QUAD, h, FIRST, 1024 * h, GA_IN2, 256 * k) for h in range(2)] for k in range(2)]
    chunks += [[(DEEP, p, PLANE + p, 0, GA_IN1 + p, 0) for p in range(4)]]
    chunks += [[(ONE, 0, HID_MID1, 0, GA_OUT1, 1024 * k)] for k in range(2)]
    chunks += [[(TWO, 0, PLANE, 0, GA_SKIP, 512 * k)] for k in range(4)]
    chunks += [[(ONE, 0, HID + 1, 0, VIEWS1, 512)], [(ONE, 0, HID + 2, 0, VIEWS1, 0)]]
    chunks += [[(ONE, 0, HID + 3, 0, VIEWS1, 1024 * k)] for k in range(2)]
    for k, job in zip((3, 4, 5), chunks[9]):
        chunks[k].append(job)
    chunks[9] = chunks[9][3:]
    return chunks


def weights_kernel(
    rows_n,
    hid_mid2,
    ga_out2,
    hid_in2,
    views2,
    first_low,
    ga_in2,
    hid_mid1,
    ga_out1,
    planes,
    ga_skip,
    hid_in1,
    views1,
    ga_in1,
    done,
    lhs_buf,
    rhs_buf,
    deep,
    chunk_buf,
    own,
    got1,
    got2a,
    got2b,
    got3a,
    got3b,
    got_low,
    got_high,
    lhs_sem,
    rhs_sem,
    *sems,
):
    (s1, r1, s2a, r2a, s2b, r2b, s3a, r3a, s3b, r3b, s_up, r_low, s_down, r_high, b_up, b_down, r_back) = sems
    sources = [hid_mid2, ga_out2, hid_in2, views2, first_low, ga_in2, hid_mid1, ga_out1, ga_skip, views1]
    for stack in (hid_in1, planes, ga_in1):
        sources += [stack.at[p] for p in range(4)]
    chunks = plan_jobs()
    jobs = [job for chunk in chunks for job in chunk]
    count = len(chunks)
    depth = chunk_buf.shape[0]
    img, z = lax.axis_index("img"), lax.axis_index("rows")
    y, x, c = img // 4, lax.rem(img // 2, 2), lax.rem(img, 2)
    root = rows_n // 2
    sibling = {"img": img + 1 - 2 * c}
    beside_x = {"img": img + 2 - 4 * x}
    beside_y = {"img": img + 4 - 8 * y}
    higher, lower = {"rows": z + 1}, {"rows": z - 1}
    half = CHUNK_LANES // 2
    left, right = slice(0, half), slice(half, 2 * half)

    def fetch(index):
        kind, _, lhs, lhs_start, rhs, rhs_start = jobs[index]
        lhs_width, rhs_width = WIDTHS[kind]
        slot = index % 2
        return (
            pltpu.make_async_copy(
                sources[lhs].at[:, lhs_start : lhs_start + lhs_width],
                lhs_buf.at[slot, :, :lhs_width],
                lhs_sem.at[slot],
            ),
            pltpu.make_async_copy(
                sources[rhs].at[:, rhs_start : rhs_start + rhs_width],
                rhs_buf.at[slot, :, :rhs_width],
                rhs_sem.at[slot],
            ),
        )

    for copy in fetch(0):
        copy.start()

    barrier = pltpu.get_barrier_semaphore()
    for peer in (sibling, beside_x, beside_y):
        pl.semaphore_signal(barrier, inc=1, device_id=peer, device_id_type=MESH)

    @pl.when(z > 0)
    def _():
        pl.semaphore_signal(barrier, inc=1, device_id=lower, device_id_type=MESH)

    @pl.when(z < rows_n - 1)
    def _():
        pl.semaphore_signal(barrier, inc=1, device_id=higher, device_id_type=MESH)

    pl.semaphore_wait(barrier, 3 + jnp.minimum(z, 1) + jnp.minimum(rows_n - 1 - z, 1))

    def put(slot, result, first, parts):
        width = CHUNK_LANES // parts
        rows = CHUNK_ROWS
        for m in range(result.shape[0] // (rows * parts)):
            shard = first + m
            for h in range(parts):
                piece = result[(m * parts + h) * rows : (m * parts + h + 1) * rows]
                chunk_buf[slot, shard // 4, shard // 2 % 2, shard % 2, :, h * width : (h + 1) * width] = piece

    def multiply(index, slot):
        kind, part = jobs[index][:2]
        lhs_width, rhs_width = WIDTHS[kind]
        here = index % 2

        def product():
            return lax.dot_general(
                lhs_buf[here, :, :lhs_width],
                rhs_buf[here, :, :rhs_width],
                (((0,), (0,)), ((), ())),
                preferred_element_type=F32,
            )

        if kind == ONE:
            put(slot, product().astype(BF16), 0, 1)
        elif kind == TWO:
            put(slot, product().astype(BF16), 0, 2)
        elif kind == QUAD:
            put(slot, product().astype(BF16), 4 * part, 4)
        elif kind == HALF:
            result = product().astype(BF16)
            for m in range(8):
                piece = result[m * CHUNK_ROWS : (m + 1) * CHUNK_ROWS]
                chunk_buf[slot, m // 4, m // 2 % 2, m % 2, :, (left, right)[part]] = piece
        elif part == 0:
            deep[...] = product()
        elif part == 3:
            put(slot, (deep[...] + product()).astype(BF16), 0, 2)
        else:
            deep[...] += product()

    def remote(source, target, send, recv, peer):
        return pltpu.make_async_remote_copy(
            src_ref=source,
            dst_ref=target,
            send_sem=send,
            recv_sem=recv,
            device_id=peer,
            device_id_type=MESH,
        )

    def to_core(t):
        source = chunk_buf.at[lax.rem(t, depth), :, :, 1 - c]
        return remote(source, got1.at[t], s1.at[t], r1.at[t], sibling)

    def to_2a(t):
        return remote(own.at[t, :, 1 - x, :, left], got2a.at[t], s2a.at[t], r2a.at[t], beside_x)

    def to_2b(t):
        return remote(own.at[t, 1 - y, :, :, right], got2b.at[t], s2b.at[t], r2b.at[t], beside_y)

    def to_3a(t):
        return remote(own.at[t, 1 - y, x, :, left], got3a.at[t], s3a.at[t], r3a.at[t], beside_y)

    def to_3b(t):
        return remote(own.at[t, y, 1 - x, :, right], got3b.at[t], s3b.at[t], r3b.at[t], beside_x)

    def up(t):
        return remote(own.at[t, y, x], got_low.at[t], s_up.at[t], r_low.at[t], higher)

    def down(t):
        return remote(own.at[t, y, x], got_high.at[t], s_down.at[t], r_high.at[t], lower)

    def back_up(t):
        return remote(done.at[t], done.at[t], b_up.at[t], r_back.at[t], higher)

    def back_down(t):
        return remote(done.at[t], done.at[t], b_down.at[t], r_back.at[t], lower)

    def compute(t):
        @pl.when(t >= depth)
        def _():
            to_core(t - depth).wait_send()

        slot = lax.rem(t, depth)
        index = 0
        for k, chunk in enumerate(chunks):
            first = index
            index += len(chunk)

            @pl.when(t == k)
            def _(first=first, chunk=chunk):
                for n in range(first, first + len(chunk)):
                    for copy in fetch(n):
                        copy.wait()
                    if n + 1 < len(jobs):
                        for copy in fetch(n + 1):
                            copy.start()
                    multiply(n, slot)

        to_core(t).start()

    def stage1(t):
        to_core(t).wait_recv()
        slot = lax.rem(t, depth)
        for a in range(2):
            for b in range(2):
                own[t, a, b] = chunk_buf[slot, a, b, c] + got1[t, a, b]
        to_2a(t).start()
        to_2b(t).start()

    def stage2(t):
        to_2a(t).wait_recv()
        for a in range(2):
            own[t, a, x, :, left] = own[t, a, x, :, left] + got2a[t, a]
        to_3a(t).start()
        to_2b(t).wait_recv()
        for a in range(2):
            own[t, y, a, :, right] = own[t, y, a, :, right] + got2b[t, a]
        to_3b(t).start()

    def stage3(t):
        to_3a(t).wait_recv()
        own[t, y, x, :, left] = own[t, y, x, :, left] + got3a[t]
        to_3b(t).wait_recv()
        own[t, y, x, :, right] = own[t, y, x, :, right] + got3b[t]

        @pl.when(z == 0)
        def _():
            up(t).start()

        @pl.when(z == rows_n - 1)
        def _():
            down(t).start()

    def stage4(t):
        @pl.when((z > 0) & (z < root))
        def _():
            up(t).wait_recv()
            own[t, y, x] = own[t, y, x] + got_low[t]
            up(t).start()

        @pl.when((z < rows_n - 1) & (z > root))
        def _():
            down(t).wait_recv()
            own[t, y, x] = own[t, y, x] + got_high[t]
            down(t).start()

    def stage5(t):
        @pl.when(z == root)
        def _():
            up(t).wait_recv()
            down(t).wait_recv()
            total = own[t, y, x].astype(F32) + got_low[t].astype(F32) + got_high[t].astype(F32)
            done[t] = total.astype(BF16)
            back_up(t).start()
            back_down(t).start()

    def stage6(t):
        @pl.when(z > root)
        def _():
            back_up(t).wait_recv()

            @pl.when(z < rows_n - 1)
            def _():
                back_up(t).start()

        @pl.when((z < root) & (z > 0))
        def _():
            back_down(t).wait_recv()
            back_down(t).start()

    def stage7(t):
        @pl.when(z == 0)
        def _():
            back_down(t).wait_recv()

    stages = (compute, stage1, stage2, stage3, stage4, stage5, stage6, stage7)

    def step(s, carry):
        for lag, work in enumerate(stages):
            t = s - lag

            @pl.when((t >= 0) & (t < count))
            def _(t=t, work=work):
                work(t)

        return carry

    lax.fori_loop(0, count + len(stages) - 1, step, 0)

    def finish(t, carry):
        @pl.when(t >= count - depth)
        def _():
            to_core(t).wait_send()

        for copy in (to_2a(t), to_2b(t), to_3a(t), to_3b(t)):
            copy.wait_send()

        @pl.when(z < root)
        def _():
            up(t).wait_send()

        @pl.when(z > root)
        def _():
            down(t).wait_send()

        @pl.when((z >= root) & (z < rows_n - 1))
        def _():
            back_up(t).wait_send()

        @pl.when((z <= root) & (z > 0))
        def _():
            back_down(t).wait_send()

        return carry

    lax.fori_loop(0, count, finish, 0)


def summed_weights(rows_n, ident, operands):
    count = len(plan_jobs())
    low = operands[0].shape[0]
    rows, lanes = CHUNK_ROWS, CHUNK_LANES
    dma = pltpu.SemaphoreType.DMA
    depth = 3
    buffers = [
        (2, low, 1024),
        (2, low, 1024),
        None,
        (depth, 2, 2, 2, rows, lanes),
        (count, 2, 2, rows, lanes),
        (count, 2, 2, rows, lanes),
        (count, 2, rows, lanes // 2),
        (count, 2, rows, lanes // 2),
        (count, rows, lanes // 2),
        (count, rows, lanes // 2),
        (count, rows, lanes),
        (count, rows, lanes),
    ]
    scratch = [pltpu.VMEM(b, BF16) if b else pltpu.VMEM((1024, 512), F32) for b in buffers]
    return pl.pallas_call(
        functools.partial(weights_kernel, rows_n),
        in_specs=[pl.BlockSpec(memory_space=pl.ANY)] * len(operands),
        out_specs=pl.BlockSpec(memory_space=pltpu.VMEM),
        out_shape=jax.ShapeDtypeStruct((count, rows, lanes), BF16),
        scratch_shapes=scratch + [dma((2,)), dma((2,))] + [dma((count,))] * 17,
        compiler_params=pltpu.CompilerParams(
            collective_id=ident, has_side_effects=True, vmem_limit_bytes=63 * 1024 * 1024
        ),
        cost_estimate=pl.CostEstimate(
            flops=40_000_000_000, bytes_accessed=100_000_000, transcendentals=0
        ),
    )(*operands)


def unpack_kernel(sums_n, done, *refs):
    sums, outs = refs[:sums_n], refs[sums_n:]
    in1, mid1, out1, skip, in2, mid2, out2 = outs[:7]
    rows, lanes = CHUNK_ROWS, CHUNK_LANES
    half = lanes // 2

    def wide(k):
        return done[k].astype(F32)

    def stacked(first, count, parts, out):
        width = lanes // parts
        for k in range(count):
            for h in range(parts):
                piece = done[first + k, :, h * width : (h + 1) * width]
                out[h * rows : (h + 1) * rows, k * width : (k + 1) * width] = piece.astype(F32)

    for k in range(2):
        out2[:, k * lanes : (k + 1) * lanes] = wide(k)
        out1[:, k * lanes : (k + 1) * lanes] = wide(10 + k)
    taps2 = [(2 + k // 2, k % 2) for k in range(8)] + [(6, 0)]
    taps1 = [(19, 1), (17, 0), (18, 0), (16, 1), (6, 1), (16, 0), (19, 0), (17, 1), (18, 1)]
    for out, taps in ((mid1, taps1), (mid2, taps2)):
        for k, (chunk, side) in enumerate(taps):
            out[k] = done[chunk, :, side * half : (side + 1) * half].astype(F32)
    stacked(7, 2, 4, in2)
    stacked(9, 1, 2, in1)
    stacked(12, 4, 2, skip)
    rest = list(outs[7:])
    for ref in sums:
        for k in range(ref.shape[0]):
            rest.pop(0)[...] = ref[k : k + 1, :]


def unpack(done, sums):
    rows = CHUNK_ROWS
    shapes = [(128, 512), (9, rows, 512), (rows, 2048), (128, 2048), (256, 512), (9, rows, 512), (rows, 2048)]
    shapes += [(1, x.shape[1]) for x in sums for _ in range(x.shape[0])]
    vmem = pl.BlockSpec(memory_space=pltpu.VMEM)
    outs = pl.pallas_call(
        functools.partial(unpack_kernel, len(sums)),
        in_specs=[vmem] * (1 + len(sums)),
        out_specs=[vmem] * len(shapes),
        out_shape=[jax.ShapeDtypeStruct(shape, F32) for shape in shapes],
        compiler_params=pltpu.CompilerParams(vmem_limit_bytes=32 * 1024 * 1024),
    )(done, *sums)
    return outs[:7], [x.reshape(-1) for x in outs[7:]]


def masks_kernel(rows_low, extent, mask_in, mask_out, mask_above, mask_edges):
    side = extent[...]
    side_low = side // 2
    low0 = lax.axis_index("rows") * rows_low
    column = lax.broadcasted_iota(jnp.int32, side.shape, 1)

    def inside(row, col, limit):
        kept = (row >= 0) & (row < limit) & (col < limit)
        return jnp.where(kept, 1.0, 0.0).astype(BF16)

    for i in range(rows_low):
        for p in range(2):
            for q in range(2):
                mask_in[2 * p + q, :, i] = inside(2 * (low0 + i) + p, 2 * column + q, side)
        mask_out[:, i] = inside(low0 + i, column, side_low)
    for q in range(2):
        mask_above[q, :, 0] = inside(2 * low0 - 1, 2 * column + q, side)
    mask_edges[0, :, 0] = inside(low0 - 1, column, side_low)
    mask_edges[1, :, 0] = inside(low0 + rows_low, column, side_low)


def masks_of(extent, rows_low):
    images, columns, lanes = extent.shape
    vmem = pl.BlockSpec(memory_space=pltpu.VMEM)
    shapes = [
        (4, images, rows_low, columns, lanes),
        (images, rows_low, columns, lanes),
        (2, images, 1, columns, lanes),
        (2, images, 1, columns, lanes),
    ]
    return pl.pallas_call(
        functools.partial(masks_kernel, rows_low),
        in_specs=[vmem],
        out_specs=[vmem] * 4,
        out_shape=[jax.ShapeDtypeStruct(shape, BF16) for shape in shapes],
        compiler_params=pltpu.CompilerParams(vmem_limit_bytes=24 * 1024 * 1024),
    )(extent)


def body(
    image_in,
    extent,
    weight_in1,
    weight_mid1,
    weight_out1,
    weight_skip,
    weight_in2,
    weight_mid2,
    weight_out2,
    gain_in1,
    shift_in1,
    gain_mid1,
    shift_mid1,
    gain_out1,
    shift_out1,
    gain_skip,
    shift_skip,
    gain_in2,
    shift_in2,
    gain_mid2,
    shift_mid2,
    gain_out2,
    shift_out2,
    cotangent,
):
    images, rows_here, columns, inputs = image_in.shape
    middle, outputs = weight_out1.shape
    rows_low, cols_low = rows_here // 2, columns // 2
    low = images * rows_low * cols_low
    rows_n, img_n = lax.axis_size("rows"), lax.axis_size("img")
    blocks = images // IMAGES
    per_block = low // blocks
    edge = images * cols_low
    run = Exchange(rows_n, img_n, blocks)
    upto = 3 * blocks // 5

    def early_blocks(x):
        shape = (x.shape[0], edge // blocks, x.shape[2])
        return x, pl.BlockSpec(shape, lambda b: (0, jnp.minimum(b, upto - 1), 0))

    def late_blocks(x):
        shape = (x.shape[0], edge // blocks, x.shape[2])
        return x, pl.BlockSpec(shape, lambda b: (0, jnp.maximum(b - upto, 0), 0))


    columns8 = jnp.broadcast_to(extent[:, None, None], (images, cols_low, 128))
    mask_in, mask_out, mask_above, mask_edges = (
        m.reshape(m.shape[:-4] + (-1, 128)) for m in masks_of(columns8, rows_low)
    )

    group_images = 256 // (rows_here * columns)
    order = np.arange(256).reshape(group_images, rows_low, 2, cols_low, 2)
    order = order.transpose(2, 4, 0, 1, 3).reshape(-1)
    perm = jnp.asarray(np.eye(256, dtype=np.float32)[order], BF16)

    def row(vector):
        return vector.reshape(1, -1)

    g_in1, s_in1, g_mid1, s_mid1 = row(gain_in1), row(shift_in1), row(gain_mid1), row(shift_mid1)
    g_out1, s_out1, g_skip, s_skip = row(gain_out1), row(shift_out1), row(gain_skip), row(shift_skip)
    g_in2, s_in2, g_mid2, s_mid2 = row(gain_in2), row(shift_in2), row(gain_mid2), row(shift_mid2)
    g_out2, s_out2 = row(gain_out2), row(shift_out2)
    kernel_mid1 = weight_mid1.transpose(1, 2, 0, 3).reshape(9 * middle, middle)
    kernel_mid2 = weight_mid2.transpose(1, 2, 0, 3).reshape(9 * middle, middle)
    cot = cotangent.reshape(low, outputs)

    dev_mid_out = [((low, middle), BF16, BY_ROWS), ((blocks, 1, middle), F32, BY_BLOCK)]
    dev_out_out = [((low, outputs), BF16, BY_ROWS), ((blocks, 1, outputs), F32, BY_BLOCK)]
    hidden_out = [((low, middle), BF16, BY_ROWS)]
    wide_out = [((low, outputs), BF16, BY_ROWS)]
    late_mid, late_wide = [hidden_out[0] + (True,)], [wide_out[0] + (True,)]
    acc_mid, acc_out = ((per_block, middle), F32), ((per_block, outputs), F32)
    unit_flops = 2 * low * middle * middle

    def normal(dev, centre, stats, gain, shift, kind=BY_ROWS):
        return [(dev, kind), (centre, BY_BLOCK), (stats, WHOLE), (gain, WHOLE), (shift, WHOLE)]

    planes, d_in1, c_in1, d_skip, c_skip, n_in1, n_skip, halo_in1, halo_c_in1 = run(
        open_kernel,
        [
            (image_in.reshape(4 * low, inputs), BY_ROWS),
            (perm, WHOLE),
            (mask_in, BY_PLANES),
            (mask_out, BY_ROWS),
            (weight_in1, WHOLE),
            (weight_skip, WHOLE),
        ],
        [
            ((4, low, inputs), BF16, BY_PLANES, True),
            ((4, low, middle), BF16, BY_PLANES),
            ((blocks, 1, middle), F32, BY_BLOCK),
        ]
        + dev_out_out,
        True,
        3,
        (middle, outputs),
        scratch=[((4, per_block, middle), F32), acc_out],
        flops=20 * unit_flops,
        edges=[(1, 2, True, 1), (1, 3, True, 1)],
        centres=(2, (1,)),
        edge=edge,
        early=True,
    )
    hid_in1, d_mid1, c_mid1, edges_mid1, n_mid1, halo_mid1, halo_c_mid1 = run(
        functools.partial(mid1_kernel, rows_low),
        [
            (d_in1, BY_PLANES),
            (c_in1, BY_BLOCK),
            (mask_in, BY_PLANES),
            (halo_in1, BY_PLANES),
            (halo_c_in1[0], BY_BLOCK),
            (mask_above, BY_PLANES),
            (n_in1, WHOLE),
            (g_in1, WHOLE),
            (s_in1, WHOLE),
            (mask_out, BY_ROWS),
            (kernel_mid1, WHOLE),
        ],
        [((4, low, middle), BF16, BY_PLANES, True)] + dev_mid_out,
        True,
        3,
        (middle,),
        scratch=[((5, per_block, middle), BF16), acc_mid],
        flops=9 * unit_flops,
        edges=[(1, None, False, -1)],
        upto=upto,
        centres=(2, (-1,)),
        edge=edge,
    )
    hid_mid1, d_out1, c_out1, n_out1, rest_mid1 = run(
        expand_kernel,
        normal(d_mid1, c_mid1, n_mid1, g_mid1, s_mid1) + [(mask_out, BY_ROWS), (weight_out1, WHOLE)],
        late_mid + dev_out_out,
        True,
        3,
        (outputs,),
        scratch=[acc_out],
        relay=(edges_mid1, (-1,)),
        flops=4 * unit_flops,
    )
    join = normal(d_out1, c_out1, n_out1, g_out1, s_out1) + normal(d_skip, c_skip, n_skip, g_skip, s_skip)
    both = [(1, None, True, 1), (1, None, False, -1)]
    first_low, d_in2, c_in2, n_in2, halo_in2, halo_c_in2 = run(
        join_kernel,
        join + [(mask_out, BY_ROWS), (weight_in2, WHOLE)],
        wide_out + dev_mid_out,
        True,
        3,
        (middle,),
        scratch=[acc_mid],
        flops=4 * unit_flops,
        defer=2,
        edges=both,
        centres=(2, (1, -1)),
        edge=edge,
    )

    hid_in2, d_mid2, c_mid2, edges_mid2, n_mid2, halo_mid2, halo_c_mid2 = run(
        functools.partial(mid2_kernel, rows_low),
        [
            (d_in2, BY_ROWS),
            (c_in2, BY_BLOCK),
            (halo_in2, BY_PLANES),
            (halo_c_in2, PAIR_BLOCK),
            (mask_edges, BY_PLANES),
            (n_in2, WHOLE),
            (g_in2, WHOLE),
            (s_in2, WHOLE),
            (mask_out, BY_ROWS),
            (kernel_mid2, WHOLE),
        ],
        late_mid + dev_mid_out,
        True,
        3,
        (middle,),
        scratch=[((per_block, 9 * middle), BF16), acc_mid],
        flops=9 * unit_flops,
        edges=both,
        upto=upto,
        centres=(2, (1, -1)),
        edge=edge,
    )
    hid_mid2, d_out2, c_out2, n_out2, rest_mid2 = run(
        expand_kernel,
        normal(d_mid2, c_mid2, n_mid2, g_mid2, s_mid2) + [(mask_out, BY_ROWS), (weight_out2, WHOLE)],
        late_mid + dev_out_out,
        True,
        3,
        (outputs,),
        scratch=[acc_out],
        relay=(edges_mid2, (1, -1)),
        flops=4 * unit_flops,
    )
    block_out, gn_out2, z_out2 = run(
        final_kernel,
        normal(d_out2, c_out2, n_out2, g_out2, s_out2)
        + [(first_low, BY_ROWS), (cot, BY_ROWS), (mask_out, BY_ROWS)],
        late_wide + wide_out,
        False,
        2,
        (outputs,),
    )

    ga_out2, gn_mid2, z_mid2, halo_gn_mid2 = run(
        back_expand_kernel,
        [
            (gn_out2, BY_ROWS),
            (d_out2, BY_ROWS),
            (c_out2, BY_BLOCK),
            (n_out2, WHOLE),
            (g_out2, WHOLE),
            (z_out2, WHOLE),
            (mask_out, BY_ROWS),
            (weight_out2, WHOLE),
        ]
        + normal(d_mid2, c_mid2, n_mid2, g_mid2, s_mid2),
        late_wide + hidden_out,
        False,
        2,
        (middle,),
        scratch=[acc_mid],
        flops=4 * unit_flops,
        defer=2,
        edges=both,
        edge=edge,
    )
    views2, gn_in2, z_in2 = run(
        functools.partial(back_mid2_kernel, rows_low, upto),
        [
            (gn_mid2, BY_ROWS),
            (d_mid2, BY_ROWS),
            (c_mid2, BY_BLOCK),
            (halo_gn_mid2, BY_PLANES),
            early_blocks(halo_mid2),
            late_blocks(rest_mid2),
            (halo_c_mid2, PAIR_BLOCK),
            (mask_edges, BY_PLANES),
            (n_mid2, WHOLE),
            (g_mid2, WHOLE),
            (z_mid2, WHOLE),
            (mask_out, BY_ROWS),
            (kernel_mid2, WHOLE),
        ]
        + normal(d_in2, c_in2, n_in2, g_in2, s_in2),
        [((low, 9 * middle), BF16, BY_ROWS, True)] + hidden_out,
        False,
        2,
        (middle,),
        scratch=[acc_mid],
        flops=9 * unit_flops,
    )
    ga_in2, gs1, z_sum1 = run(
        back_join_kernel,
        [
            (gn_in2, BY_ROWS),
            (d_in2, BY_ROWS),
            (c_in2, BY_BLOCK),
            (n_in2, WHOLE),
            (g_in2, WHOLE),
            (z_in2, WHOLE),
            (mask_out, BY_ROWS),
            (weight_in2, WHOLE),
            (gn_out2, BY_ROWS),
        ]
        + join,
        late_mid + wide_out,
        False,
        3,
        (outputs,),
        scratch=[acc_out],
        flops=4 * unit_flops,
    )

    ga_out1, ga_skip, gn_mid1, grad_skip_in, z_mid1, halo_gn_mid1 = run(
        back_split_kernel,
        [
            (gs1, BY_ROWS),
            (d_out1, BY_ROWS),
            (c_out1, BY_BLOCK),
            (n_out1, WHOLE),
            (g_out1, WHOLE),
            (d_skip, BY_ROWS),
            (c_skip, BY_BLOCK),
            (n_skip, WHOLE),
            (g_skip, WHOLE),
            (z_sum1, WHOLE),
            (mask_out, BY_ROWS),
            (weight_out1, WHOLE),
            (weight_skip, WHOLE),
        ]
        + normal(d_mid1, c_mid1, n_mid1, g_mid1, s_mid1),
        late_wide + late_wide + hidden_out + [((low, inputs), BF16, BY_ROWS, True)],
        False,
        2,
        (middle,),
        scratch=[acc_mid, ((per_block, inputs), F32)],
        flops=12 * unit_flops,
        edges=[(2, None, False, -1)],
        edge=edge,
    )
    views1, gn_in1, z_in1 = run(
        functools.partial(back_mid1_kernel, rows_low, upto),
        [
            (gn_mid1, BY_ROWS),
            (d_mid1, BY_ROWS),
            (c_mid1, BY_BLOCK),
            (halo_gn_mid1[0], BY_ROWS),
            early_blocks(halo_mid1),
            late_blocks(rest_mid1),
            (halo_c_mid1[0], BY_BLOCK),
            (mask_edges[1], BY_ROWS),
            (n_mid1, WHOLE),
            (g_mid1, WHOLE),
            (z_mid1, WHOLE),
            (mask_out, BY_ROWS),
            (kernel_mid1, WHOLE),
            (d_in1, BY_PLANES),
            (c_in1, BY_BLOCK),
            (mask_in, BY_PLANES),
            (n_in1, WHOLE),
            (g_in1, WHOLE),
            (s_in1, WHOLE),
        ],
        [((low, 4 * middle), BF16, BY_ROWS, True), ((4, low, middle), BF16, BY_PLANES)],
        False,
        2,
        (middle,),
        scratch=[((4, per_block, middle), F32)],
        flops=9 * unit_flops,
    )
    ga_in1, grad_image, block_out = stage(
        back_image_kernel,
        blocks,
        [
            (gn_in1, BY_PLANES),
            (d_in1, BY_PLANES),
            (c_in1, BY_BLOCK),
            (n_in1, WHOLE),
            (g_in1, WHOLE),
            (z_in1, WHOLE),
            (mask_in, BY_PLANES),
            (weight_in1, WHOLE),
            (grad_skip_in, BY_ROWS),
            (perm, WHOLE),
            (block_out, BY_ROWS),
        ],
        [((4, low, middle), BF16, BY_PLANES, True), ((4 * low, inputs), BF16, BY_ROWS)] + wide_out,
        scratch=[((4, per_block, inputs), BF16)],
        flops=12 * unit_flops,
    )
    sums = [z_in1, z_mid1, z_sum1, z_in2, z_mid2, z_out2]

    if (rows_n, img_n) == (4, 8):
        done = summed_weights(
            rows_n,
            run.calls,
            [
                hid_mid2,
                ga_out2,
                hid_in2,
                views2,
                first_low,
                ga_in2,
                hid_mid1,
                ga_out1,
                planes,
                ga_skip,
                hid_in1,
                views1,
                ga_in1,
            ],
        )
        grads, rows_of = unpack(done, sums)
        dw_in1, dw_mid1, dw_out1, dw_skip, dw_in2, dw_mid2, dw_out2 = grads
        dw_mid1, dw_mid2 = (
            g.reshape(3, 3, -1, middle).transpose(2, 0, 1, 3) for g in (dw_mid1, dw_mid2)
        )
    else:
        def weight_term(values, upstream):
            return lax.dot_general(
                values, upstream, (((0,), (0,)), ((), ())), preferred_element_type=F32
            ).astype(BF16)

        def reduced(grad):
            shard = lax.psum_scatter(grad, "img", scatter_dimension=0, tiled=True)
            return lax.psum(shard, "rows").astype(F32)

        dw_out2 = reduced(weight_term(hid_mid2, ga_out2))
        dw_mid2 = reduced(weight_term(hid_in2, views2))
        dw_in2 = reduced(weight_term(first_low, ga_in2))
        dw_out1 = reduced(weight_term(hid_mid1, ga_out1))
        dw_skip = reduced(weight_term(planes[0], ga_skip))
        m = middle
        dw_00 = weight_term(hid_in1[0], views1[:, m : 2 * m])
        dw_01 = weight_term(hid_in1[1], views1[:, m : 3 * m])
        dw_10 = weight_term(hid_in1[2], views1[:, : 2 * m])
        dw_11 = weight_term(hid_in1[3], views1)
        dw_mid1 = jnp.concatenate(
            [
                dw_11[:, 3 * m :],
                dw_10[:, :m],
                dw_11[:, :m],
                dw_01[:, m:],
                dw_00,
                dw_01[:, :m],
                dw_11[:, 2 * m : 3 * m],
                dw_10[:, m:],
                dw_11[:, m : 2 * m],
            ],
            axis=1,
        )
        dw_mid1 = reduced(dw_mid1)
        dw_in1 = reduced(
            weight_term(planes.reshape(4 * low, inputs), ga_in1.reshape(4 * low, middle))
        )
        rows_of = [x[k] for x in sums for k in range(x.shape[0])]
    kernel_shape = (middle // img_n, 3, 3, middle)
    (
        shift_in1_g,
        gain_in1_g,
        shift_mid1_g,
        gain_mid1_g,
        shift_sum1_g,
        gain_out1_g,
        gain_skip_g,
        shift_in2_g,
        gain_in2_g,
        shift_mid2_g,
        gain_mid2_g,
        shift_out2_g,
        gain_out2_g,
    ) = rows_of
    return (
        block_out.reshape(images, rows_low, cols_low, outputs),
        grad_image.reshape(images, rows_here, columns, inputs),
        dw_in1,
        dw_mid1.reshape(kernel_shape),
        dw_out1,
        dw_skip,
        dw_in2,
        dw_mid2.reshape(kernel_shape),
        dw_out2,
        gain_in1_g,
        shift_in1_g,
        gain_mid1_g,
        shift_mid1_g,
        gain_out1_g,
        shift_sum1_g,
        gain_skip_g,
        shift_sum1_g,
        gain_in2_g,
        shift_in2_g,
        gain_mid2_g,
        shift_mid2_g,
        gain_out2_g,
        shift_out2_g,
    )


def solution(mesh):
    image = P("img", "rows", None, None)
    in_specs = (image, P("img")) + (P(),) * 21 + (image,)
    out_specs = (
        image,
        image,
        P("img", None),
        P("img", None, None, None),
        P("img", None),
        P("img", None),
        P("img", None),
        P("img", None, None, None),
        P("img", None),
    ) + (P(),) * 14
    return jax.shard_map(body, mesh=mesh, in_specs=in_specs, out_specs=out_specs, check_vma=False)
```

```python
import functools

import jax
import jax.numpy as jnp
import numpy as np
from jax import lax
from jax.experimental import pallas as pl
from jax.experimental.pallas import tpu as pltpu
from jax.sharding import PartitionSpec as P

EPSILON = 1e-05
F32 = jnp.float32
BF16 = jnp.bfloat16
LANES = 512
ROWS = 32
IMAGES = 16
VMEM_BYTES = 48 * 1024 * 1024
MESH = pl.DeviceIdType.MESH
BY_ROWS, BY_PLANES, FIRST_PLANE, BY_BLOCK, PAIR_BLOCK, WHOLE, APART = range(7)


def dot(a, b):
    return jnp.dot(a, b, preferred_element_type=F32)


def dot_t(a, b):
    return lax.dot_general(a, b, (((1,), (1,)), ((), ())), preferred_element_type=F32)


def load(ref, rows, lanes):
    value = ref[rows, lanes].astype(F32)
    return value.reshape(value.shape[0] // 8, 8, value.shape[1])


def store(ref, rows, lanes, value):
    ref[rows, lanes] = value.reshape(value.shape[0] * 8, value.shape[2]).astype(ref.dtype)


def load_mask(ref, rows):
    mask = load(ref, rows, slice(None))
    return jnp.concatenate([mask] * (LANES // 128), axis=-1)


def sweep(total, step, init, rows=ROWS):
    def body(i, carry):
        return step(pl.ds(pl.multiple_of(i * rows, rows), rows), i, carry)

    return lax.fori_loop(0, total // rows, body, init, unroll=True)


def lane_blocks(width):
    return [slice(k * LANES, (k + 1) * LANES) for k in range(width // LANES)]


def tall(row):
    return jnp.broadcast_to(row, (8, row.shape[-1]))


def column_sum(value):
    return jnp.sum(value, axis=0)


def total_of(part):
    return jnp.sum(part, axis=0, keepdims=True)


def zeros8():
    return jnp.zeros((8, LANES), F32)


def tally(first, parts, centre_ref, stats_ref, fill=None):
    width = parts[0][0].shape[-1]
    for lanes in lane_blocks(width):
        if fill is not None:
            fill(lanes)
        sums = (zeros8(), zeros8())
        for acc, mask_ref, dev in parts:

            def add(rows, i, carry, acc=acc, mask_ref=mask_ref):
                mask = load_mask(mask_ref, rows)
                return (
                    carry[0] + column_sum(load(acc, rows, lanes) * mask),
                    carry[1] + column_sum(mask),
                )

            sums = sweep(acc.shape[0], add, sums)
        total, count = total_of(sums[0]), total_of(sums[1])
        centre = total / jnp.maximum(count, 1.0)
        centre_ref[:, lanes] = centre
        centre8 = tall(centre)
        squares = zeros8()
        for acc, mask_ref, dev in parts:

            def square(rows, i, carry, acc=acc, mask_ref=mask_ref, dev=dev):
                away = load(acc, rows, lanes) - centre8
                store(dev, rows, lanes, away)
                return carry + column_sum(load_mask(mask_ref, rows) * away * away)

            squares = sweep(acc.shape[0], square, squares)
        squares = total_of(squares)
        count_old, mean_old, squares_old = (
            jnp.where(first, jnp.zeros_like(count), stats_ref[k : k + 1, lanes]) for k in range(3)
        )
        both = count_old + count
        share = count / jnp.maximum(both, 1.0)
        delta = centre - mean_old
        stats_ref[0:1, lanes] = both
        stats_ref[1:2, lanes] = mean_old + delta * share
        stats_ref[2:3, lanes] = squares_old + squares + delta * delta * count_old * share


def affine(stats_ref, gain_ref, shift_ref, centre_ref, lanes):
    scale = lax.rsqrt(stats_ref[2:3, lanes] + EPSILON)
    slope = gain_ref[:, lanes] * scale
    base = shift_ref[:, lanes] + (centre_ref[:, lanes] - stats_ref[1:2, lanes]) * slope
    return tall(0.5 * slope), tall(0.5 * base)


def silu_half(half):
    return half + half * jnp.tanh(half)


def gate_half(half):
    tanh = jnp.tanh(half)
    return (0.5 + 0.5 * tanh) * (1.0 + half * (1.0 - tanh))


def silu_and_gate(half):
    tanh = jnp.tanh(half)
    return half + half * tanh, (0.5 + 0.5 * tanh) * (1.0 + half * (1.0 - tanh))


def back_coefs(stats_ref, gain_ref, centre_ref, sums, lanes):
    shift_sum, gain_sum = sums
    pixels = stats_ref[0:1, lanes]
    scale = lax.rsqrt(stats_ref[2:3, lanes] + EPSILON)
    slope = gain_ref[:, lanes] * scale
    per_pixel = slope / pixels
    away = (centre_ref[:, lanes] - stats_ref[1:2, lanes]) * scale
    return (
        tall(slope),
        tall(-per_pixel * scale * gain_sum),
        tall(-per_pixel * (shift_sum + away * gain_sum)),
    )


def unit_sum(stats_ref, centre_ref, lanes, gn_sum, gd_sum):
    scale = lax.rsqrt(stats_ref[2:3, lanes] + EPSILON)
    return scale * (gd_sum + (centre_ref[:, lanes] - stats_ref[1:2, lanes]) * gn_sum)


def accumulate(first, ref, row, lanes, value):
    old = jnp.where(first, jnp.zeros_like(value), ref[row : row + 1, lanes])
    ref[row : row + 1, lanes] = old + value


def shifted(value, by):
    if by == 0:
        return value
    rolled = pltpu.roll(value, (-by) % 8, axis=1)
    column = lax.broadcasted_iota(jnp.int32, value.shape, 1)
    return jnp.where(column == (0 if by < 0 else 7), 0.0, rolled)


def from_above(value, edge, rows_low):
    if rows_low == 1:
        return edge
    images = value.shape[0] // rows_low
    image = value.reshape((images, rows_low) + value.shape[1:])
    return jnp.concatenate([edge[:, None], image[:, :-1]], axis=1).reshape(value.shape)


def from_below(value, edge, rows_low):
    if rows_low == 1:
        return edge
    images = value.shape[0] // rows_low
    image = value.reshape((images, rows_low) + value.shape[1:])
    return jnp.concatenate([image[:, 1:], edge[:, None]], axis=1).reshape(value.shape)


def edge_rows(i, rows_low):
    return pl.ds(pl.multiple_of(i * (ROWS // rows_low), ROWS // rows_low), ROWS // rows_low)


def either(upto, early, late, rows, lanes):
    here = pl.program_id(0) < upto
    return jnp.where(here, load(early, rows, lanes), load(late, rows, lanes))


def first_step():
    return pl.program_id(0) == 0


def open_kernel(
    image_ref,
    perm_ref,
    mask_ref,
    mask_out,
    weight_ref,
    weight_skip,
    planes_ref,
    dev_ref,
    centre_ref,
    dev_skip,
    centre_skip,
    stats_ref,
    acc,
    acc_skip,
    flush,
):
    planes, low, _ = planes_ref.shape
    group = perm_ref.shape[0]
    part = group // planes
    for g in range(image_ref.shape[0] // group):
        mask = jnp.concatenate(
            [mask_ref[p, g * part : (g + 1) * part, :] for p in range(planes)], axis=0
        )
        mask = jnp.concatenate([mask] * (group // 128), axis=1)
        perm = perm_ref[...] * mask
        moved = dot(perm, image_ref[g * group : (g + 1) * group, :]).astype(BF16)
        for p in range(planes):
            planes_ref[p, g * part : (g + 1) * part, :] = moved[p * part : (p + 1) * part]
    for p in range(planes):
        acc[p] = dot(planes_ref[p], weight_ref[...])
    width = acc.shape[-1]
    tally(
        first_step(),
        [(acc.at[p], mask_ref.at[p], dev_ref.at[p]) for p in range(planes)],
        centre_ref,
        stats_ref.at[:, :width],
    )
    flush()

    def fill(lanes):
        acc_skip[:, lanes] = dot(planes_ref[0], weight_skip[:, lanes])

    tally(first_step(), [(acc_skip, mask_out, dev_skip)], centre_skip, stats_ref.at[:, width:], fill)


def mid1_kernel(
    rows_low,
    dev_in,
    centre_in,
    mask_ref,
    halo,
    halo_centre,
    halo_mask,
    stats_in,
    gain,
    shift,
    mask_out,
    weight,
    hidden,
    dev_out,
    centre_out,
    stats_out,
    taps,
    acc,
):
    low, width = acc.shape
    steps = []
    for lanes in lane_blocks(width):
        slope, base = affine(stats_in, gain, shift, centre_in, lanes)
        slope_edge, base_edge = affine(stats_in, gain, shift, halo_centre, lanes)

        def act(p, rows, lanes=lanes, slope=slope, base=base):
            mask = load_mask(mask_ref.at[p], rows)
            value = silu_half(load(dev_in.at[p], rows, lanes) * slope + base) * mask
            store(hidden.at[p], rows, lanes, value)
            return value

        def act_edge(q, i, lanes=lanes, slope_edge=slope_edge, base_edge=base_edge):
            rows = edge_rows(i, rows_low)
            half = load(halo.at[q], rows, lanes) * slope_edge + base_edge
            return silu_half(half) * load_mask(halo_mask.at[q], rows)

        def step0(rows, i, carry):
            act(0, rows)
            return carry

        def step1(rows, i, carry):
            store(taps.at[0], rows, lanes, shifted(act(1, rows), -1))
            return carry

        def step2(rows, i, carry):
            store(taps.at[1], rows, lanes, from_above(act(2, rows), act_edge(0, i), rows_low))
            return carry

        def step3(rows, i, carry):
            odd = act(3, rows)
            store(taps.at[2], rows, lanes, shifted(odd, -1))
            above = from_above(odd, act_edge(1, i), rows_low)
            store(taps.at[3], rows, lanes, above)
            store(taps.at[4], rows, lanes, shifted(above, -1))
            return carry

        steps.append((step0, step1, step2, step3))

    def tap(t, u):
        k = (3 * t + u) * width
        return weight[k : k + width]

    def plane(p):
        for some in steps:
            sweep(low, some[p], 0)

    plane(0)
    plane(1)
    acc[...] = dot(hidden[0], tap(1, 1))
    plane(2)
    acc[...] += dot(hidden[1], tap(1, 2)) + dot(taps[0], tap(1, 0))
    plane(3)
    acc[...] += dot(hidden[2], tap(2, 1)) + dot(taps[1], tap(0, 1))
    acc[...] += (
        dot(hidden[3], tap(2, 2))
        + dot(taps[2], tap(2, 0))
        + dot(taps[3], tap(0, 2))
        + dot(taps[4], tap(0, 0))
    )
    tally(first_step(), [(acc, mask_out, dev_out)], centre_out, stats_out)


def expand_kernel(
    dev_in, centre_in, stats_in, gain, shift, mask, weight, hidden, dev_out, centre_out, stats_out, acc
):
    for lanes in lane_blocks(dev_in.shape[1]):
        slope, base = affine(stats_in, gain, shift, centre_in, lanes)

        def step(rows, i, carry):
            half = load(dev_in, rows, lanes) * slope + base
            store(hidden, rows, lanes, silu_half(half) * load_mask(mask, rows))
            return carry

        sweep(dev_in.shape[0], step, 0)

    def fill(lanes):
        acc[:, lanes] = dot(hidden[...], weight[:, lanes])

    tally(first_step(), [(acc, mask, dev_out)], centre_out, stats_out, fill)


def join_kernel(
    dev_a,
    centre_a,
    stats_a,
    gain_a,
    shift_a,
    dev_b,
    centre_b,
    stats_b,
    gain_b,
    shift_b,
    mask,
    weight,
    first_low,
    dev_out,
    centre_out,
    stats_out,
    acc,
):
    for lanes in lane_blocks(dev_a.shape[1]):
        slope_a, base_a = affine(stats_a, gain_a, shift_a, centre_a, lanes)
        slope_b, base_b = affine(stats_b, gain_b, shift_b, centre_b, lanes)
        base = base_a + base_b

        def step(rows, i, carry):
            half = load(dev_a, rows, lanes) * slope_a + load(dev_b, rows, lanes) * slope_b + base
            store(first_low, rows, lanes, silu_half(half) * load_mask(mask, rows))
            return carry

        sweep(dev_a.shape[0], step, 0)
        part = dot(first_low[:, lanes], weight[lanes, :])
        acc[...] = part if lanes.start == 0 else acc[...] + part
    tally(first_step(), [(acc, mask, dev_out)], centre_out, stats_out)


def mid2_kernel(
    rows_low,
    dev_in,
    centre_in,
    halo,
    halo_centre,
    halo_mask,
    stats_in,
    gain,
    shift,
    mask,
    weight,
    hidden,
    dev_out,
    centre_out,
    stats_out,
    taps,
    acc,
):
    low, width = acc.shape
    for lanes in lane_blocks(width):
        slope, base = affine(stats_in, gain, shift, centre_in, lanes)
        edges = [affine(stats_in, gain, shift, halo_centre.at[e], lanes) for e in range(2)]

        def act_edge(e, i):
            rows = edge_rows(i, rows_low)
            half = load(halo.at[e], rows, lanes) * edges[e][0] + edges[e][1]
            return silu_half(half) * load_mask(halo_mask.at[e], rows)

        def step(rows, i, carry):
            value = silu_half(load(dev_in, rows, lanes) * slope + base) * load_mask(mask, rows)
            store(hidden, rows, lanes, value)
            lines = (
                from_above(value, act_edge(0, i), rows_low),
                value,
                from_below(value, act_edge(1, i), rows_low),
            )
            for t in range(3):
                for u in range(3):
                    start = (3 * t + u) * width + lanes.start
                    store(taps, rows, slice(start, start + LANES), shifted(lines[t], u - 1))
            return carry

        sweep(low, step, 0)
    acc[...] = dot(taps[...], weight[...])
    tally(first_step(), [(acc, mask, dev_out)], centre_out, stats_out)


def final_kernel(dev, centre, stats, gain, shift, first_low, cot, mask, block_out, gn_ref, sums):
    first = first_step()
    for lanes in lane_blocks(dev.shape[1]):
        slope, base = affine(stats, gain, shift, centre, lanes)

        def step(rows, i, carry):
            away = load(dev, rows, lanes)
            half = away * slope + base + 0.5 * load(first_low, rows, lanes)
            valid = load_mask(mask, rows)
            value, gate = silu_and_gate(half)
            store(block_out, rows, lanes, value * valid)
            gn = gate * valid * load(cot, rows, lanes)
            store(gn_ref, rows, lanes, gn)
            return carry[0] + column_sum(gn), carry[1] + column_sum(gn * away)

        gn_sum, gd_sum = sweep(dev.shape[0], step, (zeros8(), zeros8()))
        gn_sum, gd_sum = total_of(gn_sum), total_of(gd_sum)
        accumulate(first, sums, 0, lanes, gn_sum)
        accumulate(first, sums, 1, lanes, unit_sum(stats, centre, lanes, gn_sum, gd_sum))


def scaled(gn, away, mask, coefs):
    return (gn * coefs[0] + away * coefs[1] + coefs[2]) * mask


def gate_sums(first, grads, dev, centre, stats, gain, shift, mask, gn_ref, sums, parts, fill=None):
    width = gn_ref.shape[-1]
    planes = range(parts) if parts else [None]
    for lanes in lane_blocks(width):
        slope, base = affine(stats, gain, shift, centre, lanes)
        carry = (zeros8(), zeros8())
        for p in planes:
            if fill is not None and lanes.start == 0:
                fill[p]()
            grad_p, dev_p, mask_p, gn_p = (
                r if p is None else r.at[p] for r in (grads, dev, mask, gn_ref)
            )

            def step(rows, i, carry, grad_p=grad_p, dev_p=dev_p, mask_p=mask_p, gn_p=gn_p):
                away = load(dev_p, rows, lanes)
                gate = gate_half(away * slope + base) * load_mask(mask_p, rows)
                gn = gate * load(grad_p, rows, lanes)
                store(gn_p, rows, lanes, gn)
                return carry[0] + column_sum(gn), carry[1] + column_sum(gn * away)

            carry = sweep(grad_p.shape[0], step, carry)
        gn_sum, gd_sum = total_of(carry[0]), total_of(carry[1])
        accumulate(first, sums, 0, lanes, gn_sum)
        accumulate(first, sums, 1, lanes, unit_sum(stats, centre, lanes, gn_sum, gd_sum))


def back_expand_kernel(
    gn,
    dev,
    centre,
    stats,
    gain,
    sums_in,
    mask,
    weight,
    dev_m,
    centre_m,
    stats_m,
    gain_m,
    shift_m,
    ga,
    gn_m,
    sums_m,
    acc,
):
    for lanes in lane_blocks(dev.shape[1]):
        coefs = back_coefs(
            stats, gain, centre, (sums_in[0:1, lanes], sums_in[1:2, lanes]), lanes
        )

        def step(rows, i, carry):
            away = load(dev, rows, lanes)
            store(ga, rows, lanes, scaled(load(gn, rows, lanes), away, load_mask(mask, rows), coefs))
            return carry

        sweep(dev.shape[0], step, 0)
        part = dot_t(ga[:, lanes], weight[:, lanes])
        acc[...] = part if lanes.start == 0 else acc[...] + part
    gate_sums(first_step(), acc, dev_m, centre_m, stats_m, gain_m, shift_m, mask, gn_m, sums_m, 0)


def back_mid2_kernel(
    rows_low,
    upto,
    gn,
    dev,
    centre,
    halo_gn,
    halo_dev,
    rest_dev,
    halo_centre,
    halo_mask,
    stats,
    gain,
    sums_in,
    mask,
    weight,
    dev_m,
    centre_m,
    stats_m,
    gain_m,
    shift_m,
    views,
    gn_m,
    sums_m,
    acc,
):
    low, width = acc.shape
    for lanes in lane_blocks(width):
        sums = (sums_in[0:1, lanes], sums_in[1:2, lanes])
        coefs = back_coefs(stats, gain, centre, sums, lanes)
        edges = [back_coefs(stats, gain, halo_centre.at[e], sums, lanes) for e in range(2)]

        def edge(e, i):
            rows = edge_rows(i, rows_low)
            return scaled(
                load(halo_gn.at[e], rows, lanes),
                either(upto, halo_dev.at[e], rest_dev.at[e], rows, lanes),
                load_mask(halo_mask.at[e], rows),
                edges[e],
            )

        def step(rows, i, carry):
            value = scaled(
                load(gn, rows, lanes), load(dev, rows, lanes), load_mask(mask, rows), coefs
            )
            lines = (
                from_below(value, edge(1, i), rows_low),
                value,
                from_above(value, edge(0, i), rows_low),
            )
            for t in range(3):
                for u in range(3):
                    start = (3 * t + u) * width + lanes.start
                    store(views, rows, slice(start, start + LANES), shifted(lines[t], 1 - u))
            return carry

        sweep(low, step, 0)
    total = dot_t(views[:, :width], weight[:width])
    for k in range(width, 9 * width, width):
        total += dot_t(views[:, k : k + width], weight[k : k + width])
    acc[...] = total
    gate_sums(first_step(), acc, dev_m, centre_m, stats_m, gain_m, shift_m, mask, gn_m, sums_m, 0)


def back_join_kernel(
    gn_in,
    dev_in,
    centre_in,
    stats_in,
    gain_in,
    sums_in,
    mask,
    weight,
    residual,
    dev_a,
    centre_a,
    stats_a,
    gain_a,
    shift_a,
    dev_b,
    centre_b,
    stats_b,
    gain_b,
    shift_b,
    ga,
    gs_ref,
    sums,
    acc,
):
    first = first_step()
    for lanes in lane_blocks(dev_in.shape[1]):
        coefs = back_coefs(
            stats_in, gain_in, centre_in, (sums_in[0:1, lanes], sums_in[1:2, lanes]), lanes
        )

        def step(rows, i, carry):
            away = load(dev_in, rows, lanes)
            value = scaled(load(gn_in, rows, lanes), away, load_mask(mask, rows), coefs)
            store(ga, rows, lanes, value)
            return carry

        sweep(dev_in.shape[0], step, 0)
    for lanes in lane_blocks(dev_a.shape[1]):
        acc[:, lanes] = dot_t(ga[...], weight[lanes, :])
        slope_a, base_a = affine(stats_a, gain_a, shift_a, centre_a, lanes)
        slope_b, base_b = affine(stats_b, gain_b, shift_b, centre_b, lanes)
        base = base_a + base_b

        def gate(rows, i, carry):
            away_a, away_b = load(dev_a, rows, lanes), load(dev_b, rows, lanes)
            half = away_a * slope_a + away_b * slope_b + base
            grad = load(residual, rows, lanes) + load(acc, rows, lanes)
            gs = gate_half(half) * load_mask(mask, rows) * grad
            store(gs_ref, rows, lanes, gs)
            return (
                carry[0] + column_sum(gs),
                carry[1] + column_sum(gs * away_a),
                carry[2] + column_sum(gs * away_b),
            )

        carry = sweep(dev_a.shape[0], gate, (zeros8(), zeros8(), zeros8()))
        gs_sum, a_sum, b_sum = (total_of(part) for part in carry)
        accumulate(first, sums, 0, lanes, gs_sum)
        accumulate(first, sums, 1, lanes, unit_sum(stats_a, centre_a, lanes, gs_sum, a_sum))
        accumulate(first, sums, 2, lanes, unit_sum(stats_b, centre_b, lanes, gs_sum, b_sum))


def back_split_kernel(
    gs,
    dev_a,
    centre_a,
    stats_a,
    gain_a,
    dev_b,
    centre_b,
    stats_b,
    gain_b,
    sums_in,
    mask,
    weight_a,
    weight_b,
    dev_m,
    centre_m,
    stats_m,
    gain_m,
    shift_m,
    ga_a,
    ga_b,
    gn_m,
    grad_skip,
    sums_m,
    acc,
    acc_skip,
):
    for lanes in lane_blocks(dev_a.shape[1]):
        shift_sum = sums_in[0:1, lanes]
        coefs_a = back_coefs(stats_a, gain_a, centre_a, (shift_sum, sums_in[1:2, lanes]), lanes)
        coefs_b = back_coefs(stats_b, gain_b, centre_b, (shift_sum, sums_in[2:3, lanes]), lanes)

        def step(rows, i, carry):
            value, valid = load(gs, rows, lanes), load_mask(mask, rows)
            store(ga_a, rows, lanes, scaled(value, load(dev_a, rows, lanes), valid, coefs_a))
            store(ga_b, rows, lanes, scaled(value, load(dev_b, rows, lanes), valid, coefs_b))
            return carry

        sweep(dev_a.shape[0], step, 0)
        part = dot_t(ga_a[:, lanes], weight_a[:, lanes])
        acc[...] = part if lanes.start == 0 else acc[...] + part
        part = dot_t(ga_b[:, lanes], weight_b[:, lanes])
        acc_skip[...] = part if lanes.start == 0 else acc_skip[...] + part
    grad_skip[...] = acc_skip[...].astype(BF16)
    gate_sums(first_step(), acc, dev_m, centre_m, stats_m, gain_m, shift_m, mask, gn_m, sums_m, 0)


def back_mid1_kernel(
    rows_low,
    upto,
    gn,
    dev,
    centre,
    halo_gn,
    halo_dev,
    rest_dev,
    halo_centre,
    halo_mask,
    stats,
    gain,
    sums_in,
    mask,
    weight,
    dev_m,
    centre_m,
    mask_m,
    stats_m,
    gain_m,
    shift_m,
    views,
    gn_m,
    sums_m,
    acc,
):
    _, low, width = acc.shape
    for lanes in lane_blocks(width):
        sums = (sums_in[0:1, lanes], sums_in[1:2, lanes])
        coefs = back_coefs(stats, gain, centre, sums, lanes)
        coefs_edge = back_coefs(stats, gain, halo_centre, sums, lanes)

        def step(rows, i, carry):
            value = scaled(
                load(gn, rows, lanes), load(dev, rows, lanes), load_mask(mask, rows), coefs
            )
            some = edge_rows(i, rows_low)
            edge = scaled(
                load(halo_gn, some, lanes),
                either(upto, halo_dev.at[0], rest_dev.at[0], some, lanes),
                load_mask(halo_mask, some),
                coefs_edge,
            )
            below = from_below(value, edge, rows_low)
            for k, view in enumerate((below, value, shifted(value, 1), shifted(below, 1))):
                start = k * width + lanes.start
                store(views, rows, slice(start, start + LANES), view)
            return carry

        sweep(low, step, 0)

    def view(k):
        return views[:, k * width : (k + 1) * width]

    def tap(t, u):
        k = (3 * t + u) * width
        return weight[k : k + width]

    def plane0():
        acc[0] = dot_t(view(1), tap(1, 1))

    def plane1():
        acc[1] = dot_t(view(1), tap(1, 2)) + dot_t(view(2), tap(1, 0))

    def plane2():
        acc[2] = dot_t(view(1), tap(2, 1)) + dot_t(view(0), tap(0, 1))

    def plane3():
        acc[3] = (
            dot_t(view(1), tap(2, 2))
            + dot_t(view(2), tap(2, 0))
            + dot_t(view(0), tap(0, 2))
            + dot_t(view(3), tap(0, 0))
        )

    gate_sums(
        first_step(),
        acc,
        dev_m,
        centre_m,
        stats_m,
        gain_m,
        shift_m,
        mask_m,
        gn_m,
        sums_m,
        4,
        (plane0, plane1, plane2, plane3),
    )


def back_image_kernel(
    gn,
    dev,
    centre,
    stats,
    gain,
    sums_in,
    mask_ref,
    weight,
    grad_skip,
    perm_ref,
    handed,
    ga,
    image,
    hand,
    planes_ref,
):
    planes, low, width = ga.shape
    for p in range(planes):
        for lanes in lane_blocks(width):
            coefs = back_coefs(
                stats, gain, centre, (sums_in[0:1, lanes], sums_in[1:2, lanes]), lanes
            )

            def step(rows, i, carry):
                away = load(dev.at[p], rows, lanes)
                valid = load_mask(mask_ref.at[p], rows)
                value = scaled(load(gn.at[p], rows, lanes), away, valid, coefs)
                store(ga.at[p], rows, lanes, value)
                return carry

            sweep(low, step, 0)
        grad = dot_t(ga[p], weight[...])
        if p == 0:
            grad += grad_skip[...].astype(F32)
        planes_ref[p] = grad.astype(BF16)
    hand[...] = handed[...]
    group = perm_ref.shape[0]
    part = group // planes
    for g in range(image.shape[0] // group):
        rows = slice(g * part, (g + 1) * part)
        mask = jnp.concatenate([mask_ref[p, rows, :] for p in range(planes)], axis=0)
        mask = jnp.concatenate([mask] * (group // 128), axis=1)
        perm = perm_ref[...] * mask
        here = jnp.concatenate([planes_ref[p, rows, :] for p in range(planes)], axis=0)
        back = lax.dot_general(
            perm, here, (((0,), (0,)), ((), ())), preferred_element_type=F32
        )
        image[g * group : (g + 1) * group, :] = back.astype(BF16)


def spec_of(shape, kind, blocks):
    if isinstance(kind, pl.BlockSpec):
        return kind
    if kind == BY_ROWS:
        return pl.BlockSpec((shape[0] // blocks, shape[1]), lambda b: (b, 0))
    if kind == BY_PLANES:
        return pl.BlockSpec((shape[0], shape[1] // blocks, shape[2]), lambda b: (0, b, 0))
    if kind == FIRST_PLANE:
        return pl.BlockSpec((None, shape[1] // blocks, shape[2]), lambda b: (0, b, 0))
    if kind == BY_BLOCK:
        return pl.BlockSpec((None,) + tuple(shape[1:]), lambda b: (b, 0, 0))
    if kind == PAIR_BLOCK:
        return pl.BlockSpec((2, None) + tuple(shape[2:]), lambda b: (0, b, 0, 0))
    if kind == APART:
        return pl.BlockSpec(memory_space=pl.ANY)
    zero = (0,) * len(shape)
    return pl.BlockSpec(tuple(shape), lambda b: zero, pipeline_mode=pl.Buffered(1))


def out_spec(shape, kind, blocks):
    if not isinstance(kind, pl.BlockSpec) and kind == WHOLE:
        zero = (0,) * len(shape)
        return pl.BlockSpec(tuple(shape), lambda b: zero)
    return spec_of(shape, kind, blocks)


def placed(shape, dtype, kind, late=False):
    return pltpu.HBM(shape, dtype) if late else jax.ShapeDtypeStruct(shape, dtype)


def stage(kernel, blocks, ins, outs, scratch=(), flops=0):
    return call(kernel, blocks, ins, outs, scratch, flops, [], [], {})


def call(kernel, blocks, ins, outs, scratch, flops, more_specs, more_shapes, params):
    moved = sum(x.size * x.dtype.itemsize for x, _ in ins)
    moved += sum(int(np.prod(item[0])) * jnp.dtype(item[1]).itemsize for item in outs)
    made = [pltpu.VMEM(*item) if isinstance(item, tuple) else item for item in scratch]
    return pl.pallas_call(
        kernel,
        grid=(blocks,),
        in_specs=[spec_of(x.shape, kind, blocks) for x, kind in ins],
        out_specs=[out_spec(item[0], item[2], blocks) for item in outs] + more_specs,
        out_shape=[placed(*item) for item in outs] + more_shapes,
        scratch_shapes=made,
        compiler_params=pltpu.CompilerParams(
            dimension_semantics=("arbitrary",), vmem_limit_bytes=VMEM_BYTES, **params
        ),
        cost_estimate=pl.CostEstimate(flops=flops, bytes_accessed=moved, transcendentals=0),
    )(*[x for x, _ in ins])


def merge_rows(buf, peers, merge, mean_only):
    if not merge:
        total = buf[0]
        for k in range(1, peers):
            total = total + buf[k]
        return total
    counts = [buf[k, 0:1, :] for k in range(peers)]
    means = [buf[k, 1:2, :] for k in range(peers)]
    count, weighted = counts[0], counts[0] * means[0]
    for k in range(1, peers):
        count = count + counts[k]
        weighted = weighted + counts[k] * means[k]
    safe = jnp.maximum(count, 1.0)
    mean = weighted / safe
    squares = jnp.zeros_like(mean)
    for k in range(peers):
        squares = squares + buf[k, 2:3, :] + counts[k] * jnp.square(means[k] - mean)
    if mean_only:
        squares = squares / safe
    return jnp.concatenate([count, mean, squares], axis=0)


class Exchange:
    def __init__(self, rows_n, img_n, blocks):
        self.rows_n, self.img_n, self.blocks = rows_n, img_n, blocks
        self.calls = 0

    def __call__(
        self,
        kernel,
        ins,
        outs,
        merge,
        lines,
        widths,
        scratch=(),
        flops=0,
        edges=(),
        centres=None,
        edge=0,
        early=False,
        upto=None,
        defer=1,
        relay=None,
    ):
        ident, self.calls = self.calls, self.calls + 1
        total, dma = sum(widths), pltpu.SemaphoreType.DMA
        any_space = pl.BlockSpec(memory_space=pl.ANY)
        specs = [out_spec((lines, w), WHOLE, 1) for w in widths]
        shapes = [jax.ShapeDtypeStruct((lines, w), F32) for w in widths]
        extra = []
        upto = upto or self.blocks
        kept = upto < self.blocks
        if edges:
            middle = outs[edges[0][0]][0][-1]
            some = edge // self.blocks
            specs.append(any_space)
            shapes.append(jax.ShapeDtypeStruct((len(edges), upto * some, middle), BF16))
            extra += [
                ((len(edges), edge, middle), BF16),
                dma((len(edges), self.blocks)),
                dma((len(edges), self.blocks)),
                dma((len(edges),)),
            ]
        if centres:
            count, shape = len(centres[1]), outs[centres[0]][0]
            specs.append(any_space)
            shapes.append(jax.ShapeDtypeStruct((count,) + tuple(shape), F32))
            extra += [(tuple(shape), F32), dma((count,)), dma((count,)), dma((count,))]
        if kept:
            spec = pl.BlockSpec((len(edges), some, middle), lambda b: (0, jnp.maximum(b - upto, 0), 0))
            outs = outs + [((len(edges), edge - upto * some, middle), BF16, spec, True)]
        if relay:
            ins = ins + [(relay[0], APART)]
            specs.append(any_space)
            shapes.append(jax.ShapeDtypeStruct(relay[0].shape, BF16))
            extra += [dma((len(relay[1]),))] * 3
        extra += [
            ((self.rows_n, lines, total), F32),
            ((self.img_n, lines, total), F32),
            ((lines, total), F32),
            dma((self.rows_n,)),
            dma((self.rows_n,)),
            dma((self.img_n,)),
            dma((self.img_n,)),
        ]
        return call(
            functools.partial(
                self.kernel,
                kernel,
                len(ins),
                len(outs),
                len(scratch),
                merge,
                widths,
                edges,
                centres,
                early,
                upto,
                defer,
                relay[1] if relay else (),
            ),
            self.blocks,
            ins,
            outs,
            [((lines, total), F32)] + list(scratch) + extra,
            flops,
            specs,
            shapes,
            dict(collective_id=ident, has_side_effects=True),
        )

    def kernel(
        self,
        kernel,
        ins_n,
        outs_n,
        scratch_n,
        merge,
        widths,
        edges,
        centres,
        early,
        upto,
        defer,
        relay,
        *refs,
    ):
        kept = upto < self.blocks
        rows_n, img_n, blocks = self.rows_n, self.img_n, self.blocks
        refs = list(refs)

        def take(count):
            taken = refs[:count]
            del refs[:count]
            return taken

        ins, outs, totals = take(ins_n), take(outs_n), take(len(widths))
        halo = take(1)[0] if edges else None
        halo_centres = take(1)[0] if centres else None
        relayed = take(1)[0] if relay else None
        carried = ins.pop() if relay else None
        kept_rows = outs.pop() if kept else None
        mine = take(1)[0]
        scratch = take(scratch_n)
        if edges:
            edge_buf, edge_send, edge_recv, edge_local = take(4)
        if centres:
            centre_buf, centre_send, centre_recv, centre_local = take(4)
        if relay:
            relay_send, relay_recv, relay_local = take(3)
        buf_r, buf_i, part, send_r, recv_r, send_i, recv_i = refs
        block = pl.program_id(0)
        row, img = lax.axis_index("rows"), lax.axis_index("img")
        barrier = pltpu.get_barrier_semaphore()

        @pl.when(block == 0)
        def _():
            for k in range(1, rows_n):
                peer = {"rows": lax.rem(row + k, rows_n)}
                pl.semaphore_signal(barrier, inc=1, device_id=peer, device_id_type=MESH)
            for k in range(1, img_n):
                peer = {"img": lax.rem(img + k, img_n)}
                pl.semaphore_signal(barrier, inc=1, device_id=peer, device_id_type=MESH)

        def remote(source, target, send, recv, peer):
            return pltpu.make_async_remote_copy(
                src_ref=source,
                dst_ref=target,
                send_sem=send,
                recv_sem=recv,
                device_id=peer,
                device_id_type=MESH,
            )

        def sends(direction):
            return row < rows_n - 1 if direction > 0 else row > 0

        def receives(direction):
            return row > 0 if direction > 0 else row < rows_n - 1

        def edge_copy(e, b):
            some = edge_buf.shape[1] // blocks
            here = pl.ds(pl.multiple_of(b * some, some), some)
            return remote(
                edge_buf.at[e, here],
                halo.at[e, here],
                edge_send.at[e, b],
                edge_recv.at[e, b],
                {"rows": row + edges[e][3]},
            )

        def keep_edges():
            some = edge_buf.shape[1] // blocks
            here = pl.ds(pl.multiple_of(block * some, some), some)
            for e, (out, plane, last_row, _) in enumerate(edges):
                source = outs[out] if plane is None else outs[out].at[plane]
                for lanes in lane_blocks(source.shape[1]):
                    value = load(source, slice(None), lanes)
                    lines = value.reshape((some // 8, -1) + value.shape[1:])
                    store(edge_buf.at[e], here, lanes, lines[:, -1 if last_row else 0])
                if kept:
                    kept_rows[e] = edge_buf[e, here]

        def send_edges(b):
            for e, spec in enumerate(edges):

                @pl.when(sends(spec[3]))
                def _(e=e):
                    edge_copy(e, b).start()

        def relay_copy(k):
            peer = {"rows": row + relay[k]}
            return remote(carried.at[k], relayed.at[k], relay_send.at[k], relay_recv.at[k], peer)

        def relay_own(k):
            return pltpu.make_async_copy(carried.at[k], relayed.at[k], relay_local.at[k])

        def greet():
            @pl.when(block == 0)
            def _():
                pl.semaphore_wait(barrier, rows_n + img_n - 2)
                for k, direction in enumerate(relay):

                    @pl.when(sends(direction))
                    def _(k=k):
                        relay_copy(k).start()

                    @pl.when(jnp.logical_not(receives(direction)))
                    def _(k=k):
                        relay_own(k).start()

        def flush():
            greet()
            keep_edges()
            send_edges(block)

        if early:
            kernel(*ins, *outs, mine, *scratch, flush)
        else:
            kernel(*ins, *outs, mine, *scratch)
            greet()
            if edges:
                keep_edges()

                @pl.when(block < jnp.minimum(blocks - defer, upto))
                def _():
                    send_edges(block)

        if centres:
            centre_buf[pl.ds(block, 1)] = outs[centres[0]][...][None]

        def exchange(axis, me, peers, source, buf, send, recv, then=None):
            copies = []
            for k in range(1, peers):
                peer = {axis: lax.rem(me + k, peers)}
                copies.append(remote(source, buf.at[me], send.at[k], recv.at[me], peer))
                copies[-1].start()
            if then is not None:
                then()
            buf[pl.ds(me, 1)] = source[...][None]
            for k in range(1, peers):
                peer = lax.rem(me + k, peers)
                remote(source, buf.at[peer], send.at[k], recv.at[peer], {axis: peer}).wait_recv()
            return copies

        @pl.when(block == blocks - 1)
        def _():
            def centre_copy(k):
                peer = {"rows": row + centres[1][k]}
                return remote(
                    centre_buf, halo_centres.at[k], centre_send.at[k], centre_recv.at[k], peer
                )

            directions = centres[1] if centres else ()

            def rest():
                for k, direction in enumerate(directions):

                    @pl.when(sends(direction))
                    def _(k=k):
                        centre_copy(k).start()

                if edges and not early:
                    for b in range(blocks - defer, upto):
                        send_edges(b)

            copies = exchange("rows", row, rows_n, mine, buf_r, send_r, recv_r, rest)
            part[...] = merge_rows(buf_r, rows_n, merge, False)
            copies += exchange("img", img, img_n, part, buf_i, send_i, recv_i)
            total = merge_rows(buf_i, img_n, merge, True)
            start = 0
            for out, width in zip(totals, widths):
                out[...] = total[:, start : start + width]
                start += width
            for k, direction in enumerate(directions):
                own = pltpu.make_async_copy(centre_buf, halo_centres.at[k], centre_local.at[k])

                @pl.when(receives(direction))
                def _(k=k):
                    centre_copy(k).wait_recv()

                @pl.when(jnp.logical_not(receives(direction)))
                def _(own=own):
                    own.start()
                    own.wait()

                @pl.when(sends(direction))
                def _(k=k):
                    centre_copy(k).wait_send()

            for k, direction in enumerate(relay):

                @pl.when(receives(direction))
                def _(k=k):
                    relay_copy(k).wait_recv()

                @pl.when(jnp.logical_not(receives(direction)))
                def _(k=k):
                    relay_own(k).wait()

                @pl.when(sends(direction))
                def _(k=k):
                    relay_copy(k).wait_send()

            for e, spec in enumerate(edges):
                mine_kept = edge_buf.at[e, : halo.shape[1]]
                own = pltpu.make_async_copy(mine_kept, halo.at[e], edge_local.at[e])

                @pl.when(receives(spec[3]))
                def _(e=e):
                    for b in range(upto):
                        edge_copy(e, b).wait_recv()

                @pl.when(jnp.logical_not(receives(spec[3])))
                def _(own=own):
                    own.start()
                    own.wait()

                @pl.when(sends(spec[3]))
                def _(e=e):
                    for b in range(upto):
                        edge_copy(e, b).wait_send()

            for copy in copies:
                copy.wait_send()


CHUNK_ROWS = 64
CHUNK_LANES = 1024


HID_MID2, GA_OUT2, HID_IN2, VIEWS2, FIRST, GA_IN2, HID_MID1, GA_OUT1, GA_SKIP, VIEWS1 = range(10)
HID, PLANE, GA_IN1 = 10, 14, 18
ONE, TWO, HALF, QUAD, DEEP = range(5)
WIDTHS = {ONE: (512, 1024), TWO: (1024, 512), HALF: (512, 512), QUAD: (1024, 256), DEEP: (1024, 512)}


def plan_jobs():
    chunks = [[(ONE, 0, HID_MID2, 0, GA_OUT2, 1024 * k)] for k in range(2)]
    chunks += [[(ONE, 0, HID_IN2, 0, VIEWS2, 1024 * k)] for k in range(4)]
    chunks += [[(HALF, 0, HID_IN2, 0, VIEWS2, 4096), (HALF, 1, HID, 0, VIEWS1, 512)]]
    chunks += [[(QUAD, h, FIRST, 1024 * h, GA_IN2, 256 * k) for h in range(2)] for k in range(2)]
    chunks += [[(DEEP, p, PLANE + p, 0, GA_IN1 + p, 0) for p in range(4)]]
    chunks += [[(ONE, 0, HID_MID1, 0, GA_OUT1, 1024 * k)] for k in range(2)]
    chunks += [[(TWO, 0, PLANE, 0, GA_SKIP, 512 * k)] for k in range(4)]
    chunks += [[(ONE, 0, HID + 1, 0, VIEWS1, 512)], [(ONE, 0, HID + 2, 0, VIEWS1, 0)]]
    chunks += [[(ONE, 0, HID + 3, 0, VIEWS1, 1024 * k)] for k in range(2)]
    for k, job in zip((3, 4, 5), chunks[9]):
        chunks[k].append(job)
    chunks[9] = chunks[9][3:]
    return chunks


def weights_kernel(
    rows_n,
    hid_mid2,
    ga_out2,
    hid_in2,
    views2,
    first_low,
    ga_in2,
    hid_mid1,
    ga_out1,
    planes,
    ga_skip,
    hid_in1,
    views1,
    ga_in1,
    done,
    lhs_buf,
    rhs_buf,
    deep,
    chunk_buf,
    own,
    got1,
    got2a,
    got2b,
    got3a,
    got3b,
    got_low,
    got_high,
    lhs_sem,
    rhs_sem,
    *sems,
):
    (s1, r1, s2a, r2a, s2b, r2b, s3a, r3a, s3b, r3b, s_up, r_low, s_down, r_high, b_up, b_down, r_back) = sems
    sources = [hid_mid2, ga_out2, hid_in2, views2, first_low, ga_in2, hid_mid1, ga_out1, ga_skip, views1]
    for stack in (hid_in1, planes, ga_in1):
        sources += [stack.at[p] for p in range(4)]
    chunks = plan_jobs()
    jobs = [job for chunk in chunks for job in chunk]
    count = len(chunks)
    depth = chunk_buf.shape[0]
    img, z = lax.axis_index("img"), lax.axis_index("rows")
    y, x, c = img // 4, lax.rem(img // 2, 2), lax.rem(img, 2)
    root = rows_n // 2
    sibling = {"img": img + 1 - 2 * c}
    beside_x = {"img": img + 2 - 4 * x}
    beside_y = {"img": img + 4 - 8 * y}
    higher, lower = {"rows": z + 1}, {"rows": z - 1}
    half = CHUNK_LANES // 2
    left, right = slice(0, half), slice(half, 2 * half)

    def fetch(index):
        kind, _, lhs, lhs_start, rhs, rhs_start = jobs[index]
        lhs_width, rhs_width = WIDTHS[kind]
        slot = index % 2
        return (
            pltpu.make_async_copy(
                sources[lhs].at[:, lhs_start : lhs_start + lhs_width],
                lhs_buf.at[slot, :, :lhs_width],
                lhs_sem.at[slot],
            ),
            pltpu.make_async_copy(
                sources[rhs].at[:, rhs_start : rhs_start + rhs_width],
                rhs_buf.at[slot, :, :rhs_width],
                rhs_sem.at[slot],
            ),
        )

    for copy in fetch(0):
        copy.start()

    barrier = pltpu.get_barrier_semaphore()
    for peer in (sibling, beside_x, beside_y):
        pl.semaphore_signal(barrier, inc=1, device_id=peer, device_id_type=MESH)

    @pl.when(z > 0)
    def _():
        pl.semaphore_signal(barrier, inc=1, device_id=lower, device_id_type=MESH)

    @pl.when(z < rows_n - 1)
    def _():
        pl.semaphore_signal(barrier, inc=1, device_id=higher, device_id_type=MESH)

    pl.semaphore_wait(barrier, 3 + jnp.minimum(z, 1) + jnp.minimum(rows_n - 1 - z, 1))

    def put(slot, result, first, parts):
        width = CHUNK_LANES // parts
        rows = CHUNK_ROWS
        for m in range(result.shape[0] // (rows * parts)):
            shard = first + m
            for h in range(parts):
                piece = result[(m * parts + h) * rows : (m * parts + h + 1) * rows]
                chunk_buf[slot, shard // 4, shard // 2 % 2, shard % 2, :, h * width : (h + 1) * width] = piece

    def multiply(index, slot):
        kind, part = jobs[index][:2]
        lhs_width, rhs_width = WIDTHS[kind]
        here = index % 2

        def product():
            return lax.dot_general(
                lhs_buf[here, :, :lhs_width],
                rhs_buf[here, :, :rhs_width],
                (((0,), (0,)), ((), ())),
                preferred_element_type=F32,
            )

        if kind == ONE:
            put(slot, product().astype(BF16), 0, 1)
        elif kind == TWO:
            put(slot, product().astype(BF16), 0, 2)
        elif kind == QUAD:
            put(slot, product().astype(BF16), 4 * part, 4)
        elif kind == HALF:
            result = product().astype(BF16)
            for m in range(8):
                piece = result[m * CHUNK_ROWS : (m + 1) * CHUNK_ROWS]
                chunk_buf[slot, m // 4, m // 2 % 2, m % 2, :, (left, right)[part]] = piece
        elif part == 0:
            deep[...] = product()
        elif part == 3:
            put(slot, (deep[...] + product()).astype(BF16), 0, 2)
        else:
            deep[...] += product()

    def remote(source, target, send, recv, peer):
        return pltpu.make_async_remote_copy(
            src_ref=source,
            dst_ref=target,
            send_sem=send,
            recv_sem=recv,
            device_id=peer,
            device_id_type=MESH,
        )

    def to_core(t):
        source = chunk_buf.at[lax.rem(t, depth), :, :, 1 - c]
        return remote(source, got1.at[t], s1.at[t], r1.at[t], sibling)

    def to_2a(t):
        return remote(own.at[t, :, 1 - x, :, left], got2a.at[t], s2a.at[t], r2a.at[t], beside_x)

    def to_2b(t):
        return remote(own.at[t, 1 - y, :, :, right], got2b.at[t], s2b.at[t], r2b.at[t], beside_y)

    def to_3a(t):
        return remote(own.at[t, 1 - y, x, :, left], got3a.at[t], s3a.at[t], r3a.at[t], beside_y)

    def to_3b(t):
        return remote(own.at[t, y, 1 - x, :, right], got3b.at[t], s3b.at[t], r3b.at[t], beside_x)

    def up(t):
        return remote(own.at[t, y, x], got_low.at[t], s_up.at[t], r_low.at[t], higher)

    def down(t):
        return remote(own.at[t, y, x], got_high.at[t], s_down.at[t], r_high.at[t], lower)

    def back_up(t):
        return remote(done.at[t], done.at[t], b_up.at[t], r_back.at[t], higher)

    def back_down(t):
        return remote(done.at[t], done.at[t], b_down.at[t], r_back.at[t], lower)

    def compute(t):
        @pl.when(t >= depth)
        def _():
            to_core(t - depth).wait_send()

        slot = lax.rem(t, depth)
        index = 0
        for k, chunk in enumerate(chunks):
            first = index
            index += len(chunk)

            @pl.when(t == k)
            def _(first=first, chunk=chunk):
                for n in range(first, first + len(chunk)):
                    for copy in fetch(n):
                        copy.wait()
                    if n + 1 < len(jobs):
                        for copy in fetch(n + 1):
                            copy.start()
                    multiply(n, slot)

        to_core(t).start()

    def stage1(t):
        to_core(t).wait_recv()
        slot = lax.rem(t, depth)
        for a in range(2):
            for b in range(2):
                own[t, a, b] = chunk_buf[slot, a, b, c] + got1[t, a, b]
        to_2a(t).start()
        to_2b(t).start()

    def stage2(t):
        to_2a(t).wait_recv()
        for a in range(2):
            own[t, a, x, :, left] = own[t, a, x, :, left] + got2a[t, a]
        to_3a(t).start()
        to_2b(t).wait_recv()
        for a in range(2):
            own[t, y, a, :, right] = own[t, y, a, :, right] + got2b[t, a]
        to_3b(t).start()

    def stage3(t):
        to_3a(t).wait_recv()
        own[t, y, x, :, left] = own[t, y, x, :, left] + got3a[t]
        to_3b(t).wait_recv()
        own[t, y, x, :, right] = own[t, y, x, :, right] + got3b[t]

        @pl.when(z == 0)
        def _():
            up(t).start()

        @pl.when(z == rows_n - 1)
        def _():
            down(t).start()

    def stage4(t):
        @pl.when((z > 0) & (z < root))
        def _():
            up(t).wait_recv()
            own[t, y, x] = own[t, y, x] + got_low[t]
            up(t).start()

        @pl.when((z < rows_n - 1) & (z > root))
        def _():
            down(t).wait_recv()
            own[t, y, x] = own[t, y, x] + got_high[t]
            down(t).start()

    def stage5(t):
        @pl.when(z == root)
        def _():
            up(t).wait_recv()
            down(t).wait_recv()
            total = own[t, y, x].astype(F32) + got_low[t].astype(F32) + got_high[t].astype(F32)
            done[t] = total.astype(BF16)
            back_up(t).start()
            back_down(t).start()

    def stage6(t):
        @pl.when(z > root)
        def _():
            back_up(t).wait_recv()

            @pl.when(z < rows_n - 1)
            def _():
                back_up(t).start()

        @pl.when((z < root) & (z > 0))
        def _():
            back_down(t).wait_recv()
            back_down(t).start()

    def stage7(t):
        @pl.when(z == 0)
        def _():
            back_down(t).wait_recv()

    stages = (compute, stage1, stage2, stage3, stage4, stage5, stage6, stage7)

    order = [(k + 1, work) for k, work in enumerate(stages) if k] + [(0, compute)]

    def step(s, carry):
        for lag, work in order:
            t = s - lag

            @pl.when((t >= 0) & (t < count))
            def _(t=t, work=work):
                work(t)

        return carry

    lax.fori_loop(0, count + len(stages), step, 0)

    def finish(t, carry):
        @pl.when(t >= count - depth)
        def _():
            to_core(t).wait_send()

        for copy in (to_2a(t), to_2b(t), to_3a(t), to_3b(t)):
            copy.wait_send()

        @pl.when(z < root)
        def _():
            up(t).wait_send()

        @pl.when(z > root)
        def _():
            down(t).wait_send()

        @pl.when((z >= root) & (z < rows_n - 1))
        def _():
            back_up(t).wait_send()

        @pl.when((z <= root) & (z > 0))
        def _():
            back_down(t).wait_send()

        return carry

    lax.fori_loop(0, count, finish, 0)


def summed_weights(rows_n, ident, operands):
    count = len(plan_jobs())
    low = operands[0].shape[0]
    rows, lanes = CHUNK_ROWS, CHUNK_LANES
    dma = pltpu.SemaphoreType.DMA
    depth = 3
    buffers = [
        (2, low, 1024),
        (2, low, 1024),
        None,
        (depth, 2, 2, 2, rows, lanes),
        (count, 2, 2, rows, lanes),
        (count, 2, 2, rows, lanes),
        (count, 2, rows, lanes // 2),
        (count, 2, rows, lanes // 2),
        (count, rows, lanes // 2),
        (count, rows, lanes // 2),
        (count, rows, lanes),
        (count, rows, lanes),
    ]
    scratch = [pltpu.VMEM(b, BF16) if b else pltpu.VMEM((1024, 512), F32) for b in buffers]
    return pl.pallas_call(
        functools.partial(weights_kernel, rows_n),
        in_specs=[pl.BlockSpec(memory_space=pl.ANY)] * len(operands),
        out_specs=pl.BlockSpec(memory_space=pltpu.VMEM),
        out_shape=jax.ShapeDtypeStruct((count, rows, lanes), BF16),
        scratch_shapes=scratch + [dma((2,)), dma((2,))] + [dma((count,))] * 17,
        compiler_params=pltpu.CompilerParams(
            collective_id=ident, has_side_effects=True, vmem_limit_bytes=63 * 1024 * 1024
        ),
        cost_estimate=pl.CostEstimate(
            flops=40_000_000_000, bytes_accessed=100_000_000, transcendentals=0
        ),
    )(*operands)


def unpack_kernel(sums_n, done, *refs):
    sums, outs = refs[:sums_n], refs[sums_n:]
    in1, mid1, out1, skip, in2, mid2, out2 = outs[:7]
    rows, lanes = CHUNK_ROWS, CHUNK_LANES
    half = lanes // 2

    def wide(k):
        return done[k].astype(F32)

    def stacked(first, count, parts, out):
        width = lanes // parts
        for k in range(count):
            for h in range(parts):
                piece = done[first + k, :, h * width : (h + 1) * width]
                out[h * rows : (h + 1) * rows, k * width : (k + 1) * width] = piece.astype(F32)

    for k in range(2):
        out2[:, k * lanes : (k + 1) * lanes] = wide(k)
        out1[:, k * lanes : (k + 1) * lanes] = wide(10 + k)
    taps2 = [(2 + k // 2, k % 2) for k in range(8)] + [(6, 0)]
    taps1 = [(19, 1), (17, 0), (18, 0), (16, 1), (6, 1), (16, 0), (19, 0), (17, 1), (18, 1)]
    for out, taps in ((mid1, taps1), (mid2, taps2)):
        for k, (chunk, side) in enumerate(taps):
            out[k] = done[chunk, :, side * half : (side + 1) * half].astype(F32)
    stacked(7, 2, 4, in2)
    stacked(9, 1, 2, in1)
    stacked(12, 4, 2, skip)
    rest = list(outs[7:])
    for ref in sums:
        for k in range(ref.shape[0]):
            rest.pop(0)[...] = ref[k : k + 1, :]


def unpack(done, sums):
    rows = CHUNK_ROWS
    shapes = [(128, 512), (9, rows, 512), (rows, 2048), (128, 2048), (256, 512), (9, rows, 512), (rows, 2048)]
    shapes += [(1, x.shape[1]) for x in sums for _ in range(x.shape[0])]
    vmem = pl.BlockSpec(memory_space=pltpu.VMEM)
    outs = pl.pallas_call(
        functools.partial(unpack_kernel, len(sums)),
        in_specs=[vmem] * (1 + len(sums)),
        out_specs=[vmem] * len(shapes),
        out_shape=[jax.ShapeDtypeStruct(shape, F32) for shape in shapes],
        compiler_params=pltpu.CompilerParams(vmem_limit_bytes=32 * 1024 * 1024),
    )(done, *sums)
    return outs[:7], [x.reshape(-1) for x in outs[7:]]


def masks_kernel(rows_low, extent, mask_in, mask_out, mask_above, mask_edges):
    side = extent[...]
    side_low = side // 2
    low0 = lax.axis_index("rows") * rows_low
    column = lax.broadcasted_iota(jnp.int32, side.shape, 1)

    def inside(row, col, limit):
        kept = (row >= 0) & (row < limit) & (col < limit)
        return jnp.where(kept, 1.0, 0.0).astype(BF16)

    for i in range(rows_low):
        for p in range(2):
            for q in range(2):
                mask_in[2 * p + q, :, i] = inside(2 * (low0 + i) + p, 2 * column + q, side)
        mask_out[:, i] = inside(low0 + i, column, side_low)
    for q in range(2):
        mask_above[q, :, 0] = inside(2 * low0 - 1, 2 * column + q, side)
    mask_edges[0, :, 0] = inside(low0 - 1, column, side_low)
    mask_edges[1, :, 0] = inside(low0 + rows_low, column, side_low)


def masks_of(extent, rows_low):
    images, columns, lanes = extent.shape
    vmem = pl.BlockSpec(memory_space=pltpu.VMEM)
    shapes = [
        (4, images, rows_low, columns, lanes),
        (images, rows_low, columns, lanes),
        (2, images, 1, columns, lanes),
        (2, images, 1, columns, lanes),
    ]
    return pl.pallas_call(
        functools.partial(masks_kernel, rows_low),
        in_specs=[vmem],
        out_specs=[vmem] * 4,
        out_shape=[jax.ShapeDtypeStruct(shape, BF16) for shape in shapes],
        compiler_params=pltpu.CompilerParams(vmem_limit_bytes=24 * 1024 * 1024),
    )(extent)


def body(
    image_in,
    extent,
    weight_in1,
    weight_mid1,
    weight_out1,
    weight_skip,
    weight_in2,
    weight_mid2,
    weight_out2,
    gain_in1,
    shift_in1,
    gain_mid1,
    shift_mid1,
    gain_out1,
    shift_out1,
    gain_skip,
    shift_skip,
    gain_in2,
    shift_in2,
    gain_mid2,
    shift_mid2,
    gain_out2,
    shift_out2,
    cotangent,
):
    images, rows_here, columns, inputs = image_in.shape
    middle, outputs = weight_out1.shape
    rows_low, cols_low = rows_here // 2, columns // 2
    low = images * rows_low * cols_low
    rows_n, img_n = lax.axis_size("rows"), lax.axis_size("img")
    blocks = images // IMAGES
    per_block = low // blocks
    edge = images * cols_low
    run = Exchange(rows_n, img_n, blocks)
    upto = 3 * blocks // 5

    def early_blocks(x):
        shape = (x.shape[0], edge // blocks, x.shape[2])
        return x, pl.BlockSpec(shape, lambda b: (0, jnp.minimum(b, upto - 1), 0))

    def late_blocks(x):
        shape = (x.shape[0], edge // blocks, x.shape[2])
        return x, pl.BlockSpec(shape, lambda b: (0, jnp.maximum(b - upto, 0), 0))


    columns8 = jnp.broadcast_to(extent[:, None, None], (images, cols_low, 128))
    mask_in, mask_out, mask_above, mask_edges = (
        m.reshape(m.shape[:-4] + (-1, 128)) for m in masks_of(columns8, rows_low)
    )

    group_images = 256 // (rows_here * columns)
    order = np.arange(256).reshape(group_images, rows_low, 2, cols_low, 2)
    order = order.transpose(2, 4, 0, 1, 3).reshape(-1)
    perm = jnp.asarray(np.eye(256, dtype=np.float32)[order], BF16)

    def row(vector):
        return vector.reshape(1, -1)

    g_in1, s_in1, g_mid1, s_mid1 = row(gain_in1), row(shift_in1), row(gain_mid1), row(shift_mid1)
    g_out1, s_out1, g_skip, s_skip = row(gain_out1), row(shift_out1), row(gain_skip), row(shift_skip)
    g_in2, s_in2, g_mid2, s_mid2 = row(gain_in2), row(shift_in2), row(gain_mid2), row(shift_mid2)
    g_out2, s_out2 = row(gain_out2), row(shift_out2)
    kernel_mid1 = weight_mid1.transpose(1, 2, 0, 3).reshape(9 * middle, middle)
    kernel_mid2 = weight_mid2.transpose(1, 2, 0, 3).reshape(9 * middle, middle)
    cot = cotangent.reshape(low, outputs)

    dev_mid_out = [((low, middle), BF16, BY_ROWS), ((blocks, 1, middle), F32, BY_BLOCK)]
    dev_out_out = [((low, outputs), BF16, BY_ROWS), ((blocks, 1, outputs), F32, BY_BLOCK)]
    hidden_out = [((low, middle), BF16, BY_ROWS)]
    wide_out = [((low, outputs), BF16, BY_ROWS)]
    late_mid, late_wide = [hidden_out[0] + (True,)], [wide_out[0] + (True,)]
    acc_mid, acc_out = ((per_block, middle), F32), ((per_block, outputs), F32)
    unit_flops = 2 * low * middle * middle

    def normal(dev, centre, stats, gain, shift, kind=BY_ROWS):
        return [(dev, kind), (centre, BY_BLOCK), (stats, WHOLE), (gain, WHOLE), (shift, WHOLE)]

    planes, d_in1, c_in1, d_skip, c_skip, n_in1, n_skip, halo_in1, halo_c_in1 = run(
        open_kernel,
        [
            (image_in.reshape(4 * low, inputs), BY_ROWS),
            (perm, WHOLE),
            (mask_in, BY_PLANES),
            (mask_out, BY_ROWS),
            (weight_in1, WHOLE),
            (weight_skip, WHOLE),
        ],
        [
            ((4, low, inputs), BF16, BY_PLANES, True),
            ((4, low, middle), BF16, BY_PLANES),
            ((blocks, 1, middle), F32, BY_BLOCK),
        ]
        + dev_out_out,
        True,
        3,
        (middle, outputs),
        scratch=[((4, per_block, middle), F32), acc_out],
        flops=20 * unit_flops,
        edges=[(1, 2, True, 1), (1, 3, True, 1)],
        centres=(2, (1,)),
        edge=edge,
        early=True,
    )
    hid_in1, d_mid1, c_mid1, edges_mid1, n_mid1, halo_mid1, halo_c_mid1 = run(
        functools.partial(mid1_kernel, rows_low),
        [
            (d_in1, BY_PLANES),
            (c_in1, BY_BLOCK),
            (mask_in, BY_PLANES),
            (halo_in1, BY_PLANES),
            (halo_c_in1[0], BY_BLOCK),
            (mask_above, BY_PLANES),
            (n_in1, WHOLE),
            (g_in1, WHOLE),
            (s_in1, WHOLE),
            (mask_out, BY_ROWS),
            (kernel_mid1, WHOLE),
        ],
        [((4, low, middle), BF16, BY_PLANES, True)] + dev_mid_out,
        True,
        3,
        (middle,),
        scratch=[((5, per_block, middle), BF16), acc_mid],
        flops=9 * unit_flops,
        edges=[(1, None, False, -1)],
        upto=upto,
        centres=(2, (-1,)),
        edge=edge,
    )
    hid_mid1, d_out1, c_out1, n_out1 = run(
        expand_kernel,
        normal(d_mid1, c_mid1, n_mid1, g_mid1, s_mid1) + [(mask_out, BY_ROWS), (weight_out1, WHOLE)],
        late_mid + dev_out_out,
        True,
        3,
        (outputs,),
        scratch=[acc_out],
        flops=4 * unit_flops,
    )
    join = normal(d_out1, c_out1, n_out1, g_out1, s_out1) + normal(d_skip, c_skip, n_skip, g_skip, s_skip)
    both = [(1, None, True, 1), (1, None, False, -1)]
    first_low, d_in2, c_in2, n_in2, halo_in2, halo_c_in2 = run(
        join_kernel,
        join + [(mask_out, BY_ROWS), (weight_in2, WHOLE)],
        wide_out + dev_mid_out,
        True,
        3,
        (middle,),
        scratch=[acc_mid],
        flops=4 * unit_flops,
        defer=2,
        edges=both,
        centres=(2, (1, -1)),
        edge=edge,
    )

    hid_in2, d_mid2, c_mid2, edges_mid2, n_mid2, halo_mid2, halo_c_mid2 = run(
        functools.partial(mid2_kernel, rows_low),
        [
            (d_in2, BY_ROWS),
            (c_in2, BY_BLOCK),
            (halo_in2, BY_PLANES),
            (halo_c_in2, PAIR_BLOCK),
            (mask_edges, BY_PLANES),
            (n_in2, WHOLE),
            (g_in2, WHOLE),
            (s_in2, WHOLE),
            (mask_out, BY_ROWS),
            (kernel_mid2, WHOLE),
        ],
        late_mid + dev_mid_out,
        True,
        3,
        (middle,),
        scratch=[((per_block, 9 * middle), BF16), acc_mid],
        flops=9 * unit_flops,
        edges=both,
        upto=upto,
        centres=(2, (1, -1)),
        edge=edge,
    )
    hid_mid2, d_out2, c_out2, n_out2 = run(
        expand_kernel,
        normal(d_mid2, c_mid2, n_mid2, g_mid2, s_mid2) + [(mask_out, BY_ROWS), (weight_out2, WHOLE)],
        late_mid + dev_out_out,
        True,
        3,
        (outputs,),
        scratch=[acc_out],
        flops=4 * unit_flops,
    )
    block_out, gn_out2, z_out2, rest_mid2 = run(
        final_kernel,
        normal(d_out2, c_out2, n_out2, g_out2, s_out2)
        + [(first_low, BY_ROWS), (cot, BY_ROWS), (mask_out, BY_ROWS)],
        late_wide + wide_out,
        False,
        2,
        (outputs,),
        relay=(edges_mid2, (1, -1)),
    )

    ga_out2, gn_mid2, z_mid2, halo_gn_mid2 = run(
        back_expand_kernel,
        [
            (gn_out2, BY_ROWS),
            (d_out2, BY_ROWS),
            (c_out2, BY_BLOCK),
            (n_out2, WHOLE),
            (g_out2, WHOLE),
            (z_out2, WHOLE),
            (mask_out, BY_ROWS),
            (weight_out2, WHOLE),
        ]
        + normal(d_mid2, c_mid2, n_mid2, g_mid2, s_mid2),
        late_wide + hidden_out,
        False,
        2,
        (middle,),
        scratch=[acc_mid],
        flops=4 * unit_flops,
        defer=2,
        edges=both,
        edge=edge,
    )
    views2, gn_in2, z_in2 = run(
        functools.partial(back_mid2_kernel, rows_low, upto),
        [
            (gn_mid2, BY_ROWS),
            (d_mid2, BY_ROWS),
            (c_mid2, BY_BLOCK),
            (halo_gn_mid2, BY_PLANES),
            early_blocks(halo_mid2),
            late_blocks(rest_mid2),
            (halo_c_mid2, PAIR_BLOCK),
            (mask_edges, BY_PLANES),
            (n_mid2, WHOLE),
            (g_mid2, WHOLE),
            (z_mid2, WHOLE),
            (mask_out, BY_ROWS),
            (kernel_mid2, WHOLE),
        ]
        + normal(d_in2, c_in2, n_in2, g_in2, s_in2),
        [((low, 9 * middle), BF16, BY_ROWS, True)] + hidden_out,
        False,
        2,
        (middle,),
        scratch=[acc_mid],
        flops=9 * unit_flops,
    )
    ga_in2, gs1, z_sum1, rest_mid1 = run(
        back_join_kernel,
        [
            (gn_in2, BY_ROWS),
            (d_in2, BY_ROWS),
            (c_in2, BY_BLOCK),
            (n_in2, WHOLE),
            (g_in2, WHOLE),
            (z_in2, WHOLE),
            (mask_out, BY_ROWS),
            (weight_in2, WHOLE),
            (gn_out2, BY_ROWS),
        ]
        + join,
        late_mid + wide_out,
        False,
        3,
        (outputs,),
        relay=(edges_mid1, (-1,)),
        scratch=[acc_out],
        flops=4 * unit_flops,
    )

    ga_out1, ga_skip, gn_mid1, grad_skip_in, z_mid1, halo_gn_mid1 = run(
        back_split_kernel,
        [
            (gs1, BY_ROWS),
            (d_out1, BY_ROWS),
            (c_out1, BY_BLOCK),
            (n_out1, WHOLE),
            (g_out1, WHOLE),
            (d_skip, BY_ROWS),
            (c_skip, BY_BLOCK),
            (n_skip, WHOLE),
            (g_skip, WHOLE),
            (z_sum1, WHOLE),
            (mask_out, BY_ROWS),
            (weight_out1, WHOLE),
            (weight_skip, WHOLE),
        ]
        + normal(d_mid1, c_mid1, n_mid1, g_mid1, s_mid1),
        late_wide + late_wide + hidden_out + [((low, inputs), BF16, BY_ROWS, True)],
        False,
        2,
        (middle,),
        scratch=[acc_mid, ((per_block, inputs), F32)],
        flops=12 * unit_flops,
        edges=[(2, None, False, -1)],
        edge=edge,
    )
    views1, gn_in1, z_in1 = run(
        functools.partial(back_mid1_kernel, rows_low, upto),
        [
            (gn_mid1, BY_ROWS),
            (d_mid1, BY_ROWS),
            (c_mid1, BY_BLOCK),
            (halo_gn_mid1[0], BY_ROWS),
            early_blocks(halo_mid1),
            late_blocks(rest_mid1),
            (halo_c_mid1[0], BY_BLOCK),
            (mask_edges[1], BY_ROWS),
            (n_mid1, WHOLE),
            (g_mid1, WHOLE),
            (z_mid1, WHOLE),
            (mask_out, BY_ROWS),
            (kernel_mid1, WHOLE),
            (d_in1, BY_PLANES),
            (c_in1, BY_BLOCK),
            (mask_in, BY_PLANES),
            (n_in1, WHOLE),
            (g_in1, WHOLE),
            (s_in1, WHOLE),
        ],
        [((low, 4 * middle), BF16, BY_ROWS, True), ((4, low, middle), BF16, BY_PLANES)],
        False,
        2,
        (middle,),
        scratch=[((4, per_block, middle), F32)],
        flops=9 * unit_flops,
    )
    ga_in1, grad_image, block_out = stage(
        back_image_kernel,
        blocks,
        [
            (gn_in1, BY_PLANES),
            (d_in1, BY_PLANES),
            (c_in1, BY_BLOCK),
            (n_in1, WHOLE),
            (g_in1, WHOLE),
            (z_in1, WHOLE),
            (mask_in, BY_PLANES),
            (weight_in1, WHOLE),
            (grad_skip_in, BY_ROWS),
            (perm, WHOLE),
            (block_out, BY_ROWS),
        ],
        [((4, low, middle), BF16, BY_PLANES, True), ((4 * low, inputs), BF16, BY_ROWS)] + wide_out,
        scratch=[((4, per_block, inputs), BF16)],
        flops=12 * unit_flops,
    )
    sums = [z_in1, z_mid1, z_sum1, z_in2, z_mid2, z_out2]

    if (rows_n, img_n) == (4, 8):
        done = summed_weights(
            rows_n,
            run.calls,
            [
                hid_mid2,
                ga_out2,
                hid_in2,
                views2,
                first_low,
                ga_in2,
                hid_mid1,
                ga_out1,
                planes,
                ga_skip,
                hid_in1,
                views1,
                ga_in1,
            ],
        )
        grads, rows_of = unpack(done, sums)
        dw_in1, dw_mid1, dw_out1, dw_skip, dw_in2, dw_mid2, dw_out2 = grads
        dw_mid1, dw_mid2 = (
            g.reshape(3, 3, -1, middle).transpose(2, 0, 1, 3) for g in (dw_mid1, dw_mid2)
        )
    else:
        def weight_term(values, upstream):
            return lax.dot_general(
                values, upstream, (((0,), (0,)), ((), ())), preferred_element_type=F32
            ).astype(BF16)

        def reduced(grad):
            shard = lax.psum_scatter(grad, "img", scatter_dimension=0, tiled=True)
            return lax.psum(shard, "rows").astype(F32)

        dw_out2 = reduced(weight_term(hid_mid2, ga_out2))
        dw_mid2 = reduced(weight_term(hid_in2, views2))
        dw_in2 = reduced(weight_term(first_low, ga_in2))
        dw_out1 = reduced(weight_term(hid_mid1, ga_out1))
        dw_skip = reduced(weight_term(planes[0], ga_skip))
        m = middle
        dw_00 = weight_term(hid_in1[0], views1[:, m : 2 * m])
        dw_01 = weight_term(hid_in1[1], views1[:, m : 3 * m])
        dw_10 = weight_term(hid_in1[2], views1[:, : 2 * m])
        dw_11 = weight_term(hid_in1[3], views1)
        dw_mid1 = jnp.concatenate(
            [
                dw_11[:, 3 * m :],
                dw_10[:, :m],
                dw_11[:, :m],
                dw_01[:, m:],
                dw_00,
                dw_01[:, :m],
                dw_11[:, 2 * m : 3 * m],
                dw_10[:, m:],
                dw_11[:, m : 2 * m],
            ],
            axis=1,
        )
        dw_mid1 = reduced(dw_mid1)
        dw_in1 = reduced(
            weight_term(planes.reshape(4 * low, inputs), ga_in1.reshape(4 * low, middle))
        )
        rows_of = [x[k] for x in sums for k in range(x.shape[0])]
    kernel_shape = (middle // img_n, 3, 3, middle)
    (
        shift_in1_g,
        gain_in1_g,
        shift_mid1_g,
        gain_mid1_g,
        shift_sum1_g,
        gain_out1_g,
        gain_skip_g,
        shift_in2_g,
        gain_in2_g,
        shift_mid2_g,
        gain_mid2_g,
        shift_out2_g,
        gain_out2_g,
    ) = rows_of
    return (
        block_out.reshape(images, rows_low, cols_low, outputs),
        grad_image.reshape(images, rows_here, columns, inputs),
        dw_in1,
        dw_mid1.reshape(kernel_shape),
        dw_out1,
        dw_skip,
        dw_in2,
        dw_mid2.reshape(kernel_shape),
        dw_out2,
        gain_in1_g,
        shift_in1_g,
        gain_mid1_g,
        shift_mid1_g,
        gain_out1_g,
        shift_sum1_g,
        gain_skip_g,
        shift_sum1_g,
        gain_in2_g,
        shift_in2_g,
        gain_mid2_g,
        shift_mid2_g,
        gain_out2_g,
        shift_out2_g,
    )


def solution(mesh):
    image = P("img", "rows", None, None)
    in_specs = (image, P("img")) + (P(),) * 21 + (image,)
    out_specs = (
        image,
        image,
        P("img", None),
        P("img", None, None, None),
        P("img", None),
        P("img", None),
        P("img", None),
        P("img", None, None, None),
        P("img", None),
    ) + (P(),) * 14
    return jax.shard_map(body, mesh=mesh, in_specs=in_specs, out_specs=out_specs, check_vma=False)
```
